32 devices in a mesh: expert: 8 (over z, x), tensor: 4 (over y, core).
Axes of the slice: x: 2, y: 2, z: 4, core: 2. Of those that a mesh axis runs over, the one named last changes fastest.
Arguments:
- tokens: bfloat16 [2, 1024, 768], P(None, 'expert'), may hold values from -6 to 6
- out_grad: bfloat16 [2, 1024, 768], P(None, 'expert'), may hold values from -6 to 6
- routes: int32 [2, 1024, 2], P(None, 'expert'), may hold values from 0 to 7, as said below
- lengths: int32 [2, 7], replicated, may hold values from 1 to 512, 1024 in all within a row
- parents: int32 [2, 7], replicated, may hold values from 0 to 5, as said below
- attn_gain: bfloat16 [768], P('expert'), may hold values from 0.5 to 1.5
- ffn_gain: bfloat16 [768], P('expert'), may hold values from 0.5 to 1.5
- w_query: bfloat16 [768, 768], P('expert', 'tensor'), may hold values from -0.21875 to 0.21875
- w_key: bfloat16 [768, 768], P('expert', 'tensor'), may hold values from -0.21875 to 0.21875
- w_value: bfloat16 [768, 768], P('expert', 'tensor'), may hold values from -0.21875 to 0.21875
- w_out: bfloat16 [768, 768], P('tensor', 'expert'), may hold values from -0.875 to 0.875
- router: bfloat16 [768, 8], P('expert'), may hold values from -0.15625 to 0.15625
- shared_gate: bfloat16 [768, 2048], P('expert', 'tensor'), may hold values from -0.21875 to 0.21875
- shared_up: bfloat16 [768, 2048], P('expert', 'tensor'), may hold values from -0.21875 to 0.21875
- shared_down: bfloat16 [2048, 768], P('tensor', 'expert'), may hold values from -0.125 to 0.125
- expert_gate: bfloat16 [8, 768, 2048], P('expert', None, 'tensor'), may hold values from -0.21875 to 0.21875
- expert_up: bfloat16 [8, 768, 2048], P('expert', None, 'tensor'), may hold values from -0.21875 to 0.21875
- expert_down: bfloat16 [8, 2048, 768], P('expert', 'tensor'), may hold values from -0.125 to 0.125
Outputs:
- out: bfloat16 [2, 1024, 768], P(None, 'expert')
- grad_tokens: float32 [2, 1024, 768], P(None, 'expert')
- grad_attn_gain: float32 [768], P('expert')
- grad_ffn_gain: float32 [768], P('expert')
- grad_w_query: float32 [768, 768], P('expert', 'tensor')
- grad_w_key: float32 [768, 768], P('expert', 'tensor')
- grad_w_value: float32 [768, 768], P('expert', 'tensor')
- grad_w_out: float32 [768, 768], P('tensor', 'expert')
- grad_router: float32 [768, 8], P('expert')
- grad_shared_gate: float32 [768, 2048], P('expert', 'tensor')
- grad_shared_up: float32 [768, 2048], P('expert', 'tensor')
- grad_shared_down: float32 [2048, 768], P('tensor', 'expert')
- grad_expert_gate: float32 [8, 768, 2048], P('expert', None, 'tensor')
- grad_expert_up: float32 [8, 768, 2048], P('expert', None, 'tensor')
- grad_expert_down: float32 [8, 2048, 768], P('expert', 'tensor')
The draws below stay inside these ranges and needn't reach their ends.
Inputs may be any that keep to these rules, and one draw needn't show every extreme that they name: In each aligned block of 128 rows of routes (the rows of one device in one micro-batch) the two experts of a token differ, no expert is named more than 64 times, and some expert is named exactly 64 times in every block. parents[m, s] < s for s >= 1 and parents[m, 0] = 0, so every path ends at segment 0; the last segment's parent is segment 7 - 2.
All inputs are finite; a program needn't handle non-finite values.
Results may differ from the reference program's by a relative error of at most 0.017.
Values may be sent and summed in bfloat16 or wider, within the bound.
A program may use at most 192 MiB of HBM per device.

```python
import math
import jax
import jax.numpy as jnp
import numpy as np
from jax import lax

D = 768
HEADS = 12
HEAD = 64
FFE = 2048
FS = 2048
ROWS = 128
MB = 2
SEGS = 7
EXPERTS = 8
OWNERS = 1
CAP = 64
TREE = 1024
MOST = 512


def draw_routes(key, part):
    key = jax.random.fold_in(key, 7)
    hot_key, order_key, block_key = jax.random.split(key, 3)
    hot_expert = jax.random.randint(hot_key, (), 0, EXPERTS).astype(jnp.int32)
    expert_order = jax.random.permutation(order_key, EXPERTS - 1).astype(jnp.int32)
    others = expert_order + (expert_order >= hot_expert).astype(jnp.int32)
    spare_rows = ROWS - CAP
    tickets = jnp.repeat(jnp.arange(EXPERTS - 1, dtype=jnp.int32), CAP)

    def one_block(block_seed):
        shuffle_key, rows_key, swap_key = jax.random.split(block_seed, 3)
        taken_ids = jnp.sort(jax.random.permutation(shuffle_key, tickets)[:2 * ROWS - CAP])
        named_ids = jnp.take(others, taken_ids)
        first_pick = jnp.concatenate([named_ids[:spare_rows], jnp.full((CAP,), hot_expert, jnp.int32)])
        second_pick = named_ids[spare_rows:]
        pair_ids = jnp.stack([first_pick, second_pick], axis=1)
        pair_ids = jnp.take(pair_ids, jax.random.permutation(rows_key, ROWS), axis=0)
        flip_bits = jax.random.randint(swap_key, (ROWS, 1), 0, 2)
        return jnp.where(flip_bits == 1, pair_ids[:, ::-1], pair_ids)
    block_keys = jax.random.split(block_key, MB * TREE // ROWS)
    return jax.vmap(one_block)(block_keys).reshape(MB, TREE, 2).astype(jnp.int32)


def draw_parents(key, part):
    key = jax.random.fold_in(key, 13)
    depth_index = jnp.arange(SEGS, dtype=jnp.int32)
    raw_picks = jax.random.randint(key, (MB, SEGS), 0, 1 << 20)
    chosen = raw_picks % jnp.maximum(depth_index, 1)[None, :]
    chosen = jnp.where(depth_index[None, :] == SEGS - 1, SEGS - 2, chosen)
    return chosen.astype(jnp.int32)


def steps_of(rng, dims, cuts, least, high):
    def one(dim, parts):
        draws = jax.random.uniform(jax.random.fold_in(jax.random.fold_in(rng, 6), dim), (parts,), jnp.float32, least / len(cuts), high / len(cuts))
        return jnp.repeat(jnp.exp(draws), dims[dim] // parts).reshape((-1,) + (1,) * (len(dims) - dim - 1))

    loudness = one(*cuts[0])
    for cut in cuts[1:]:
        loudness = loudness * one(*cut)
    return loudness


def split_up(count, total, bound, skew):
    weights = [(1 << 20) // math.isqrt(grade ** skew) + 1 for grade in range(2, count + 1)]
    rest, given = total - bound - (count - 1), [1] * (count - 1)
    while rest > 0:
        candidates = [i for i in range(count - 1) if given[i] < bound]
        pool, budget = sum([weights[i] for i in candidates]), rest
        for i in candidates:
            extra = min(bound - given[i], max(1, budget * weights[i] // pool), rest)
            given[i] = given[i] + extra
            rest = rest - extra
    return np.array([bound] + given)


def ragged(stream_key, number_of, total, limit, lean):
    if number_of == 2:
        one = jax.random.randint(stream_key, (), max(1, total - limit), min(limit, total - 1) + 1)
        return jnp.stack([one, total - one])
    sizes = jnp.asarray(split_up(number_of, total, limit, lean), jnp.int32)
    pairs = (number_of - 1) // 2
    donor, receiver = sizes[1:1 + 2 * pairs:2], sizes[2:2 + 2 * pairs:2]
    room = jnp.minimum(donor - 1, limit - receiver)
    moved = jax.random.randint(jax.random.fold_in(stream_key, 1), (pairs,), 0, 1 << 20) % (room + 1)
    sizes = sizes.at[1:1 + 2 * pairs:2].set(donor - moved).at[2:2 + 2 * pairs:2].set(receiver + moved)
    return sizes[jax.random.permutation(jax.random.fold_in(stream_key, 2), number_of)]


def centred(rng, shape, deviation, most, cuts=(), kind=jnp.bfloat16):
    entries = deviation * jax.random.normal(rng, shape, jnp.float32)
    if cuts:
        entries = entries * steps_of(rng, shape, cuts, -0.22, 0.18)
    return jnp.clip(entries, -most, most).astype(kind)


def setup_inputs(seed: int = 0) -> dict:
    key_of = jax.random.split(jax.random.key(seed), 19)
    tokens = centred(key_of[0], (MB, TREE, D), 1.0, 6.0, ((1, 8),))
    out_grad = centred(key_of[1], (MB, TREE, D), 1.0, 6.0, ((1, 8),))
    routes = draw_routes(jax.random.fold_in(key_of[18], 71), 0)
    lengths = jax.vmap(lambda own: ragged(own, SEGS, TREE, MOST, 2))(jax.random.split(key_of[3], MB)).reshape((MB, SEGS)).astype(jnp.int32)
    parents = draw_parents(jax.random.fold_in(key_of[18], 71), 0)
    attn_gain = jnp.clip(1.0 + 0.1 * jax.random.normal(key_of[5], (D,), jnp.float32), 0.5, 1.5).astype(jnp.bfloat16)
    ffn_gain = jnp.clip(1.0 + 0.1 * jax.random.normal(key_of[6], (D,), jnp.float32), 0.5, 1.5).astype(jnp.bfloat16)
    w_query = centred(key_of[7], (D, D), D ** -0.5, 0.21875, ((0, 8), (1, 4)))
    w_key = centred(key_of[8], (D, D), D ** -0.5, 0.21875, ((0, 8), (1, 4)))
    w_value = centred(key_of[9], (D, D), D ** -0.5, 0.21875, ((0, 8), (1, 4)))
    w_out = centred(key_of[10], (D, D), (max(1, D * 64 // TREE)) ** -0.5, 0.875, ((0, 4), (1, 8)))
    router = centred(key_of[11], (D, EXPERTS), (2 * D) ** -0.5, 0.15625, ((0, 8),))
    shared_gate = centred(key_of[12], (D, FS), D ** -0.5, 0.21875, ((0, 8), (1, 4)))
    shared_up = centred(key_of[13], (D, FS), D ** -0.5, 0.21875, ((0, 8), (1, 4)))
    shared_down = centred(key_of[14], (FS, D), FS ** -0.5, 0.125, ((0, 4), (1, 8)))
    expert_gate = centred(key_of[15], (EXPERTS * OWNERS, D, FFE // OWNERS), D ** -0.5, 0.21875, ((0, 8), (2, 4)))
    expert_up = centred(key_of[16], (EXPERTS * OWNERS, D, FFE // OWNERS), D ** -0.5, 0.21875, ((0, 8), (2, 4)))
    expert_down = centred(key_of[17], (EXPERTS * OWNERS, FFE // OWNERS, D), FFE ** -0.5, 0.125, ((0, 8), (1, 4)))
    return {"tokens": tokens, "out_grad": out_grad, "routes": routes, "lengths": lengths, "parents": parents, "attn_gain": attn_gain, "ffn_gain": ffn_gain, "w_query": w_query, "w_key": w_key, "w_value": w_value, "w_out": w_out, "router": router, "shared_gate": shared_gate, "shared_up": shared_up, "shared_down": shared_down, "expert_gate": expert_gate, "expert_up": expert_up, "expert_down": expert_down}


EPSILON = 1e-06
ROPE_BASE = 10000.0
HIGHEST_PRECISION = lax.Precision.HIGHEST

@jax.custom_vjp
def low(v):
    return lax.optimization_barrier(v.astype(jnp.bfloat16)).astype(jnp.float32)

@jax.custom_vjp
def low_back(v):
    return v

def low_keep(v):
    return (low(v), None)

def low_pass(kept, grad):
    return (grad,)

def back_keep(v):
    return (v, None)

def back_low(kept, grad):
    return (low(grad),)
low.defvjp(low_keep, low_pass)
low_back.defvjp(back_keep, back_low)

def product(left, right):
    return jnp.dot(left, right, precision=HIGHEST_PRECISION, preferred_element_type=jnp.float32)

def tree_tables(lengths, parents):
    seg_count = lengths.shape[0]
    identity = jnp.arange(seg_count, dtype=jnp.int32)
    current = identity
    ancestry = jnp.zeros((seg_count, seg_count), jnp.float32)
    for depth_level in range(seg_count):
        chosen_mask = current[:, None] == identity[None, :]
        ancestry = jnp.maximum(ancestry, chosen_mask.astype(jnp.float32))
        current = lax.optimization_barrier(jnp.sum(jnp.where(chosen_mask, parents[None, :], 0), axis=1)).astype(jnp.int32)
    seg_ends = jnp.cumsum(lengths).astype(jnp.int32)
    starts = (seg_ends - lengths).astype(jnp.int32)
    sizes_float = lengths.astype(jnp.float32)
    offsets = lax.optimization_barrier(jnp.sum(ancestry * sizes_float[None, :], axis=1)) - sizes_float
    return (ancestry, starts, seg_ends, offsets)

def row_tables(row_ids, starts, seg_ends, offsets):
    member = ((row_ids[:, None] >= starts[None, :]) & (row_ids[:, None] < seg_ends[None, :])).astype(jnp.float32)
    position_shift = offsets - starts.astype(jnp.float32)
    position = lax.optimization_barrier(jnp.sum(member * position_shift[None, :], axis=1)) + row_ids.astype(jnp.float32)
    return (member, position)

def rotate(head_values, position):
    half_width = head_values.shape[-1] // 2
    frequency = ROPE_BASE ** (-jnp.arange(half_width, dtype=jnp.float32) / half_width)
    angles = position[:, None] * frequency[None, :]
    cosines = jnp.cos(angles)[:, None, :]
    sine_values = jnp.sin(angles)[:, None, :]
    first_half = head_values[..., :half_width]
    second_half = head_values[..., half_width:]
    return jnp.concatenate([first_half * cosines - second_half * sine_values, second_half * cosines + first_half * sine_values], axis=-1)

def attend(queries, key_heads, value_heads, reach, member, row_ids):
    row_count = queries.shape[0]
    block_rows = math.gcd(row_count, 512)
    score_scale = HEAD ** (-0.5)

    def one_block(block_index):
        first_row = block_index * block_rows
        query_block = lax.dynamic_slice_in_dim(queries, first_row, block_rows, 0)
        reach_block = lax.dynamic_slice_in_dim(reach, first_row, block_rows, 0)
        rows_block = lax.dynamic_slice_in_dim(row_ids, first_row, block_rows, 0)
        linked = product(reach_block, member.T) > 0.5
        seen = linked & (row_ids[None, :] <= rows_block[:, None])
        scores = low_back(jnp.einsum('qhd,khd->hqk', query_block, key_heads, precision=HIGHEST_PRECISION) * score_scale)
        weights_exp = jnp.where(seen[None], jnp.exp(scores), 0.0)
        row_total = lax.optimization_barrier(jnp.sum(weights_exp, axis=2))
        summed = low_back(jnp.einsum('hqk,khd->qhd', low(weights_exp), value_heads, precision=HIGHEST_PRECISION))
        return (summed / jnp.transpose(row_total)[:, :, None]).reshape(block_rows, -1)
    blocks = lax.map(jax.checkpoint(one_block), jnp.arange(row_count // block_rows, dtype=jnp.int32))
    return blocks.reshape(row_count, -1)

def forward(tokens_now, member, position, reach, row_ids, choose, attn_gain, ffn_gain, w_query, w_key, w_value, w_out, router, shared_gate, shared_up, shared_down, expert_gate, expert_up, expert_down):
    row_count = tokens_now.shape[0]
    norm_one = lax.rsqrt(lax.optimization_barrier(jnp.mean(tokens_now * tokens_now, axis=1, keepdims=True)) + EPSILON)
    normed_one = low(tokens_now * norm_one * attn_gain)
    query_pre = low_back(product(normed_one, w_query)).reshape(row_count, HEADS, HEAD)
    key_pre = low_back(product(normed_one, w_key)).reshape(row_count, HEADS, HEAD)
    value_heads = low(low_back(product(normed_one, w_value))).reshape(row_count, HEADS, HEAD)
    queries = low(rotate(query_pre, position))
    key_heads = low(rotate(key_pre, position))
    mixed = attend(queries, key_heads, value_heads, reach, member, row_ids)
    attn_out = low_back(product(low(mixed), w_out))
    residual = tokens_now + attn_out
    norm_two = lax.rsqrt(lax.optimization_barrier(jnp.mean(residual * residual, axis=1, keepdims=True)) + EPSILON)
    normed_two = low(residual * norm_two * ffn_gain)
    shared_g = low_back(product(normed_two, shared_gate))
    shared_u = low_back(product(normed_two, shared_up))
    shared_out = low_back(product(low(jax.nn.silu(shared_g) * shared_u), shared_down))
    logits = low_back(product(normed_two, router))
    chosen = lax.optimization_barrier(jnp.sum(choose * logits[:, None, :], axis=2))
    gate_values = jax.nn.softmax(chosen, axis=1)
    expert_weight = lax.optimization_barrier(jnp.sum(choose * gate_values[:, :, None], axis=1))
    owners = expert_gate.shape[0] // EXPERTS
    part_width = expert_gate.shape[2]
    gate_all = expert_gate.reshape(EXPERTS, owners, D, part_width).transpose(0, 2, 1, 3).reshape(EXPERTS, D, owners * part_width)
    up_all = expert_up.reshape(EXPERTS, owners, D, part_width).transpose(0, 2, 1, 3).reshape(EXPERTS, D, owners * part_width)
    down_all = expert_down.reshape(EXPERTS, owners * part_width, D)

    def expert_step(running, pieces):
        gate_one, up_one, down_one, weight_one = pieces
        gate_val = low_back(product(normed_two, gate_one))
        up_val = low_back(product(normed_two, up_one))
        expert_out = low_back(product(low(jax.nn.silu(gate_val) * up_val), down_one))
        return (running + weight_one[:, None] * expert_out, None)
    moe_out, unused = lax.scan(jax.checkpoint(expert_step), jnp.zeros_like(tokens_now), (gate_all, up_all, down_all, jnp.transpose(expert_weight)))
    return residual + shared_out + moe_out

def reference(tokens, out_grad, routes, lengths, parents, attn_gain, ffn_gain, w_query, w_key, w_value, w_out, router, shared_gate, shared_up, shared_down, expert_gate, expert_up, expert_down):
    weights = tuple((weight_arg.astype(jnp.float32) for weight_arg in (attn_gain, ffn_gain, w_query, w_key, w_value, w_out, router, shared_gate, shared_up, shared_down, expert_gate, expert_up, expert_down)))
    layer_outputs = []
    token_gradients = []
    weight_gradients = None
    row_ids = jnp.arange(TREE, dtype=jnp.int32)
    labels = jnp.arange(EXPERTS, dtype=jnp.int32)
    for micro_step in range(MB):
        ancestry, starts, seg_ends, offsets = tree_tables(lengths[micro_step], parents[micro_step])
        member, position = row_tables(row_ids, starts, seg_ends, offsets)
        reach = product(member, ancestry)
        choose = (routes[micro_step][:, :, None] == labels[None, None, :]).astype(jnp.float32)

        def run_layer(tokens_now, *layer_weights):
            return forward(tokens_now, member, position, reach, row_ids, choose, *layer_weights)
        result, pullback = jax.vjp(run_layer, tokens[micro_step].astype(jnp.float32), *weights)
        gradients = pullback(out_grad[micro_step].astype(jnp.float32))
        layer_outputs.append(result.astype(jnp.bfloat16))
        token_gradients.append(gradients[0])
        if weight_gradients is None:
            weight_gradients = gradients[1:]
        else:
            weight_gradients = tuple((earlier + latest for earlier, latest in zip(weight_gradients, gradients[1:])))
    gradient_first_norm, gradient_second_norm, gradient_query_weight, gradient_key_weight, gradient_value_weight, gradient_output_weight, gradient_router_matrix, gradient_shared_gate_weight, gradient_shared_up_weight, gradient_shared_down_weight, gradient_expert_gate_weight, gradient_expert_up_weight, gradient_expert_down_weight = weight_gradients
    return (jnp.stack(layer_outputs), jnp.stack(token_gradients), gradient_first_norm, gradient_second_norm, gradient_query_weight, gradient_key_weight, gradient_value_weight, gradient_output_weight, gradient_router_matrix, gradient_shared_gate_weight, gradient_shared_up_weight, gradient_shared_down_weight, gradient_expert_gate_weight, gradient_expert_up_weight, gradient_expert_down_weight)
```

```python
import functools
import math

import jax
import jax.numpy as jnp
from jax import lax
from jax.experimental import pallas as pl
from jax.experimental.pallas import tpu as pltpu
from jax.sharding import PartitionSpec as P

HEAD = 64


EPSILON = 1e-06
ROPE_BASE = 10000.0
KEY_BLOCK = 2048


def matmul(left, right):
    return jnp.dot(left, right, preferred_element_type=jnp.float32)


def tree_tables(lengths, parents):
    seg_count = lengths.shape[0]
    identity = jnp.arange(seg_count, dtype=jnp.int32)
    current = identity
    ancestry = jnp.zeros((seg_count, seg_count), jnp.float32)
    for depth_level in range(seg_count):
        chosen_mask = current[:, None] == identity[None, :]
        ancestry = jnp.maximum(ancestry, chosen_mask.astype(jnp.float32))
        current = jnp.sum(jnp.where(chosen_mask, parents[None, :], 0), axis=1)
    seg_ends = jnp.cumsum(lengths)
    starts = seg_ends - lengths
    sizes_float = lengths.astype(jnp.float32)
    offsets = jnp.sum(ancestry * sizes_float[None, :], axis=1) - sizes_float
    return (ancestry, starts, seg_ends, offsets)


def row_tables(row_ids, starts, seg_ends, offsets):
    member = (
        (row_ids[:, None] >= starts[None, :]) & (row_ids[:, None] < seg_ends[None, :])
    ).astype(jnp.float32)
    position_shift = offsets - starts.astype(jnp.float32)
    position = jnp.sum(member * position_shift[None, :], axis=1) + row_ids.astype(jnp.float32)
    return (member, position)


def rotary_tables(position, half_width):
    frequency = ROPE_BASE ** (-jnp.arange(half_width, dtype=jnp.float32) / half_width)
    angles = position[:, None] * frequency[None, :]
    return (jnp.cos(angles)[:, None, :], jnp.sin(angles)[:, None, :])


def rotate(head_values, position):
    half_width = head_values.shape[-1] // 2
    cosines, sine_values = rotary_tables(position, half_width)
    first_half = head_values[..., :half_width]
    second_half = head_values[..., half_width:]
    return jnp.concatenate(
        [
            first_half * cosines - second_half * sine_values,
            second_half * cosines + first_half * sine_values,
        ],
        axis=-1,
    )


def rotate_back(grad_heads, position):
    half_width = grad_heads.shape[-1] // 2
    cosines, sine_values = rotary_tables(position, half_width)
    first_half = grad_heads[..., :half_width]
    second_half = grad_heads[..., half_width:]
    return jnp.concatenate(
        [
            first_half * cosines + second_half * sine_values,
            second_half * cosines - first_half * sine_values,
        ],
        axis=-1,
    )


def silu_parts(gate_val):
    sigmoid_val = jax.nn.sigmoid(gate_val)
    return (gate_val * sigmoid_val, sigmoid_val * (1.0 + gate_val * (1.0 - sigmoid_val)))


def rms_back(grad_normed, source, norm_scale, gain):
    weighted = grad_normed * gain
    inner_mean = jnp.mean(weighted * source, axis=1, keepdims=True)
    return (
        norm_scale * weighted - norm_scale**3 * source * inner_mean,
        jnp.sum(grad_normed * source * norm_scale, axis=0),
    )


def visible(reach_rows, query_ids, key_member, key_ids):
    linked = matmul(reach_rows, key_member.T) > 0.5
    return linked & (key_ids[None, :] <= query_ids[:, None])


def score_block(query_heads, key_heads, seen, score_scale):
    scores = (
        jnp.einsum("qhd,khd->hqk", query_heads, key_heads, preferred_element_type=jnp.float32)
        * score_scale
    )
    return jnp.where(seen[None], jnp.exp(scores), 0.0)


def score_grads(weights_exp, grad_summed, value_heads, delta_rows):
    grad_exp = jnp.einsum(
        "qhd,khd->hqk", grad_summed, value_heads, preferred_element_type=jnp.float32
    )
    return (weights_exp * (grad_exp - jnp.transpose(delta_rows)[:, :, None])).astype(jnp.bfloat16)


def plain_body(
    tokens,
    out_grad,
    routes,
    lengths,
    parents,
    attn_gain,
    ffn_gain,
    w_query,
    w_key,
    w_value,
    w_out,
    router,
    shared_gate,
    shared_up,
    shared_down,
    expert_gate,
    expert_up,
    expert_down,
):
    micro_count, row_count, model_width = tokens.shape
    devices = lax.axis_size("expert")
    tree_rows = row_count * devices
    expert_count = router.shape[1]
    owners = devices // expert_count
    capacity = 4 * row_count // expert_count
    score_scale = HEAD ** (-0.5)
    local_rows = lax.axis_index("expert") * row_count + jnp.arange(row_count, dtype=jnp.int32)
    part_gate = expert_gate[0]
    part_up = expert_up[0]
    part_down = expert_down[0]
    labels = jnp.arange(expert_count, dtype=jnp.int32)
    slot_ids = jnp.arange(expert_count * capacity, dtype=jnp.int32)
    pair_ids = jnp.arange(2 * row_count, dtype=jnp.int32)
    block_size = math.gcd(tree_rows, KEY_BLOCK)
    block_count = tree_rows // block_size
    layer_outputs = []
    token_gradients = []
    dense_sums = None
    expert_sums = None
    for micro_step in range(micro_count):
        gathered = (
            lax.all_gather(attn_gain, "expert", axis=0, tiled=True),
            lax.all_gather(ffn_gain, "expert", axis=0, tiled=True),
            lax.all_gather(w_query, "expert", axis=0, tiled=True),
            lax.all_gather(w_key, "expert", axis=0, tiled=True),
            lax.all_gather(w_value, "expert", axis=0, tiled=True),
            lax.all_gather(w_out, "expert", axis=1, tiled=True),
            lax.all_gather(router, "expert", axis=0, tiled=True),
            lax.all_gather(shared_gate, "expert", axis=0, tiled=True),
            lax.all_gather(shared_up, "expert", axis=0, tiled=True),
            lax.all_gather(shared_down, "expert", axis=1, tiled=True),
        )
        (
            gain_one,
            gain_two,
            query_weight,
            key_weight,
            value_weight,
            out_weight,
            router_weight,
            gate_weight,
            up_weight,
            down_weight,
        ) = gathered
        local_width = query_weight.shape[1]
        head_count = local_width // HEAD
        ancestry, starts, seg_ends, offsets = tree_tables(lengths[micro_step], parents[micro_step])
        member, position = row_tables(local_rows, starts, seg_ends, offsets)
        reach = matmul(member, ancestry)
        tokens_now = tokens[micro_step].astype(jnp.float32)
        norm_one = lax.rsqrt(jnp.mean(tokens_now * tokens_now, axis=1, keepdims=True) + EPSILON)
        normed_one = (tokens_now * norm_one * gain_one).astype(jnp.bfloat16)
        query_pre = matmul(normed_one, query_weight).reshape(row_count, head_count, HEAD)
        key_pre = matmul(normed_one, key_weight).reshape(row_count, head_count, HEAD)
        value_low = matmul(normed_one, value_weight).astype(jnp.bfloat16)
        queries = rotate(query_pre, position).astype(jnp.bfloat16)
        key_heads = rotate(key_pre, position).astype(jnp.bfloat16)
        key_value = jnp.concatenate([key_heads.reshape(row_count, local_width), value_low], axis=1)
        all_pairs = lax.all_gather(key_value, "expert", axis=0, tiled=True)

        def key_block_parts(block_index):
            first_key = block_index * block_size
            key_block = lax.dynamic_slice_in_dim(all_pairs, first_key, block_size, 0)
            key_ids = first_key + jnp.arange(block_size, dtype=jnp.int32)
            key_member, unused = row_tables(key_ids, starts, seg_ends, offsets)
            seen = visible(reach, local_rows, key_member, key_ids)
            block_keys = key_block[:, :local_width].reshape(block_size, head_count, HEAD)
            block_values = key_block[:, local_width:].reshape(block_size, head_count, HEAD)
            return (seen, block_keys, block_values)

        def forward_step(block_index, totals):
            seen, block_keys, block_values = key_block_parts(block_index)
            weights_exp = score_block(queries, block_keys, seen, score_scale)
            summed_part = jnp.einsum(
                "hqk,khd->qhd",
                weights_exp.astype(jnp.bfloat16),
                block_values,
                preferred_element_type=jnp.float32,
            )
            return (
                totals[0] + summed_part.reshape(row_count, local_width),
                totals[1] + jnp.transpose(jnp.sum(weights_exp, axis=2)),
            )

        initial = (
            jnp.zeros((row_count, local_width), jnp.float32),
            jnp.zeros((row_count, head_count), jnp.float32),
        )
        summed, row_total = lax.fori_loop(0, block_count, forward_step, initial)
        mixed = summed.reshape(row_count, head_count, HEAD) / row_total[:, :, None]
        mixed_low = mixed.reshape(row_count, local_width).astype(jnp.bfloat16)
        attn_out = lax.psum(matmul(mixed_low, out_weight), "tensor")
        residual = tokens_now + attn_out
        norm_two = lax.rsqrt(jnp.mean(residual * residual, axis=1, keepdims=True) + EPSILON)
        normed_two = (residual * norm_two * gain_two).astype(jnp.bfloat16)
        shared_g = matmul(normed_two, gate_weight)
        shared_u = matmul(normed_two, up_weight)
        shared_act, shared_slope = silu_parts(shared_g)
        shared_h = (shared_act * shared_u).astype(jnp.bfloat16)
        shared_y = matmul(shared_h, down_weight)
        logits = matmul(normed_two, router_weight)
        route_now = routes[micro_step]
        choose = (route_now[:, :, None] == labels[None, None, :]).astype(jnp.float32)
        gate_values = jax.nn.softmax(jnp.sum(choose * logits[:, None, :], axis=2), axis=1)
        flat_routes = route_now.reshape(2 * row_count)
        expert_hits = (flat_routes[:, None] == labels[None, :]).astype(jnp.int32)
        slot_rank = jnp.sum((jnp.cumsum(expert_hits, axis=0) - expert_hits) * expert_hits, axis=1)
        slot_index = flat_routes * capacity + slot_rank
        slot_match = slot_index[None, :] == slot_ids[:, None]
        filled = jnp.any(slot_match, axis=1)
        source = jnp.sum(jnp.where(slot_match, pair_ids[None, :], 0), axis=1)

        def to_owners(table, row_index):
            picked = jnp.take(table, row_index, axis=0)
            picked = jnp.where(filled[:, None], picked, jnp.zeros_like(picked))
            spread = jnp.broadcast_to(
                picked.reshape(expert_count, 1, capacity, model_width),
                (expert_count, owners, capacity, model_width),
            )
            return spread.reshape(devices, capacity, model_width)

        def from_owners(returned):
            merged = jnp.sum(
                returned.reshape(expert_count, owners, capacity, model_width), axis=1
            ).reshape(expert_count * capacity, model_width)
            return jnp.take(merged, slot_index, axis=0).reshape(row_count, 2, model_width)

        arrived = lax.all_to_all(
            to_owners(normed_two, source // 2), "expert", split_axis=0, concat_axis=0, tiled=True
        )
        slot_count = arrived.shape[1]
        flat_in = arrived.reshape(devices * slot_count, model_width)
        expert_g = matmul(flat_in, part_gate)
        expert_u = matmul(flat_in, part_up)
        expert_act, expert_unused = silu_parts(expert_g)
        expert_h = (expert_act * expert_u).astype(jnp.bfloat16)
        partial_out = matmul(expert_h, part_down).reshape(devices, slot_count, model_width)
        combined = lax.all_to_all(
            partial_out.astype(jnp.bfloat16), "expert", split_axis=0, concat_axis=0, tiled=True
        ).astype(partial_out.dtype)
        hidden_width = expert_g.shape[1]
        combined, arrived, kept_g, kept_u, kept_h = (
            combined,
            arrived,
            expert_g.reshape(devices, slot_count, hidden_width),
            expert_u.reshape(devices, slot_count, hidden_width),
            expert_h.reshape(devices, slot_count, hidden_width),
        )
        expert_y = from_owners(combined)
        cot_low = out_grad[micro_step]
        cotangent = cot_low.astype(jnp.float32)
        moe_part = jnp.sum(gate_values[:, :, None] * expert_y, axis=1)
        gate_dots = jnp.sum(cotangent[:, None, :] * expert_y, axis=2)
        ffn_out, grad_gate = (
            lax.psum((shared_y + moe_part).astype(jnp.bfloat16), "tensor").astype(jnp.float32),
            lax.psum(gate_dots.astype(jnp.bfloat16), "tensor").astype(jnp.float32),
        )
        layer_outputs.append((residual + ffn_out).astype(jnp.bfloat16))
        grad_shared_h = matmul(cot_low, down_weight.T)
        grad_shared_g = (grad_shared_h * shared_u * shared_slope).astype(jnp.bfloat16)
        grad_shared_u = (grad_shared_h * shared_act).astype(jnp.bfloat16)
        grad_chosen = gate_values * (
            grad_gate - jnp.sum(gate_values * grad_gate, axis=1, keepdims=True)
        )
        grad_logits = jnp.sum(choose * grad_chosen[:, :, None], axis=1).astype(jnp.bfloat16)
        grad_pairs_out = (
            (gate_values[:, :, None] * cotangent[:, None, :])
            .astype(jnp.bfloat16)
            .reshape(2 * row_count, model_width)
        )
        arrived_grad = lax.all_to_all(
            to_owners(grad_pairs_out, source), "expert", split_axis=0, concat_axis=0, tiled=True
        )
        slot_total = arrived_grad.shape[0] * arrived_grad.shape[1]
        flat_grad = arrived_grad.reshape(slot_total, model_width)
        flat_in = arrived.reshape(slot_total, model_width)
        hidden_width = kept_g.shape[2]
        expert_g = kept_g.reshape(slot_total, hidden_width)
        expert_u = kept_u.reshape(slot_total, hidden_width)
        expert_h = kept_h.reshape(slot_total, hidden_width)
        expert_act, expert_slope = silu_parts(expert_g)
        grad_hidden = matmul(flat_grad, part_down.T)
        grad_expert_g = (grad_hidden * expert_u * expert_slope).astype(jnp.bfloat16)
        grad_expert_u = (grad_hidden * expert_act).astype(jnp.bfloat16)
        grad_in = matmul(grad_expert_g, part_gate.T) + matmul(grad_expert_u, part_up.T)
        returned = lax.all_to_all(
            grad_in.reshape(arrived_grad.shape[0], arrived_grad.shape[1], model_width),
            "expert",
            split_axis=0,
            concat_axis=0,
            tiled=True,
        )
        normed_part = (
            matmul(grad_shared_g, gate_weight.T)
            + matmul(grad_shared_u, up_weight.T)
            + jnp.sum(from_owners(returned), axis=1)
        )
        grad_normed_two = lax.psum(normed_part, "tensor") + matmul(grad_logits, router_weight.T)
        grad_norm_part, grad_gain_two = rms_back(grad_normed_two, residual, norm_two, gain_two)
        grad_residual = cotangent + grad_norm_part
        grad_attn = grad_residual.astype(jnp.bfloat16)
        grad_mixed = matmul(grad_attn, out_weight.T).reshape(row_count, head_count, HEAD)
        grad_summed = (grad_mixed / row_total[:, :, None]).astype(jnp.bfloat16)
        delta_rows = jnp.sum(grad_mixed * mixed, axis=2) / row_total

        def block_terms(block_index):
            seen, block_keys, block_values = key_block_parts(block_index)
            weights_exp = score_block(queries, block_keys, seen, score_scale)
            grad_scores = score_grads(weights_exp, grad_summed, block_values, delta_rows)
            return (weights_exp, grad_scores, block_keys)

        zero_query = jnp.zeros((row_count, head_count, HEAD), jnp.float32)

        def key_step(gradient_query_weight, block_index):
            weights_exp, grad_scores, block_keys = block_terms(block_index)
            gradient_query_weight = (
                gradient_query_weight
                + jnp.einsum(
                    "hqk,khd->qhd", grad_scores, block_keys, preferred_element_type=jnp.float32
                )
                * score_scale
            )
            grad_keys = (
                jnp.einsum("hqk,qhd->khd", grad_scores, queries, preferred_element_type=jnp.float32)
                * score_scale
            )
            grad_values = jnp.einsum(
                "hqk,qhd->khd",
                weights_exp.astype(jnp.bfloat16),
                grad_summed,
                preferred_element_type=jnp.float32,
            )
            return (
                gradient_query_weight,
                jnp.concatenate(
                    [
                        grad_keys.reshape(block_size, local_width),
                        grad_values.reshape(block_size, local_width),
                    ],
                    axis=1,
                ),
            )

        gradient_query_weight, key_terms = lax.scan(
            key_step, zero_query, jnp.arange(block_count, dtype=jnp.int32)
        )
        grad_pairs = lax.psum_scatter(
            key_terms.reshape(tree_rows, 2 * local_width), "expert", scatter_dimension=0, tiled=True
        )
        grad_keys_rot = grad_pairs[:, :local_width].reshape(row_count, head_count, HEAD)
        grad_query_pre = (
            rotate_back(gradient_query_weight, position)
            .reshape(row_count, local_width)
            .astype(jnp.bfloat16)
        )
        grad_key_pre = (
            rotate_back(grad_keys_rot, position)
            .reshape(row_count, local_width)
            .astype(jnp.bfloat16)
        )
        grad_value_low = grad_pairs[:, local_width:].astype(jnp.bfloat16)
        normed_grad = (
            matmul(grad_query_pre, query_weight.T)
            + matmul(grad_key_pre, key_weight.T)
            + matmul(grad_value_low, value_weight.T)
        )
        grad_normed_one = lax.psum(normed_grad.astype(jnp.bfloat16), "tensor").astype(jnp.float32)
        grad_norm_first, grad_gain_one = rms_back(grad_normed_one, tokens_now, norm_one, gain_one)
        token_gradients.append(grad_residual + grad_norm_first)
        dense_step = (
            grad_gain_one,
            grad_gain_two,
            matmul(normed_one.T, grad_query_pre),
            matmul(normed_one.T, grad_key_pre),
            matmul(normed_one.T, grad_value_low),
            matmul(mixed_low.T, grad_attn),
            matmul(normed_two.T, grad_logits),
            matmul(normed_two.T, grad_shared_g),
            matmul(normed_two.T, grad_shared_u),
            matmul(shared_h.T, cot_low),
        )
        expert_step = (
            matmul(flat_in.T, grad_expert_g),
            matmul(flat_in.T, grad_expert_u),
            matmul(expert_h.T, flat_grad),
        )
        if dense_sums is None:
            dense_sums = dense_step
            expert_sums = expert_step
        else:
            dense_sums = tuple(
                (earlier + latest for earlier, latest in zip(dense_sums, dense_step))
            )
            expert_sums = tuple(
                (earlier + latest for earlier, latest in zip(expert_sums, expert_step))
            )
    final_gate, final_up, final_down = expert_sums
    reduced = (
        lax.psum_scatter(dense_sums[0], "expert", scatter_dimension=0, tiled=True),
        lax.psum_scatter(dense_sums[1], "expert", scatter_dimension=0, tiled=True),
        lax.psum_scatter(dense_sums[2], "expert", scatter_dimension=0, tiled=True),
        lax.psum_scatter(dense_sums[3], "expert", scatter_dimension=0, tiled=True),
        lax.psum_scatter(dense_sums[4], "expert", scatter_dimension=0, tiled=True),
        lax.psum_scatter(dense_sums[5], "expert", scatter_dimension=1, tiled=True),
        lax.psum_scatter(dense_sums[6], "expert", scatter_dimension=0, tiled=True),
        lax.psum_scatter(dense_sums[7], "expert", scatter_dimension=0, tiled=True),
        lax.psum_scatter(dense_sums[8], "expert", scatter_dimension=0, tiled=True),
        lax.psum_scatter(dense_sums[9], "expert", scatter_dimension=1, tiled=True),
    )
    return (
        jnp.stack(layer_outputs),
        jnp.stack(token_gradients),
        reduced[0],
        reduced[1],
        reduced[2],
        reduced[3],
        reduced[4],
        reduced[5],
        reduced[6],
        reduced[7],
        reduced[8],
        reduced[9],
        final_gate[None],
        final_up[None],
        final_down[None],
    )


MESH = pl.DeviceIdType.MESH
BF = jnp.bfloat16
F32 = jnp.float32
EXACT = lax.Precision.HIGHEST
VMEM_LIMIT = 62 * 2**20


def product(left, right, dims, precision=None):
    return lax.dot_general(
        left, right, (dims, ((), ())), preferred_element_type=F32, precision=precision
    )


def dot(left, right, precision=None):
    return product(left, right, ((1,), (0,)), precision)


def dot_nt(left, right, precision=None):
    return product(left, right, ((1,), (1,)), precision)


def dot_tn(left, right, precision=None):
    return product(left, right, ((0,), (0,)), precision)


def iota(shape, dim):
    return lax.broadcasted_iota(jnp.int32, shape, dim)


class Net:
    def __init__(self, expert_size, send_sems, recv_sems):
        self.e = lax.axis_index("expert")
        self.t = lax.axis_index("tensor")
        self.n = expert_size
        self.nz = expert_size // 2
        self.z = self.e // 2
        self.x = self.e % 2
        self.core = self.t % 2
        self.send_sems = send_sems
        self.recv_sems = recv_sems
        self.sends = 0
        self.recvs = 0
        self.open = []

    def recv_slots(self, count):
        first = self.recvs
        self.recvs += count
        return first

    def ids(self, to):
        return {"expert": to[0], "tensor": to[1]}

    def push(self, src, dst, to, slot):
        copy = pltpu.make_async_remote_copy(
            src_ref=src,
            dst_ref=dst,
            send_sem=self.send_sems.at[self.sends],
            recv_sem=self.recv_sems.at[slot],
            device_id=self.ids(to),
            device_id_type=MESH,
        )
        self.sends += 1
        copy.start()
        self.open.append(copy)

    def landed(self, dst, slot):
        pltpu.make_async_remote_copy(
            src_ref=dst,
            dst_ref=dst,
            send_sem=self.send_sems.at[0],
            recv_sem=self.recv_sems.at[slot],
            device_id=self.ids(self.other_core()),
            device_id_type=MESH,
        ).wait_recv()

    def drain_some(self, copies):
        for copy in copies:
            copy.wait_send()
        self.open = [c for c in self.open if not any(c is copy for copy in copies)]

    def drain(self):
        for copy in self.open:
            copy.wait_send()

    def other_core(self):
        return (self.e, self.t + 1 - 2 * self.core)

    def across_y(self):
        return (self.e, (self.t + 2) % 4)

    def across_x(self):
        return (self.e + 1 - 2 * self.x, self.t)

    def peer(self, step):
        return (self.e + step) % self.n

    def greet(self):
        barrier = pltpu.get_barrier_semaphore()
        partners = [(self.peer(d), self.t) for d in range(1, self.n)]
        partners += [self.other_core(), self.across_y()]
        for to in partners:
            pl.semaphore_signal(barrier, inc=1, device_id=self.ids(to), device_id_type=MESH)
        return lambda: pl.semaphore_wait(barrier, len(partners))


class Gather:
    def __init__(self, net, block):
        self.net, self.block = net, block
        self.slot = net.recv_slots(net.n)

    def start(self):
        net = self.net
        own = self.block(net.e)
        for d in range(1, net.nz):
            to = ((net.z + d) % net.nz * 2 + net.x, net.t)
            net.push(own, own, to, self.slot + net.e)
        net.push(own, own, net.across_x(), self.slot + net.e)

    def forward(self):
        net = self.net
        for d in range(1, net.nz):
            source = (net.z + d) % net.nz * 2 + net.x
            part = self.block(source)
            net.landed(part, self.slot + source)
            net.push(part, part, net.across_x(), self.slot + source)

    def finish(self):
        net = self.net
        for d in range(net.nz):
            source = (net.z + d) % net.nz * 2 + 1 - net.x
            net.landed(self.block(source), self.slot + source)


class Scatter:
    def __init__(self, net, block, from_x, from_z):
        self.net, self.block = net, block
        self.from_x, self.from_z = from_x, from_z
        self.slot_x = net.recv_slots(net.nz)
        self.slot_z = net.recv_slots(net.nz)

    def start(self):
        net = self.net
        for d in range(1, net.nz + 1):
            zz = (net.z + d) % net.nz
            net.push(
                self.block(zz * 2 + 1 - net.x), self.from_x.at[zz], net.across_x(), self.slot_x + zz
            )

    def forward(self):
        net = self.net
        for d in range(1, net.nz):
            zz = (net.z + d) % net.nz
            net.landed(self.from_x.at[zz], self.slot_x + zz)
            pair = self.block(zz * 2 + net.x)[...].astype(F32) + self.from_x[zz].astype(F32)
            self.from_x[zz] = pair.astype(BF)
            net.push(
                self.from_x.at[zz],
                self.from_z.at[net.z],
                (zz * 2 + net.x, net.t),
                self.slot_z + net.z,
            )

    def finish(self):
        net = self.net
        net.landed(self.from_x.at[net.z], self.slot_x + net.z)
        total = self.block(net.e)[...].astype(F32) + self.from_x[net.z].astype(F32)
        for d in range(1, net.nz):
            zz = (net.z + d) % net.nz
            net.landed(self.from_z.at[zz], self.slot_z + zz)
            total = total + self.from_z[zz].astype(F32)
        return total


class Exchange:
    def __init__(self, net, outgoing, incoming):
        self.net, self.outgoing, self.incoming = net, outgoing, incoming
        self.slot = net.recv_slots(net.n)

    def start(self):
        net = self.net
        for d in range(1, net.n):
            to = net.peer(d)
            net.push(self.outgoing(to), self.incoming(net.e), (to, net.t), self.slot + net.e)

    def arrive(self, d):
        source = self.net.peer(d)
        self.net.landed(self.incoming(source), self.slot + source)
        return source


class CoreSum:
    def __init__(self, net, out_buf, in_buf):
        self.net, self.out_buf, self.in_buf = net, out_buf, in_buf
        self.slot = net.recv_slots(1)

    def start(self, value):
        self.out_buf[...] = value.astype(self.out_buf.dtype)
        self.net.push(self.out_buf, self.in_buf, self.net.other_core(), self.slot)

    def finish(self):
        self.net.landed(self.in_buf, self.slot)
        return self.in_buf[...].astype(F32)


class YSum:
    def __init__(self, net, out_buf, in_buf):
        self.net, self.out_buf, self.in_buf = net, out_buf, in_buf
        self.slot = net.recv_slots(1)

    def start(self, value):
        self.out_buf[...] = value.astype(self.out_buf.dtype)
        self.net.push(self.out_buf, self.in_buf, self.net.across_y(), self.slot)

    def finish(self):
        self.net.landed(self.in_buf, self.slot)
        return self.out_buf[...].astype(F32) + self.in_buf[...].astype(F32)


class CoreShare:
    def __init__(self, net, halves):
        self.net, self.halves = net, halves
        self.slot = net.recv_slots(1)

    def start(self, value):
        net = self.net
        self.halves[net.core] = value.astype(self.halves.dtype)
        part = self.halves.at[net.core]
        net.push(part, part, net.other_core(), self.slot)
        self.copy = net.open[-1]

    def finish(self):
        net = self.net
        net.landed(self.halves.at[1 - net.core], self.slot)
        return jnp.concatenate([self.halves[0], self.halves[1]], axis=1)


def silu_both(value):
    gate = jax.nn.sigmoid(value)
    return value * gate, gate * (1.0 + value * (1.0 - gate))


def norm_back(grad_normed, source, scale, gain):
    weighted = grad_normed * gain
    inner = jnp.mean(weighted * source, axis=1, keepdims=True)
    return scale * weighted - scale * scale * scale * source * inner


PLACES = ["tok", "cot", "routes", "lengths", "parents", "wq", "wk", "wv", "wo", "ext"]
PLACES += ["sg", "su", "sd", "eg", "eu", "ed"]
PLACES += ["out", "gtok", "dqkv", "dwo", "dext", "dshared", "dgains", "deg", "deu", "ded"]


def scratch_shapes(s):
    n, rows, width, half = s["n"], s["rows"], s["width"], s["half"]
    depth, hidden, shared, slots = s["depth"], s["hidden"], s["shared"], s["slots"]
    micro, local, heads, nz = s["micro"], s["local"], s["heads"], s["n"] // 2
    tree = n * local
    vm = pltpu.VMEM
    return dict(
        w_small=vm((3, n, depth, width), BF),
        w_o=vm((n, depth, width), BF),
        w_ext=vm((n, depth, 128), BF),
        w_sh=vm((3, n, depth, shared), BF),
        pairs=vm((2, micro, n, local, width), BF),
        q_rows=vm((micro, heads * local, width), BF),
        expo=vm((micro, heads * local, tree), F32),
        mixed=vm((rows, width), F32),
        choice=vm((rows, n * slots), BF),
        res=vm((rows, 2 * half), F32),
        n_one=vm((rows, 2 * half), BF),
        n_two=vm((2, rows, half), BF),
        mixed_low=vm((rows, width), BF),
        c_out=vm((n, slots, half), BF),
        c_in=vm((2, n, slots, half), BF),
        h_out=vm((n, 8, slots), F32),
        h_in=vm((n, 8, slots), F32),
        x_out=vm((n, slots, half), BF),
        x_in=vm((2, n, slots, half), BF),
        gate_col=vm((n, slots, 1), F32),
        e_h=vm((n * slots, hidden), BF),
        e_dg=vm((n * slots, hidden), BF),
        e_du=vm((n * slots, hidden), BF),
        y_part=vm((2, n, slots, half), BF),
        g_part=vm((2, n, slots, half), BF),
        y_core=vm((n, slots, half), BF),
        g_core=vm((n, slots, half), BF),
        y_out=vm((n, slots, half), BF),
        g_out=vm((n, slots, half), BF),
        y_in=vm((n, slots, half), BF),
        g_in=vm((n, slots, half), BF),
        d_out=vm((n, 8, slots), F32),
        d_in=vm((n, 8, slots), F32),
        d_tensor=vm((4, 8, slots), F32),
        core_buf=vm((4, rows, half), F32),
        core_low=vm((4, rows, half), BF),
        y_buf=vm((8, rows, half), BF),
        share=vm((2, 2, rows, half), F32),
        share_low=vm((2, rows, half), BF),
        kv_part=vm((micro, 2, n, local, width), BF),
        kv_fx=vm((micro, nz, 2, local, width), BF),
        kv_fz=vm((micro, nz, 2, local, width), BF),
        sh_part=vm((3, n, depth, shared), BF),
        sh_fx=vm((nz, 3, depth, shared), BF),
        sh_fz=vm((nz, 3, depth, shared), BF),
        o_part=vm((2, n, depth, width), BF),
        o_fx=vm((nz, 2, depth, width), BF),
        o_fz=vm((nz, 2, depth, width), BF),
        kvw_part=vm((2, n, depth, width), BF),
        kvw_fx=vm((nz, 2, depth, width), BF),
        kvw_fz=vm((nz, 2, depth, width), BF),
        ext_part=vm((n, depth, 128), BF),
        ext_fx=vm((nz, depth, 128), BF),
        ext_fz=vm((nz, depth, 128), BF),
        gains_out=vm((n, 8, 128), F32),
        gains_in=vm((n, 8, 128), F32),
        stage=vm((2, half, hidden), F32),
        stage_d=vm((hidden, half), F32),
        save_sems=pltpu.SemaphoreType.DMA((6,)),
        send_sems=pltpu.SemaphoreType.DMA((180,)),
        recv_sems=pltpu.SemaphoreType.DMA((200,)),
    )


def layer_kernel(s, names, *refs):
    r = dict(zip(names, refs))
    n, rows, width, half = s["n"], s["rows"], s["width"], s["half"]
    depth, hidden, shared, slots = s["depth"], s["hidden"], s["shared"], s["slots"]
    micro, local, heads = s["micro"], s["local"], s["heads"]
    model, tree, cap = 2 * half, n * local, slots // micro
    experts = s["experts"]
    net = Net(n, r["send_sems"], r["recv_sems"])
    me, core = net.e, net.core
    ready = net.greet()
    my_half = pl.ds(pl.multiple_of(core * half, 128), half)

    for i, name in enumerate(("wq", "wk", "wv")):
        r["w_small"][i, me] = r[name][...]
    r["w_o"][me] = r["wo"][...]
    r["w_ext"][me] = r["ext"][...]
    for i, name in enumerate(("sg", "su", "sd")):
        r["w_sh"][i, me] = r[name][...]
    get_small = Gather(net, lambda b: r["w_small"].at[:, b])
    get_ext = Gather(net, lambda b: r["w_ext"].at[b])
    get_o = Gather(net, lambda b: r["w_o"].at[b])
    get_sh = [Gather(net, lambda b, i=i: r["w_sh"].at[i, b]) for i in range(3)]
    get_pairs = Gather(net, lambda b: r["pairs"].at[:, :, b])
    ready()
    get_small.start()
    get_ext.start()

    lane = iota((rows, 128), 1) - 8
    hot_one = lane == r["routes"][:, 0:1]
    hot_two = lane == r["routes"][:, 1:2]
    hits = (hot_one | hot_two).astype(F32)
    row_a, row_b = iota((rows, rows), 0), iota((rows, rows), 1)
    earlier = ((row_b < row_a) & (row_a // local == row_b // local)).astype(BF)
    rank = dot(earlier, hits.astype(BF))
    rank = jnp.where(hits > 0.5, rank, -1.0)
    spread = (iota((128, n * slots), 0) - 8 == iota((128, n * slots), 1) // slots).astype(BF)
    rank_wide = dot(rank.astype(BF), spread)
    column = iota((rows, n * slots), 1) % slots
    same_micro = column // cap == iota((rows, n * slots), 0) // local
    taken = (rank_wide == (column % cap).astype(F32)) & same_micro
    r["choice"][...] = taken.astype(BF)

    send_c = Exchange(net, lambda b: r["c_out"].at[b], lambda b: r["c_in"].at[core, b])
    send_h = Exchange(net, lambda b: r["h_out"].at[b], lambda b: r["h_in"].at[b])
    picked = dot_tn(r["choice"][...], r["cot"][:, my_half]).astype(BF).reshape(n, slots, half)
    r["c_out"][...] = picked
    r["c_in"][core, me] = r["c_out"][me]
    hit_rows = dot_tn(hits.astype(BF), r["choice"][...])[8:16]
    for b in range(n):
        r["h_out"][b] = hit_rows[:, b * slots : (b + 1) * slots]
    r["h_in"][me] = r["h_out"][me]

    def segments(m):
        starts, ends, paths, shifts, begin = [], [], [], [], 0
        for seg in range(s["segs"]):
            size = r["lengths"][m, seg]
            starts.append(begin)
            ends.append(begin + size)
            begin = begin + size
            if seg == 0:
                paths.append(jnp.int32(1))
                shifts.append(jnp.int32(0))
            else:
                parent = r["parents"][m, seg]
                path, shift = jnp.int32(0), jnp.int32(0)
                for other in range(seg):
                    is_parent = parent == other
                    path = jnp.where(is_parent, paths[other], path)
                    shift = jnp.where(
                        is_parent, shifts[other] + ends[other] - starts[other], shift
                    )
                paths.append(path + (1 << seg))
                shifts.append(shift)
        return starts, ends, paths, shifts

    tables = [segments(m) for m in range(micro)]

    def row_values(m, ids):
        starts, ends, paths, shifts = tables[m]
        path, place, own = jnp.zeros_like(ids), jnp.zeros_like(ids), jnp.zeros_like(ids)
        for seg in range(s["segs"]):
            inside = (ids >= starts[seg]) & (ids < ends[seg])
            path = jnp.where(inside, paths[seg], path)
            place = jnp.where(inside, ids - starts[seg] + shifts[seg], place)
            own = jnp.where(inside, 1 << seg, own)
        return path, place, own

    place = jnp.concatenate(
        [row_values(m, me * local + iota((local, 1), 0))[1] for m in range(micro)], axis=0
    )
    turn = iota((1, width), 1) % 32
    frequency = jnp.exp(turn.astype(F32) * (-math.log(ROPE_BASE) / 32.0))
    angle = place.astype(F32) * frequency
    cosine, sine = jnp.cos(angle), jnp.sin(angle)
    swap_r, swap_c = iota((width, width), 0), iota((width, width), 1)
    lower = swap_c % HEAD < HEAD // 2
    swap = jnp.where(lower & (swap_r == swap_c + HEAD // 2), -1.0, 0.0)
    swap = jnp.where(~lower & (swap_r == swap_c - HEAD // 2), 1.0, swap)
    swap_low = swap.astype(BF)

    tok = r["tok"][...].astype(F32)
    scale_one = lax.rsqrt(jnp.mean(tok * tok, axis=1, keepdims=True) + EPSILON)

    get_small.forward()
    get_ext.forward()
    get_ext.finish()
    ext_all = r["w_ext"][...].reshape(model, 128)
    ext_turned = ext_all.astype(F32).T
    gain_one, gain_two = ext_turned[0:1], ext_turned[1:2]
    r["n_one"][...] = (tok * scale_one * gain_one).astype(BF)
    get_small.finish()

    def small(i):
        return r["w_small"][i].reshape(model, width)

    def turned(weight):
        normed = r["n_one"][...]
        plain = dot(normed, weight)
        swapped = dot(normed, dot(weight, swap_low).astype(BF))
        return (plain * cosine + swapped * sine).astype(BF)

    keys = turned(small(1)).reshape(micro, local, width)
    values = dot(r["n_one"][...], small(2)).astype(BF).reshape(micro, local, width)
    for m in range(micro):
        r["pairs"][0, m, me] = keys[m]
        r["pairs"][1, m, me] = values[m]
    get_pairs.start()
    get_o.start()
    queries = turned(small(0)).reshape(micro, local, width)
    head_of = iota((1, width), 1) // HEAD
    head_masks = [head_of == h for h in range(heads)]

    def by_head(block):
        return jnp.concatenate(
            [jnp.where(mask, block, jnp.zeros_like(block)) for mask in head_masks], axis=0
        )

    def join_heads(stack):
        total = jnp.zeros((local, width), F32)
        for h, mask in enumerate(head_masks):
            total = total + jnp.where(mask, stack[h * local : (h + 1) * local], 0.0)
        return total

    for m in range(micro):
        r["q_rows"][m] = by_head(queries[m])
    get_pairs.forward()
    send_c.start()
    send_h.start()
    for g in get_sh:
        g.start()
    get_pairs.finish()
    score_scale = HEAD**-0.5
    totals = []
    for m in range(micro):
        key_rows = r["pairs"][0, m].reshape(tree, width)
        value_rows = r["pairs"][1, m].reshape(tree, width)
        ids = me * local + iota((heads * local, 1), 0) % local
        path, unused, unused_two = row_values(m, ids)
        key_ids = iota((1, tree), 1)
        unused, unused_two, key_seg = row_values(m, key_ids)
        seen = ((path & key_seg) != 0) & (key_ids <= ids)
        scores = dot_nt(r["q_rows"][m], key_rows) * score_scale
        expo = jnp.where(seen, jnp.exp(scores), 0.0)
        r["expo"][m] = expo
        total = jnp.sum(expo, axis=1, keepdims=True)
        totals.append(total)
        mixed = join_heads(dot(expo.astype(BF), value_rows) / total)
        r["mixed"][m * local : (m + 1) * local] = mixed
    r["mixed_low"][...] = r["mixed"][...].astype(BF)
    get_o.forward()
    get_o.finish()

    def o_half(h):
        return r["w_o"][pl.ds(h * (n // 2), n // 2)].reshape(half, width)

    core_bufs = [r["core_buf"].at[i] for i in range(4)]
    core_bufs[2:2] = [r["core_low"].at[i] for i in range(4)]
    core_sum = [CoreSum(net, core_bufs[2 * i], core_bufs[2 * i + 1]) for i in range(4)]
    y_sum = [YSum(net, r["y_buf"].at[2 * i], r["y_buf"].at[2 * i + 1]) for i in range(4)]
    share = [CoreShare(net, r["share"].at[i]) for i in (0, 1, 0)]

    core_sum[0].start(dot_nt(r["mixed_low"][...], o_half(1 - core)))
    mine = dot_nt(r["mixed_low"][...], o_half(core))
    y_sum[0].start(mine + core_sum[0].finish())
    slot_c = net.recv_slots(n)
    slot_x = net.recv_slots(n)

    def hand_over(buf, source, slot):
        part = buf.at[core, source]
        net.push(part, part, net.other_core(), slot + source)

    def take_over(buf, slot):
        for b in range(n):
            net.landed(buf.at[1 - core, b], slot + b)

    handed_c = len(net.open)
    hand_over(r["c_in"], me, slot_c)
    for d in range(1, n):
        hand_over(r["c_in"], send_c.arrive(d), slot_c)
    handed_c = net.open[handed_c:]
    share[0].start(y_sum[0].finish())
    res = tok + share[0].finish()
    r["res"][...] = res
    scale_two = lax.rsqrt(jnp.mean(res * res, axis=1, keepdims=True) + EPSILON)
    normed_two = (res * scale_two * gain_two).astype(BF)
    for h in range(2):
        r["n_two"][h] = normed_two[:, h * half : (h + 1) * half]

    send_x = Exchange(net, lambda b: r["x_out"].at[b], lambda b: r["x_in"].at[core, b])
    r["x_out"][...] = (
        dot_tn(r["choice"][...], r["n_two"][core]).astype(BF).reshape(n, slots, half)
    )
    send_x.start()
    r["x_in"][core, me] = r["x_out"][me]
    hand_over(r["x_in"], me, slot_x)

    logits = dot(normed_two, ext_all)
    z_one = jnp.sum(jnp.where(hot_one, logits, 0.0), axis=1, keepdims=True)
    z_two = jnp.sum(jnp.where(hot_two, logits, 0.0), axis=1, keepdims=True)
    z_top = jnp.maximum(z_one, z_two)
    e_one, e_two = jnp.exp(z_one - z_top), jnp.exp(z_two - z_top)
    gates = jnp.where(hot_one, e_one, jnp.where(hot_two, e_two, 0.0)) / (e_one + e_two)

    for g in get_sh:
        g.forward()
    for g in get_sh:
        g.finish()

    def wide(i):
        return r["w_sh"][i].reshape(model, shared)

    def wide_half(i, h):
        return r["w_sh"][i, pl.ds(h * (n // 2), n // 2)].reshape(half, shared)

    shared_g = dot(normed_two, wide(0))
    shared_u = dot(normed_two, wide(1))
    act, slope = silu_both(shared_g)
    shared_h = (act * shared_u).astype(BF)
    grad_h = dot(r["cot"][...], wide(2))
    grad_g = (grad_h * shared_u * slope).astype(BF)
    grad_u = (grad_h * act).astype(BF)
    core_sum[1].start(dot_nt(grad_g, wide_half(0, 1 - core)) + dot_nt(grad_u, wide_half(1, 1 - core)))
    core_sum[2].start(dot_nt(shared_h, wide_half(2, 1 - core)))
    shared_grad = dot_nt(grad_g, wide_half(0, core)) + dot_nt(grad_u, wide_half(1, core))
    shared_y = dot_nt(shared_h, wide_half(2, core))
    r["sh_part"][0] = dot_tn(normed_two, grad_g).astype(BF).reshape(n, depth, shared)
    r["sh_part"][1] = dot_tn(normed_two, grad_u).astype(BF).reshape(n, depth, shared)
    r["sh_part"][2] = dot_tn(r["cot"][...], shared_h).astype(BF).reshape(n, depth, shared)
    sum_sh = Scatter(net, lambda b: r["sh_part"].at[:, b], r["sh_fx"], r["sh_fz"])

    for d in range(1, n):
        hand_over(r["x_in"], send_x.arrive(d), slot_x)
    for d in range(1, n):
        send_h.arrive(d)
    take_over(r["c_in"], slot_c)
    take_over(r["x_in"], slot_x)
    net.drain_some(handed_c)
    ext_low = ext_turned.astype(BF)
    z_all = dot_nt(ext_low[:, :half], r["x_in"][0].reshape(n * slots, half))
    z_all = (z_all + dot_nt(ext_low[:, half:], r["x_in"][1].reshape(n * slots, half)))[8:16]
    hit_all = jnp.concatenate([r["h_in"][b] for b in range(n)], axis=1)
    own_row = iota((8, n * slots), 0) == me
    z_own = jnp.sum(jnp.where(own_row, z_all, 0.0), axis=0, keepdims=True)
    z_other = jnp.sum(jnp.where(own_row, 0.0, z_all * hit_all), axis=0, keepdims=True)
    z_top = jnp.maximum(z_own, z_other)
    e_own, e_other = jnp.exp(z_own - z_top), jnp.exp(z_other - z_top)
    gate_row = e_own / (e_own + e_other)
    eye = iota((slots, slots), 0) == iota((slots, slots), 1)
    for b in range(n):
        part = jnp.where(eye, gate_row[:, b * slots : (b + 1) * slots], 0.0)
        r["gate_col"][b] = jnp.sum(part, axis=1, keepdims=True)

    group = 2

    def expert_step(i, carry):
        span = pl.ds(i * group, group)
        flat = pl.ds(pl.multiple_of(i * group * slots, group * slots), group * slots)
        count = group * slots
        x_half = [r["x_in"][h, span].reshape(count, half) for h in range(2)]
        c_half = [r["c_in"][h, span].reshape(count, half) for h in range(2)]
        gate = r["gate_col"][span].reshape(count, 1)
        cut = [slice(0, half), slice(half, model)]
        gate_pre = dot(x_half[0], r["eg"][cut[0]]) + dot(x_half[1], r["eg"][cut[1]])
        up_pre = dot(x_half[0], r["eu"][cut[0]]) + dot(x_half[1], r["eu"][cut[1]])
        act, slope = silu_both(gate_pre)
        hid = (act * up_pre).astype(BF)
        grad_y = [(gate * c.astype(F32)).astype(BF) for c in c_half]
        grad_hid = dot_nt(grad_y[0], r["ed"][:, cut[0]]) + dot_nt(grad_y[1], r["ed"][:, cut[1]])
        grad_g = (grad_hid * up_pre * slope).astype(BF)
        grad_u = (grad_hid * act).astype(BF)
        r["e_h"][flat] = hid
        r["e_dg"][flat] = grad_g
        r["e_du"][flat] = grad_u
        dots = jnp.zeros((count, 1), F32)
        for h in range(2):
            y = dot(hid, r["ed"][:, cut[h]])
            r["y_part"][h, span] = y.astype(BF).reshape(group, slots, half)
            dots = dots + jnp.sum(y * c_half[h].astype(F32), axis=1, keepdims=True)
            back = dot_nt(grad_g, r["eg"][cut[h]]) + dot_nt(grad_u, r["eu"][cut[h]])
            r["g_part"][h, span] = back.astype(BF).reshape(group, slots, half)
            r["c_in"][h, span] = grad_y[h].reshape(group, slots, half)
        for b in range(group):
            part = jnp.where(eye, dots[b * slots : (b + 1) * slots], 0.0)
            line = jnp.sum(part, axis=0, keepdims=True)
            r["d_out"][i * group + b] = jnp.broadcast_to(line, (8, slots))
        return carry

    lax.fori_loop(0, n // group, expert_step, 0)

    send_g = Exchange(net, lambda b: r["g_out"].at[b], lambda b: r["g_in"].at[b])
    send_y = Exchange(net, lambda b: r["y_out"].at[b], lambda b: r["y_in"].at[b])
    send_d = Exchange(net, lambda b: r["d_out"].at[b], lambda b: r["d_in"].at[b])
    slot_gc, slot_yc = net.recv_slots(1), net.recv_slots(1)
    net.push(r["g_part"].at[1 - core], r["g_core"], net.other_core(), slot_gc)
    net.push(r["y_part"].at[1 - core], r["y_core"], net.other_core(), slot_yc)
    send_d.start()
    r["d_in"][me] = r["d_out"][me]
    net.landed(r["g_core"], slot_gc)
    r["g_out"][...] = (r["g_part"][core].astype(F32) + r["g_core"][...].astype(F32)).astype(BF)
    send_g.start()
    r["g_in"][me] = r["g_out"][me]
    net.landed(r["y_core"], slot_yc)
    r["y_out"][...] = (r["y_part"][core].astype(F32) + r["y_core"][...].astype(F32)).astype(BF)
    send_y.start()
    r["y_in"][me] = r["y_out"][me]
    sum_sh.start()

    dg_all, du_all = r["e_dg"], r["e_du"]
    saves = []
    for h in range(2):
        cut = slice(h * half, (h + 1) * half)
        rows_x = r["x_in"][h].reshape(n * slots, half)
        for i, (target, grads) in enumerate((("deg", dg_all), ("deu", du_all))):
            if h == 1:
                saves[i].wait()
            r["stage"][i] = dot_tn(rows_x, grads[...])
            save = pltpu.make_async_copy(r["stage"].at[i], r[target].at[cut], r["save_sems"].at[2 * h + i])
            save.start()
            saves.append(save)
        if h == 1:
            saves[2].wait()
        r["stage_d"][...] = dot_tn(r["e_h"][...], r["c_in"][h].reshape(n * slots, half))
        save = pltpu.make_async_copy(r["stage_d"], r["ded"].at[:, cut], r["save_sems"].at[4 + h])
        save.start()
        saves.append(save)

    for d in range(1, n):
        send_d.arrive(d)
    eight = iota((8, slots), 0)
    d_rows = jnp.zeros((8, slots), F32)
    for b in range(n):
        d_rows = d_rows + jnp.where(eight == b, r["d_in"][b], 0.0)
    d_core = CoreSum(net, r["d_tensor"].at[0], r["d_tensor"].at[1])
    d_y = YSum(net, r["d_tensor"].at[2], r["d_tensor"].at[3])
    d_core.start(d_rows)
    d_y.start(d_rows + d_core.finish())

    for d in range(1, n):
        send_g.arrive(d)
    moe_grad = dot(r["choice"][...], r["g_in"][...].reshape(n * slots, half))
    y_sum[1].start(moe_grad + shared_grad + core_sum[1].finish())
    d_rows = d_y.finish()
    grad_gate = jnp.zeros((rows, 128), F32)
    for b in range(n):
        cut = slice(b * slots, (b + 1) * slots)
        part = r["choice"][:, cut].astype(F32) * d_rows[b : b + 1]
        grad_gate = jnp.where(lane == b, jnp.sum(part, axis=1, keepdims=True), grad_gate)
    inner = jnp.sum(gates * grad_gate, axis=1, keepdims=True)
    grad_logits = (gates * (grad_gate - inner)).astype(BF)
    share[1].start(y_sum[1].finish())
    grad_two = share[1].finish() + dot_nt(grad_logits, ext_all)
    res = r["res"][...]
    cot = r["cot"][...].astype(F32)
    grad_res = cot + norm_back(grad_two, res, scale_two, gain_two)
    gain_two_row = jnp.sum(grad_two * res * scale_two, axis=0, keepdims=True)
    r["ext_part"][...] = dot_tn(normed_two, grad_logits).astype(BF).reshape(n, depth, 128)
    sum_ext = Scatter(net, lambda b: r["ext_part"].at[b], r["ext_fx"], r["ext_fz"])
    sum_ext.start()
    grad_attn = grad_res.astype(BF)

    o_all = r["w_o"][...].reshape(model, width)
    grad_mixed = dot(grad_attn, o_all)
    kv_sums = []
    grad_queries = []
    for m in range(micro):
        cut = slice(m * local, (m + 1) * local)
        key_rows = r["pairs"][0, m].reshape(tree, width)
        value_rows = r["pairs"][1, m].reshape(tree, width)
        gm = by_head(grad_mixed[cut])
        mixed3 = jnp.concatenate([r["mixed"][cut]] * heads, axis=0)
        delta = jnp.sum(gm * mixed3, axis=1, keepdims=True) / totals[m]
        grad_summed = (gm / totals[m]).astype(BF)
        expo = r["expo"][m]
        ds = (expo * (dot_nt(grad_summed, value_rows) - delta)).astype(BF)
        grad_k = dot_tn(ds, r["q_rows"][m]) * score_scale
        grad_v = dot_tn(expo.astype(BF), grad_summed)
        r["kv_part"][m, 0] = grad_k.astype(BF).reshape(n, local, width)
        r["kv_part"][m, 1] = grad_v.astype(BF).reshape(n, local, width)
        kv = Scatter(
            net,
            lambda b, m=m: r["kv_part"].at[m, :, b],
            r["kv_fx"].at[m],
            r["kv_fz"].at[m],
        )
        kv.start()
        kv_sums.append(kv)
        grad_queries.append(join_heads(dot(ds, key_rows)) * score_scale)

    def turned_back(grad):
        return (grad * cosine - dot(grad, swap, EXACT) * sine).astype(BF)

    grad_q = turned_back(jnp.concatenate(grad_queries, axis=0))
    r["o_part"][0] = dot_tn(grad_attn, r["mixed_low"][...]).astype(BF).reshape(n, depth, width)
    r["o_part"][1] = dot_tn(r["n_one"][...], grad_q).astype(BF).reshape(n, depth, width)
    sum_o = Scatter(net, lambda b: r["o_part"].at[:, b], r["o_fx"], r["o_fz"])
    for kv in kv_sums:
        kv.forward()
    sum_o.start()
    sum_sh.forward()
    sum_ext.forward()

    for d in range(1, n):
        send_y.arrive(d)
    moe_y = jnp.zeros((rows, half), F32)
    weighed_hi, weighed_lo = [], []
    for b in range(n):
        gate = jnp.sum(jnp.where(lane == b, gates, 0.0), axis=1, keepdims=True)
        gate_hi = gate.astype(BF).astype(F32)
        pick = r["choice"][:, b * slots : (b + 1) * slots].astype(F32)
        weighed_hi.append((pick * gate_hi).astype(BF))
        weighed_lo.append((pick * (gate - gate_hi)).astype(BF))
    y_rows = r["y_in"][...].reshape(n * slots, half)
    moe_y = dot(jnp.concatenate(weighed_hi, axis=1), y_rows)
    moe_y = moe_y + dot(jnp.concatenate(weighed_lo, axis=1), y_rows)
    y_sum[2].start(moe_y + shared_y + core_sum[2].finish())

    sums = [kv.finish() for kv in kv_sums]
    grad_k = turned_back(jnp.concatenate([p[0] for p in sums], axis=0))
    grad_v = jnp.concatenate([p[1] for p in sums], axis=0).astype(BF)

    def small_half(i, h):
        return r["w_small"][i, pl.ds(h * (n // 2), n // 2)].reshape(half, width)

    def grad_one_half(h):
        total = dot_nt(grad_q, small_half(0, h)) + dot_nt(grad_k, small_half(1, h))
        return total + dot_nt(grad_v, small_half(2, h))

    core_sum[3].start(grad_one_half(1 - core))
    mine = grad_one_half(core)
    y_sum[3].start(mine + core_sum[3].finish())
    r["kvw_part"][0] = dot_tn(r["n_one"][...], grad_k).astype(BF).reshape(n, depth, width)
    r["kvw_part"][1] = dot_tn(r["n_one"][...], grad_v).astype(BF).reshape(n, depth, width)
    sum_kvw = Scatter(
        net, lambda b: r["kvw_part"].at[:, b], r["kvw_fx"], r["kvw_fz"]
    )
    sum_kvw.start()
    net.drain_some([share[0].copy])
    share[2].start(y_sum[3].finish())
    share_out = CoreShare(net, r["share_low"])
    res_half = jnp.where(core == 0, r["res"][:, :half], r["res"][:, half:])
    share_out.start(res_half + y_sum[2].finish())
    sum_o.forward()
    sum_kvw.forward()

    grad_one = share[2].finish()
    tok = r["tok"][...].astype(F32)
    r["gtok"][...] = grad_res + norm_back(grad_one, tok, scale_one, gain_one)
    gain_one_row = jnp.sum(grad_one * tok * scale_one, axis=0, keepdims=True)
    block_of = iota((n, model), 0) == iota((n, model), 1) // depth
    to_lane = (iota((model, 128), 0) % depth == iota((model, 128), 1)).astype(F32)
    first = dot(jnp.where(block_of, gain_one_row, 0.0), to_lane, EXACT)
    second = dot(jnp.where(block_of, gain_two_row, 0.0), to_lane, EXACT)
    for b in range(n):
        both = jnp.where(iota((8, 128), 0) == 0, first[b : b + 1], second[b : b + 1])
        r["gains_out"][b] = both
    send_gains = Exchange(net, lambda b: r["gains_out"].at[b], lambda b: r["gains_in"].at[b])
    send_gains.start()
    r["gains_in"][me] = r["gains_out"][me]
    r["out"][...] = share_out.finish()

    sum_sh_total = sum_sh.finish()
    r["dshared"][...] = sum_sh_total
    r["dext"][...] = sum_ext.finish()
    o_total = sum_o.finish()
    r["dwo"][...] = o_total[0]
    r["dqkv"][0] = o_total[1]
    kvw_total = sum_kvw.finish()
    r["dqkv"][1] = kvw_total[0]
    r["dqkv"][2] = kvw_total[1]
    gains = jnp.zeros((8, 128), F32)
    for d in range(1, n):
        send_gains.arrive(d)
    for b in range(n):
        gains = gains + r["gains_in"][b]
    r["dgains"][...] = gains
    for save in saves[3:]:
        save.wait()
    net.drain()


def fits(mesh):
    return mesh.shape["expert"] == 8 and mesh.shape["tensor"] == 4


def fused_body(
    tokens,
    out_grad,
    routes,
    lengths,
    parents,
    attn_gain,
    ffn_gain,
    w_query,
    w_key,
    w_value,
    w_out,
    router,
    shared_gate,
    shared_up,
    shared_down,
    expert_gate,
    expert_up,
    expert_down,
):
    micro, local, model = tokens.shape
    n = lax.axis_size("expert")
    experts = router.shape[1]
    depth, width = w_query.shape
    cap = 4 * local // experts
    hidden, shared = expert_gate.shape[2], shared_gate.shape[1]
    s = dict(
        n=n,
        micro=micro,
        local=local,
        rows=micro * local,
        half=model // 2,
        depth=depth,
        width=width,
        heads=width // HEAD,
        hidden=hidden,
        shared=shared,
        slots=micro * cap,
        experts=experts,
        segs=lengths.shape[1],
    )
    rows = micro * local
    ext = jnp.concatenate(
        [
            attn_gain[:, None],
            ffn_gain[:, None],
            jnp.zeros((depth, 6), BF),
            router,
            jnp.zeros((depth, 120 - experts), BF),
        ],
        axis=1,
    )
    scratch = scratch_shapes(s)
    names = PLACES + list(scratch)
    shape = jax.ShapeDtypeStruct
    vmem, smem = pl.BlockSpec(memory_space=pltpu.VMEM), pl.BlockSpec(memory_space=pltpu.SMEM)
    out, gtok, dqkv, dwo, dext, dshared, dgains, deg, deu, ded = pl.pallas_call(
        functools.partial(layer_kernel, s, names),
        out_shape=(
            shape((rows, model), BF),
            shape((rows, model), F32),
            shape((3, depth, width), F32),
            shape((depth, width), F32),
            shape((depth, 128), F32),
            shape((3, depth, shared), F32),
            shape((8, 128), F32),
            shape((model, hidden), F32),
            shape((model, hidden), F32),
            shape((hidden, model), F32),
        ),
        in_specs=[vmem] * 3 + [smem] * 2 + [vmem] * 11,
        out_specs=[vmem] * 7 + [pl.BlockSpec(memory_space=pl.ANY)] * 3,
        scratch_shapes=list(scratch.values()),
        compiler_params=pltpu.CompilerParams(
            collective_id=0, has_side_effects=True, vmem_limit_bytes=VMEM_LIMIT
        ),
    )(
        tokens.reshape(rows, model),
        out_grad.reshape(rows, model),
        routes.reshape(rows, 2),
        lengths,
        parents,
        w_query,
        w_key,
        w_value,
        w_out.T,
        ext,
        shared_gate,
        shared_up,
        shared_down.T,
        expert_gate[0],
        expert_up[0],
        expert_down[0],
    )
    return (
        out.reshape(micro, local, model),
        gtok.reshape(micro, local, model),
        dgains[0, :depth],
        dgains[1, :depth],
        dqkv[0],
        dqkv[1],
        dqkv[2],
        dwo.T,
        dext[:, 8 : 8 + experts],
        dshared[0],
        dshared[1],
        dshared[2].T,
        deg[None],
        deu[None],
        ded[None],
    )


def solution(mesh):
    in_specs = (
        P(None, "expert", None),
        P(None, "expert", None),
        P(None, "expert", None),
        P(),
        P(),
        P("expert"),
        P("expert"),
        P("expert", "tensor"),
        P("expert", "tensor"),
        P("expert", "tensor"),
        P("tensor", "expert"),
        P("expert", None),
        P("expert", "tensor"),
        P("expert", "tensor"),
        P("tensor", "expert"),
        P("expert", None, "tensor"),
        P("expert", None, "tensor"),
        P("expert", "tensor", None),
    )
    out_specs = (
        P(None, "expert", None),
        P(None, "expert", None),
        P("expert"),
        P("expert"),
        P("expert", "tensor"),
        P("expert", "tensor"),
        P("expert", "tensor"),
        P("tensor", "expert"),
        P("expert", None),
        P("expert", "tensor"),
        P("expert", "tensor"),
        P("tensor", "expert"),
        P("expert", None, "tensor"),
        P("expert", None, "tensor"),
        P("expert", "tensor", None),
    )
    chosen = fused_body if fits(mesh) else plain_body
    return jax.shard_map(chosen, mesh=mesh, in_specs=in_specs, out_specs=out_specs, check_vma=False)
```

```python
import functools
import math
import types

import jax
import jax.numpy as jnp
from jax import lax
from jax.experimental import pallas as pl
from jax.experimental.pallas import tpu as pltpu
from jax.sharding import PartitionSpec as P

HEAD = 64


EPSILON = 1e-06
ROPE_BASE = 10000.0
KEY_BLOCK = 2048


def matmul(left, right):
    return jnp.dot(left, right, preferred_element_type=jnp.float32)


def tree_tables(lengths, parents):
    seg_count = lengths.shape[0]
    identity = jnp.arange(seg_count, dtype=jnp.int32)
    current = identity
    ancestry = jnp.zeros((seg_count, seg_count), jnp.float32)
    for depth_level in range(seg_count):
        chosen_mask = current[:, None] == identity[None, :]
        ancestry = jnp.maximum(ancestry, chosen_mask.astype(jnp.float32))
        current = jnp.sum(jnp.where(chosen_mask, parents[None, :], 0), axis=1)
    seg_ends = jnp.cumsum(lengths)
    starts = seg_ends - lengths
    sizes_float = lengths.astype(jnp.float32)
    offsets = jnp.sum(ancestry * sizes_float[None, :], axis=1) - sizes_float
    return (ancestry, starts, seg_ends, offsets)


def row_tables(row_ids, starts, seg_ends, offsets):
    member = (
        (row_ids[:, None] >= starts[None, :]) & (row_ids[:, None] < seg_ends[None, :])
    ).astype(jnp.float32)
    position_shift = offsets - starts.astype(jnp.float32)
    position = jnp.sum(member * position_shift[None, :], axis=1) + row_ids.astype(jnp.float32)
    return (member, position)


def rotary_tables(position, half_width):
    frequency = ROPE_BASE ** (-jnp.arange(half_width, dtype=jnp.float32) / half_width)
    angles = position[:, None] * frequency[None, :]
    return (jnp.cos(angles)[:, None, :], jnp.sin(angles)[:, None, :])


def rotate(head_values, position):
    half_width = head_values.shape[-1] // 2
    cosines, sine_values = rotary_tables(position, half_width)
    first_half = head_values[..., :half_width]
    second_half = head_values[..., half_width:]
    return jnp.concatenate(
        [
            first_half * cosines - second_half * sine_values,
            second_half * cosines + first_half * sine_values,
        ],
        axis=-1,
    )


def rotate_back(grad_heads, position):
    half_width = grad_heads.shape[-1] // 2
    cosines, sine_values = rotary_tables(position, half_width)
    first_half = grad_heads[..., :half_width]
    second_half = grad_heads[..., half_width:]
    return jnp.concatenate(
        [
            first_half * cosines + second_half * sine_values,
            second_half * cosines - first_half * sine_values,
        ],
        axis=-1,
    )


def silu_parts(gate_val):
    sigmoid_val = jax.nn.sigmoid(gate_val)
    return (gate_val * sigmoid_val, sigmoid_val * (1.0 + gate_val * (1.0 - sigmoid_val)))


def rms_back(grad_normed, source, norm_scale, gain):
    weighted = grad_normed * gain
    inner_mean = jnp.mean(weighted * source, axis=1, keepdims=True)
    return (
        norm_scale * weighted - norm_scale**3 * source * inner_mean,
        jnp.sum(grad_normed * source * norm_scale, axis=0),
    )


def visible(reach_rows, query_ids, key_member, key_ids):
    linked = matmul(reach_rows, key_member.T) > 0.5
    return linked & (key_ids[None, :] <= query_ids[:, None])


def score_block(query_heads, key_heads, seen, score_scale):
    scores = (
        jnp.einsum("qhd,khd->hqk", query_heads, key_heads, preferred_element_type=jnp.float32)
        * score_scale
    )
    return jnp.where(seen[None], jnp.exp(scores), 0.0)


def score_grads(weights_exp, grad_summed, value_heads, delta_rows):
    grad_exp = jnp.einsum(
        "qhd,khd->hqk", grad_summed, value_heads, preferred_element_type=jnp.float32
    )
    return (weights_exp * (grad_exp - jnp.transpose(delta_rows)[:, :, None])).astype(jnp.bfloat16)


def plain_body(
    tokens,
    out_grad,
    routes,
    lengths,
    parents,
    attn_gain,
    ffn_gain,
    w_query,
    w_key,
    w_value,
    w_out,
    router,
    shared_gate,
    shared_up,
    shared_down,
    expert_gate,
    expert_up,
    expert_down,
):
    micro_count, row_count, model_width = tokens.shape
    devices = lax.axis_size("expert")
    tree_rows = row_count * devices
    expert_count = router.shape[1]
    owners = devices // expert_count
    capacity = 4 * row_count // expert_count
    score_scale = HEAD ** (-0.5)
    local_rows = lax.axis_index("expert") * row_count + jnp.arange(row_count, dtype=jnp.int32)
    part_gate = expert_gate[0]
    part_up = expert_up[0]
    part_down = expert_down[0]
    labels = jnp.arange(expert_count, dtype=jnp.int32)
    slot_ids = jnp.arange(expert_count * capacity, dtype=jnp.int32)
    pair_ids = jnp.arange(2 * row_count, dtype=jnp.int32)
    block_size = math.gcd(tree_rows, KEY_BLOCK)
    block_count = tree_rows // block_size
    layer_outputs = []
    token_gradients = []
    dense_sums = None
    expert_sums = None
    for micro_step in range(micro_count):
        gathered = (
            lax.all_gather(attn_gain, "expert", axis=0, tiled=True),
            lax.all_gather(ffn_gain, "expert", axis=0, tiled=True),
            lax.all_gather(w_query, "expert", axis=0, tiled=True),
            lax.all_gather(w_key, "expert", axis=0, tiled=True),
            lax.all_gather(w_value, "expert", axis=0, tiled=True),
            lax.all_gather(w_out, "expert", axis=1, tiled=True),
            lax.all_gather(router, "expert", axis=0, tiled=True),
            lax.all_gather(shared_gate, "expert", axis=0, tiled=True),
            lax.all_gather(shared_up, "expert", axis=0, tiled=True),
            lax.all_gather(shared_down, "expert", axis=1, tiled=True),
        )
        (
            gain_one,
            gain_two,
            query_weight,
            key_weight,
            value_weight,
            out_weight,
            router_weight,
            gate_weight,
            up_weight,
            down_weight,
        ) = gathered
        local_width = query_weight.shape[1]
        head_count = local_width // HEAD
        ancestry, starts, seg_ends, offsets = tree_tables(lengths[micro_step], parents[micro_step])
        member, position = row_tables(local_rows, starts, seg_ends, offsets)
        reach = matmul(member, ancestry)
        tokens_now = tokens[micro_step].astype(jnp.float32)
        norm_one = lax.rsqrt(jnp.mean(tokens_now * tokens_now, axis=1, keepdims=True) + EPSILON)
        normed_one = (tokens_now * norm_one * gain_one).astype(jnp.bfloat16)
        query_pre = matmul(normed_one, query_weight).reshape(row_count, head_count, HEAD)
        key_pre = matmul(normed_one, key_weight).reshape(row_count, head_count, HEAD)
        value_low = matmul(normed_one, value_weight).astype(jnp.bfloat16)
        queries = rotate(query_pre, position).astype(jnp.bfloat16)
        key_heads = rotate(key_pre, position).astype(jnp.bfloat16)
        key_value = jnp.concatenate([key_heads.reshape(row_count, local_width), value_low], axis=1)
        all_pairs = lax.all_gather(key_value, "expert", axis=0, tiled=True)

        def key_block_parts(block_index):
            first_key = block_index * block_size
            key_block = lax.dynamic_slice_in_dim(all_pairs, first_key, block_size, 0)
            key_ids = first_key + jnp.arange(block_size, dtype=jnp.int32)
            key_member, unused = row_tables(key_ids, starts, seg_ends, offsets)
            seen = visible(reach, local_rows, key_member, key_ids)
            block_keys = key_block[:, :local_width].reshape(block_size, head_count, HEAD)
            block_values = key_block[:, local_width:].reshape(block_size, head_count, HEAD)
            return (seen, block_keys, block_values)

        def forward_step(block_index, totals):
            seen, block_keys, block_values = key_block_parts(block_index)
            weights_exp = score_block(queries, block_keys, seen, score_scale)
            summed_part = jnp.einsum(
                "hqk,khd->qhd",
                weights_exp.astype(jnp.bfloat16),
                block_values,
                preferred_element_type=jnp.float32,
            )
            return (
                totals[0] + summed_part.reshape(row_count, local_width),
                totals[1] + jnp.transpose(jnp.sum(weights_exp, axis=2)),
            )

        initial = (
            jnp.zeros((row_count, local_width), jnp.float32),
            jnp.zeros((row_count, head_count), jnp.float32),
        )
        summed, row_total = lax.fori_loop(0, block_count, forward_step, initial)
        mixed = summed.reshape(row_count, head_count, HEAD) / row_total[:, :, None]
        mixed_low = mixed.reshape(row_count, local_width).astype(jnp.bfloat16)
        attn_out = lax.psum(matmul(mixed_low, out_weight), "tensor")
        residual = tokens_now + attn_out
        norm_two = lax.rsqrt(jnp.mean(residual * residual, axis=1, keepdims=True) + EPSILON)
        normed_two = (residual * norm_two * gain_two).astype(jnp.bfloat16)
        shared_g = matmul(normed_two, gate_weight)
        shared_u = matmul(normed_two, up_weight)
        shared_act, shared_slope = silu_parts(shared_g)
        shared_h = (shared_act * shared_u).astype(jnp.bfloat16)
        shared_y = matmul(shared_h, down_weight)
        logits = matmul(normed_two, router_weight)
        route_now = routes[micro_step]
        choose = (route_now[:, :, None] == labels[None, None, :]).astype(jnp.float32)
        gate_values = jax.nn.softmax(jnp.sum(choose * logits[:, None, :], axis=2), axis=1)
        flat_routes = route_now.reshape(2 * row_count)
        expert_hits = (flat_routes[:, None] == labels[None, :]).astype(jnp.int32)
        slot_rank = jnp.sum((jnp.cumsum(expert_hits, axis=0) - expert_hits) * expert_hits, axis=1)
        slot_index = flat_routes * capacity + slot_rank
        slot_match = slot_index[None, :] == slot_ids[:, None]
        filled = jnp.any(slot_match, axis=1)
        source = jnp.sum(jnp.where(slot_match, pair_ids[None, :], 0), axis=1)

        def to_owners(table, row_index):
            picked = jnp.take(table, row_index, axis=0)
            picked = jnp.where(filled[:, None], picked, jnp.zeros_like(picked))
            spread = jnp.broadcast_to(
                picked.reshape(expert_count, 1, capacity, model_width),
                (expert_count, owners, capacity, model_width),
            )
            return spread.reshape(devices, capacity, model_width)

        def from_owners(returned):
            merged = jnp.sum(
                returned.reshape(expert_count, owners, capacity, model_width), axis=1
            ).reshape(expert_count * capacity, model_width)
            return jnp.take(merged, slot_index, axis=0).reshape(row_count, 2, model_width)

        arrived = lax.all_to_all(
            to_owners(normed_two, source // 2), "expert", split_axis=0, concat_axis=0, tiled=True
        )
        slot_count = arrived.shape[1]
        flat_in = arrived.reshape(devices * slot_count, model_width)
        expert_g = matmul(flat_in, part_gate)
        expert_u = matmul(flat_in, part_up)
        expert_act, expert_unused = silu_parts(expert_g)
        expert_h = (expert_act * expert_u).astype(jnp.bfloat16)
        partial_out = matmul(expert_h, part_down).reshape(devices, slot_count, model_width)
        combined = lax.all_to_all(
            partial_out.astype(jnp.bfloat16), "expert", split_axis=0, concat_axis=0, tiled=True
        ).astype(partial_out.dtype)
        hidden_width = expert_g.shape[1]
        combined, arrived, kept_g, kept_u, kept_h = (
            combined,
            arrived,
            expert_g.reshape(devices, slot_count, hidden_width),
            expert_u.reshape(devices, slot_count, hidden_width),
            expert_h.reshape(devices, slot_count, hidden_width),
        )
        expert_y = from_owners(combined)
        cot_low = out_grad[micro_step]
        cotangent = cot_low.astype(jnp.float32)
        moe_part = jnp.sum(gate_values[:, :, None] * expert_y, axis=1)
        gate_dots = jnp.sum(cotangent[:, None, :] * expert_y, axis=2)
        ffn_out, grad_gate = (
            lax.psum((shared_y + moe_part).astype(jnp.bfloat16), "tensor").astype(jnp.float32),
            lax.psum(gate_dots.astype(jnp.bfloat16), "tensor").astype(jnp.float32),
        )
        layer_outputs.append((residual + ffn_out).astype(jnp.bfloat16))
        grad_shared_h = matmul(cot_low, down_weight.T)
        grad_shared_g = (grad_shared_h * shared_u * shared_slope).astype(jnp.bfloat16)
        grad_shared_u = (grad_shared_h * shared_act).astype(jnp.bfloat16)
        grad_chosen = gate_values * (
            grad_gate - jnp.sum(gate_values * grad_gate, axis=1, keepdims=True)
        )
        grad_logits = jnp.sum(choose * grad_chosen[:, :, None], axis=1).astype(jnp.bfloat16)
        grad_pairs_out = (
            (gate_values[:, :, None] * cotangent[:, None, :])
            .astype(jnp.bfloat16)
            .reshape(2 * row_count, model_width)
        )
        arrived_grad = lax.all_to_all(
            to_owners(grad_pairs_out, source), "expert", split_axis=0, concat_axis=0, tiled=True
        )
        slot_total = arrived_grad.shape[0] * arrived_grad.shape[1]
        flat_grad = arrived_grad.reshape(slot_total, model_width)
        flat_in = arrived.reshape(slot_total, model_width)
        hidden_width = kept_g.shape[2]
        expert_g = kept_g.reshape(slot_total, hidden_width)
        expert_u = kept_u.reshape(slot_total, hidden_width)
        expert_h = kept_h.reshape(slot_total, hidden_width)
        expert_act, expert_slope = silu_parts(expert_g)
        grad_hidden = matmul(flat_grad, part_down.T)
        grad_expert_g = (grad_hidden * expert_u * expert_slope).astype(jnp.bfloat16)
        grad_expert_u = (grad_hidden * expert_act).astype(jnp.bfloat16)
        grad_in = matmul(grad_expert_g, part_gate.T) + matmul(grad_expert_u, part_up.T)
        returned = lax.all_to_all(
            grad_in.reshape(arrived_grad.shape[0], arrived_grad.shape[1], model_width),
            "expert",
            split_axis=0,
            concat_axis=0,
            tiled=True,
        )
        normed_part = (
            matmul(grad_shared_g, gate_weight.T)
            + matmul(grad_shared_u, up_weight.T)
            + jnp.sum(from_owners(returned), axis=1)
        )
        grad_normed_two = lax.psum(normed_part, "tensor") + matmul(grad_logits, router_weight.T)
        grad_norm_part, grad_gain_two = rms_back(grad_normed_two, residual, norm_two, gain_two)
        grad_residual = cotangent + grad_norm_part
        grad_attn = grad_residual.astype(jnp.bfloat16)
        grad_mixed = matmul(grad_attn, out_weight.T).reshape(row_count, head_count, HEAD)
        grad_summed = (grad_mixed / row_total[:, :, None]).astype(jnp.bfloat16)
        delta_rows = jnp.sum(grad_mixed * mixed, axis=2) / row_total

        def block_terms(block_index):
            seen, block_keys, block_values = key_block_parts(block_index)
            weights_exp = score_block(queries, block_keys, seen, score_scale)
            grad_scores = score_grads(weights_exp, grad_summed, block_values, delta_rows)
            return (weights_exp, grad_scores, block_keys)

        zero_query = jnp.zeros((row_count, head_count, HEAD), jnp.float32)

        def key_step(gradient_query_weight, block_index):
            weights_exp, grad_scores, block_keys = block_terms(block_index)
            gradient_query_weight = (
                gradient_query_weight
                + jnp.einsum(
                    "hqk,khd->qhd", grad_scores, block_keys, preferred_element_type=jnp.float32
                )
                * score_scale
            )
            grad_keys = (
                jnp.einsum("hqk,qhd->khd", grad_scores, queries, preferred_element_type=jnp.float32)
                * score_scale
            )
            grad_values = jnp.einsum(
                "hqk,qhd->khd",
                weights_exp.astype(jnp.bfloat16),
                grad_summed,
                preferred_element_type=jnp.float32,
            )
            return (
                gradient_query_weight,
                jnp.concatenate(
                    [
                        grad_keys.reshape(block_size, local_width),
                        grad_values.reshape(block_size, local_width),
                    ],
                    axis=1,
                ),
            )

        gradient_query_weight, key_terms = lax.scan(
            key_step, zero_query, jnp.arange(block_count, dtype=jnp.int32)
        )
        grad_pairs = lax.psum_scatter(
            key_terms.reshape(tree_rows, 2 * local_width), "expert", scatter_dimension=0, tiled=True
        )
        grad_keys_rot = grad_pairs[:, :local_width].reshape(row_count, head_count, HEAD)
        grad_query_pre = (
            rotate_back(gradient_query_weight, position)
            .reshape(row_count, local_width)
            .astype(jnp.bfloat16)
        )
        grad_key_pre = (
            rotate_back(grad_keys_rot, position)
            .reshape(row_count, local_width)
            .astype(jnp.bfloat16)
        )
        grad_value_low = grad_pairs[:, local_width:].astype(jnp.bfloat16)
        normed_grad = (
            matmul(grad_query_pre, query_weight.T)
            + matmul(grad_key_pre, key_weight.T)
            + matmul(grad_value_low, value_weight.T)
        )
        grad_normed_one = lax.psum(normed_grad.astype(jnp.bfloat16), "tensor").astype(jnp.float32)
        grad_norm_first, grad_gain_one = rms_back(grad_normed_one, tokens_now, norm_one, gain_one)
        token_gradients.append(grad_residual + grad_norm_first)
        dense_step = (
            grad_gain_one,
            grad_gain_two,
            matmul(normed_one.T, grad_query_pre),
            matmul(normed_one.T, grad_key_pre),
            matmul(normed_one.T, grad_value_low),
            matmul(mixed_low.T, grad_attn),
            matmul(normed_two.T, grad_logits),
            matmul(normed_two.T, grad_shared_g),
            matmul(normed_two.T, grad_shared_u),
            matmul(shared_h.T, cot_low),
        )
        expert_step = (
            matmul(flat_in.T, grad_expert_g),
            matmul(flat_in.T, grad_expert_u),
            matmul(expert_h.T, flat_grad),
        )
        if dense_sums is None:
            dense_sums = dense_step
            expert_sums = expert_step
        else:
            dense_sums = tuple(
                (earlier + latest for earlier, latest in zip(dense_sums, dense_step))
            )
            expert_sums = tuple(
                (earlier + latest for earlier, latest in zip(expert_sums, expert_step))
            )
    final_gate, final_up, final_down = expert_sums
    reduced = (
        lax.psum_scatter(dense_sums[0], "expert", scatter_dimension=0, tiled=True),
        lax.psum_scatter(dense_sums[1], "expert", scatter_dimension=0, tiled=True),
        lax.psum_scatter(dense_sums[2], "expert", scatter_dimension=0, tiled=True),
        lax.psum_scatter(dense_sums[3], "expert", scatter_dimension=0, tiled=True),
        lax.psum_scatter(dense_sums[4], "expert", scatter_dimension=0, tiled=True),
        lax.psum_scatter(dense_sums[5], "expert", scatter_dimension=1, tiled=True),
        lax.psum_scatter(dense_sums[6], "expert", scatter_dimension=0, tiled=True),
        lax.psum_scatter(dense_sums[7], "expert", scatter_dimension=0, tiled=True),
        lax.psum_scatter(dense_sums[8], "expert", scatter_dimension=0, tiled=True),
        lax.psum_scatter(dense_sums[9], "expert", scatter_dimension=1, tiled=True),
    )
    return (
        jnp.stack(layer_outputs),
        jnp.stack(token_gradients),
        reduced[0],
        reduced[1],
        reduced[2],
        reduced[3],
        reduced[4],
        reduced[5],
        reduced[6],
        reduced[7],
        reduced[8],
        reduced[9],
        final_gate[None],
        final_up[None],
        final_down[None],
    )


MESH = pl.DeviceIdType.MESH
BF = jnp.bfloat16
F32 = jnp.float32
EXACT = lax.Precision.HIGHEST
VMEM_LIMIT = 63 * 2**20


def product(left, right, dims, precision=None):
    return lax.dot_general(
        left, right, (dims, ((), ())), preferred_element_type=F32, precision=precision
    )


def dot(left, right, precision=None):
    return product(left, right, ((1,), (0,)), precision)


def dot_nt(left, right, precision=None):
    return product(left, right, ((1,), (1,)), precision)


def dot_tn(left, right, precision=None):
    return product(left, right, ((0,), (0,)), precision)


def iota(shape, dim):
    return lax.broadcasted_iota(jnp.int32, shape, dim)


class Net:
    def __init__(self, expert_size, send_sems, recv_sems):
        self.e = lax.axis_index("expert")
        self.t = lax.axis_index("tensor")
        self.n = expert_size
        self.nz = expert_size // 2
        self.z = self.e // 2
        self.x = self.e % 2
        self.y = self.t // 2
        self.core = self.t % 2
        self.send_sems = send_sems
        self.recv_sems = recv_sems
        self.sends = 0
        self.recvs = 0
        self.open = []

    def recv_slots(self, count):
        first = self.recvs
        self.recvs += count
        return first

    def ids(self, to):
        return {"expert": to[0], "tensor": to[1]}

    def push(self, src, dst, to, slot, when=None):
        copy = pltpu.make_async_remote_copy(
            src_ref=src,
            dst_ref=dst,
            send_sem=self.send_sems.at[self.sends],
            recv_sem=self.recv_sems.at[slot],
            device_id=self.ids(to),
            device_id_type=MESH,
        )
        self.sends += 1
        if when is None:
            copy.start()
        else:
            pl.when(when)(copy.start)
        self.open.append((copy, when))

    def landed(self, dst, slot, when=None):
        copy = pltpu.make_async_remote_copy(
            src_ref=dst,
            dst_ref=dst,
            send_sem=self.send_sems.at[0],
            recv_sem=self.recv_sems.at[slot],
            device_id=self.ids(self.other_core()),
            device_id_type=MESH,
        )
        if when is None:
            copy.wait_recv()
        else:
            pl.when(when)(copy.wait_recv)

    def drain(self, first=0, last=None):
        last = len(self.open) if last is None else last
        for copy, when in self.open[first:last]:
            if when is None:
                copy.wait_send()
            else:
                pl.when(when)(copy.wait_send)
        self.open[first:last] = []

    def other_core(self):
        return (self.e, self.t + 1 - 2 * self.core)

    def across_y(self):
        return (self.e, (self.t + 2) % 4)

    def across_x(self):
        return (self.e + 1 - 2 * self.x, self.t)

    def peer(self, step):
        return (self.e + step) % self.n

    def greet(self):
        barrier = pltpu.get_barrier_semaphore()
        partners = [(self.peer(d), self.t) for d in range(1, self.n)]
        partners += [self.other_core(), self.across_y()]
        for to in partners:
            pl.semaphore_signal(barrier, inc=1, device_id=self.ids(to), device_id_type=MESH)
        return lambda: pl.semaphore_wait(barrier, len(partners))


class Gather:
    def __init__(self, net, block, chunks=1, on_land=None):
        self.net, self.block, self.chunks, self.on_land = net, block, chunks, on_land
        self.slot = net.recv_slots(net.n * chunks)

    def start(self):
        net = self.net
        for k in range(self.chunks):
            own, slot = self.block(net.e, k), self.slot + net.e * self.chunks + k
            for way in (1, -1):
                there = net.z + way
                fits_in = (there >= 0) & (there < net.nz)
                net.push(own, own, (there % net.nz * 2 + net.x, net.t), slot, fits_in)
            net.push(own, own, net.across_x(), slot)

    def step(self, distance):
        net = self.net
        for k in range(self.chunks):
            for way in (1, -1):
                source, there = net.z - way * distance, net.z + way
                real = (source >= 0) & (source < net.nz)
                onward = real & (there >= 0) & (there < net.nz)
                b = source % net.nz * 2 + net.x
                part, slot = self.block(b, k), self.slot + b * self.chunks + k
                net.landed(part, slot, real)
                net.push(part, part, (there % net.nz * 2 + net.x, net.t), slot, onward)
                net.push(part, part, net.across_x(), slot, real)
                if self.on_land is not None:
                    self.on_land(b, real)

    def finish(self):
        net = self.net
        for d in range(net.nz):
            b = (net.z + d) % net.nz * 2 + 1 - net.x
            for k in range(self.chunks):
                net.landed(self.block(b, k), self.slot + b * self.chunks + k)
            if self.on_land is not None:
                self.on_land(b, None)


class Scatter:
    def __init__(self, net, block, from_x, from_z):
        self.net, self.block = net, block
        self.from_x, self.from_z = from_x, from_z
        self.slot_x = net.recv_slots(net.nz)
        self.slot_z = net.recv_slots(net.nz)

    def start(self):
        net = self.net
        for d in range(1, net.nz + 1):
            zz = (net.z + d) % net.nz
            net.push(
                self.block(zz * 2 + 1 - net.x), self.from_x.at[zz], net.across_x(), self.slot_x + zz
            )

    def forward(self):
        net = self.net
        for d in range(1, net.nz):
            zz = (net.z + d) % net.nz
            net.landed(self.from_x.at[zz], self.slot_x + zz)
            pair = self.block(zz * 2 + net.x)[...].astype(F32) + self.from_x[zz].astype(F32)
            self.from_x[zz] = pair.astype(BF)
            net.push(
                self.from_x.at[zz],
                self.from_z.at[net.z],
                (zz * 2 + net.x, net.t),
                self.slot_z + net.z,
            )

    def finish(self):
        net = self.net
        net.landed(self.from_x.at[net.z], self.slot_x + net.z)
        total = self.block(net.e)[...].astype(F32) + self.from_x[net.z].astype(F32)
        for d in range(1, net.nz):
            zz = (net.z + d) % net.nz
            net.landed(self.from_z.at[zz], self.slot_z + zz)
            total = total + self.from_z[zz].astype(F32)
        return total


class Exchange:
    def __init__(self, net, outgoing, incoming):
        self.net, self.outgoing, self.incoming = net, outgoing, incoming
        self.slot = net.recv_slots(net.n)

    def start(self):
        net = self.net
        for d in range(1, net.n):
            to = net.peer(d)
            net.push(self.outgoing(to), self.incoming(net.e), (to, net.t), self.slot + net.e)

    def arrive(self, d):
        source = self.net.peer(d)
        self.net.landed(self.incoming(source), self.slot + source)
        return source

    def finish(self):
        for d in range(1, self.net.n):
            self.arrive(d)


class Dispatch:
    def __init__(self, net, outgoing, incoming):
        self.net, self.outgoing, self.incoming = net, outgoing, incoming
        self.send = Exchange(
            net, lambda b: outgoing.at[b], lambda b: incoming.at[b, net.core, net.y]
        )
        self.slot_y = net.recv_slots(net.n)
        self.slot_core = net.recv_slots(1)

    def start(self):
        net = self.net
        self.send.start()
        self.incoming[net.e, net.core, net.y] = self.outgoing[net.e]

    def relay_y(self):
        net = self.net
        for d in range(net.n):
            b = net.e if d == 0 else self.send.arrive(d)
            part = self.incoming.at[b, net.core, net.y]
            net.push(part, part, net.across_y(), self.slot_y + b)

    def relay_core(self):
        net = self.net
        for d in range(net.n):
            b = net.peer(d)
            net.landed(self.incoming.at[b, net.core, 1 - net.y], self.slot_y + b)
        part = self.incoming.at[:, net.core]
        net.push(part, part, net.other_core(), self.slot_core)

    def finish(self):
        self.net.landed(self.incoming.at[:, 1 - self.net.core], self.slot_core)


class Swap:
    def __init__(self, net, out_buf, in_buf, partner):
        self.net, self.out_buf, self.in_buf, self.partner = net, out_buf, in_buf, partner
        self.slot = net.recv_slots(1)

    def start(self, value):
        self.out_buf[...] = value.astype(self.out_buf.dtype)
        self.send()

    def send(self):
        self.net.push(self.out_buf, self.in_buf, self.partner, self.slot)

    def other(self):
        self.net.landed(self.in_buf, self.slot)
        return self.in_buf[...].astype(F32)

    def both(self):
        return self.out_buf[...].astype(F32) + self.other()


class Share:
    def __init__(self, net, halves):
        self.net, self.halves = net, halves
        self.slot = net.recv_slots(1)

    def start(self, value):
        net = self.net
        self.halves[net.core] = value.astype(self.halves.dtype)
        part = self.halves.at[net.core]
        net.push(part, part, net.other_core(), self.slot)

    def finish(self):
        net = self.net
        net.landed(self.halves.at[1 - net.core], self.slot)
        return jnp.concatenate([self.halves[0], self.halves[1]], axis=1)


def silu_both(value):
    gate = jax.nn.sigmoid(value)
    return value * gate, gate * (1.0 + value * (1.0 - gate))


def norm_scale(value):
    return lax.rsqrt(jnp.mean(value * value, axis=1, keepdims=True) + EPSILON)


def norm_back(grad_normed, source, scale, gain):
    weighted = grad_normed * gain
    inner = jnp.mean(weighted * source, axis=1, keepdims=True)
    return scale * weighted - scale * scale * scale * source * inner


PLACES = ["tok", "cot", "routes", "lengths", "parents", "gain_a", "gain_b", "wq", "wk", "wv"]
PLACES += ["wo", "router", "sg", "su", "sd", "eg", "eu", "ed"]
RESULTS = ["out", "gtok", "dga", "dgb", "dwq", "dwk", "dwv", "dwo", "drouter"]
RESULTS += ["dsg", "dsu", "dsd", "deg", "deu", "ded"]


def scratch_shapes(s):
    n, local, half = s.n, s.local, s.half
    depth, hidden, shared, cap = s.depth, s.hidden, s.shared, s.cap
    micro, nz = s.micro, s.n // 2
    model, wide, stack, tree = 2 * half, 2 * s.width, s.heads * local, n * local
    part = cap // 4
    vm = pltpu.VMEM
    return dict(
        w_kv=vm((n, depth, wide), BF),
        w_qo=vm((n, depth, wide), BF),
        w_sh=vm((3, n, depth, shared), BF),
        ext_in=vm((n, 16, 128), BF),
        tok_all=vm((n, 2, 2, micro * local // 4, model), BF),
        cos_all=vm((n, micro * local, 128), F32),
        sin_all=vm((n, micro * local, 128), F32),
        kv=vm((micro, n, local, wide), BF),
        q_rows=vm((micro, stack, wide), BF),
        expo=vm((micro, stack, tree), F32),
        total=vm((micro, stack, 1), F32),
        mixed=vm((micro, local, wide), F32),
        mixed_low=vm((micro * local, wide), BF),
        choice=vm((micro, local, n * cap), BF),
        choice_wide=vm((micro, local, n * 128), BF),
        res=vm((micro, local, model), F32),
        n_one=vm((micro * local, model), BF),
        n_two=vm((micro * local, model), BF),
        c_out=vm((micro, n, part, model), BF),
        c_in=vm((micro, n, 2, 2, part, model), BF),
        x_out=vm((micro, n, part, model), BF),
        x_in=vm((micro, n, 2, 2, part, model), BF),
        h_out=vm((micro, n, 16, 128), BF),
        h_in=vm((micro, n, 16, 128), BF),
        gate_col=vm((micro, n * cap, 1), F32),
        e_h=vm((micro, n * cap, hidden), BF),
        e_dg=vm((micro, n * cap, hidden), BF),
        e_du=vm((micro, n * cap, hidden), BF),
        y_core=vm((micro, n, cap, half), BF),
        g_core=vm((micro, n, cap, half), BF),
        y_in=vm((micro, n, cap, half), BF),
        g_in=vm((micro, n, cap, half), BF),
        d_out=vm((micro, n, 8, 128), F32),
        d_in=vm((micro, n, 8, 128), F32),
        d_tensor=vm((micro, 4, 8, 128), F32),
        core_a=vm((micro, 2, local, half), F32),
        core_b=vm((4, micro * local, half), BF),
        core_c=vm((micro, 2, local, half), F32),
        s_grads=vm((3, micro * local, shared), BF),
        s_own=vm((2, micro * local, half), F32),
        y_swap=vm((4, micro, 2, local, half), BF),
        share_a=vm((micro, 2, local, half), F32),
        share_b=vm((micro, 2, local, half), F32),
        share_c=vm((micro, 2, local, half), F32),
        share_out=vm((micro, 2, local, half), BF),
        kv_part=vm((micro, n, local, wide), BF),
        kv_fx=vm((micro, nz, local, wide), BF),
        kv_fz=vm((micro, nz, local, wide), BF),
        sh_part=vm((3, n, depth, shared), BF),
        sh_fx=vm((3, nz, depth, shared), BF),
        sh_fz=vm((3, nz, depth, shared), BF),
        w_part=vm((2, n, depth, wide), BF),
        w_fx=vm((2, nz, depth, wide), BF),
        w_fz=vm((2, nz, depth, wide), BF),
        gains_out=vm((n, 16, 128), F32),
        gains_in=vm((n, 16, 128), F32),
        stage=vm((2, half, hidden), F32),
        stage_d=vm((hidden, half), F32),
        save_sems=pltpu.SemaphoreType.DMA((6,)),
        send_sems=pltpu.SemaphoreType.DMA((SENDS,)),
        recv_sems=pltpu.SemaphoreType.DMA((RECVS,)),
    )


SENDS = 400
RECVS = 400


def layer_kernel(s, names, *refs):
    r = types.SimpleNamespace(**dict(zip(names, refs)))
    n, local, width, half = s.n, s.local, s.width, s.half
    depth, hidden, shared, cap = s.depth, s.hidden, s.shared, s.cap
    micro, heads = s.micro, s.heads
    rows, model, tree, wide, stack = micro * local, 2 * half, n * local, 2 * width, heads * local
    part = cap // 4
    net = Net(n, r.send_sems, r.recv_sems)
    me, core, y = net.e, net.core, net.y
    ready = net.greet()
    micros = range(micro)
    my_half = pl.ds(pl.multiple_of(core * half, 128), half)
    other_half = pl.ds(pl.multiple_of((1 - core) * half, 128), half)

    def rows_of(m):
        return slice(m * local, (m + 1) * local)

    left = (iota((width, wide), 1) == iota((width, wide), 0)).astype(BF)
    right = (iota((width, wide), 1) == iota((width, wide), 0) + width).astype(BF)
    r.w_kv[me] = (dot(r.wk[...], left) + dot(r.wv[...], right)).astype(BF)
    r.tok_all[me] = r.tok[...].reshape(2, 2, rows // 4, model)
    r.w_qo[me] = (dot(r.wq[...], left) + dot_tn(r.wo[...], right)).astype(BF)
    ext = [r.gain_a[...].astype(F32), r.gain_b[...].astype(F32), jnp.zeros((6, depth), F32)]
    ext = jnp.concatenate(ext + [r.router[...].astype(F32)], axis=0).astype(BF)
    pad = (iota((depth, 128), 1) == iota((depth, 128), 0)).astype(BF)
    r.ext_in[me] = dot(ext, pad).astype(BF)
    for i, name in enumerate(("sg", "su", "sd")):
        r.w_sh[i, me] = getattr(r, name)[...]

    slot_ty, slot_tc = net.recv_slots(n), net.recv_slots(n)

    def token_on(b, when):
        quarter = r.tok_all.at[b, core, y]
        net.push(quarter, quarter, net.across_y(), slot_ty + b, when)

    get_kv = Gather(net, lambda b, k: r.w_kv.at[b])
    get_qo = Gather(net, lambda b, k: r.w_qo.at[b])
    get_tok = Gather(net, lambda b, k: r.tok_all.at[b, core, y], on_land=token_on)
    get_sh = [Gather(net, lambda b, k, i=i: r.w_sh.at[i, b]) for i in range(3)]
    get_ext = Exchange(net, lambda b: r.ext_in.at[me], lambda b: r.ext_in.at[b])
    ready()
    get_ext.start()
    get_tok.start()
    get_kv.start()
    get_qo.start()

    eye = (iota((128, 128), 0) == iota((128, 128), 1)).astype(BF)
    routes = dot_nt(eye, r.routes[...].astype(BF))
    lane = iota((local, 16), 1) - 8
    earlier = (iota((local, local), 1) < iota((local, local), 0)).astype(BF)

    def spread(span):
        of_lane = iota((16, n * span), 1) // span
        return (iota((16, n * span), 0) - 8 == of_lane).astype(BF)

    hot_one, hot_two, quarter = [], [], []
    send_c = [Dispatch(net, r.c_out.at[m], r.c_in.at[m]) for m in micros]
    send_h = [
        Exchange(net, lambda b, m=m: r.h_out.at[m, b], lambda b, m=m: r.h_in.at[m, b])
        for m in micros
    ]
    for m in micros:
        one = lane == routes[:, 2 * m : 2 * m + 1].astype(jnp.int32)
        two = lane == routes[:, 2 * m + 1 : 2 * m + 2].astype(jnp.int32)
        hot_one.append(one)
        hot_two.append(two)
        hits = (one | two).astype(F32)
        rank = jnp.where(hits > 0.5, dot(earlier, hits.astype(BF)), -1.0).astype(BF)

        def taken(span, first=0):
            wanted = iota((local, n * span), 1) % span + first
            return (dot(rank, spread(span)) == wanted.astype(F32)).astype(BF)

        r.choice[m] = taken(cap)
        r.choice_wide[m] = taken(128)
        quarter.append(taken(part, (core * 2 + y) * part))
        hit_rows = dot_tn(hits.astype(BF), r.choice_wide[m]).astype(BF)
        for b in range(n):
            r.h_out[m, b] = hit_rows[:, b * 128 : (b + 1) * 128]
        r.h_in[m, me] = r.h_out[m, me]
        picked = dot_tn(quarter[m], r.cot[rows_of(m)]).astype(BF)
        r.c_out[m] = picked.reshape(n, part, model)

    def segments(m):
        starts, ends, paths, shifts, begin = [], [], [], [], 0
        for seg in range(s.segs):
            size = r.lengths[m, seg]
            starts.append(begin)
            ends.append(begin + size)
            begin = begin + size
            if seg == 0:
                paths.append(jnp.int32(1))
                shifts.append(jnp.int32(0))
            else:
                parent = r.parents[m, seg]
                path, shift = jnp.int32(0), jnp.int32(0)
                for other in range(seg):
                    is_parent = parent == other
                    path = jnp.where(is_parent, paths[other], path)
                    shift = jnp.where(
                        is_parent, shifts[other] + ends[other] - starts[other], shift
                    )
                paths.append(path + (1 << seg))
                shifts.append(shift)
        return starts, ends, paths, shifts

    tables = [segments(m) for m in micros]

    def row_values(m, ids):
        starts, ends, paths, shifts = tables[m]
        path, place, own = jnp.zeros_like(ids), jnp.zeros_like(ids), jnp.zeros_like(ids)
        for seg in range(s.segs):
            inside = (ids >= starts[seg]) & (ids < ends[seg])
            path = jnp.where(inside, paths[seg], path)
            place = jnp.where(inside, ids - starts[seg] + shifts[seg], place)
            own = jnp.where(inside, 1 << seg, own)
        return path, place, own

    turn = (iota((1, 128), 1) % (HEAD // 2)).astype(F32)
    frequency = jnp.exp(turn * (-math.log(ROPE_BASE) / (HEAD // 2)))

    def angle_step(b, carry):
        ids = b * local + iota((local, 1), 0)
        place = jnp.concatenate([row_values(m, ids)[1] for m in micros], axis=0)
        angle = place.astype(F32) * frequency
        r.cos_all[b] = jnp.cos(angle)
        r.sin_all[b] = jnp.sin(angle)
        return carry

    lax.fori_loop(0, n, angle_step, 0)
    is_left = iota((1, wide), 1) < width
    swap_r, swap_c = iota((wide, wide), 0), iota((wide, wide), 1)
    lower = swap_c % HEAD < HEAD // 2
    swap = jnp.where(lower & (swap_r == swap_c + HEAD // 2), -1.0, 0.0)
    swap = jnp.where(~lower & (swap_r == swap_c - HEAD // 2), 1.0, swap)
    swap = jnp.where(is_left, swap, 0.0)
    swap_low = swap.astype(BF)

    def turns(b):
        cosine = jnp.concatenate([r.cos_all[b]] * (wide // 128), axis=1)
        sine = jnp.concatenate([r.sin_all[b]] * (wide // 128), axis=1)
        return jnp.where(is_left, cosine, 1.0), sine

    for distance in range(1, net.nz):
        get_tok.step(distance)
        get_kv.step(distance)
        get_qo.step(distance)
    get_tok.finish()
    get_ext.finish()
    for d in range(1, n):
        b = net.peer(d)
        net.landed(r.tok_all.at[b, core, 1 - y], slot_ty + b)
        both = r.tok_all.at[b, core]
        net.push(both, both, net.other_core(), slot_tc + b)

    def lay(b):
        place = iota((128, model), 0)
        return (place < depth) & (place + b * depth == iota((128, model), 1))

    ext_all = jnp.zeros((16, model), F32)
    for b in range(n):
        ext_all = ext_all + dot(r.ext_in[b], lay(b).astype(BF))
    gain_one, gain_two = ext_all[0:1], ext_all[1:2]
    ext_low = ext_all.astype(BF)
    get_kv.finish()
    w_kv = r.w_kv[...].reshape(model, wide)
    w_kv_swapped = dot(w_kv, swap_low).astype(BF)

    def normed(block):
        value = block.astype(F32)
        return (value * norm_scale(value) * gain_one).astype(BF)

    def key_value(b):
        block = normed(r.tok_all[b].reshape(rows, model))
        cosine, sine = turns(b)
        both = (dot(block, w_kv) * cosine + dot(block, w_kv_swapped) * sine).astype(BF)
        for m in micros:
            r.kv[m, b] = both[rows_of(m)]

    key_value(me)

    def key_value_step(d, carry):
        b = net.peer(d)
        net.landed(r.tok_all.at[b, 1 - core], slot_tc + b)
        key_value(b)
        return carry

    lax.fori_loop(1, n, key_value_step, 0)
    get_qo.finish()
    r.n_one[...] = normed(r.tok[...])
    w_qo = r.w_qo[...].reshape(model, wide)
    cosine, sine = turns(me)
    cosine = jnp.where(is_left, cosine, 0.0)
    queries = dot(r.n_one[...], w_qo) * cosine
    queries = queries + dot(r.n_one[...], dot(w_qo, swap_low).astype(BF)) * sine
    queries = queries.astype(BF)
    for m in micros:
        send_c[m].start()
        send_h[m].start()
    get_sh[0].start()

    head_of = iota((1, wide), 1) // HEAD
    q_masks = [head_of == h for h in range(heads)]
    v_masks = [head_of == heads + h for h in range(heads)]

    def by_head(block, masks):
        return jnp.concatenate(
            [jnp.where(mask, block, jnp.zeros_like(block)) for mask in masks], axis=0
        )

    def join_heads(value, masks):
        total = jnp.zeros((local, wide), F32)
        for h, mask in enumerate(masks):
            total = total + jnp.where(mask, value[h * local : (h + 1) * local], 0.0)
        return total

    def o_half(h):
        return r.w_qo[pl.ds(h * (n // 2), n // 2)].reshape(half, wide)

    core_a = [Swap(net, r.core_a.at[m, 0], r.core_a.at[m, 1], net.other_core()) for m in micros]
    core_c = [Swap(net, r.core_c.at[m, 0], r.core_c.at[m, 1], net.other_core()) for m in micros]
    core_b = [
        Swap(net, r.core_b.at[2 * i], r.core_b.at[2 * i + 1], net.other_core()) for i in range(2)
    ]
    y_swap = [
        [Swap(net, r.y_swap.at[i, m, 0], r.y_swap.at[i, m, 1], net.across_y()) for m in micros]
        for i in range(4)
    ]
    share_a = [Share(net, r.share_a.at[m]) for m in micros]
    share_b = [Share(net, r.share_b.at[m]) for m in micros]
    share_c = [Share(net, r.share_c.at[m]) for m in micros]
    share_out = [Share(net, r.share_out.at[m]) for m in micros]

    score_scale = HEAD**-0.5
    for m in micros:
        r.q_rows[m] = by_head(queries[rows_of(m)], q_masks)
        kv_rows = r.kv[m].reshape(tree, wide)
        ids = me * local + iota((stack, 1), 0) % local
        path, unused, unused_two = row_values(m, ids)
        key_ids = iota((1, tree), 1)
        unused, unused_two, key_seg = row_values(m, key_ids)
        seen = ((path & key_seg) != 0) & (key_ids <= ids)
        scores = dot_nt(r.q_rows[m], kv_rows) * score_scale
        expo = jnp.where(seen, jnp.exp(scores), 0.0)
        r.expo[m] = expo
        total = jnp.sum(expo, axis=1, keepdims=True)
        r.total[m] = total
        mixed = join_heads(dot(expo.astype(BF), kv_rows) / total, v_masks)
        r.mixed[m] = mixed
        r.mixed_low[rows_of(m)] = mixed.astype(BF)
        core_a[m].start(dot_nt(r.mixed_low[rows_of(m)], o_half(1 - core)))
    for m in micros:
        mine = dot_nt(r.mixed_low[rows_of(m)], o_half(core))
        y_swap[0][m].start(mine + core_a[m].other())
    get_sh[0].step(1)
    for m in micros:
        send_c[m].relay_y()
    for m in micros:
        share_a[m].start(y_swap[0][m].both())

    send_x = [Dispatch(net, r.x_out.at[m], r.x_in.at[m]) for m in micros]
    scale_two = []
    for m in micros:
        res = r.tok[rows_of(m)].astype(F32) + share_a[m].finish()
        r.res[m] = res
        scale_two.append(norm_scale(res))
        normed_two = (res * scale_two[m] * gain_two).astype(BF)
        r.n_two[rows_of(m)] = normed_two
        r.x_out[m] = dot_tn(quarter[m], normed_two).astype(BF).reshape(n, part, model)
        send_x[m].start()

    gates = []
    for m in micros:
        logits = dot_nt(r.n_two[rows_of(m)], ext_low)
        z_one = jnp.sum(jnp.where(hot_one[m], logits, 0.0), axis=1, keepdims=True)
        z_two = jnp.sum(jnp.where(hot_two[m], logits, 0.0), axis=1, keepdims=True)
        z_top = jnp.maximum(z_one, z_two)
        e_one, e_two = jnp.exp(z_one - z_top), jnp.exp(z_two - z_top)
        chosen = jnp.where(hot_one[m], e_one, jnp.where(hot_two[m], e_two, 0.0))
        gates.append(chosen / (e_one + e_two))
    for m in micros:
        send_c[m].relay_core()
    get_sh[0].step(2)
    get_sh[0].step(3)
    for m in micros:
        send_x[m].relay_y()
    get_sh[1].start()
    get_sh[2].start()
    for m in micros:
        send_x[m].relay_core()
    for m in micros:
        send_h[m].finish()
        send_c[m].finish()

    slot_gc = net.recv_slots(micro)
    slot_yc = net.recv_slots(micro)
    send_g = [
        Exchange(net, lambda b, m=m: r.g_core.at[m, b], lambda b, m=m: r.g_in.at[m, b])
        for m in micros
    ]
    send_y = [
        Exchange(net, lambda b, m=m: r.y_core.at[m, b], lambda b, m=m: r.y_in.at[m, b])
        for m in micros
    ]
    send_d = [
        Exchange(net, lambda b, m=m: r.d_out.at[m, b], lambda b, m=m: r.d_in.at[m, b])
        for m in micros
    ]
    slot_eye = eye[:cap]
    slot_line = iota((cap, 128), 0) == iota((cap, 128), 1)
    own_lane = iota((n * cap, 16), 1) - 8 == me
    group = 4
    halves = [slice(0, half), slice(half, model)]

    def expert(m):
        x_rows = r.x_in[m].reshape(n * cap, model)
        z_all = dot_nt(x_rows, ext_low)
        hit = jnp.concatenate([dot_nt(slot_eye, r.h_in[m, b]) for b in range(n)], axis=0)
        z_own = jnp.sum(jnp.where(own_lane, z_all, 0.0), axis=1, keepdims=True)
        z_other = jnp.sum(jnp.where(own_lane, 0.0, z_all * hit), axis=1, keepdims=True)
        z_top = jnp.maximum(z_own, z_other)
        e_own, e_other = jnp.exp(z_own - z_top), jnp.exp(z_other - z_top)
        r.gate_col[m] = e_own / (e_own + e_other)
        count = group * cap

        def step(i, carry):
            span = pl.ds(i * group, group)
            flat = pl.ds(pl.multiple_of(i * count, count), count)
            x = r.x_in[m, span].reshape(count, model)
            c = r.c_in[m, span].reshape(count, model)
            gate = r.gate_col[m, flat]
            gate_pre = dot(x, r.eg[...])
            up_pre = dot(x, r.eu[...])
            act, slope = silu_both(gate_pre)
            hid = (act * up_pre).astype(BF)
            grad_y = (gate * c.astype(F32)).astype(BF)
            grad_hid = dot_nt(grad_y, r.ed[...])
            grad_g = (grad_hid * up_pre * slope).astype(BF)
            grad_u = (grad_hid * act).astype(BF)
            r.e_h[m, flat] = hid
            r.e_dg[m, flat] = grad_g
            r.e_du[m, flat] = grad_u
            dots = jnp.zeros((count, 1), F32)
            for cut in halves:
                out = dot(hid, r.ed[:, cut])
                r.tok_all[span, 0, m, :, cut] = out.astype(BF).reshape(group, cap, half)
                dots = dots + jnp.sum(out * c[:, cut].astype(F32), axis=1, keepdims=True)
                back = dot_nt(grad_g, r.eg[cut]) + dot_nt(grad_u, r.eu[cut])
                r.tok_all[span, 1, m, :, cut] = back.astype(BF).reshape(group, cap, half)
            r.c_in[m, span] = grad_y.reshape(group, 2, 2, part, model)
            for b in range(group):
                line = jnp.where(slot_line, dots[b * cap : (b + 1) * cap], 0.0)
                line = jnp.sum(line, axis=0, keepdims=True)
                r.d_out[m, i * group + b] = jnp.broadcast_to(line, (8, 128))
            return carry

        lax.fori_loop(0, n // group, step, 0)
        net.push(r.tok_all.at[:, 1, m, :, other_half], r.g_core.at[m], net.other_core(), slot_gc + m)
        net.push(r.tok_all.at[:, 0, m, :, other_half], r.y_core.at[m], net.other_core(), slot_yc + m)

    def return_g(m):
        send_d[m].start()
        r.d_in[m, me] = r.d_out[m, me]
        net.landed(r.g_core.at[m], slot_gc + m)
        r.g_core[m] = (r.tok_all[:, 1, m, :, my_half].astype(F32) + r.g_core[m].astype(F32)).astype(BF)
        send_g[m].start()
        r.g_in[m, me] = r.g_core[m, me]

    def return_y(m):
        net.landed(r.y_core.at[m], slot_yc + m)
        r.y_core[m] = (r.tok_all[:, 0, m, :, my_half].astype(F32) + r.y_core[m].astype(F32)).astype(BF)
        send_y[m].start()
        r.y_in[m, me] = r.y_core[m, me]

    net.drain()
    for m in micros:
        send_x[m].finish()
        expert(m)
    for m in micros:
        return_g(m)

    for distance in range(1, net.nz):
        get_sh[1].step(distance)
        get_sh[2].step(distance)
    for g in get_sh:
        g.finish()

    def wide_half(i, h):
        return r.w_sh[i, pl.ds(h * (n // 2), n // 2)].reshape(half, shared)

    def shared_step(m, carry):
        here = pl.ds(pl.multiple_of(m * local, local), local)
        normed_two = r.n_two[here]
        shared_g = dot(normed_two, r.w_sh[0].reshape(model, shared))
        shared_u = dot(normed_two, r.w_sh[1].reshape(model, shared))
        act, slope = silu_both(shared_g)
        shared_h = (act * shared_u).astype(BF)
        grad_h = dot(r.cot[here], r.w_sh[2].reshape(model, shared))
        grad_g = (grad_h * shared_u * slope).astype(BF)
        grad_u = (grad_h * act).astype(BF)
        r.s_grads[0, here] = grad_g
        r.s_grads[1, here] = grad_u
        r.s_grads[2, here] = shared_h
        other, own = 1 - core, core
        back = dot_nt(grad_g, wide_half(0, other)) + dot_nt(grad_u, wide_half(1, other))
        r.core_b[0, here] = back.astype(BF)
        r.core_b[2, here] = dot_nt(shared_h, wide_half(2, other)).astype(BF)
        back = dot_nt(grad_g, wide_half(0, own)) + dot_nt(grad_u, wide_half(1, own))
        r.s_own[0, here] = back
        r.s_own[1, here] = dot_nt(shared_h, wide_half(2, own))
        return carry

    lax.fori_loop(0, micro, shared_step, 0)
    for swap_b in core_b:
        swap_b.send()
    for i, (rows_a, rows_b) in enumerate(((r.n_two, 0), (r.n_two, 1), (r.cot, 2))):
        grads = dot_tn(rows_a[...], r.s_grads[rows_b])
        r.sh_part[i] = grads.astype(BF).reshape(n, depth, shared)
    sum_sh = [
        Scatter(net, lambda b, i=i: r.sh_part.at[i, b], r.sh_fx.at[i], r.sh_fz.at[i])
        for i in range(3)
    ]

    saves = []

    def all_slots(ref, cut):
        return ref[..., cut].reshape(micro * n * cap, -1)

    def save(source, target, i):
        copy = pltpu.make_async_copy(source, target, r.save_sems.at[i])
        copy.start()
        saves.append(copy)

    for h, cut in enumerate(halves):
        for i, (target, grads) in enumerate(((r.deg, r.e_dg), (r.deu, r.e_du))):
            if h == 1:
                saves[i].wait()
            r.stage[i] = dot_tn(all_slots(r.x_in, cut), all_slots(grads, slice(None)))
            save(r.stage.at[i], target.at[cut], 2 * h + i)
        if h == 1:
            saves[2].wait()
        r.stage_d[...] = dot_tn(all_slots(r.e_h, slice(None)), all_slots(r.c_in, cut))
        save(r.stage_d, r.ded.at[:, cut], 4 + h)

    d_core = [Swap(net, r.d_tensor.at[m, 0], r.d_tensor.at[m, 1], net.other_core()) for m in micros]
    d_y = [Swap(net, r.d_tensor.at[m, 2], r.d_tensor.at[m, 3], net.across_y()) for m in micros]
    eight = iota((8, 128), 0)
    d_rows = []
    for m in micros:
        send_d[m].finish()
        line = jnp.zeros((8, 128), F32)
        for b in range(n):
            line = line + jnp.where(eight == b, r.d_in[m, b], 0.0)
        d_rows.append(line)
        d_core[m].start(line)
    shared_grad = r.s_own[0] + core_b[0].other()
    for m in micros:
        d_y[m].start(d_rows[m] + d_core[m].other())
    for m in micros:
        send_g[m].finish()
        moe_grad = dot(r.choice[m], r.g_in[m].reshape(n * cap, half))
        y_swap[1][m].start(moe_grad + shared_grad[rows_of(m)])
    for m in micros:
        return_y(m)
    grad_logits = []
    for m in micros:
        d_all = d_y[m].both()
        grad_gate = jnp.zeros((local, 16), F32)
        for b in range(n):
            picked = r.choice_wide[m, :, b * 128 : (b + 1) * 128].astype(F32) * d_all[b : b + 1]
            grad_gate = jnp.where(lane == b, jnp.sum(picked, axis=1, keepdims=True), grad_gate)
        inner = jnp.sum(gates[m] * grad_gate, axis=1, keepdims=True)
        grad_logits.append((gates[m] * (grad_gate - inner)).astype(BF))
        share_b[m].start(y_swap[1][m].both())

    w_qo = r.w_qo[...].reshape(model, wide)
    kv_sums, grad_queries, gain_rows = [], [], []
    for m in micros:
        grad_two = share_b[m].finish() + dot(grad_logits[m], ext_low)
        res = r.res[m]
        cot = r.cot[rows_of(m)].astype(F32)
        grad_res = cot + norm_back(grad_two, res, scale_two[m], gain_two)
        r.gtok[rows_of(m)] = grad_res
        gain_rows.append(jnp.sum(grad_two * res * scale_two[m], axis=0, keepdims=True))
        kv_rows = r.kv[m].reshape(tree, wide)
        total = r.total[m]
        gm = by_head(dot(grad_res.astype(BF), w_qo), v_masks)
        mixed = jnp.concatenate([r.mixed[m]] * heads, axis=0)
        delta = jnp.sum(gm * mixed, axis=1, keepdims=True) / total
        grad_summed = (gm / total).astype(BF)
        expo = r.expo[m]
        ds = (expo * (dot_nt(grad_summed, kv_rows) - delta)).astype(BF)
        grad_kv = dot_tn(ds, r.q_rows[m]) * score_scale + dot_tn(expo.astype(BF), grad_summed)
        r.kv_part[m] = grad_kv.astype(BF).reshape(n, local, wide)
        kv_sums.append(
            Scatter(net, lambda b, m=m: r.kv_part.at[m, b], r.kv_fx.at[m], r.kv_fz.at[m])
        )
        kv_sums[m].start()
        grad_queries.append(join_heads(dot(ds, kv_rows), q_masks) * score_scale)

    cosine, sine = turns(me)

    def turned_back(grad):
        return (grad * cosine - dot(grad, swap, EXACT) * sine).astype(BF)

    for m in micros:
        kv_sums[m].forward()
    grad_q = turned_back(jnp.concatenate(grad_queries, axis=0))
    grad_attn = r.gtok[...].astype(BF)
    part_qo = dot_tn(r.n_one[...], grad_q) + dot_tn(grad_attn, r.mixed_low[...])
    r.w_part[0] = part_qo.astype(BF).reshape(n, depth, wide)
    sum_w = [
        Scatter(net, lambda b, i=i: r.w_part.at[i, b], r.w_fx.at[i], r.w_fz.at[i])
        for i in range(2)
    ]
    sum_w[0].start()

    shared_y = r.s_own[1] + core_b[1].other()
    for m in micros:
        send_y[m].finish()
        gate_wide = dot(gates[m], spread(cap).astype(F32), EXACT)
        gate_high = gate_wide.astype(BF).astype(F32)
        pick = r.choice[m].astype(F32)
        y_rows = r.y_in[m].reshape(n * cap, half)
        moe_y = dot((pick * gate_high).astype(BF), y_rows)
        moe_y = moe_y + dot((pick * (gate_wide - gate_high)).astype(BF), y_rows)
        y_swap[2][m].start(moe_y + shared_y[rows_of(m)])
    for g in sum_sh:
        g.start()

    def weight_half(ref, h):
        return ref[pl.ds(h * (n // 2), n // 2)].reshape(half, wide)

    grad_kvs = []
    for m in micros:
        total = kv_sums[m].finish()
        cos_m, sin_m = cosine[rows_of(m)], sine[rows_of(m)]
        grad_kv = (total * cos_m - dot(total, swap, EXACT) * sin_m).astype(BF)
        grad_kvs.append(grad_kv)
        q_m = grad_q[rows_of(m)]
        other = dot_nt(q_m, weight_half(r.w_qo, 1 - core))
        core_c[m].start(other + dot_nt(grad_kv, weight_half(r.w_kv, 1 - core)))
    for m in micros:
        mine = dot_nt(grad_q[rows_of(m)], weight_half(r.w_qo, core))
        mine = mine + dot_nt(grad_kvs[m], weight_half(r.w_kv, core))
        y_swap[3][m].start(mine + core_c[m].other())
    part_kv = dot_tn(r.n_one[...], jnp.concatenate(grad_kvs, axis=0))
    r.w_part[1] = part_kv.astype(BF).reshape(n, depth, wide)
    sum_w[1].start()
    sum_w[0].forward()
    for m in micros:
        share_c[m].start(y_swap[3][m].both())
    for m in micros:
        res_half = jnp.where(core == 0, r.res[m, :, :half], r.res[m, :, half:])
        share_out[m].start(res_half + y_swap[2][m].both())
    sum_w[1].forward()
    for g in sum_sh:
        g.forward()

    gain_one_row = jnp.zeros((1, model), F32)
    for m in micros:
        grad_one = share_c[m].finish()
        tok = r.tok[rows_of(m)].astype(F32)
        scale_one = norm_scale(tok)
        r.gtok[rows_of(m)] += norm_back(grad_one, tok, scale_one, gain_one)
        gain_one_row = gain_one_row + jnp.sum(grad_one * tok * scale_one, axis=0, keepdims=True)
    grad_router = jnp.zeros((16, model), F32)
    for m in micros:
        grad_router = grad_router + dot_tn(grad_logits[m], r.n_two[rows_of(m)])
    line = iota((16, model), 0)
    small = jnp.where(line == 0, gain_one_row, grad_router)
    small = jnp.where(line == 1, gain_rows[0] + gain_rows[1], small)
    for b in range(n):
        r.gains_out[b] = dot_nt(small, lay(b).astype(F32), EXACT)
    send_gains = Exchange(net, lambda b: r.gains_out.at[b], lambda b: r.gains_in.at[b])
    send_gains.start()
    r.gains_in[me] = r.gains_out[me]
    for m in micros:
        r.out[rows_of(m)] = share_out[m].finish()

    qo = sum_w[0].finish()
    r.dwq[...] = dot_nt(qo, left.astype(F32), EXACT)
    depth_eye = (iota((depth, depth), 0) == iota((depth, depth), 1)).astype(F32)
    r.dwo[...] = dot_tn(dot_nt(qo, right.astype(F32), EXACT), depth_eye, EXACT)
    kv = sum_w[1].finish()
    r.dwk[...] = dot_nt(kv, left.astype(F32), EXACT)
    r.dwv[...] = dot_nt(kv, right.astype(F32), EXACT)
    for i, target in enumerate((r.dsg, r.dsu, r.dsd)):
        target[...] = sum_sh[i].finish()
    send_gains.finish()
    gains = jnp.zeros((16, 128), F32)
    for b in range(n):
        gains = gains + r.gains_in[b]
    r.dga[...] = gains[0:1, :depth]
    r.dgb[...] = gains[1:2, :depth]
    r.drouter[...] = gains[8:16, :depth]
    for copy in saves[3:]:
        copy.wait()
    net.drain()


def settle_kernel(count, *refs):
    sources, targets, sems = refs[:count], refs[count : 2 * count], refs[2 * count]
    copies = [
        pltpu.make_async_copy(a, b, sems.at[i]) for i, (a, b) in enumerate(zip(sources, targets))
    ]
    for copy in copies:
        copy.start()
    for copy in copies:
        copy.wait()


def fits(mesh):
    return mesh.shape["expert"] == 8 and mesh.shape["tensor"] == 4


def fused_body(
    tokens,
    out_grad,
    routes,
    lengths,
    parents,
    attn_gain,
    ffn_gain,
    w_query,
    w_key,
    w_value,
    w_out,
    router,
    shared_gate,
    shared_up,
    shared_down,
    expert_gate,
    expert_up,
    expert_down,
):
    micro, local, model = tokens.shape
    n = lax.axis_size("expert")
    experts = router.shape[1]
    depth, width = w_query.shape
    hidden, shared = expert_gate.shape[2], shared_gate.shape[1]
    s = types.SimpleNamespace(
        n=n,
        micro=micro,
        local=local,
        half=model // 2,
        depth=depth,
        width=width,
        heads=width // HEAD,
        hidden=hidden,
        shared=shared,
        cap=4 * local // experts,
        segs=lengths.shape[1],
    )
    rows = micro * local
    scratch = scratch_shapes(s)
    names = PLACES + RESULTS + list(scratch)
    shape = jax.ShapeDtypeStruct
    vmem, smem = pl.BlockSpec(memory_space=pltpu.VMEM), pl.BlockSpec(memory_space=pltpu.SMEM)
    hbm = pl.BlockSpec(memory_space=pl.ANY)
    results = (
        shape((rows, model), BF),
        shape((rows, model), F32),
        shape((1, depth), F32),
        shape((1, depth), F32),
        shape((depth, width), F32),
        shape((depth, width), F32),
        shape((depth, width), F32),
        shape((width, depth), F32),
        shape((experts, depth), F32),
        shape((depth, shared), F32),
        shape((depth, shared), F32),
        shape((depth, shared), F32),
        shape((model, hidden), F32),
        shape((model, hidden), F32),
        shape((hidden, model), F32),
    )
    found = pl.pallas_call(
        functools.partial(layer_kernel, s, names),
        out_shape=results,
        in_specs=[vmem] * 3 + [smem] * 2 + [vmem] * 13,
        out_specs=[vmem] * 12 + [hbm] * 3,
        scratch_shapes=list(scratch.values()),
        compiler_params=pltpu.CompilerParams(
            collective_id=0, has_side_effects=True, vmem_limit_bytes=VMEM_LIMIT
        ),
    )(
        tokens.reshape(rows, model),
        out_grad.reshape(rows, model),
        routes.transpose(0, 2, 1).reshape(2 * micro, local),
        lengths,
        parents,
        attn_gain.reshape(1, depth),
        ffn_gain.reshape(1, depth),
        w_query,
        w_key,
        w_value,
        w_out,
        router.T,
        shared_gate,
        shared_up,
        shared_down.T,
        expert_gate[0],
        expert_up[0],
        expert_down[0],
    )
    settled = pl.pallas_call(
        functools.partial(settle_kernel, len(results)),
        out_shape=results,
        in_specs=[vmem] * len(results),
        out_specs=[hbm] * len(results),
        scratch_shapes=[pltpu.SemaphoreType.DMA((len(results),))],
        compiler_params=pltpu.CompilerParams(vmem_limit_bytes=VMEM_LIMIT),
    )(*found)
    out, gtok, dga, dgb, dwq, dwk, dwv, dwo, drouter, dsg, dsu, dsd, deg, deu, ded = settled
    return (
        out.reshape(micro, local, model),
        gtok.reshape(micro, local, model),
        dga.reshape(depth),
        dgb.reshape(depth),
        dwq,
        dwk,
        dwv,
        dwo,
        drouter.T,
        dsg,
        dsu,
        dsd.T,
        deg[None],
        deu[None],
        ded[None],
    )


def solution(mesh):
    in_specs = (
        P(None, "expert", None),
        P(None, "expert", None),
        P(None, "expert", None),
        P(),
        P(),
        P("expert"),
        P("expert"),
        P("expert", "tensor"),
        P("expert", "tensor"),
        P("expert", "tensor"),
        P("tensor", "expert"),
        P("expert", None),
        P("expert", "tensor"),
        P("expert", "tensor"),
        P("tensor", "expert"),
        P("expert", None, "tensor"),
        P("expert", None, "tensor"),
        P("expert", "tensor", None),
    )
    out_specs = (
        P(None, "expert", None),
        P(None, "expert", None),
        P("expert"),
        P("expert"),
        P("expert", "tensor"),
        P("expert", "tensor"),
        P("expert", "tensor"),
        P("tensor", "expert"),
        P("expert", None),
        P("expert", "tensor"),
        P("expert", "tensor"),
        P("tensor", "expert"),
        P("expert", None, "tensor"),
        P("expert", None, "tensor"),
        P("expert", "tensor", None),
    )
    chosen = fused_body if fits(mesh) else plain_body
    return jax.shard_map(chosen, mesh=mesh, in_specs=in_specs, out_specs=out_specs, check_vma=False)
```

```python
import functools
import math
import types

import jax
import jax.numpy as jnp
from jax import lax
from jax.experimental import pallas as pl
from jax.experimental.pallas import tpu as pltpu
from jax.sharding import PartitionSpec as P

HEAD = 64


EPSILON = 1e-06
ROPE_BASE = 10000.0
KEY_BLOCK = 2048


def matmul(left, right):
    return jnp.dot(left, right, preferred_element_type=jnp.float32)


def tree_tables(lengths, parents):
    seg_count = lengths.shape[0]
    identity = jnp.arange(seg_count, dtype=jnp.int32)
    current = identity
    ancestry = jnp.zeros((seg_count, seg_count), jnp.float32)
    for depth_level in range(seg_count):
        chosen_mask = current[:, None] == identity[None, :]
        ancestry = jnp.maximum(ancestry, chosen_mask.astype(jnp.float32))
        current = jnp.sum(jnp.where(chosen_mask, parents[None, :], 0), axis=1)
    seg_ends = jnp.cumsum(lengths)
    starts = seg_ends - lengths
    sizes_float = lengths.astype(jnp.float32)
    offsets = jnp.sum(ancestry * sizes_float[None, :], axis=1) - sizes_float
    return (ancestry, starts, seg_ends, offsets)


def row_tables(row_ids, starts, seg_ends, offsets):
    member = (
        (row_ids[:, None] >= starts[None, :]) & (row_ids[:, None] < seg_ends[None, :])
    ).astype(jnp.float32)
    position_shift = offsets - starts.astype(jnp.float32)
    position = jnp.sum(member * position_shift[None, :], axis=1) + row_ids.astype(jnp.float32)
    return (member, position)


def rotary_tables(position, half_width):
    frequency = ROPE_BASE ** (-jnp.arange(half_width, dtype=jnp.float32) / half_width)
    angles = position[:, None] * frequency[None, :]
    return (jnp.cos(angles)[:, None, :], jnp.sin(angles)[:, None, :])


def rotate(head_values, position):
    half_width = head_values.shape[-1] // 2
    cosines, sine_values = rotary_tables(position, half_width)
    first_half = head_values[..., :half_width]
    second_half = head_values[..., half_width:]
    return jnp.concatenate(
        [
            first_half * cosines - second_half * sine_values,
            second_half * cosines + first_half * sine_values,
        ],
        axis=-1,
    )


def rotate_back(grad_heads, position):
    half_width = grad_heads.shape[-1] // 2
    cosines, sine_values = rotary_tables(position, half_width)
    first_half = grad_heads[..., :half_width]
    second_half = grad_heads[..., half_width:]
    return jnp.concatenate(
        [
            first_half * cosines + second_half * sine_values,
            second_half * cosines - first_half * sine_values,
        ],
        axis=-1,
    )


def silu_parts(gate_val):
    sigmoid_val = jax.nn.sigmoid(gate_val)
    return (gate_val * sigmoid_val, sigmoid_val * (1.0 + gate_val * (1.0 - sigmoid_val)))


def rms_back(grad_normed, source, norm_scale, gain):
    weighted = grad_normed * gain
    inner_mean = jnp.mean(weighted * source, axis=1, keepdims=True)
    return (
        norm_scale * weighted - norm_scale**3 * source * inner_mean,
        jnp.sum(grad_normed * source * norm_scale, axis=0),
    )


def visible(reach_rows, query_ids, key_member, key_ids):
    linked = matmul(reach_rows, key_member.T) > 0.5
    return linked & (key_ids[None, :] <= query_ids[:, None])


def score_block(query_heads, key_heads, seen, score_scale):
    scores = (
        jnp.einsum("qhd,khd->hqk", query_heads, key_heads, preferred_element_type=jnp.float32)
        * score_scale
    )
    return jnp.where(seen[None], jnp.exp(scores), 0.0)


def score_grads(weights_exp, grad_summed, value_heads, delta_rows):
    grad_exp = jnp.einsum(
        "qhd,khd->hqk", grad_summed, value_heads, preferred_element_type=jnp.float32
    )
    return (weights_exp * (grad_exp - jnp.transpose(delta_rows)[:, :, None])).astype(jnp.bfloat16)


def plain_body(
    tokens,
    out_grad,
    routes,
    lengths,
    parents,
    attn_gain,
    ffn_gain,
    w_query,
    w_key,
    w_value,
    w_out,
    router,
    shared_gate,
    shared_up,
    shared_down,
    expert_gate,
    expert_up,
    expert_down,
):
    micro_count, row_count, model_width = tokens.shape
    devices = lax.axis_size("expert")
    tree_rows = row_count * devices
    expert_count = router.shape[1]
    owners = devices // expert_count
    capacity = 4 * row_count // expert_count
    score_scale = HEAD ** (-0.5)
    local_rows = lax.axis_index("expert") * row_count + jnp.arange(row_count, dtype=jnp.int32)
    part_gate = expert_gate[0]
    part_up = expert_up[0]
    part_down = expert_down[0]
    labels = jnp.arange(expert_count, dtype=jnp.int32)
    slot_ids = jnp.arange(expert_count * capacity, dtype=jnp.int32)
    pair_ids = jnp.arange(2 * row_count, dtype=jnp.int32)
    block_size = math.gcd(tree_rows, KEY_BLOCK)
    block_count = tree_rows // block_size
    layer_outputs = []
    token_gradients = []
    dense_sums = None
    expert_sums = None
    for micro_step in range(micro_count):
        gathered = (
            lax.all_gather(attn_gain, "expert", axis=0, tiled=True),
            lax.all_gather(ffn_gain, "expert", axis=0, tiled=True),
            lax.all_gather(w_query, "expert", axis=0, tiled=True),
            lax.all_gather(w_key, "expert", axis=0, tiled=True),
            lax.all_gather(w_value, "expert", axis=0, tiled=True),
            lax.all_gather(w_out, "expert", axis=1, tiled=True),
            lax.all_gather(router, "expert", axis=0, tiled=True),
            lax.all_gather(shared_gate, "expert", axis=0, tiled=True),
            lax.all_gather(shared_up, "expert", axis=0, tiled=True),
            lax.all_gather(shared_down, "expert", axis=1, tiled=True),
        )
        (
            gain_one,
            gain_two,
            query_weight,
            key_weight,
            value_weight,
            out_weight,
            router_weight,
            gate_weight,
            up_weight,
            down_weight,
        ) = gathered
        local_width = query_weight.shape[1]
        head_count = local_width // HEAD
        ancestry, starts, seg_ends, offsets = tree_tables(lengths[micro_step], parents[micro_step])
        member, position = row_tables(local_rows, starts, seg_ends, offsets)
        reach = matmul(member, ancestry)
        tokens_now = tokens[micro_step].astype(jnp.float32)
        norm_one = lax.rsqrt(jnp.mean(tokens_now * tokens_now, axis=1, keepdims=True) + EPSILON)
        normed_one = (tokens_now * norm_one * gain_one).astype(jnp.bfloat16)
        query_pre = matmul(normed_one, query_weight).reshape(row_count, head_count, HEAD)
        key_pre = matmul(normed_one, key_weight).reshape(row_count, head_count, HEAD)
        value_low = matmul(normed_one, value_weight).astype(jnp.bfloat16)
        queries = rotate(query_pre, position).astype(jnp.bfloat16)
        key_heads = rotate(key_pre, position).astype(jnp.bfloat16)
        key_value = jnp.concatenate([key_heads.reshape(row_count, local_width), value_low], axis=1)
        all_pairs = lax.all_gather(key_value, "expert", axis=0, tiled=True)

        def key_block_parts(block_index):
            first_key = block_index * block_size
            key_block = lax.dynamic_slice_in_dim(all_pairs, first_key, block_size, 0)
            key_ids = first_key + jnp.arange(block_size, dtype=jnp.int32)
            key_member, unused = row_tables(key_ids, starts, seg_ends, offsets)
            seen = visible(reach, local_rows, key_member, key_ids)
            block_keys = key_block[:, :local_width].reshape(block_size, head_count, HEAD)
            block_values = key_block[:, local_width:].reshape(block_size, head_count, HEAD)
            return (seen, block_keys, block_values)

        def forward_step(block_index, totals):
            seen, block_keys, block_values = key_block_parts(block_index)
            weights_exp = score_block(queries, block_keys, seen, score_scale)
            summed_part = jnp.einsum(
                "hqk,khd->qhd",
                weights_exp.astype(jnp.bfloat16),
                block_values,
                preferred_element_type=jnp.float32,
            )
            return (
                totals[0] + summed_part.reshape(row_count, local_width),
                totals[1] + jnp.transpose(jnp.sum(weights_exp, axis=2)),
            )

        initial = (
            jnp.zeros((row_count, local_width), jnp.float32),
            jnp.zeros((row_count, head_count), jnp.float32),
        )
        summed, row_total = lax.fori_loop(0, block_count, forward_step, initial)
        mixed = summed.reshape(row_count, head_count, HEAD) / row_total[:, :, None]
        mixed_low = mixed.reshape(row_count, local_width).astype(jnp.bfloat16)
        attn_out = lax.psum(matmul(mixed_low, out_weight), "tensor")
        residual = tokens_now + attn_out
        norm_two = lax.rsqrt(jnp.mean(residual * residual, axis=1, keepdims=True) + EPSILON)
        normed_two = (residual * norm_two * gain_two).astype(jnp.bfloat16)
        shared_g = matmul(normed_two, gate_weight)
        shared_u = matmul(normed_two, up_weight)
        shared_act, shared_slope = silu_parts(shared_g)
        shared_h = (shared_act * shared_u).astype(jnp.bfloat16)
        shared_y = matmul(shared_h, down_weight)
        logits = matmul(normed_two, router_weight)
        route_now = routes[micro_step]
        choose = (route_now[:, :, None] == labels[None, None, :]).astype(jnp.float32)
        gate_values = jax.nn.softmax(jnp.sum(choose * logits[:, None, :], axis=2), axis=1)
        flat_routes = route_now.reshape(2 * row_count)
        expert_hits = (flat_routes[:, None] == labels[None, :]).astype(jnp.int32)
        slot_rank = jnp.sum((jnp.cumsum(expert_hits, axis=0) - expert_hits) * expert_hits, axis=1)
        slot_index = flat_routes * capacity + slot_rank
        slot_match = slot_index[None, :] == slot_ids[:, None]
        filled = jnp.any(slot_match, axis=1)
        source = jnp.sum(jnp.where(slot_match, pair_ids[None, :], 0), axis=1)

        def to_owners(table, row_index):
            picked = jnp.take(table, row_index, axis=0)
            picked = jnp.where(filled[:, None], picked, jnp.zeros_like(picked))
            spread = jnp.broadcast_to(
                picked.reshape(expert_count, 1, capacity, model_width),
                (expert_count, owners, capacity, model_width),
            )
            return spread.reshape(devices, capacity, model_width)

        def from_owners(returned):
            merged = jnp.sum(
                returned.reshape(expert_count, owners, capacity, model_width), axis=1
            ).reshape(expert_count * capacity, model_width)
            return jnp.take(merged, slot_index, axis=0).reshape(row_count, 2, model_width)

        arrived = lax.all_to_all(
            to_owners(normed_two, source // 2), "expert", split_axis=0, concat_axis=0, tiled=True
        )
        slot_count = arrived.shape[1]
        flat_in = arrived.reshape(devices * slot_count, model_width)
        expert_g = matmul(flat_in, part_gate)
        expert_u = matmul(flat_in, part_up)
        expert_act, expert_unused = silu_parts(expert_g)
        expert_h = (expert_act * expert_u).astype(jnp.bfloat16)
        partial_out = matmul(expert_h, part_down).reshape(devices, slot_count, model_width)
        combined = lax.all_to_all(
            partial_out.astype(jnp.bfloat16), "expert", split_axis=0, concat_axis=0, tiled=True
        ).astype(partial_out.dtype)
        hidden_width = expert_g.shape[1]
        combined, arrived, kept_g, kept_u, kept_h = (
            combined,
            arrived,
            expert_g.reshape(devices, slot_count, hidden_width),
            expert_u.reshape(devices, slot_count, hidden_width),
            expert_h.reshape(devices, slot_count, hidden_width),
        )
        expert_y = from_owners(combined)
        cot_low = out_grad[micro_step]
        cotangent = cot_low.astype(jnp.float32)
        moe_part = jnp.sum(gate_values[:, :, None] * expert_y, axis=1)
        gate_dots = jnp.sum(cotangent[:, None, :] * expert_y, axis=2)
        ffn_out, grad_gate = (
            lax.psum((shared_y + moe_part).astype(jnp.bfloat16), "tensor").astype(jnp.float32),
            lax.psum(gate_dots.astype(jnp.bfloat16), "tensor").astype(jnp.float32),
        )
        layer_outputs.append((residual + ffn_out).astype(jnp.bfloat16))
        grad_shared_h = matmul(cot_low, down_weight.T)
        grad_shared_g = (grad_shared_h * shared_u * shared_slope).astype(jnp.bfloat16)
        grad_shared_u = (grad_shared_h * shared_act).astype(jnp.bfloat16)
        grad_chosen = gate_values * (
            grad_gate - jnp.sum(gate_values * grad_gate, axis=1, keepdims=True)
        )
        grad_logits = jnp.sum(choose * grad_chosen[:, :, None], axis=1).astype(jnp.bfloat16)
        grad_pairs_out = (
            (gate_values[:, :, None] * cotangent[:, None, :])
            .astype(jnp.bfloat16)
            .reshape(2 * row_count, model_width)
        )
        arrived_grad = lax.all_to_all(
            to_owners(grad_pairs_out, source), "expert", split_axis=0, concat_axis=0, tiled=True
        )
        slot_total = arrived_grad.shape[0] * arrived_grad.shape[1]
        flat_grad = arrived_grad.reshape(slot_total, model_width)
        flat_in = arrived.reshape(slot_total, model_width)
        hidden_width = kept_g.shape[2]
        expert_g = kept_g.reshape(slot_total, hidden_width)
        expert_u = kept_u.reshape(slot_total, hidden_width)
        expert_h = kept_h.reshape(slot_total, hidden_width)
        expert_act, expert_slope = silu_parts(expert_g)
        grad_hidden = matmul(flat_grad, part_down.T)
        grad_expert_g = (grad_hidden * expert_u * expert_slope).astype(jnp.bfloat16)
        grad_expert_u = (grad_hidden * expert_act).astype(jnp.bfloat16)
        grad_in = matmul(grad_expert_g, part_gate.T) + matmul(grad_expert_u, part_up.T)
        returned = lax.all_to_all(
            grad_in.reshape(arrived_grad.shape[0], arrived_grad.shape[1], model_width),
            "expert",
            split_axis=0,
            concat_axis=0,
            tiled=True,
        )
        normed_part = (
            matmul(grad_shared_g, gate_weight.T)
            + matmul(grad_shared_u, up_weight.T)
            + jnp.sum(from_owners(returned), axis=1)
        )
        grad_normed_two = lax.psum(normed_part, "tensor") + matmul(grad_logits, router_weight.T)
        grad_norm_part, grad_gain_two = rms_back(grad_normed_two, residual, norm_two, gain_two)
        grad_residual = cotangent + grad_norm_part
        grad_attn = grad_residual.astype(jnp.bfloat16)
        grad_mixed = matmul(grad_attn, out_weight.T).reshape(row_count, head_count, HEAD)
        grad_summed = (grad_mixed / row_total[:, :, None]).astype(jnp.bfloat16)
        delta_rows = jnp.sum(grad_mixed * mixed, axis=2) / row_total

        def block_terms(block_index):
            seen, block_keys, block_values = key_block_parts(block_index)
            weights_exp = score_block(queries, block_keys, seen, score_scale)
            grad_scores = score_grads(weights_exp, grad_summed, block_values, delta_rows)
            return (weights_exp, grad_scores, block_keys)

        zero_query = jnp.zeros((row_count, head_count, HEAD), jnp.float32)

        def key_step(gradient_query_weight, block_index):
            weights_exp, grad_scores, block_keys = block_terms(block_index)
            gradient_query_weight = (
                gradient_query_weight
                + jnp.einsum(
                    "hqk,khd->qhd", grad_scores, block_keys, preferred_element_type=jnp.float32
                )
                * score_scale
            )
            grad_keys = (
                jnp.einsum("hqk,qhd->khd", grad_scores, queries, preferred_element_type=jnp.float32)
                * score_scale
            )
            grad_values = jnp.einsum(
                "hqk,qhd->khd",
                weights_exp.astype(jnp.bfloat16),
                grad_summed,
                preferred_element_type=jnp.float32,
            )
            return (
                gradient_query_weight,
                jnp.concatenate(
                    [
                        grad_keys.reshape(block_size, local_width),
                        grad_values.reshape(block_size, local_width),
                    ],
                    axis=1,
                ),
            )

        gradient_query_weight, key_terms = lax.scan(
            key_step, zero_query, jnp.arange(block_count, dtype=jnp.int32)
        )
        grad_pairs = lax.psum_scatter(
            key_terms.reshape(tree_rows, 2 * local_width), "expert", scatter_dimension=0, tiled=True
        )
        grad_keys_rot = grad_pairs[:, :local_width].reshape(row_count, head_count, HEAD)
        grad_query_pre = (
            rotate_back(gradient_query_weight, position)
            .reshape(row_count, local_width)
            .astype(jnp.bfloat16)
        )
        grad_key_pre = (
            rotate_back(grad_keys_rot, position)
            .reshape(row_count, local_width)
            .astype(jnp.bfloat16)
        )
        grad_value_low = grad_pairs[:, local_width:].astype(jnp.bfloat16)
        normed_grad = (
            matmul(grad_query_pre, query_weight.T)
            + matmul(grad_key_pre, key_weight.T)
            + matmul(grad_value_low, value_weight.T)
        )
        grad_normed_one = lax.psum(normed_grad.astype(jnp.bfloat16), "tensor").astype(jnp.float32)
        grad_norm_first, grad_gain_one = rms_back(grad_normed_one, tokens_now, norm_one, gain_one)
        token_gradients.append(grad_residual + grad_norm_first)
        dense_step = (
            grad_gain_one,
            grad_gain_two,
            matmul(normed_one.T, grad_query_pre),
            matmul(normed_one.T, grad_key_pre),
            matmul(normed_one.T, grad_value_low),
            matmul(mixed_low.T, grad_attn),
            matmul(normed_two.T, grad_logits),
            matmul(normed_two.T, grad_shared_g),
            matmul(normed_two.T, grad_shared_u),
            matmul(shared_h.T, cot_low),
        )
        expert_step = (
            matmul(flat_in.T, grad_expert_g),
            matmul(flat_in.T, grad_expert_u),
            matmul(expert_h.T, flat_grad),
        )
        if dense_sums is None:
            dense_sums = dense_step
            expert_sums = expert_step
        else:
            dense_sums = tuple(
                (earlier + latest for earlier, latest in zip(dense_sums, dense_step))
            )
            expert_sums = tuple(
                (earlier + latest for earlier, latest in zip(expert_sums, expert_step))
            )
    final_gate, final_up, final_down = expert_sums
    reduced = (
        lax.psum_scatter(dense_sums[0], "expert", scatter_dimension=0, tiled=True),
        lax.psum_scatter(dense_sums[1], "expert", scatter_dimension=0, tiled=True),
        lax.psum_scatter(dense_sums[2], "expert", scatter_dimension=0, tiled=True),
        lax.psum_scatter(dense_sums[3], "expert", scatter_dimension=0, tiled=True),
        lax.psum_scatter(dense_sums[4], "expert", scatter_dimension=0, tiled=True),
        lax.psum_scatter(dense_sums[5], "expert", scatter_dimension=1, tiled=True),
        lax.psum_scatter(dense_sums[6], "expert", scatter_dimension=0, tiled=True),
        lax.psum_scatter(dense_sums[7], "expert", scatter_dimension=0, tiled=True),
        lax.psum_scatter(dense_sums[8], "expert", scatter_dimension=0, tiled=True),
        lax.psum_scatter(dense_sums[9], "expert", scatter_dimension=1, tiled=True),
    )
    return (
        jnp.stack(layer_outputs),
        jnp.stack(token_gradients),
        reduced[0],
        reduced[1],
        reduced[2],
        reduced[3],
        reduced[4],
        reduced[5],
        reduced[6],
        reduced[7],
        reduced[8],
        reduced[9],
        final_gate[None],
        final_up[None],
        final_down[None],
    )


MESH = pl.DeviceIdType.MESH
BF = jnp.bfloat16
F32 = jnp.float32
EXACT = lax.Precision.HIGHEST
VMEM_LIMIT = 63 * 2**20


def product(left, right, dims, precision=None):
    return lax.dot_general(
        left, right, (dims, ((), ())), preferred_element_type=F32, precision=precision
    )


def dot(left, right, precision=None):
    return product(left, right, ((1,), (0,)), precision)


def dot_nt(left, right, precision=None):
    return product(left, right, ((1,), (1,)), precision)


def dot_tn(left, right, precision=None):
    return product(left, right, ((0,), (0,)), precision)


def iota(shape, dim):
    return lax.broadcasted_iota(jnp.int32, shape, dim)


class Net:
    def __init__(self, expert_size, send_sems, recv_sems):
        self.e = lax.axis_index("expert")
        self.t = lax.axis_index("tensor")
        self.n = expert_size
        self.nz = expert_size // 2
        self.z = self.e // 2
        self.x = self.e % 2
        self.y = self.t // 2
        self.core = self.t % 2
        self.send_sems = send_sems
        self.recv_sems = recv_sems
        self.sends = 0
        self.free = []
        self.recvs = 0
        self.open = []

    def recv_slots(self, count):
        first = self.recvs
        self.recvs += count
        return first

    def ids(self, to):
        return {"expert": to[0], "tensor": to[1]}

    def push(self, src, dst, to, slot, when=None, bulk=False):
        if not self.free:
            self.free.append(self.sends)
            self.sends += 1
        send = self.free.pop(0)
        copy = pltpu.make_async_remote_copy(
            src_ref=src,
            dst_ref=dst,
            send_sem=self.send_sems.at[send],
            recv_sem=self.recv_sems.at[slot],
            device_id=self.ids(to),
            device_id_type=MESH,
        )
        if when is None:
            copy.start()
        else:
            pl.when(when)(copy.start)
        self.open.append((copy, when, send, bulk))

    def landed(self, dst, slot, when=None):
        copy = pltpu.make_async_remote_copy(
            src_ref=dst,
            dst_ref=dst,
            send_sem=self.send_sems.at[0],
            recv_sem=self.recv_sems.at[slot],
            device_id=self.ids(self.other_core()),
            device_id_type=MESH,
        )
        if when is None:
            copy.wait_recv()
        else:
            pl.when(when)(copy.wait_recv)

    def drain(self, bulk=True):
        for copy, when, send, is_bulk in self.open:
            if bulk or not is_bulk:
                if when is None:
                    copy.wait_send()
                else:
                    pl.when(when)(copy.wait_send)
                self.free.append(send)
        self.open = [one for one in self.open if one[3] and not bulk]

    def other_core(self):
        return (self.e, self.t + 1 - 2 * self.core)

    def across_y(self):
        return (self.e, (self.t + 2) % 4)

    def across_x(self):
        return (self.e + 1 - 2 * self.x, self.t)

    def peer(self, step):
        return (self.e + step) % self.n

    def greet(self):
        barrier = pltpu.get_barrier_semaphore()
        partners = [(self.peer(d), self.t) for d in range(1, self.n)]
        partners += [self.other_core(), self.across_y()]
        for to in partners:
            pl.semaphore_signal(barrier, inc=1, device_id=self.ids(to), device_id_type=MESH)
        return lambda: pl.semaphore_wait(barrier, len(partners))


class Gather:
    def __init__(self, net, block, chunks=1, on_land=None):
        self.net, self.block, self.chunks, self.on_land = net, block, chunks, on_land
        self.slot = net.recv_slots(net.n * chunks)

    def start(self):
        net = self.net
        for k in range(self.chunks):
            own, slot = self.block(net.e, k), self.slot + net.e * self.chunks + k
            for way in (1, -1):
                there = net.z + way
                fits_in = (there >= 0) & (there < net.nz)
                net.push(own, own, (there % net.nz * 2 + net.x, net.t), slot, fits_in)
            net.push(own, own, net.across_x(), slot)

    def step(self, distance):
        net = self.net
        for k in range(self.chunks):
            for way in (1, -1):
                source, there = net.z - way * distance, net.z + way
                real = (source >= 0) & (source < net.nz)
                onward = real & (there >= 0) & (there < net.nz)
                b = source % net.nz * 2 + net.x
                part, slot = self.block(b, k), self.slot + b * self.chunks + k
                net.landed(part, slot, real)
                net.push(part, part, (there % net.nz * 2 + net.x, net.t), slot, onward)
                net.push(part, part, net.across_x(), slot, real)
                if self.on_land is not None:
                    self.on_land(b, real)

    def finish(self):
        net = self.net
        for d in range(net.nz):
            b = (net.z + d) % net.nz * 2 + 1 - net.x
            for k in range(self.chunks):
                net.landed(self.block(b, k), self.slot + b * self.chunks + k)
            if self.on_land is not None:
                self.on_land(b, None)


class Scatter:
    def __init__(self, net, block, from_x, from_z):
        self.net, self.block = net, block
        self.from_x, self.from_z = from_x, from_z
        self.slot_x = net.recv_slots(net.nz)
        self.slot_z = net.recv_slots(net.nz)

    def start(self):
        net = self.net
        for d in range(1, net.nz + 1):
            zz = (net.z + d) % net.nz
            net.push(
                self.block(zz * 2 + 1 - net.x),
                self.from_x.at[zz],
                net.across_x(),
                self.slot_x + zz,
                bulk=True,
            )

    def forward(self):
        net = self.net
        for d in range(1, net.nz):
            zz = (net.z + d) % net.nz
            net.landed(self.from_x.at[zz], self.slot_x + zz)
            pair = self.block(zz * 2 + net.x)[...].astype(F32) + self.from_x[zz].astype(F32)
            self.from_x[zz] = pair.astype(BF)
            net.push(
                self.from_x.at[zz],
                self.from_z.at[net.z],
                (zz * 2 + net.x, net.t),
                self.slot_z + net.z,
            )

    def finish(self):
        net = self.net
        net.landed(self.from_x.at[net.z], self.slot_x + net.z)
        total = self.block(net.e)[...].astype(F32) + self.from_x[net.z].astype(F32)
        for d in range(1, net.nz):
            zz = (net.z + d) % net.nz
            net.landed(self.from_z.at[zz], self.slot_z + zz)
            total = total + self.from_z[zz].astype(F32)
        return total


class Exchange:
    def __init__(self, net, outgoing, incoming):
        self.net, self.outgoing, self.incoming = net, outgoing, incoming
        self.slot = net.recv_slots(net.n)

    def start(self):
        net = self.net
        for d in range(1, net.n):
            to = net.peer(d)
            net.push(self.outgoing(to), self.incoming(net.e), (to, net.t), self.slot + net.e)

    def arrive(self, d):
        source = self.net.peer(d)
        self.net.landed(self.incoming(source), self.slot + source)
        return source

    def finish(self):
        for d in range(1, self.net.n):
            self.arrive(d)


class Dispatch:
    def __init__(self, net, outgoing, incoming):
        self.net, self.outgoing, self.incoming = net, outgoing, incoming
        self.send = Exchange(
            net, lambda b: outgoing.at[b], lambda b: incoming.at[b, net.core, net.y]
        )
        self.slot_y = net.recv_slots(net.n)
        self.slot_core = net.recv_slots(1)

    def start(self):
        net = self.net
        self.send.start()
        self.incoming[net.e, net.core, net.y] = self.outgoing[net.e]

    def relay_y(self):
        net = self.net
        for d in range(net.n):
            b = net.e if d == 0 else self.send.arrive(d)
            part = self.incoming.at[b, net.core, net.y]
            net.push(part, part, net.across_y(), self.slot_y + b)

    def relay_core(self):
        net = self.net
        for d in range(net.n):
            b = net.peer(d)
            net.landed(self.incoming.at[b, net.core, 1 - net.y], self.slot_y + b)
        part = self.incoming.at[:, net.core]
        net.push(part, part, net.other_core(), self.slot_core)

    def finish(self):
        self.net.landed(self.incoming.at[:, 1 - self.net.core], self.slot_core)


class Swap:
    def __init__(self, net, out_buf, in_buf, partner):
        self.net, self.out_buf, self.in_buf, self.partner = net, out_buf, in_buf, partner
        self.slot = net.recv_slots(1)

    def start(self, value):
        self.out_buf[...] = value.astype(self.out_buf.dtype)
        self.send()

    def send(self):
        self.net.push(self.out_buf, self.in_buf, self.partner, self.slot)

    def other(self):
        self.net.landed(self.in_buf, self.slot)
        return self.in_buf[...].astype(F32)

    def both(self):
        return self.out_buf[...].astype(F32) + self.other()


class Share:
    def __init__(self, net, halves):
        self.net, self.halves = net, halves
        self.slot = net.recv_slots(1)

    def start(self, value):
        net = self.net
        self.halves[net.core] = value.astype(self.halves.dtype)
        part = self.halves.at[net.core]
        net.push(part, part, net.other_core(), self.slot)

    def finish(self):
        net = self.net
        net.landed(self.halves.at[1 - net.core], self.slot)
        return jnp.concatenate([self.halves[0], self.halves[1]], axis=1)


def silu_both(value):
    gate = jax.nn.sigmoid(value)
    return value * gate, gate * (1.0 + value * (1.0 - gate))


def norm_scale(value):
    return lax.rsqrt(jnp.mean(value * value, axis=1, keepdims=True) + EPSILON)


def norm_back(grad_normed, source, scale, gain):
    weighted = grad_normed * gain
    inner = jnp.mean(weighted * source, axis=1, keepdims=True)
    return scale * weighted - scale * scale * scale * source * inner


PLACES = ["tok", "cot", "routes", "lengths", "parents", "gain_a", "gain_b", "wq", "wk", "wv"]
PLACES += ["wo", "router", "sg", "su", "sd", "eg", "eu", "ed"]
RESULTS = ["out", "gtok", "dga", "dgb", "dwq", "dwk", "dwv", "dwo", "drouter"]
RESULTS += ["dsg", "dsu", "dsd", "deg", "deu", "ded"]


def scratch_shapes(s):
    n, local, half = s.n, s.local, s.half
    depth, hidden, shared, cap = s.depth, s.hidden, s.shared, s.cap
    micro, nz = s.micro, s.n // 2
    model, wide, stack, tree = 2 * half, 2 * s.width, s.heads * local, n * local
    part = cap // 4
    vm = pltpu.VMEM
    return dict(
        w_kv=vm((n, depth, wide), BF),
        w_qo=vm((n, depth, wide), BF),
        w_sh=vm((3, n, depth, shared), BF),
        ext_in=vm((n, 16, 128), BF),
        tok_all=vm((n, 2, 2, micro * local // 4, model), BF),
        cos_all=vm((n, micro * local, 128), F32),
        sin_all=vm((n, micro * local, 128), F32),
        kv=vm((micro, n, local, wide), BF),
        q_rows=vm((micro, stack, wide), BF),
        expo=vm((micro, stack, tree), F32),
        total=vm((micro, stack, 1), F32),
        mixed=vm((micro, local, wide), F32),
        mixed_low=vm((micro * local, wide), BF),
        choice=vm((micro, local, n * cap), BF),
        choice_half=vm((micro, local, n * cap // 2), BF),
        choice_wide=vm((micro, local, n * 128), BF),
        res=vm((micro, local, model), F32),
        n_one=vm((micro * local, model), BF),
        n_two=vm((micro * local, model), BF),
        c_out=vm((micro, n, part, model), BF),
        c_in=vm((micro, n, 2, 2, part, model), BF),
        x_out=vm((micro, n, part, model), BF),
        x_in=vm((micro, n, 2, 2, part, model), BF),
        h_out=vm((micro, n, 16, 128), BF),
        h_in=vm((micro, n, 16, 128), BF),
        gate_col=vm((micro, n * cap, 1), F32),
        e_h=vm((micro, n * cap, hidden), BF),
        e_dg=vm((micro, n * cap, hidden), BF),
        e_du=vm((micro, n * cap, hidden), BF),
        y_core=vm((micro, n, cap, half), BF),
        g_core=vm((micro, n, cap, half), BF),
        y_in=vm((micro, n, cap // 2, half), BF),
        y_far=vm((micro, n, cap // 2, half), BF),
        g_in=vm((micro, n, cap, half), BF),
        d_out=vm((micro, n, 8, 128), F32),
        d_in=vm((micro, n, 8, 128), F32),
        d_tensor=vm((micro, 4, 8, 128), F32),
        core_a=vm((micro, 2, local, half), F32),
        core_b=vm((4, micro * local, half), BF),
        core_c=vm((micro, 2, local, half), F32),
        s_grads=vm((3, micro * local, shared), BF),
        s_own=vm((2, micro * local, half), F32),
        y_swap=vm((4, micro, 2, local, half), BF),
        share_a=vm((micro, 2, local, half), F32),
        share_b=vm((micro, 2, local, half), F32),
        share_c=vm((micro, 2, local, half), F32),
        share_out=vm((micro, 2, local, half), BF),
        kv_part=vm((micro, n, local, wide), BF),
        kv_fx=vm((micro, nz, local, wide), BF),
        kv_fz=vm((micro, nz, local, wide), BF),
        sh_part=vm((3, n, depth, shared), BF),
        sh_fx=vm((3, nz, depth, shared), BF),
        sh_fz=vm((3, nz, depth, shared), BF),
        w_part=vm((2, n, depth, wide), BF),
        w_fx=vm((2, nz, depth, wide), BF),
        w_fz=vm((2, nz, depth, wide), BF),
        gains_out=vm((n, 16, 128), F32),
        gains_in=vm((n, 16, 128), F32),
        stage=vm((2, half, hidden), F32),
        stage_d=vm((hidden, half), F32),
        save_sems=pltpu.SemaphoreType.DMA((6,)),
        send_sems=pltpu.SemaphoreType.DMA((SENDS,)),
        recv_sems=pltpu.SemaphoreType.DMA((RECVS,)),
    )


SENDS = 200
RECVS = 300


def layer_kernel(s, names, *refs):
    r = types.SimpleNamespace(**dict(zip(names, refs)))
    n, local, width, half = s.n, s.local, s.width, s.half
    depth, hidden, shared, cap = s.depth, s.hidden, s.shared, s.cap
    micro, heads = s.micro, s.heads
    rows, model, tree, wide, stack = micro * local, 2 * half, n * local, 2 * width, heads * local
    part = cap // 4
    net = Net(n, r.send_sems, r.recv_sems)
    me, core, y = net.e, net.core, net.y
    ready = net.greet()
    micros = range(micro)
    my_half = pl.ds(pl.multiple_of(core * half, 128), half)
    other_half = pl.ds(pl.multiple_of((1 - core) * half, 128), half)

    def rows_of(m):
        return slice(m * local, (m + 1) * local)

    left = (iota((width, wide), 1) == iota((width, wide), 0)).astype(BF)
    right = (iota((width, wide), 1) == iota((width, wide), 0) + width).astype(BF)
    r.w_kv[me] = (dot(r.wk[...], left) + dot(r.wv[...], right)).astype(BF)
    r.tok_all[me] = r.tok[...].reshape(2, 2, rows // 4, model)
    r.w_qo[me] = (dot(r.wq[...], left) + dot_tn(r.wo[...], right)).astype(BF)
    ext = [r.gain_a[...].astype(F32), r.gain_b[...].astype(F32), jnp.zeros((6, depth), F32)]
    ext = jnp.concatenate(ext + [r.router[...].astype(F32)], axis=0).astype(BF)
    pad = (iota((depth, 128), 1) == iota((depth, 128), 0)).astype(BF)
    r.ext_in[me] = dot(ext, pad).astype(BF)
    for i, name in enumerate(("sg", "su", "sd")):
        r.w_sh[i, me] = getattr(r, name)[...]

    slot_ty, slot_tc = net.recv_slots(n), net.recv_slots(n)

    def token_on(b, when):
        quarter = r.tok_all.at[b, core, y]
        net.push(quarter, quarter, net.across_y(), slot_ty + b, when)

    get_kv = Gather(net, lambda b, k: r.w_kv.at[b])
    get_qo = Gather(net, lambda b, k: r.w_qo.at[b])
    get_tok = Gather(net, lambda b, k: r.tok_all.at[b, core, y], on_land=token_on)
    get_sh = [Gather(net, lambda b, k, i=i: r.w_sh.at[i, b]) for i in range(3)]
    get_ext = Exchange(net, lambda b: r.ext_in.at[me], lambda b: r.ext_in.at[b])
    ready()
    get_ext.start()
    get_tok.start()
    get_kv.start()
    get_qo.start()

    eye = (iota((128, 128), 0) == iota((128, 128), 1)).astype(BF)
    routes = dot_nt(eye, r.routes[...].astype(BF))
    lane = iota((local, 16), 1) - 8
    earlier = (iota((local, local), 1) < iota((local, local), 0)).astype(BF)

    def spread(span):
        of_lane = iota((16, n * span), 1) // span
        return (iota((16, n * span), 0) - 8 == of_lane).astype(BF)

    hot_one, hot_two, quarter = [], [], []
    send_c = [Dispatch(net, r.c_out.at[m], r.c_in.at[m]) for m in micros]
    send_h = [
        Exchange(net, lambda b, m=m: r.h_out.at[m, b], lambda b, m=m: r.h_in.at[m, b])
        for m in micros
    ]
    for m in micros:
        one = lane == routes[:, 2 * m : 2 * m + 1].astype(jnp.int32)
        two = lane == routes[:, 2 * m + 1 : 2 * m + 2].astype(jnp.int32)
        hot_one.append(one)
        hot_two.append(two)
        hits = (one | two).astype(F32)
        rank = jnp.where(hits > 0.5, dot(earlier, hits.astype(BF)), -1.0).astype(BF)

        def taken(span, first=0):
            wanted = iota((local, n * span), 1) % span + first
            return (dot(rank, spread(span)) == wanted.astype(F32)).astype(BF)

        r.choice[m] = taken(cap)
        r.choice_half[m] = taken(cap // 2, y * (cap // 2))
        r.choice_wide[m] = taken(128)
        quarter.append(taken(part, (core * 2 + y) * part))
        hit_rows = dot_tn(hits.astype(BF), r.choice_wide[m]).astype(BF)
        for b in range(n):
            r.h_out[m, b] = hit_rows[:, b * 128 : (b + 1) * 128]
        r.h_in[m, me] = r.h_out[m, me]
        picked = dot_tn(quarter[m], r.cot[rows_of(m)]).astype(BF)
        r.c_out[m] = picked.reshape(n, part, model)

    def segments(m):
        starts, ends, paths, shifts, begin = [], [], [], [], 0
        for seg in range(s.segs):
            size = r.lengths[m, seg]
            starts.append(begin)
            ends.append(begin + size)
            begin = begin + size
            if seg == 0:
                paths.append(jnp.int32(1))
                shifts.append(jnp.int32(0))
            else:
                parent = r.parents[m, seg]
                path, shift = jnp.int32(0), jnp.int32(0)
                for other in range(seg):
                    is_parent = parent == other
                    path = jnp.where(is_parent, paths[other], path)
                    shift = jnp.where(
                        is_parent, shifts[other] + ends[other] - starts[other], shift
                    )
                paths.append(path + (1 << seg))
                shifts.append(shift)
        return starts, ends, paths, shifts

    tables = [segments(m) for m in micros]

    def row_values(m, ids):
        starts, ends, paths, shifts = tables[m]
        path, place, own = jnp.zeros_like(ids), jnp.zeros_like(ids), jnp.zeros_like(ids)
        for seg in range(s.segs):
            inside = (ids >= starts[seg]) & (ids < ends[seg])
            path = jnp.where(inside, paths[seg], path)
            place = jnp.where(inside, ids - starts[seg] + shifts[seg], place)
            own = jnp.where(inside, 1 << seg, own)
        return path, place, own

    turn = (iota((1, 128), 1) % (HEAD // 2)).astype(F32)
    frequency = jnp.exp(turn * (-math.log(ROPE_BASE) / (HEAD // 2)))

    def angle_step(b, carry):
        ids = b * local + iota((local, 1), 0)
        place = jnp.concatenate([row_values(m, ids)[1] for m in micros], axis=0)
        angle = place.astype(F32) * frequency
        r.cos_all[b] = jnp.cos(angle)
        r.sin_all[b] = jnp.sin(angle)
        return carry

    lax.fori_loop(0, n, angle_step, 0)
    is_left = iota((1, wide), 1) < width
    swap_r, swap_c = iota((wide, wide), 0), iota((wide, wide), 1)
    lower = swap_c % HEAD < HEAD // 2
    swap = jnp.where(lower & (swap_r == swap_c + HEAD // 2), -1.0, 0.0)
    swap = jnp.where(~lower & (swap_r == swap_c - HEAD // 2), 1.0, swap)
    swap = jnp.where(is_left, swap, 0.0)
    swap_low = swap.astype(BF)

    def turns(b):
        cosine = jnp.concatenate([r.cos_all[b]] * (wide // 128), axis=1)
        sine = jnp.concatenate([r.sin_all[b]] * (wide // 128), axis=1)
        return jnp.where(is_left, cosine, 1.0), sine

    for distance in range(1, net.nz):
        get_tok.step(distance)
        get_kv.step(distance)
        get_qo.step(distance)
    get_tok.finish()
    get_ext.finish()
    for d in range(1, n):
        b = net.peer(d)
        net.landed(r.tok_all.at[b, core, 1 - y], slot_ty + b)
        both = r.tok_all.at[b, core]
        net.push(both, both, net.other_core(), slot_tc + b)

    def lay(b):
        place = iota((128, model), 0)
        return (place < depth) & (place + b * depth == iota((128, model), 1))

    ext_all = jnp.zeros((16, model), F32)
    for b in range(n):
        ext_all = ext_all + dot(r.ext_in[b], lay(b).astype(BF))
    gain_one, gain_two = ext_all[0:1], ext_all[1:2]
    ext_low = ext_all.astype(BF)
    get_kv.finish()
    w_kv = r.w_kv[...].reshape(model, wide)
    w_kv_swapped = dot(w_kv, swap_low).astype(BF)

    def normed(block):
        value = block.astype(F32)
        return (value * norm_scale(value) * gain_one).astype(BF)

    def key_value(b):
        block = normed(r.tok_all[b].reshape(rows, model))
        cosine, sine = turns(b)
        both = (dot(block, w_kv) * cosine + dot(block, w_kv_swapped) * sine).astype(BF)
        for m in micros:
            r.kv[m, b] = both[rows_of(m)]

    get_qo.finish()
    for g in get_sh:
        g.start()
    key_value(me)

    def key_value_step(d, carry):
        b = net.peer(d)
        net.landed(r.tok_all.at[b, 1 - core], slot_tc + b)
        key_value(b)
        return carry

    lax.fori_loop(1, n, key_value_step, 0)
    r.n_one[...] = normed(r.tok[...])
    w_qo = r.w_qo[...].reshape(model, wide)
    cosine, sine = turns(me)
    cosine = jnp.where(is_left, cosine, 0.0)
    queries = dot(r.n_one[...], w_qo) * cosine
    queries = queries + dot(r.n_one[...], dot(w_qo, swap_low).astype(BF)) * sine
    queries = queries.astype(BF)
    for g in get_sh:
        g.step(1)

    head_of = iota((1, wide), 1) // HEAD
    q_masks = [head_of == h for h in range(heads)]
    v_masks = [head_of == heads + h for h in range(heads)]

    def by_head(block, masks):
        return jnp.concatenate(
            [jnp.where(mask, block, jnp.zeros_like(block)) for mask in masks], axis=0
        )

    def join_heads(value, masks):
        total = jnp.zeros((local, wide), F32)
        for h, mask in enumerate(masks):
            total = total + jnp.where(mask, value[h * local : (h + 1) * local], 0.0)
        return total

    def o_half(h):
        return r.w_qo[pl.ds(h * (n // 2), n // 2)].reshape(half, wide)

    core_a = [Swap(net, r.core_a.at[m, 0], r.core_a.at[m, 1], net.other_core()) for m in micros]
    core_c = [Swap(net, r.core_c.at[m, 0], r.core_c.at[m, 1], net.other_core()) for m in micros]
    core_b = [
        Swap(net, r.core_b.at[2 * i], r.core_b.at[2 * i + 1], net.other_core()) for i in range(2)
    ]
    y_swap = [
        [Swap(net, r.y_swap.at[i, m, 0], r.y_swap.at[i, m, 1], net.across_y()) for m in micros]
        for i in range(4)
    ]
    share_a = [Share(net, r.share_a.at[m]) for m in micros]
    share_b = [Share(net, r.share_b.at[m]) for m in micros]
    share_c = [Share(net, r.share_c.at[m]) for m in micros]
    share_out = [Share(net, r.share_out.at[m]) for m in micros]

    score_scale = HEAD**-0.5
    for m in micros:
        r.q_rows[m] = by_head(queries[rows_of(m)], q_masks)
        kv_rows = r.kv[m].reshape(tree, wide)
        ids = me * local + iota((stack, 1), 0) % local
        path, unused, unused_two = row_values(m, ids)
        key_ids = iota((1, tree), 1)
        unused, unused_two, key_seg = row_values(m, key_ids)
        seen = ((path & key_seg) != 0) & (key_ids <= ids)
        scores = dot_nt(r.q_rows[m], kv_rows) * score_scale
        expo = jnp.where(seen, jnp.exp(scores), 0.0)
        r.expo[m] = expo
        total = jnp.sum(expo, axis=1, keepdims=True)
        r.total[m] = total
        mixed = join_heads(dot(expo.astype(BF), kv_rows) / total, v_masks)
        r.mixed[m] = mixed
        r.mixed_low[rows_of(m)] = mixed.astype(BF)
        core_a[m].start(dot_nt(r.mixed_low[rows_of(m)], o_half(1 - core)))
        if m == 0:
            for g in get_sh:
                g.step(2)
    for m in micros:
        mine = dot_nt(r.mixed_low[rows_of(m)], o_half(core))
        y_swap[0][m].start(mine + core_a[m].other())
    for m in micros:
        send_c[m].start()
        send_h[m].start()
    for g in get_sh:
        g.step(3)
    for m in micros:
        share_a[m].start(y_swap[0][m].both())
    for m in micros:
        send_c[m].relay_y()

    send_x = [Dispatch(net, r.x_out.at[m], r.x_in.at[m]) for m in micros]
    scale_two = []
    for m in micros:
        res = r.tok[rows_of(m)].astype(F32) + share_a[m].finish()
        r.res[m] = res
        scale_two.append(norm_scale(res))
        normed_two = (res * scale_two[m] * gain_two).astype(BF)
        r.n_two[rows_of(m)] = normed_two
        r.x_out[m] = dot_tn(quarter[m], normed_two).astype(BF).reshape(n, part, model)
        send_x[m].start()

    gates = []
    for m in micros:
        logits = dot_nt(r.n_two[rows_of(m)], ext_low)
        z_one = jnp.sum(jnp.where(hot_one[m], logits, 0.0), axis=1, keepdims=True)
        z_two = jnp.sum(jnp.where(hot_two[m], logits, 0.0), axis=1, keepdims=True)
        z_top = jnp.maximum(z_one, z_two)
        e_one, e_two = jnp.exp(z_one - z_top), jnp.exp(z_two - z_top)
        chosen = jnp.where(hot_one[m], e_one, jnp.where(hot_two[m], e_two, 0.0))
        gates.append(chosen / (e_one + e_two))
    for m in micros:
        send_c[m].relay_core()

    for g in get_sh:
        g.finish()

    def wide_half(i, h):
        return r.w_sh[i, pl.ds(h * (n // 2), n // 2)].reshape(half, shared)

    def shared_step(m, carry):
        here = pl.ds(pl.multiple_of(m * local, local), local)
        normed_two = r.n_two[here]
        shared_g = dot(normed_two, r.w_sh[0].reshape(model, shared))
        shared_u = dot(normed_two, r.w_sh[1].reshape(model, shared))
        act, slope = silu_both(shared_g)
        shared_h = (act * shared_u).astype(BF)
        grad_h = dot(r.cot[here], r.w_sh[2].reshape(model, shared))
        grad_g = (grad_h * shared_u * slope).astype(BF)
        grad_u = (grad_h * act).astype(BF)
        r.s_grads[0, here] = grad_g
        r.s_grads[1, here] = grad_u
        r.s_grads[2, here] = shared_h
        other, own = 1 - core, core
        back = dot_nt(grad_g, wide_half(0, other)) + dot_nt(grad_u, wide_half(1, other))
        r.core_b[0, here] = back.astype(BF)
        r.core_b[2, here] = dot_nt(shared_h, wide_half(2, other)).astype(BF)
        back = dot_nt(grad_g, wide_half(0, own)) + dot_nt(grad_u, wide_half(1, own))
        r.s_own[0, here] = back
        r.s_own[1, here] = dot_nt(shared_h, wide_half(2, own))
        return carry

    lax.fori_loop(0, micro, shared_step, 0)
    for swap_b in core_b:
        swap_b.send()
    for i, (rows_a, rows_b) in enumerate(((r.n_two, 0), (r.n_two, 1), (r.cot, 2))):
        grads = dot_tn(rows_a[...], r.s_grads[rows_b])
        r.sh_part[i] = grads.astype(BF).reshape(n, depth, shared)
    sum_sh = [
        Scatter(net, lambda b, i=i: r.sh_part.at[i, b], r.sh_fx.at[i], r.sh_fz.at[i])
        for i in range(3)
    ]

    for m in micros:
        send_x[m].relay_y()
    for m in micros:
        send_x[m].relay_core()
    for m in micros:
        send_h[m].finish()
        send_c[m].finish()

    slot_gc = net.recv_slots(micro)
    slot_yc = net.recv_slots(micro)
    slot_yy = net.recv_slots(micro)
    my_slots = pl.ds(pl.multiple_of(y * (cap // 2), cap // 2), cap // 2)
    far_slots = pl.ds(pl.multiple_of((1 - y) * (cap // 2), cap // 2), cap // 2)
    send_g = [
        Exchange(net, lambda b, m=m: r.g_core.at[m, b], lambda b, m=m: r.g_in.at[m, b])
        for m in micros
    ]
    send_y = [
        Exchange(net, lambda b, m=m: r.y_core.at[m, b, my_slots], lambda b, m=m: r.y_in.at[m, b])
        for m in micros
    ]
    send_d = [
        Exchange(net, lambda b, m=m: r.d_out.at[m, b], lambda b, m=m: r.d_in.at[m, b])
        for m in micros
    ]
    slot_eye = eye[:cap]
    slot_line = iota((cap, 128), 0) == iota((cap, 128), 1)
    own_lane = iota((n * cap, 16), 1) - 8 == me
    group = 4
    halves = [slice(0, half), slice(half, model)]

    def expert_gates(m):
        x_rows = r.x_in[m].reshape(n * cap, model)
        z_all = dot_nt(x_rows, ext_low)
        hit = jnp.concatenate([dot_nt(slot_eye, r.h_in[m, b]) for b in range(n)], axis=0)
        z_own = jnp.sum(jnp.where(own_lane, z_all, 0.0), axis=1, keepdims=True)
        z_other = jnp.sum(jnp.where(own_lane, 0.0, z_all * hit), axis=1, keepdims=True)
        z_top = jnp.maximum(z_own, z_other)
        e_own, e_other = jnp.exp(z_own - z_top), jnp.exp(z_other - z_top)
        r.gate_col[m] = e_own / (e_own + e_other)

    def expert_rows(m, i):
        count = group * cap
        span = slice(i * group, (i + 1) * group)
        flat = slice(i * count, (i + 1) * count)
        x = r.x_in[m, span].reshape(count, model)
        c = r.c_in[m, span].reshape(count, model)
        gate = r.gate_col[m, flat]
        gate_pre = dot(x, r.eg[...])
        up_pre = dot(x, r.eu[...])
        act, slope = silu_both(gate_pre)
        hid = (act * up_pre).astype(BF)
        grad_y = (gate * c.astype(F32)).astype(BF)
        grad_hid = dot_nt(grad_y, r.ed[...])
        grad_g = (grad_hid * up_pre * slope).astype(BF)
        grad_u = (grad_hid * act).astype(BF)
        r.e_h[m, flat] = hid
        r.e_dg[m, flat] = grad_g
        r.e_du[m, flat] = grad_u
        dots = jnp.zeros((count, 1), F32)
        for cut in halves:
            out = dot(hid, r.ed[:, cut])
            r.tok_all[span, 0, m, :, cut] = out.astype(BF).reshape(group, cap, half)
            dots = dots + jnp.sum(out * c[:, cut].astype(F32), axis=1, keepdims=True)
            back = dot_nt(grad_g, r.eg[cut]) + dot_nt(grad_u, r.eu[cut])
            r.tok_all[span, 1, m, :, cut] = back.astype(BF).reshape(group, cap, half)
        r.c_in[m, span] = grad_y.reshape(group, 2, 2, part, model)
        for b in range(group):
            line = jnp.where(slot_line, dots[b * cap : (b + 1) * cap], 0.0)
            line = jnp.sum(line, axis=0, keepdims=True)
            r.d_out[m, i * group + b] = jnp.broadcast_to(line, (8, 128))

    def expert_sent(m):
        net.push(r.tok_all.at[:, 1, m, :, other_half], r.g_core.at[m], net.other_core(), slot_gc + m)
        net.push(r.tok_all.at[:, 0, m, :, other_half], r.y_core.at[m], net.other_core(), slot_yc + m)

    def return_g(m):
        send_d[m].start()
        r.d_in[m, me] = r.d_out[m, me]
        net.landed(r.g_core.at[m], slot_gc + m)
        r.g_core[m] = (r.tok_all[:, 1, m, :, my_half].astype(F32) + r.g_core[m].astype(F32)).astype(BF)
        send_g[m].start()
        r.g_in[m, me] = r.g_core[m, me]

    def add_y(m):
        net.landed(r.y_core.at[m], slot_yc + m)
        mine = r.tok_all[:, 0, m, :, my_half].astype(F32)
        r.y_core[m] = (mine + r.y_core[m].astype(F32)).astype(BF)
        net.push(r.y_core.at[m, :, far_slots], r.y_far.at[m], net.across_y(), slot_yy + m)

    def return_y(m):
        net.landed(r.y_far.at[m], slot_yy + m)
        both = r.y_core[m, :, my_slots].astype(F32) + r.y_far[m].astype(F32)
        r.y_core[m, :, my_slots] = both.astype(BF)
        send_y[m].start()
        r.y_in[m, me] = r.y_core[m, me, my_slots]

    net.drain()
    sum_sh[0].start()
    for m in micros:
        send_x[m].finish()
        expert_gates(m)
        for i in range(n // group):
            if m > 0 and i == 1:
                return_g(m - 1)
            expert_rows(m, i)
        expert_sent(m)
    return_g(micro - 1)
    sum_sh[1].start()

    saves = []

    def all_slots(ref, cut):
        return ref[..., cut].reshape(micro * n * cap, -1)

    def save(source, target, i):
        copy = pltpu.make_async_copy(source, target, r.save_sems.at[i])
        copy.start()
        saves.append(copy)

    for h, cut in enumerate(halves):
        for i, (target, grads) in enumerate(((r.deg, r.e_dg), (r.deu, r.e_du))):
            if h == 1:
                saves[i].wait()
            r.stage[i] = dot_tn(all_slots(r.x_in, cut), all_slots(grads, slice(None)))
            save(r.stage.at[i], target.at[cut], 2 * h + i)
        if h == 1:
            saves[2].wait()
        r.stage_d[...] = dot_tn(all_slots(r.e_h, slice(None)), all_slots(r.c_in, cut))
        save(r.stage_d, r.ded.at[:, cut], 4 + h)

    for m in micros:
        add_y(m)
    d_core = [Swap(net, r.d_tensor.at[m, 0], r.d_tensor.at[m, 1], net.other_core()) for m in micros]
    d_y = [Swap(net, r.d_tensor.at[m, 2], r.d_tensor.at[m, 3], net.across_y()) for m in micros]
    eight = iota((8, 128), 0)
    d_rows = []
    for m in micros:
        send_d[m].finish()
        line = jnp.zeros((8, 128), F32)
        for b in range(n):
            line = line + jnp.where(eight == b, r.d_in[m, b], 0.0)
        d_rows.append(line)
        d_core[m].start(line)
    shared_grad = r.s_own[0] + core_b[0].other()
    for m in micros:
        d_y[m].start(d_rows[m] + d_core[m].other())
    for m in micros:
        send_g[m].finish()
        moe_grad = dot(r.choice[m], r.g_in[m].reshape(n * cap, half))
        y_swap[1][m].start(moe_grad + shared_grad[rows_of(m)])
    net.drain(bulk=False)
    sum_sh[2].start()
    for m in micros:
        return_y(m)
    grad_logits = []
    for m in micros:
        d_all = d_y[m].both()
        grad_gate = jnp.zeros((local, 16), F32)
        for b in range(n):
            picked = r.choice_wide[m, :, b * 128 : (b + 1) * 128].astype(F32) * d_all[b : b + 1]
            grad_gate = jnp.where(lane == b, jnp.sum(picked, axis=1, keepdims=True), grad_gate)
        inner = jnp.sum(gates[m] * grad_gate, axis=1, keepdims=True)
        grad_logits.append((gates[m] * (grad_gate - inner)).astype(BF))
        share_b[m].start(y_swap[1][m].both())

    sum_sh[0].forward()

    w_qo = r.w_qo[...].reshape(model, wide)
    kv_sums, grad_queries, gain_rows = [], [], []
    for m in micros:
        grad_two = share_b[m].finish() + dot(grad_logits[m], ext_low)
        res = r.res[m]
        cot = r.cot[rows_of(m)].astype(F32)
        grad_res = cot + norm_back(grad_two, res, scale_two[m], gain_two)
        r.gtok[rows_of(m)] = grad_res
        gain_rows.append(jnp.sum(grad_two * res * scale_two[m], axis=0, keepdims=True))
        kv_rows = r.kv[m].reshape(tree, wide)
        total = r.total[m]
        gm = by_head(dot(grad_res.astype(BF), w_qo), v_masks)
        mixed = jnp.concatenate([r.mixed[m]] * heads, axis=0)
        delta = jnp.sum(gm * mixed, axis=1, keepdims=True) / total
        grad_summed = (gm / total).astype(BF)
        expo = r.expo[m]
        ds = (expo * (dot_nt(grad_summed, kv_rows) - delta)).astype(BF)
        grad_kv = dot_tn(ds, r.q_rows[m]) * score_scale + dot_tn(expo.astype(BF), grad_summed)
        r.kv_part[m] = grad_kv.astype(BF).reshape(n, local, wide)
        kv_sums.append(
            Scatter(net, lambda b, m=m: r.kv_part.at[m, b], r.kv_fx.at[m], r.kv_fz.at[m])
        )
        kv_sums[m].start()
        grad_queries.append(join_heads(dot(ds, kv_rows), q_masks) * score_scale)

    cosine, sine = turns(me)

    def turned_back(grad):
        return (grad * cosine - dot(grad, swap, EXACT) * sine).astype(BF)

    for m in micros:
        kv_sums[m].forward()
    grad_q = turned_back(jnp.concatenate(grad_queries, axis=0))
    grad_attn = r.gtok[...].astype(BF)
    part_qo = dot_tn(r.n_one[...], grad_q) + dot_tn(grad_attn, r.mixed_low[...])
    r.w_part[0] = part_qo.astype(BF).reshape(n, depth, wide)
    sum_w = [
        Scatter(net, lambda b, i=i: r.w_part.at[i, b], r.w_fx.at[i], r.w_fz.at[i])
        for i in range(2)
    ]
    sum_w[0].start()

    shared_y = r.s_own[1] + core_b[1].other()
    for m in micros:
        send_y[m].finish()
        gate_wide = dot(gates[m], spread(cap // 2).astype(F32), EXACT)
        gate_high = gate_wide.astype(BF).astype(F32)
        pick = r.choice_half[m].astype(F32)
        y_rows = r.y_in[m].reshape(n * cap // 2, half)
        moe_y = dot((pick * gate_high).astype(BF), y_rows)
        moe_y = moe_y + dot((pick * (gate_wide - gate_high)).astype(BF), y_rows)
        y_swap[2][m].start(moe_y + shared_y[rows_of(m)])
    sum_sh[1].forward()

    def weight_half(ref, h):
        return ref[pl.ds(h * (n // 2), n // 2)].reshape(half, wide)

    grad_kvs = []
    for m in micros:
        total = kv_sums[m].finish()
        cos_m, sin_m = cosine[rows_of(m)], sine[rows_of(m)]
        grad_kv = (total * cos_m - dot(total, swap, EXACT) * sin_m).astype(BF)
        grad_kvs.append(grad_kv)
        q_m = grad_q[rows_of(m)]
        other = dot_nt(q_m, weight_half(r.w_qo, 1 - core))
        core_c[m].start(other + dot_nt(grad_kv, weight_half(r.w_kv, 1 - core)))
    for m in micros:
        mine = dot_nt(grad_q[rows_of(m)], weight_half(r.w_qo, core))
        mine = mine + dot_nt(grad_kvs[m], weight_half(r.w_kv, core))
        y_swap[3][m].start(mine + core_c[m].other())
    part_kv = dot_tn(r.n_one[...], jnp.concatenate(grad_kvs, axis=0))
    r.w_part[1] = part_kv.astype(BF).reshape(n, depth, wide)
    sum_w[1].start()
    sum_sh[2].forward()
    sum_w[0].forward()
    for m in micros:
        share_c[m].start(y_swap[3][m].both())
    for m in micros:
        res_half = jnp.where(core == 0, r.res[m, :, :half], r.res[m, :, half:])
        share_out[m].start(res_half + y_swap[2][m].both())
    sum_w[1].forward()

    gain_one_row = jnp.zeros((1, model), F32)
    for m in micros:
        grad_one = share_c[m].finish()
        tok = r.tok[rows_of(m)].astype(F32)
        scale_one = norm_scale(tok)
        r.gtok[rows_of(m)] += norm_back(grad_one, tok, scale_one, gain_one)
        gain_one_row = gain_one_row + jnp.sum(grad_one * tok * scale_one, axis=0, keepdims=True)
    grad_router = jnp.zeros((16, model), F32)
    for m in micros:
        grad_router = grad_router + dot_tn(grad_logits[m], r.n_two[rows_of(m)])
    line = iota((16, model), 0)
    small = jnp.where(line == 0, gain_one_row, grad_router)
    small = jnp.where(line == 1, gain_rows[0] + gain_rows[1], small)
    for b in range(n):
        r.gains_out[b] = dot_nt(small, lay(b).astype(F32), EXACT)
    send_gains = Exchange(net, lambda b: r.gains_out.at[b], lambda b: r.gains_in.at[b])
    send_gains.start()
    r.gains_in[me] = r.gains_out[me]
    for m in micros:
        r.out[rows_of(m)] = share_out[m].finish()

    qo = sum_w[0].finish()
    r.dwq[...] = dot_nt(qo, left.astype(F32), EXACT)
    depth_eye = (iota((depth, depth), 0) == iota((depth, depth), 1)).astype(F32)
    r.dwo[...] = dot_tn(dot_nt(qo, right.astype(F32), EXACT), depth_eye, EXACT)
    kv = sum_w[1].finish()
    r.dwk[...] = dot_nt(kv, left.astype(F32), EXACT)
    r.dwv[...] = dot_nt(kv, right.astype(F32), EXACT)
    for i, target in enumerate((r.dsg, r.dsu, r.dsd)):
        target[...] = sum_sh[i].finish()
    send_gains.finish()
    gains = jnp.zeros((16, 128), F32)
    for b in range(n):
        gains = gains + r.gains_in[b]
    r.dga[...] = gains[0:1, :depth]
    r.dgb[...] = gains[1:2, :depth]
    r.drouter[...] = gains[8:16, :depth]
    for copy in saves[3:]:
        copy.wait()
    net.drain()


def settle_kernel(count, *refs):
    sources, targets, stops = refs[:count], refs[count : 2 * count], refs[2 * count : 3 * count]
    sems = refs[3 * count]
    reads = [
        pltpu.make_async_copy(a, b, sems.at[0, i]) for i, (a, b) in enumerate(zip(sources, stops))
    ]
    writes = [
        pltpu.make_async_copy(a, b, sems.at[1, i]) for i, (a, b) in enumerate(zip(stops, targets))
    ]
    for read in reads:
        read.start()
    for read, write in zip(reads, writes):
        read.wait()
        write.start()
    for write in writes:
        write.wait()


def fits(mesh):
    return mesh.shape["expert"] == 8 and mesh.shape["tensor"] == 4


def fused_body(
    tokens,
    out_grad,
    routes,
    lengths,
    parents,
    attn_gain,
    ffn_gain,
    w_query,
    w_key,
    w_value,
    w_out,
    router,
    shared_gate,
    shared_up,
    shared_down,
    expert_gate,
    expert_up,
    expert_down,
):
    micro, local, model = tokens.shape
    n = lax.axis_size("expert")
    experts = router.shape[1]
    depth, width = w_query.shape
    hidden, shared = expert_gate.shape[2], shared_gate.shape[1]
    s = types.SimpleNamespace(
        n=n,
        micro=micro,
        local=local,
        half=model // 2,
        depth=depth,
        width=width,
        heads=width // HEAD,
        hidden=hidden,
        shared=shared,
        cap=4 * local // experts,
        segs=lengths.shape[1],
    )
    rows = micro * local
    scratch = scratch_shapes(s)
    names = PLACES + RESULTS + list(scratch)
    shape = jax.ShapeDtypeStruct
    vmem, smem = pl.BlockSpec(memory_space=pltpu.VMEM), pl.BlockSpec(memory_space=pltpu.SMEM)
    hbm = pl.BlockSpec(memory_space=pl.ANY)
    results = (
        shape((rows, model), BF),
        shape((rows, model), F32),
        shape((1, depth), F32),
        shape((1, depth), F32),
        shape((depth, width), F32),
        shape((depth, width), F32),
        shape((depth, width), F32),
        shape((width, depth), F32),
        shape((experts, depth), F32),
        shape((depth, shared), F32),
        shape((depth, shared), F32),
        shape((depth, shared), F32),
        shape((model, hidden), F32),
        shape((model, hidden), F32),
        shape((hidden, model), F32),
    )
    found = pl.pallas_call(
        functools.partial(layer_kernel, s, names),
        out_shape=results,
        in_specs=[vmem] * 3 + [smem] * 2 + [vmem] * 13,
        out_specs=[vmem] * 12 + [hbm] * 3,
        scratch_shapes=list(scratch.values()),
        compiler_params=pltpu.CompilerParams(
            collective_id=0, has_side_effects=True, vmem_limit_bytes=VMEM_LIMIT
        ),
    )(
        tokens.reshape(rows, model),
        out_grad.reshape(rows, model),
        routes.transpose(0, 2, 1).reshape(2 * micro, local),
        lengths,
        parents,
        attn_gain.reshape(1, depth),
        ffn_gain.reshape(1, depth),
        w_query,
        w_key,
        w_value,
        w_out,
        router.T,
        shared_gate,
        shared_up,
        shared_down.T,
        expert_gate[0],
        expert_up[0],
        expert_down[0],
    )
    settled = pl.pallas_call(
        functools.partial(settle_kernel, len(results)),
        out_shape=results,
        in_specs=[hbm] * len(results),
        out_specs=[hbm] * len(results),
        scratch_shapes=[pltpu.VMEM(one.shape, one.dtype) for one in results]
        + [pltpu.SemaphoreType.DMA((2, len(results)))],
        compiler_params=pltpu.CompilerParams(vmem_limit_bytes=VMEM_LIMIT),
    )(*found)
    out, gtok, dga, dgb, dwq, dwk, dwv, dwo, drouter, dsg, dsu, dsd, deg, deu, ded = settled
    return (
        out.reshape(micro, local, model),
        gtok.reshape(micro, local, model),
        dga.reshape(depth),
        dgb.reshape(depth),
        dwq,
        dwk,
        dwv,
        dwo,
        drouter.T,
        dsg,
        dsu,
        dsd.T,
        deg[None],
        deu[None],
        ded[None],
    )


def solution(mesh):
    in_specs = (
        P(None, "expert", None),
        P(None, "expert", None),
        P(None, "expert", None),
        P(),
        P(),
        P("expert"),
        P("expert"),
        P("expert", "tensor"),
        P("expert", "tensor"),
        P("expert", "tensor"),
        P("tensor", "expert"),
        P("expert", None),
        P("expert", "tensor"),
        P("expert", "tensor"),
        P("tensor", "expert"),
        P("expert", None, "tensor"),
        P("expert", None, "tensor"),
        P("expert", "tensor", None),
    )
    out_specs = (
        P(None, "expert", None),
        P(None, "expert", None),
        P("expert"),
        P("expert"),
        P("expert", "tensor"),
        P("expert", "tensor"),
        P("expert", "tensor"),
        P("tensor", "expert"),
        P("expert", None),
        P("expert", "tensor"),
        P("expert", "tensor"),
        P("tensor", "expert"),
        P("expert", None, "tensor"),
        P("expert", None, "tensor"),
        P("expert", "tensor", None),
    )
    chosen = fused_body if fits(mesh) else plain_body
    return jax.shard_map(chosen, mesh=mesh, in_specs=in_specs, out_specs=out_specs, check_vma=False)
```

```python
import functools
import math
import types

import jax
import jax.numpy as jnp
from jax import lax
from jax.experimental import pallas as pl
from jax.experimental.pallas import tpu as pltpu
from jax.sharding import PartitionSpec as P

HEAD = 64


EPSILON = 1e-06
ROPE_BASE = 10000.0
KEY_BLOCK = 2048


def matmul(left, right):
    return jnp.dot(left, right, preferred_element_type=jnp.float32)


def tree_tables(lengths, parents):
    seg_count = lengths.shape[0]
    identity = jnp.arange(seg_count, dtype=jnp.int32)
    current = identity
    ancestry = jnp.zeros((seg_count, seg_count), jnp.float32)
    for depth_level in range(seg_count):
        chosen_mask = current[:, None] == identity[None, :]
        ancestry = jnp.maximum(ancestry, chosen_mask.astype(jnp.float32))
        current = jnp.sum(jnp.where(chosen_mask, parents[None, :], 0), axis=1)
    seg_ends = jnp.cumsum(lengths)
    starts = seg_ends - lengths
    sizes_float = lengths.astype(jnp.float32)
    offsets = jnp.sum(ancestry * sizes_float[None, :], axis=1) - sizes_float
    return (ancestry, starts, seg_ends, offsets)


def row_tables(row_ids, starts, seg_ends, offsets):
    member = (
        (row_ids[:, None] >= starts[None, :]) & (row_ids[:, None] < seg_ends[None, :])
    ).astype(jnp.float32)
    position_shift = offsets - starts.astype(jnp.float32)
    position = jnp.sum(member * position_shift[None, :], axis=1) + row_ids.astype(jnp.float32)
    return (member, position)


def rotary_tables(position, half_width):
    frequency = ROPE_BASE ** (-jnp.arange(half_width, dtype=jnp.float32) / half_width)
    angles = position[:, None] * frequency[None, :]
    return (jnp.cos(angles)[:, None, :], jnp.sin(angles)[:, None, :])


def rotate(head_values, position):
    half_width = head_values.shape[-1] // 2
    cosines, sine_values = rotary_tables(position, half_width)
    first_half = head_values[..., :half_width]
    second_half = head_values[..., half_width:]
    return jnp.concatenate(
        [
            first_half * cosines - second_half * sine_values,
            second_half * cosines + first_half * sine_values,
        ],
        axis=-1,
    )


def rotate_back(grad_heads, position):
    half_width = grad_heads.shape[-1] // 2
    cosines, sine_values = rotary_tables(position, half_width)
    first_half = grad_heads[..., :half_width]
    second_half = grad_heads[..., half_width:]
    return jnp.concatenate(
        [
            first_half * cosines + second_half * sine_values,
            second_half * cosines - first_half * sine_values,
        ],
        axis=-1,
    )


def silu_parts(gate_val):
    sigmoid_val = jax.nn.sigmoid(gate_val)
    return (gate_val * sigmoid_val, sigmoid_val * (1.0 + gate_val * (1.0 - sigmoid_val)))


def rms_back(grad_normed, source, norm_scale, gain):
    weighted = grad_normed * gain
    inner_mean = jnp.mean(weighted * source, axis=1, keepdims=True)
    return (
        norm_scale * weighted - norm_scale**3 * source * inner_mean,
        jnp.sum(grad_normed * source * norm_scale, axis=0),
    )


def visible(reach_rows, query_ids, key_member, key_ids):
    linked = matmul(reach_rows, key_member.T) > 0.5
    return linked & (key_ids[None, :] <= query_ids[:, None])


def score_block(query_heads, key_heads, seen, score_scale):
    scores = (
        jnp.einsum("qhd,khd->hqk", query_heads, key_heads, preferred_element_type=jnp.float32)
        * score_scale
    )
    return jnp.where(seen[None], jnp.exp(scores), 0.0)


def score_grads(weights_exp, grad_summed, value_heads, delta_rows):
    grad_exp = jnp.einsum(
        "qhd,khd->hqk", grad_summed, value_heads, preferred_element_type=jnp.float32
    )
    return (weights_exp * (grad_exp - jnp.transpose(delta_rows)[:, :, None])).astype(jnp.bfloat16)


def plain_body(
    tokens,
    out_grad,
    routes,
    lengths,
    parents,
    attn_gain,
    ffn_gain,
    w_query,
    w_key,
    w_value,
    w_out,
    router,
    shared_gate,
    shared_up,
    shared_down,
    expert_gate,
    expert_up,
    expert_down,
):
    micro_count, row_count, model_width = tokens.shape
    devices = lax.axis_size("expert")
    tree_rows = row_count * devices
    expert_count = router.shape[1]
    owners = devices // expert_count
    capacity = 4 * row_count // expert_count
    score_scale = HEAD ** (-0.5)
    local_rows = lax.axis_index("expert") * row_count + jnp.arange(row_count, dtype=jnp.int32)
    part_gate = expert_gate[0]
    part_up = expert_up[0]
    part_down = expert_down[0]
    labels = jnp.arange(expert_count, dtype=jnp.int32)
    slot_ids = jnp.arange(expert_count * capacity, dtype=jnp.int32)
    pair_ids = jnp.arange(2 * row_count, dtype=jnp.int32)
    block_size = math.gcd(tree_rows, KEY_BLOCK)
    block_count = tree_rows // block_size
    layer_outputs = []
    token_gradients = []
    dense_sums = None
    expert_sums = None
    for micro_step in range(micro_count):
        gathered = (
            lax.all_gather(attn_gain, "expert", axis=0, tiled=True),
            lax.all_gather(ffn_gain, "expert", axis=0, tiled=True),
            lax.all_gather(w_query, "expert", axis=0, tiled=True),
            lax.all_gather(w_key, "expert", axis=0, tiled=True),
            lax.all_gather(w_value, "expert", axis=0, tiled=True),
            lax.all_gather(w_out, "expert", axis=1, tiled=True),
            lax.all_gather(router, "expert", axis=0, tiled=True),
            lax.all_gather(shared_gate, "expert", axis=0, tiled=True),
            lax.all_gather(shared_up, "expert", axis=0, tiled=True),
            lax.all_gather(shared_down, "expert", axis=1, tiled=True),
        )
        (
            gain_one,
            gain_two,
            query_weight,
            key_weight,
            value_weight,
            out_weight,
            router_weight,
            gate_weight,
            up_weight,
            down_weight,
        ) = gathered
        local_width = query_weight.shape[1]
        head_count = local_width // HEAD
        ancestry, starts, seg_ends, offsets = tree_tables(lengths[micro_step], parents[micro_step])
        member, position = row_tables(local_rows, starts, seg_ends, offsets)
        reach = matmul(member, ancestry)
        tokens_now = tokens[micro_step].astype(jnp.float32)
        norm_one = lax.rsqrt(jnp.mean(tokens_now * tokens_now, axis=1, keepdims=True) + EPSILON)
        normed_one = (tokens_now * norm_one * gain_one).astype(jnp.bfloat16)
        query_pre = matmul(normed_one, query_weight).reshape(row_count, head_count, HEAD)
        key_pre = matmul(normed_one, key_weight).reshape(row_count, head_count, HEAD)
        value_low = matmul(normed_one, value_weight).astype(jnp.bfloat16)
        queries = rotate(query_pre, position).astype(jnp.bfloat16)
        key_heads = rotate(key_pre, position).astype(jnp.bfloat16)
        key_value = jnp.concatenate([key_heads.reshape(row_count, local_width), value_low], axis=1)
        all_pairs = lax.all_gather(key_value, "expert", axis=0, tiled=True)

        def key_block_parts(block_index):
            first_key = block_index * block_size
            key_block = lax.dynamic_slice_in_dim(all_pairs, first_key, block_size, 0)
            key_ids = first_key + jnp.arange(block_size, dtype=jnp.int32)
            key_member, unused = row_tables(key_ids, starts, seg_ends, offsets)
            seen = visible(reach, local_rows, key_member, key_ids)
            block_keys = key_block[:, :local_width].reshape(block_size, head_count, HEAD)
            block_values = key_block[:, local_width:].reshape(block_size, head_count, HEAD)
            return (seen, block_keys, block_values)

        def forward_step(block_index, totals):
            seen, block_keys, block_values = key_block_parts(block_index)
            weights_exp = score_block(queries, block_keys, seen, score_scale)
            summed_part = jnp.einsum(
                "hqk,khd->qhd",
                weights_exp.astype(jnp.bfloat16),
                block_values,
                preferred_element_type=jnp.float32,
            )
            return (
                totals[0] + summed_part.reshape(row_count, local_width),
                totals[1] + jnp.transpose(jnp.sum(weights_exp, axis=2)),
            )

        initial = (
            jnp.zeros((row_count, local_width), jnp.float32),
            jnp.zeros((row_count, head_count), jnp.float32),
        )
        summed, row_total = lax.fori_loop(0, block_count, forward_step, initial)
        mixed = summed.reshape(row_count, head_count, HEAD) / row_total[:, :, None]
        mixed_low = mixed.reshape(row_count, local_width).astype(jnp.bfloat16)
        attn_out = lax.psum(matmul(mixed_low, out_weight), "tensor")
        residual = tokens_now + attn_out
        norm_two = lax.rsqrt(jnp.mean(residual * residual, axis=1, keepdims=True) + EPSILON)
        normed_two = (residual * norm_two * gain_two).astype(jnp.bfloat16)
        shared_g = matmul(normed_two, gate_weight)
        shared_u = matmul(normed_two, up_weight)
        shared_act, shared_slope = silu_parts(shared_g)
        shared_h = (shared_act * shared_u).astype(jnp.bfloat16)
        shared_y = matmul(shared_h, down_weight)
        logits = matmul(normed_two, router_weight)
        route_now = routes[micro_step]
        choose = (route_now[:, :, None] == labels[None, None, :]).astype(jnp.float32)
        gate_values = jax.nn.softmax(jnp.sum(choose * logits[:, None, :], axis=2), axis=1)
        flat_routes = route_now.reshape(2 * row_count)
        expert_hits = (flat_routes[:, None] == labels[None, :]).astype(jnp.int32)
        slot_rank = jnp.sum((jnp.cumsum(expert_hits, axis=0) - expert_hits) * expert_hits, axis=1)
        slot_index = flat_routes * capacity + slot_rank
        slot_match = slot_index[None, :] == slot_ids[:, None]
        filled = jnp.any(slot_match, axis=1)
        source = jnp.sum(jnp.where(slot_match, pair_ids[None, :], 0), axis=1)

        def to_owners(table, row_index):
            picked = jnp.take(table, row_index, axis=0)
            picked = jnp.where(filled[:, None], picked, jnp.zeros_like(picked))
            spread = jnp.broadcast_to(
                picked.reshape(expert_count, 1, capacity, model_width),
                (expert_count, owners, capacity, model_width),
            )
            return spread.reshape(devices, capacity, model_width)

        def from_owners(returned):
            merged = jnp.sum(
                returned.reshape(expert_count, owners, capacity, model_width), axis=1
            ).reshape(expert_count * capacity, model_width)
            return jnp.take(merged, slot_index, axis=0).reshape(row_count, 2, model_width)

        arrived = lax.all_to_all(
            to_owners(normed_two, source // 2), "expert", split_axis=0, concat_axis=0, tiled=True
        )
        slot_count = arrived.shape[1]
        flat_in = arrived.reshape(devices * slot_count, model_width)
        expert_g = matmul(flat_in, part_gate)
        expert_u = matmul(flat_in, part_up)
        expert_act, expert_unused = silu_parts(expert_g)
        expert_h = (expert_act * expert_u).astype(jnp.bfloat16)
        partial_out = matmul(expert_h, part_down).reshape(devices, slot_count, model_width)
        combined = lax.all_to_all(
            partial_out.astype(jnp.bfloat16), "expert", split_axis=0, concat_axis=0, tiled=True
        ).astype(partial_out.dtype)
        hidden_width = expert_g.shape[1]
        combined, arrived, kept_g, kept_u, kept_h = (
            combined,
            arrived,
            expert_g.reshape(devices, slot_count, hidden_width),
            expert_u.reshape(devices, slot_count, hidden_width),
            expert_h.reshape(devices, slot_count, hidden_width),
        )
        expert_y = from_owners(combined)
        cot_low = out_grad[micro_step]
        cotangent = cot_low.astype(jnp.float32)
        moe_part = jnp.sum(gate_values[:, :, None] * expert_y, axis=1)
        gate_dots = jnp.sum(cotangent[:, None, :] * expert_y, axis=2)
        ffn_out, grad_gate = (
            lax.psum((shared_y + moe_part).astype(jnp.bfloat16), "tensor").astype(jnp.float32),
            lax.psum(gate_dots.astype(jnp.bfloat16), "tensor").astype(jnp.float32),
        )
        layer_outputs.append((residual + ffn_out).astype(jnp.bfloat16))
        grad_shared_h = matmul(cot_low, down_weight.T)
        grad_shared_g = (grad_shared_h * shared_u * shared_slope).astype(jnp.bfloat16)
        grad_shared_u = (grad_shared_h * shared_act).astype(jnp.bfloat16)
        grad_chosen = gate_values * (
            grad_gate - jnp.sum(gate_values * grad_gate, axis=1, keepdims=True)
        )
        grad_logits = jnp.sum(choose * grad_chosen[:, :, None], axis=1).astype(jnp.bfloat16)
        grad_pairs_out = (
            (gate_values[:, :, None] * cotangent[:, None, :])
            .astype(jnp.bfloat16)
            .reshape(2 * row_count, model_width)
        )
        arrived_grad = lax.all_to_all(
            to_owners(grad_pairs_out, source), "expert", split_axis=0, concat_axis=0, tiled=True
        )
        slot_total = arrived_grad.shape[0] * arrived_grad.shape[1]
        flat_grad = arrived_grad.reshape(slot_total, model_width)
        flat_in = arrived.reshape(slot_total, model_width)
        hidden_width = kept_g.shape[2]
        expert_g = kept_g.reshape(slot_total, hidden_width)
        expert_u = kept_u.reshape(slot_total, hidden_width)
        expert_h = kept_h.reshape(slot_total, hidden_width)
        expert_act, expert_slope = silu_parts(expert_g)
        grad_hidden = matmul(flat_grad, part_down.T)
        grad_expert_g = (grad_hidden * expert_u * expert_slope).astype(jnp.bfloat16)
        grad_expert_u = (grad_hidden * expert_act).astype(jnp.bfloat16)
        grad_in = matmul(grad_expert_g, part_gate.T) + matmul(grad_expert_u, part_up.T)
        returned = lax.all_to_all(
            grad_in.reshape(arrived_grad.shape[0], arrived_grad.shape[1], model_width),
            "expert",
            split_axis=0,
            concat_axis=0,
            tiled=True,
        )
        normed_part = (
            matmul(grad_shared_g, gate_weight.T)
            + matmul(grad_shared_u, up_weight.T)
            + jnp.sum(from_owners(returned), axis=1)
        )
        grad_normed_two = lax.psum(normed_part, "tensor") + matmul(grad_logits, router_weight.T)
        grad_norm_part, grad_gain_two = rms_back(grad_normed_two, residual, norm_two, gain_two)
        grad_residual = cotangent + grad_norm_part
        grad_attn = grad_residual.astype(jnp.bfloat16)
        grad_mixed = matmul(grad_attn, out_weight.T).reshape(row_count, head_count, HEAD)
        grad_summed = (grad_mixed / row_total[:, :, None]).astype(jnp.bfloat16)
        delta_rows = jnp.sum(grad_mixed * mixed, axis=2) / row_total

        def block_terms(block_index):
            seen, block_keys, block_values = key_block_parts(block_index)
            weights_exp = score_block(queries, block_keys, seen, score_scale)
            grad_scores = score_grads(weights_exp, grad_summed, block_values, delta_rows)
            return (weights_exp, grad_scores, block_keys)

        zero_query = jnp.zeros((row_count, head_count, HEAD), jnp.float32)

        def key_step(gradient_query_weight, block_index):
            weights_exp, grad_scores, block_keys = block_terms(block_index)
            gradient_query_weight = (
                gradient_query_weight
                + jnp.einsum(
                    "hqk,khd->qhd", grad_scores, block_keys, preferred_element_type=jnp.float32
                )
                * score_scale
            )
            grad_keys = (
                jnp.einsum("hqk,qhd->khd", grad_scores, queries, preferred_element_type=jnp.float32)
                * score_scale
            )
            grad_values = jnp.einsum(
                "hqk,qhd->khd",
                weights_exp.astype(jnp.bfloat16),
                grad_summed,
                preferred_element_type=jnp.float32,
            )
            return (
                gradient_query_weight,
                jnp.concatenate(
                    [
                        grad_keys.reshape(block_size, local_width),
                        grad_values.reshape(block_size, local_width),
                    ],
                    axis=1,
                ),
            )

        gradient_query_weight, key_terms = lax.scan(
            key_step, zero_query, jnp.arange(block_count, dtype=jnp.int32)
        )
        grad_pairs = lax.psum_scatter(
            key_terms.reshape(tree_rows, 2 * local_width), "expert", scatter_dimension=0, tiled=True
        )
        grad_keys_rot = grad_pairs[:, :local_width].reshape(row_count, head_count, HEAD)
        grad_query_pre = (
            rotate_back(gradient_query_weight, position)
            .reshape(row_count, local_width)
            .astype(jnp.bfloat16)
        )
        grad_key_pre = (
            rotate_back(grad_keys_rot, position)
            .reshape(row_count, local_width)
            .astype(jnp.bfloat16)
        )
        grad_value_low = grad_pairs[:, local_width:].astype(jnp.bfloat16)
        normed_grad = (
            matmul(grad_query_pre, query_weight.T)
            + matmul(grad_key_pre, key_weight.T)
            + matmul(grad_value_low, value_weight.T)
        )
        grad_normed_one = lax.psum(normed_grad.astype(jnp.bfloat16), "tensor").astype(jnp.float32)
        grad_norm_first, grad_gain_one = rms_back(grad_normed_one, tokens_now, norm_one, gain_one)
        token_gradients.append(grad_residual + grad_norm_first)
        dense_step = (
            grad_gain_one,
            grad_gain_two,
            matmul(normed_one.T, grad_query_pre),
            matmul(normed_one.T, grad_key_pre),
            matmul(normed_one.T, grad_value_low),
            matmul(mixed_low.T, grad_attn),
            matmul(normed_two.T, grad_logits),
            matmul(normed_two.T, grad_shared_g),
            matmul(normed_two.T, grad_shared_u),
            matmul(shared_h.T, cot_low),
        )
        expert_step = (
            matmul(flat_in.T, grad_expert_g),
            matmul(flat_in.T, grad_expert_u),
            matmul(expert_h.T, flat_grad),
        )
        if dense_sums is None:
            dense_sums = dense_step
            expert_sums = expert_step
        else:
            dense_sums = tuple(
                (earlier + latest for earlier, latest in zip(dense_sums, dense_step))
            )
            expert_sums = tuple(
                (earlier + latest for earlier, latest in zip(expert_sums, expert_step))
            )
    final_gate, final_up, final_down = expert_sums
    reduced = (
        lax.psum_scatter(dense_sums[0], "expert", scatter_dimension=0, tiled=True),
        lax.psum_scatter(dense_sums[1], "expert", scatter_dimension=0, tiled=True),
        lax.psum_scatter(dense_sums[2], "expert", scatter_dimension=0, tiled=True),
        lax.psum_scatter(dense_sums[3], "expert", scatter_dimension=0, tiled=True),
        lax.psum_scatter(dense_sums[4], "expert", scatter_dimension=0, tiled=True),
        lax.psum_scatter(dense_sums[5], "expert", scatter_dimension=1, tiled=True),
        lax.psum_scatter(dense_sums[6], "expert", scatter_dimension=0, tiled=True),
        lax.psum_scatter(dense_sums[7], "expert", scatter_dimension=0, tiled=True),
        lax.psum_scatter(dense_sums[8], "expert", scatter_dimension=0, tiled=True),
        lax.psum_scatter(dense_sums[9], "expert", scatter_dimension=1, tiled=True),
    )
    return (
        jnp.stack(layer_outputs),
        jnp.stack(token_gradients),
        reduced[0],
        reduced[1],
        reduced[2],
        reduced[3],
        reduced[4],
        reduced[5],
        reduced[6],
        reduced[7],
        reduced[8],
        reduced[9],
        final_gate[None],
        final_up[None],
        final_down[None],
    )


MESH = pl.DeviceIdType.MESH
BF = jnp.bfloat16
F32 = jnp.float32
EXACT = lax.Precision.HIGHEST
VMEM_LIMIT = 63 * 2**20


def product(left, right, dims, precision=None):
    return lax.dot_general(
        left, right, (dims, ((), ())), preferred_element_type=F32, precision=precision
    )


def dot(left, right, precision=None):
    return product(left, right, ((1,), (0,)), precision)


def dot_nt(left, right, precision=None):
    return product(left, right, ((1,), (1,)), precision)


def dot_tn(left, right, precision=None):
    return product(left, right, ((0,), (0,)), precision)


def iota(shape, dim):
    return lax.broadcasted_iota(jnp.int32, shape, dim)


class Net:
    def __init__(self, expert_size, send_sems, recv_sems):
        self.e = lax.axis_index("expert")
        self.t = lax.axis_index("tensor")
        self.n = expert_size
        self.nz = expert_size // 2
        self.z = self.e // 2
        self.x = self.e % 2
        self.y = self.t // 2
        self.core = self.t % 2
        self.send_sems = send_sems
        self.recv_sems = recv_sems
        self.sends = 0
        self.free = []
        self.recvs = 0
        self.open = []

    def recv_slots(self, count):
        first = self.recvs
        self.recvs += count
        return first

    def ids(self, to):
        return {"expert": to[0], "tensor": to[1]}

    def send_slot(self):
        if not self.free:
            self.free.append(self.sends)
            self.sends += 1
        return self.free.pop(0)

    def push(self, src, dst, to, slot, when=None, bulk=False, shared=None):
        send = self.send_slot() if shared is None else shared
        copy = pltpu.make_async_remote_copy(
            src_ref=src,
            dst_ref=dst,
            send_sem=self.send_sems.at[send],
            recv_sem=self.recv_sems.at[slot],
            device_id=self.ids(to),
            device_id_type=MESH,
        )
        if when is None:
            copy.start()
        else:
            pl.when(when)(copy.start)
        if shared is None:
            self.open.append((copy, when, send, bulk))

    def all_sent(self, part, send):
        copy = pltpu.make_async_remote_copy(
            src_ref=part,
            dst_ref=part,
            send_sem=self.send_sems.at[send],
            recv_sem=self.recv_sems.at[0],
            device_id=self.ids(self.other_core()),
            device_id_type=MESH,
        )
        self.open.append((copy, None, send, False))

    def landed(self, dst, slot, when=None):
        copy = pltpu.make_async_remote_copy(
            src_ref=dst,
            dst_ref=dst,
            send_sem=self.send_sems.at[0],
            recv_sem=self.recv_sems.at[slot],
            device_id=self.ids(self.other_core()),
            device_id_type=MESH,
        )
        if when is None:
            copy.wait_recv()
        else:
            pl.when(when)(copy.wait_recv)

    def drain(self, bulk=True):
        for copy, when, send, is_bulk in self.open:
            if bulk or not is_bulk:
                if when is None:
                    copy.wait_send()
                else:
                    pl.when(when)(copy.wait_send)
                self.free.append(send)
        self.open = [one for one in self.open if one[3] and not bulk]

    def other_core(self):
        return (self.e, self.t + 1 - 2 * self.core)

    def across_y(self):
        return (self.e, (self.t + 2) % 4)

    def across_x(self):
        return (self.e + 1 - 2 * self.x, self.t)

    def peer(self, step):
        return (self.e + step) % self.n

    def greet(self):
        barrier = pltpu.get_barrier_semaphore()
        partners = [(self.peer(d), self.t) for d in range(1, self.n)]
        partners += [self.other_core(), self.across_y()]
        for to in partners:
            pl.semaphore_signal(barrier, inc=1, device_id=self.ids(to), device_id_type=MESH)
        return lambda: pl.semaphore_wait(barrier, len(partners))


class Gather:
    def __init__(self, net, block, chunks=1, on_land=None):
        self.net, self.block, self.chunks, self.on_land = net, block, chunks, on_land
        self.slot = net.recv_slots(net.n * chunks)

    def start(self):
        net = self.net
        for k in range(self.chunks):
            own, slot = self.block(net.e, k), self.slot + net.e * self.chunks + k
            for way in (1, -1):
                there = net.z + way
                fits_in = (there >= 0) & (there < net.nz)
                net.push(own, own, (there % net.nz * 2 + net.x, net.t), slot, fits_in)
            net.push(own, own, net.across_x(), slot)

    def step(self, distance):
        net = self.net
        for k in range(self.chunks):
            for way in (1, -1):
                source, there = net.z - way * distance, net.z + way
                real = (source >= 0) & (source < net.nz)
                onward = real & (there >= 0) & (there < net.nz)
                b = source % net.nz * 2 + net.x
                part, slot = self.block(b, k), self.slot + b * self.chunks + k
                net.landed(part, slot, real)
                net.push(part, part, (there % net.nz * 2 + net.x, net.t), slot, onward)
                net.push(part, part, net.across_x(), slot, real)
                if self.on_land is not None:
                    self.on_land(b, real)

    def land(self, b):
        net = self.net
        for k in range(self.chunks):
            net.landed(self.block(b, k), self.slot + b * self.chunks + k)
        if self.on_land is not None:
            self.on_land(b, None)

    def finish(self):
        for d in range(self.net.nz):
            self.land((self.net.z + d) % self.net.nz * 2 + 1 - self.net.x)


class Scatter:
    def __init__(self, net, block, from_x, from_z):
        self.net, self.block = net, block
        self.from_x, self.from_z = from_x, from_z
        self.slot_x = net.recv_slots(net.nz)
        self.slot_z = net.recv_slots(net.nz)

    def start(self):
        net = self.net
        for d in range(1, net.nz + 1):
            zz = (net.z + d) % net.nz
            net.push(
                self.block(zz * 2 + 1 - net.x),
                self.from_x.at[zz],
                net.across_x(),
                self.slot_x + zz,
                bulk=True,
            )

    def forward(self):
        net = self.net
        for d in range(1, net.nz):
            zz = (net.z + d) % net.nz
            net.landed(self.from_x.at[zz], self.slot_x + zz)
            pair = self.block(zz * 2 + net.x)[...].astype(F32) + self.from_x[zz].astype(F32)
            self.from_x[zz] = pair.astype(BF)
            net.push(
                self.from_x.at[zz],
                self.from_z.at[net.z],
                (zz * 2 + net.x, net.t),
                self.slot_z + net.z,
            )

    def finish(self):
        net = self.net
        net.landed(self.from_x.at[net.z], self.slot_x + net.z)
        total = self.block(net.e)[...].astype(F32) + self.from_x[net.z].astype(F32)
        for d in range(1, net.nz):
            zz = (net.z + d) % net.nz
            net.landed(self.from_z.at[zz], self.slot_z + zz)
            total = total + self.from_z[zz].astype(F32)
        return total


class Chain:
    def __init__(self, net, block, from_x, from_z):
        self.net, self.block = net, block
        self.from_x, self.from_z = from_x, from_z
        self.slot_x = net.recv_slots(net.nz)
        self.slot_z = net.recv_slots(net.nz + 1)

    def start(self):
        net = self.net
        high = net.z // 2
        for zz in (3 - 3 * high, 2 - high, 1 - net.z + 4 * high, net.z):
            net.push(
                self.block(zz * 2 + 1 - net.x),
                self.from_x.at[zz],
                net.across_x(),
                self.slot_x + zz,
                bulk=True,
            )

    def place(self, way, zz, holder):
        return zz if way == 1 else zz + (zz == holder).astype(jnp.int32) * (self.net.nz - zz)

    def step(self, distance):
        net = self.net
        for way in (1, -1):
            target, before = net.z + way * distance, net.z - way
            real = (target >= 0) & (target < net.nz)
            fed = real & (before >= 0) & (before < net.nz)
            zz = target % net.nz
            there = (net.z + way) % net.nz
            here = self.place(way, zz, net.z)
            onward = self.place(way, zz, there)

            @pl.when(real)
            def _():
                net.landed(self.from_x.at[zz], self.slot_x + zz)

            @pl.when(fed)
            def _():
                net.landed(self.from_z.at[here], self.slot_z + here)
                both = self.from_x[zz].astype(F32) + self.from_z[here].astype(F32)
                self.from_x[zz] = (both + self.block(zz * 2 + net.x)[...].astype(F32)).astype(BF)

            @pl.when(real & ~fed)
            def _():
                own = self.block(zz * 2 + net.x)[...].astype(F32)
                self.from_x[zz] = (self.from_x[zz].astype(F32) + own).astype(BF)

            net.push(
                self.from_x.at[zz],
                self.from_z.at[onward],
                (there * 2 + net.x, net.t),
                self.slot_z + onward,
                when=real,
                bulk=True,
            )

    def finish(self, target):
        net = self.net
        net.landed(self.from_x.at[net.z], self.slot_x + net.z)
        target[...] = self.block(net.e)[...].astype(F32) + self.from_x[net.z].astype(F32)
        for way in (1, -1):
            before = net.z - way
            here = self.place(way, net.z, net.z)

            @pl.when((before >= 0) & (before < net.nz))
            def _():
                net.landed(self.from_z.at[here], self.slot_z + here)
                target[...] += self.from_z[here].astype(F32)


class Exchange:
    def __init__(self, net, outgoing, incoming, rest=None):
        self.net, self.outgoing, self.incoming, self.rest = net, outgoing, incoming, rest
        self.slot = net.recv_slots(net.n if rest is None else 1)

    def start(self):
        net = self.net
        send = None if self.rest is None else net.send_slot()
        for d in range(1, net.n):
            to = net.peer(d)
            slot = self.slot + net.e if self.rest is None else self.slot
            net.push(self.outgoing(to), self.incoming(net.e), (to, net.t), slot, shared=send)
        if self.rest is not None:
            net.all_sent(self.rest, send)

    def arrive(self, d):
        source = self.net.peer(d)
        self.net.landed(self.incoming(source), self.slot + source)
        return source

    def finish(self):
        self.net.landed(self.rest, self.slot)


class Dispatch:
    def __init__(self, net, outgoing, incoming):
        self.net, self.outgoing, self.incoming = net, outgoing, incoming
        self.send = Exchange(
            net, lambda b: outgoing.at[b], lambda b: incoming.at[b, net.core, net.y]
        )
        self.slot_y = net.recv_slots(net.n)
        self.slot_core = net.recv_slots(1)

    def start(self):
        net = self.net
        self.send.start()
        self.incoming[net.e, net.core, net.y] = self.outgoing[net.e]

    def relay_y(self):
        net = self.net
        for d in range(net.n):
            b = net.e if d == 0 else self.send.arrive(d)
            part = self.incoming.at[b, net.core, net.y]
            net.push(part, part, net.across_y(), self.slot_y + b)

    def relay_core(self):
        net = self.net
        for d in range(net.n):
            b = net.peer(d)
            net.landed(self.incoming.at[b, net.core, 1 - net.y], self.slot_y + b)
        part = self.incoming.at[:, net.core]
        net.push(part, part, net.other_core(), self.slot_core)

    def finish(self):
        self.net.landed(self.incoming.at[:, 1 - self.net.core], self.slot_core)


class Swap:
    def __init__(self, net, out_buf, in_buf, partner):
        self.net, self.out_buf, self.in_buf, self.partner = net, out_buf, in_buf, partner
        self.slot = net.recv_slots(1)

    def start(self, value):
        self.out_buf[...] = value.astype(self.out_buf.dtype)
        self.send()

    def send(self):
        self.net.push(self.out_buf, self.in_buf, self.partner, self.slot)

    def other(self):
        self.net.landed(self.in_buf, self.slot)
        return self.in_buf[...].astype(F32)

    def both(self):
        return self.out_buf[...].astype(F32) + self.other()


class Share:
    def __init__(self, net, halves):
        self.net, self.halves = net, halves
        self.slot = net.recv_slots(1)

    def start(self, value):
        net = self.net
        self.halves[net.core] = value.astype(self.halves.dtype)
        part = self.halves.at[net.core]
        net.push(part, part, net.other_core(), self.slot)

    def finish(self):
        net = self.net
        net.landed(self.halves.at[1 - net.core], self.slot)
        return jnp.concatenate([self.halves[0], self.halves[1]], axis=1)


def silu_both(value):
    gate = jax.nn.sigmoid(value)
    return value * gate, gate * (1.0 + value * (1.0 - gate))


def norm_scale(value):
    return lax.rsqrt(jnp.mean(value * value, axis=1, keepdims=True) + EPSILON)


def norm_back(grad_normed, source, scale, gain):
    weighted = grad_normed * gain
    inner = jnp.mean(weighted * source, axis=1, keepdims=True)
    return scale * weighted - scale * scale * scale * source * inner


PLACES = ["tok", "cot", "routes", "lengths", "parents", "gain_a", "gain_b", "wq", "wk", "wv"]
PLACES += ["wo", "router", "sg", "su", "sd", "eg", "eu", "ed"]
RESULTS = ["out", "gtok", "dga", "dgb", "dwq", "dwk", "dwv", "dwo", "drouter"]
RESULTS += ["dsg", "dsu", "dsd", "deg", "deu", "ded"]


def scratch_shapes(s):
    n, local, half = s.n, s.local, s.half
    depth, hidden, shared, cap = s.depth, s.hidden, s.shared, s.cap
    micro, nz = s.micro, s.n // 2
    model, wide, stack, tree = 2 * half, 2 * s.width, s.heads * local, n * local
    part = cap // 4
    vm = pltpu.VMEM
    return dict(
        w_kv=vm((n, depth, wide), BF),
        w_qo=vm((n, depth, wide), BF),
        w_sh=vm((3, n, depth, shared), BF),
        ext_in=vm((n, 16, 128), BF),
        tok_all=vm((n, 2, 2, micro * local // 4, model), BF),
        cos_all=vm((n, micro * local, 128), F32),
        sin_all=vm((n, micro * local, 128), F32),
        kv=vm((micro, n, local, wide), BF),
        q_rows=vm((micro, stack, wide), BF),
        expo=vm((micro, stack, tree), F32),
        total=vm((micro, stack, 1), F32),
        mixed=vm((micro, local, wide), F32),
        mixed_low=vm((micro * local, wide), BF),
        choice_half=vm((micro, local, n * cap // 2), BF),
        choice_wide=vm((micro, local, n * 128), BF),
        res=vm((micro, local, model), F32),
        n_one=vm((micro * local, model), BF),
        n_two=vm((micro * local, model), BF),
        c_out=vm((micro, n, part, model), BF),
        c_in=vm((micro, n, 2, 2, part, model), BF),
        x_out=vm((micro, n, part, model), BF),
        x_in=vm((micro, n, 2, 2, part, model), BF),
        h_out=vm((micro, n, 16, 128), BF),
        h_in=vm((micro, n, 16, 128), BF),
        gate_col=vm((micro, n * cap, 1), F32),
        e_h=vm((micro, n * cap, hidden), BF),
        e_dg=vm((micro, n * cap, hidden), BF),
        e_du=vm((micro, n * cap, hidden), BF),
        y_core=vm((micro, n, cap, half), BF),
        g_core=vm((micro, n, cap, half), BF),
        y_in=vm((micro, n, cap // 2, half), BF),
        y_far=vm((micro, n, cap // 2, half), BF),
        g_in=vm((micro, n, cap // 2, half), BF),
        g_far=vm((micro, n, cap // 2, half), BF),
        d_out=vm((micro, n, 8, 128), F32),
        d_in=vm((micro, n, 8, 128), F32),
        d_tensor=vm((micro, 4, 8, 128), F32),
        core_a=vm((micro, 2, local, half), F32),
        core_b=vm((4, micro * local, half), BF),
        core_c=vm((micro, 2, local, half), F32),
        s_grads=vm((3, micro * local, shared), BF),
        s_own=vm((2, micro * local, half), F32),
        y_swap=vm((4, micro, 2, local, half), BF),
        share_a=vm((micro, 2, local, half), F32),
        share_b=vm((micro, 2, local, half), F32),
        share_c=vm((micro, 2, local, half), F32),
        share_out=vm((micro, 2, local, half), BF),
        kv_part=vm((micro, n, local, wide), BF),
        kv_fx=vm((micro, 2, nz, local // 2, wide), BF),
        kv_fz=vm((micro, 2, nz, local // 2, wide), BF),
        sh_part=vm((3, n, depth, shared), BF),
        sh_fx=vm((3, nz, depth, shared), BF),
        sh_fz=vm((3, nz + 1, depth, shared), BF),
        w_part=vm((2, n, depth, wide), BF),
        w_fx=vm((2, nz, depth, wide), BF),
        w_fz=vm((2, nz, depth, wide), BF),
        gains_out=vm((n, 16, 128), F32),
        gains_in=vm((n, 16, 128), F32),
        stage=vm((2, half, hidden), F32),
        stage_d=vm((hidden, half), F32),
        save_sems=pltpu.SemaphoreType.DMA((6,)),
        send_sems=pltpu.SemaphoreType.DMA((SENDS,)),
        recv_sems=pltpu.SemaphoreType.DMA((RECVS,)),
    )


SENDS = 182
RECVS = 251


def layer_kernel(s, names, *refs):
    r = types.SimpleNamespace(**dict(zip(names, refs)))
    n, local, width, half = s.n, s.local, s.width, s.half
    depth, hidden, shared, cap = s.depth, s.hidden, s.shared, s.cap
    micro, heads = s.micro, s.heads
    rows, model, tree, wide, stack = micro * local, 2 * half, n * local, 2 * width, heads * local
    part = cap // 4
    net = Net(n, r.send_sems, r.recv_sems)
    me, core, y = net.e, net.core, net.y
    ready = net.greet()
    micros = range(micro)
    my_half = pl.ds(pl.multiple_of(core * half, 128), half)
    other_half = pl.ds(pl.multiple_of((1 - core) * half, 128), half)

    def rows_of(m):
        return slice(m * local, (m + 1) * local)

    left = (iota((width, wide), 1) == iota((width, wide), 0)).astype(BF)
    right = (iota((width, wide), 1) == iota((width, wide), 0) + width).astype(BF)
    r.w_kv[me] = (dot(r.wk[...], left) + dot(r.wv[...], right)).astype(BF)
    r.tok_all[me] = r.tok[...].reshape(2, 2, rows // 4, model)
    r.w_qo[me] = (dot(r.wq[...], left) + dot_tn(r.wo[...], right)).astype(BF)
    ext = [r.gain_a[...].astype(F32), r.gain_b[...].astype(F32), jnp.zeros((6, depth), F32)]
    ext = jnp.concatenate(ext + [r.router[...].astype(F32)], axis=0).astype(BF)
    pad = (iota((depth, 128), 1) == iota((depth, 128), 0)).astype(BF)
    r.ext_in[me] = dot(ext, pad).astype(BF)
    for i, name in enumerate(("sg", "su", "sd")):
        r.w_sh[i, me] = getattr(r, name)[...]

    slot_ty, slot_tc = net.recv_slots(n), net.recv_slots(n)

    def token_on(b, when):
        quarter = r.tok_all.at[b, core, y]
        net.push(quarter, quarter, net.across_y(), slot_ty + b, when)

    get_kv = Gather(net, lambda b, k: r.w_kv.at[b])
    get_qo = Gather(net, lambda b, k: r.w_qo.at[b])
    get_tok = Gather(net, lambda b, k: r.tok_all.at[b, core, y], on_land=token_on)
    get_sh = [Gather(net, lambda b, k, i=i: r.w_sh.at[i, b]) for i in range(3)]
    get_ext = Exchange(net, lambda b: r.ext_in.at[me], lambda b: r.ext_in.at[b], r.ext_in.at[0 : n - 1])
    ready()
    get_ext.start()
    get_kv.start()
    get_tok.start()
    get_qo.start()

    eye = (iota((128, 128), 0) == iota((128, 128), 1)).astype(BF)
    routes = dot_nt(eye, r.routes[...].astype(BF))
    lane = iota((local, 16), 1) - 8
    earlier = (iota((local, local), 1) < iota((local, local), 0)).astype(BF)

    def spread(span):
        of_lane = iota((16, n * span), 1) // span
        return (iota((16, n * span), 0) - 8 == of_lane).astype(BF)

    hot_one, hot_two, quarter = [], [], []
    send_c = [Dispatch(net, r.c_out.at[m], r.c_in.at[m]) for m in micros]
    send_h = [
        Exchange(
            net,
            lambda b, m=m: r.h_out.at[m, b],
            lambda b, m=m: r.h_in.at[m, b],
            r.h_in.at[m, 0 : n - 1],
        )
        for m in micros
    ]
    for m in micros:
        one = lane == routes[:, 2 * m : 2 * m + 1].astype(jnp.int32)
        two = lane == routes[:, 2 * m + 1 : 2 * m + 2].astype(jnp.int32)
        hot_one.append(one)
        hot_two.append(two)
        hits = (one | two).astype(F32)
        rank = jnp.where(hits > 0.5, dot(earlier, hits.astype(BF)), -1.0).astype(BF)

        def taken(span, first=0):
            wanted = iota((local, n * span), 1) % span + first
            return (dot(rank, spread(span)) == wanted.astype(F32)).astype(BF)

        r.choice_half[m] = taken(cap // 2, y * (cap // 2))
        r.choice_wide[m] = taken(128)
        quarter.append(taken(part, (core * 2 + y) * part))
        hit_rows = dot_tn(hits.astype(BF), r.choice_wide[m]).astype(BF)
        for b in range(n):
            r.h_out[m, b] = hit_rows[:, b * 128 : (b + 1) * 128]
        r.h_in[m, me] = r.h_out[m, me]
        picked = dot_tn(quarter[m], r.cot[rows_of(m)]).astype(BF)
        r.c_out[m] = picked.reshape(n, part, model)

    def segments(m):
        starts, ends, paths, shifts, begin = [], [], [], [], 0
        for seg in range(s.segs):
            size = r.lengths[m, seg]
            starts.append(begin)
            ends.append(begin + size)
            begin = begin + size
            if seg == 0:
                paths.append(jnp.int32(1))
                shifts.append(jnp.int32(0))
            else:
                parent = r.parents[m, seg]
                path, shift = jnp.int32(0), jnp.int32(0)
                for other in range(seg):
                    is_parent = parent == other
                    path = jnp.where(is_parent, paths[other], path)
                    shift = jnp.where(
                        is_parent, shifts[other] + ends[other] - starts[other], shift
                    )
                paths.append(path + (1 << seg))
                shifts.append(shift)
        return starts, ends, paths, shifts

    tables = [segments(m) for m in micros]

    def row_values(m, ids):
        starts, ends, paths, shifts = tables[m]
        path, place, own = jnp.zeros_like(ids), jnp.zeros_like(ids), jnp.zeros_like(ids)
        for seg in range(s.segs):
            inside = (ids >= starts[seg]) & (ids < ends[seg])
            path = jnp.where(inside, paths[seg], path)
            place = jnp.where(inside, ids - starts[seg] + shifts[seg], place)
            own = jnp.where(inside, 1 << seg, own)
        return path, place, own

    turn = (iota((1, 128), 1) % (HEAD // 2)).astype(F32)
    frequency = jnp.exp(turn * (-math.log(ROPE_BASE) / (HEAD // 2)))

    def angle_step(b, carry):
        ids = b * local + iota((local, 1), 0)
        place = jnp.concatenate([row_values(m, ids)[1] for m in micros], axis=0)
        angle = place.astype(F32) * frequency
        r.cos_all[b] = jnp.cos(angle)
        r.sin_all[b] = jnp.sin(angle)
        return carry

    lax.fori_loop(0, n, angle_step, 0)
    is_left = iota((1, wide), 1) < width
    swap_r, swap_c = iota((wide, wide), 0), iota((wide, wide), 1)
    lower = swap_c % HEAD < HEAD // 2
    swap = jnp.where(lower & (swap_r == swap_c + HEAD // 2), -1.0, 0.0)
    swap = jnp.where(~lower & (swap_r == swap_c - HEAD // 2), 1.0, swap)
    swap = jnp.where(is_left, swap, 0.0)
    swap_low = swap.astype(BF)

    def turns(b):
        cosine = jnp.concatenate([r.cos_all[b]] * (wide // 128), axis=1)
        sine = jnp.concatenate([r.sin_all[b]] * (wide // 128), axis=1)
        return jnp.where(is_left, cosine, 1.0), sine

    for distance in range(1, net.nz):
        get_kv.step(distance)
        get_tok.step(distance)
        get_qo.step(distance)
    get_ext.finish()
    high = net.z // 2
    near = [net.z + 1 - 2 * (net.z % 2), 2 - high, 3 - 3 * high]
    column = [zz * 2 + net.x for zz in near]
    across = [zz * 2 + 1 - net.x for zz in [net.z] + near]

    def token_core(b):
        net.landed(r.tok_all.at[b, core, 1 - y], slot_ty + b)
        both = r.tok_all.at[b, core]
        net.push(both, both, net.other_core(), slot_tc + b)

    for b in column:
        token_core(b)

    def lay(b):
        place = iota((128, model), 0)
        return (place < depth) & (place + b * depth == iota((128, model), 1))

    ext_all = jnp.zeros((16, model), F32)
    for b in range(n):
        ext_all = ext_all + dot(r.ext_in[b], lay(b).astype(BF))
    gain_one, gain_two = ext_all[0:1], ext_all[1:2]
    ext_low = ext_all.astype(BF)
    get_kv.finish()
    w_kv = r.w_kv[...].reshape(model, wide)
    w_kv_swapped = dot(w_kv, swap_low).astype(BF)

    def normed(block):
        value = block.astype(F32)
        return (value * norm_scale(value) * gain_one).astype(BF)

    def key_value(b):
        block = normed(r.tok_all[b].reshape(rows, model))
        cosine, sine = turns(b)
        both = (dot(block, w_kv) * cosine + dot(block, w_kv_swapped) * sine).astype(BF)
        for m in micros:
            r.kv[m, b] = both[rows_of(m)]

    for g in get_sh:
        g.start()
    key_value(me)

    def key_value_of(b):
        net.landed(r.tok_all.at[b, 1 - core], slot_tc + b)
        key_value(b)

    for b in across[:2]:
        get_tok.land(b)
    for b in column:
        key_value_of(b)
    for b in across[2:]:
        get_tok.land(b)
    for b in across[:2]:
        token_core(b)
    for b in across[:2]:
        key_value_of(b)
    for b in across[2:]:
        token_core(b)
    get_qo.finish()
    for g in get_sh:
        g.step(1)
    for b in across[2:]:
        key_value_of(b)
    r.n_one[...] = normed(r.tok[...])
    w_qo = r.w_qo[...].reshape(model, wide)
    cosine, sine = turns(me)
    cosine = jnp.where(is_left, cosine, 0.0)
    queries = dot(r.n_one[...], w_qo) * cosine
    queries = queries + dot(r.n_one[...], dot(w_qo, swap_low).astype(BF)) * sine
    queries = queries.astype(BF)
    for m in micros:
        send_c[m].start()
        send_h[m].start()

    head_of = iota((1, wide), 1) // HEAD
    q_masks = [head_of == h for h in range(heads)]
    v_masks = [head_of == heads + h for h in range(heads)]

    def by_head(block, masks):
        return jnp.concatenate(
            [jnp.where(mask, block, jnp.zeros_like(block)) for mask in masks], axis=0
        )

    def join_heads(value, masks):
        total = jnp.zeros((local, wide), F32)
        for h, mask in enumerate(masks):
            total = total + jnp.where(mask, value[h * local : (h + 1) * local], 0.0)
        return total

    def o_half(h):
        return r.w_qo[pl.ds(h * (n // 2), n // 2)].reshape(half, wide)

    core_a = [Swap(net, r.core_a.at[m, 0], r.core_a.at[m, 1], net.other_core()) for m in micros]
    core_c = [Swap(net, r.core_c.at[m, 0], r.core_c.at[m, 1], net.other_core()) for m in micros]
    core_b = [
        Swap(net, r.core_b.at[2 * i], r.core_b.at[2 * i + 1], net.other_core()) for i in range(2)
    ]
    y_swap = [
        [Swap(net, r.y_swap.at[i, m, 0], r.y_swap.at[i, m, 1], net.across_y()) for m in micros]
        for i in range(4)
    ]
    share_a = [Share(net, r.share_a.at[m]) for m in micros]
    share_b = [Share(net, r.share_b.at[m]) for m in micros]
    share_c = [Share(net, r.share_c.at[m]) for m in micros]
    share_out = [Share(net, r.share_out.at[m]) for m in micros]

    score_scale = HEAD**-0.5
    for m in micros:
        r.q_rows[m] = by_head(queries[rows_of(m)], q_masks)
        kv_rows = r.kv[m].reshape(tree, wide)
        ids = me * local + iota((stack, 1), 0) % local
        path, unused, unused_two = row_values(m, ids)
        key_ids = iota((1, tree), 1)
        unused, unused_two, key_seg = row_values(m, key_ids)
        seen = ((path & key_seg) != 0) & (key_ids <= ids)
        scores = dot_nt(r.q_rows[m], kv_rows) * score_scale
        expo = jnp.where(seen, jnp.exp(scores), 0.0)
        r.expo[m] = expo
        total = jnp.sum(expo, axis=1, keepdims=True)
        r.total[m] = total
        mixed = join_heads(dot(expo.astype(BF), kv_rows) / total, v_masks)
        r.mixed[m] = mixed
        r.mixed_low[rows_of(m)] = mixed.astype(BF)
        core_a[m].start(dot_nt(r.mixed_low[rows_of(m)], o_half(1 - core)))
    for g in get_sh:
        g.step(2)
    for m in micros:
        mine = dot_nt(r.mixed_low[rows_of(m)], o_half(core))
        y_swap[0][m].start(mine + core_a[m].other())
    for m in micros:
        share_a[m].start(y_swap[0][m].both())

    send_x = [Dispatch(net, r.x_out.at[m], r.x_in.at[m]) for m in micros]
    scale_two = []
    for m in micros:
        res = r.tok[rows_of(m)].astype(F32) + share_a[m].finish()
        r.res[m] = res
        scale_two.append(norm_scale(res))
        normed_two = (res * scale_two[m] * gain_two).astype(BF)
        r.n_two[rows_of(m)] = normed_two
        r.x_out[m] = dot_tn(quarter[m], normed_two).astype(BF).reshape(n, part, model)
        send_x[m].start()

    for g in get_sh:
        g.step(3)
    for m in micros:
        send_c[m].relay_y()
    gates = []
    for m in micros:
        logits = dot_nt(r.n_two[rows_of(m)], ext_low)
        z_one = jnp.sum(jnp.where(hot_one[m], logits, 0.0), axis=1, keepdims=True)
        z_two = jnp.sum(jnp.where(hot_two[m], logits, 0.0), axis=1, keepdims=True)
        z_top = jnp.maximum(z_one, z_two)
        e_one, e_two = jnp.exp(z_one - z_top), jnp.exp(z_two - z_top)
        chosen = jnp.where(hot_one[m], e_one, jnp.where(hot_two[m], e_two, 0.0))
        gates.append(chosen / (e_one + e_two))

    for m in micros:
        send_x[m].relay_y()
    for g in get_sh:
        g.finish()

    def wide_half(i, h):
        return r.w_sh[i, pl.ds(h * (n // 2), n // 2)].reshape(half, shared)

    def shared_step(m, carry):
        here = pl.ds(pl.multiple_of(m * local, local), local)
        normed_two = r.n_two[here]
        shared_g = dot(normed_two, r.w_sh[0].reshape(model, shared))
        shared_u = dot(normed_two, r.w_sh[1].reshape(model, shared))
        act, slope = silu_both(shared_g)
        shared_h = (act * shared_u).astype(BF)
        grad_h = dot(r.cot[here], r.w_sh[2].reshape(model, shared))
        grad_g = (grad_h * shared_u * slope).astype(BF)
        grad_u = (grad_h * act).astype(BF)
        r.s_grads[0, here] = grad_g
        r.s_grads[1, here] = grad_u
        r.s_grads[2, here] = shared_h
        other, own = 1 - core, core
        back = dot_nt(grad_g, wide_half(0, other)) + dot_nt(grad_u, wide_half(1, other))
        r.core_b[0, here] = back.astype(BF)
        r.core_b[2, here] = dot_nt(shared_h, wide_half(2, other)).astype(BF)
        back = dot_nt(grad_g, wide_half(0, own)) + dot_nt(grad_u, wide_half(1, own))
        r.s_own[0, here] = back
        r.s_own[1, here] = dot_nt(shared_h, wide_half(2, own))
        return carry

    lax.fori_loop(0, micro, shared_step, 0)
    for swap_b in core_b:
        swap_b.send()
    for i, (rows_a, rows_b) in enumerate(((r.n_two, 0), (r.n_two, 1), (r.cot, 2))):
        grads = dot_tn(rows_a[...], r.s_grads[rows_b])
        r.sh_part[i] = grads.astype(BF).reshape(n, depth, shared)
    sum_sh = [
        Chain(net, lambda b, i=i: r.sh_part.at[i, b], r.sh_fx.at[i], r.sh_fz.at[i])
        for i in range(3)
    ]

    for m in micros:
        send_c[m].relay_core()
    for m in micros:
        send_x[m].relay_core()
    for m in micros:
        send_h[m].finish()
        send_c[m].finish()

    slot_gc = net.recv_slots(micro)
    slot_yc = net.recv_slots(micro)
    slot_yy = net.recv_slots(micro)
    slot_gy = net.recv_slots(micro)
    my_slots = pl.ds(pl.multiple_of(y * (cap // 2), cap // 2), cap // 2)
    far_slots = pl.ds(pl.multiple_of((1 - y) * (cap // 2), cap // 2), cap // 2)
    send_g = [
        Exchange(
            net,
            lambda b, m=m: r.g_core.at[m, b, my_slots],
            lambda b, m=m: r.g_in.at[m, b],
            r.g_in.at[m, 0 : n - 1],
        )
        for m in micros
    ]
    send_y = [
        Exchange(
            net,
            lambda b, m=m: r.y_core.at[m, b, my_slots],
            lambda b, m=m: r.y_in.at[m, b],
            r.y_in.at[m, 0 : n - 1],
        )
        for m in micros
    ]
    send_d = [
        Exchange(
            net,
            lambda b, m=m: r.d_out.at[m, b],
            lambda b, m=m: r.d_in.at[m, b],
            r.d_in.at[m, 0 : n - 1],
        )
        for m in micros
    ]
    slot_eye = eye[:cap]
    slot_line = iota((cap, 128), 0) == iota((cap, 128), 1)
    own_lane = iota((n * cap, 16), 1) - 8 == me
    group = 4
    halves = [slice(0, half), slice(half, model)]

    def expert_gates(m):
        x_rows = r.x_in[m].reshape(n * cap, model)
        z_all = dot_nt(x_rows, ext_low)
        hit = jnp.concatenate([dot_nt(slot_eye, r.h_in[m, b]) for b in range(n)], axis=0)
        z_own = jnp.sum(jnp.where(own_lane, z_all, 0.0), axis=1, keepdims=True)
        z_other = jnp.sum(jnp.where(own_lane, 0.0, z_all * hit), axis=1, keepdims=True)
        z_top = jnp.maximum(z_own, z_other)
        e_own, e_other = jnp.exp(z_own - z_top), jnp.exp(z_other - z_top)
        r.gate_col[m] = e_own / (e_own + e_other)

    def expert_rows(m, i):
        count = group * cap
        span = slice(i * group, (i + 1) * group)
        flat = slice(i * count, (i + 1) * count)
        x = r.x_in[m, span].reshape(count, model)
        c = r.c_in[m, span].reshape(count, model)
        gate = r.gate_col[m, flat]
        gate_pre = dot(x, r.eg[...])
        up_pre = dot(x, r.eu[...])
        act, slope = silu_both(gate_pre)
        hid = (act * up_pre).astype(BF)
        grad_y = (gate * c.astype(F32)).astype(BF)
        grad_hid = dot_nt(grad_y, r.ed[...])
        grad_g = (grad_hid * up_pre * slope).astype(BF)
        grad_u = (grad_hid * act).astype(BF)
        r.e_h[m, flat] = hid
        r.e_dg[m, flat] = grad_g
        r.e_du[m, flat] = grad_u
        dots = jnp.zeros((count, 1), F32)
        for cut in halves:
            out = dot(hid, r.ed[:, cut])
            r.tok_all[span, 0, m, :, cut] = out.astype(BF).reshape(group, cap, half)
            dots = dots + jnp.sum(out * c[:, cut].astype(F32), axis=1, keepdims=True)
            back = dot_nt(grad_g, r.eg[cut]) + dot_nt(grad_u, r.eu[cut])
            r.tok_all[span, 1, m, :, cut] = back.astype(BF).reshape(group, cap, half)
        r.c_in[m, span] = grad_y.reshape(group, 2, 2, part, model)
        for b in range(group):
            line = jnp.where(slot_line, dots[b * cap : (b + 1) * cap], 0.0)
            line = jnp.sum(line, axis=0, keepdims=True)
            r.d_out[m, i * group + b] = jnp.broadcast_to(line, (8, 128))

    def expert_sent(m):
        net.push(r.tok_all.at[:, 1, m, :, other_half], r.g_core.at[m], net.other_core(), slot_gc + m)
        net.push(r.tok_all.at[:, 0, m, :, other_half], r.y_core.at[m], net.other_core(), slot_yc + m)

    def add_g(m):
        net.landed(r.g_core.at[m], slot_gc + m)
        mine = r.tok_all[:, 1, m, :, my_half].astype(F32)
        r.g_core[m] = (mine + r.g_core[m].astype(F32)).astype(BF)
        net.push(r.g_core.at[m, :, far_slots], r.g_far.at[m], net.across_y(), slot_gy + m)

    def return_g(m):
        net.landed(r.g_far.at[m], slot_gy + m)
        both = r.g_core[m, :, my_slots].astype(F32) + r.g_far[m].astype(F32)
        r.g_core[m, :, my_slots] = both.astype(BF)
        send_g[m].start()
        send_d[m].start()
        r.g_in[m, me] = r.g_core[m, me, my_slots]
        r.d_in[m, me] = r.d_out[m, me]

    def add_y(m):
        net.landed(r.y_core.at[m], slot_yc + m)
        mine = r.tok_all[:, 0, m, :, my_half].astype(F32)
        r.y_core[m] = (mine + r.y_core[m].astype(F32)).astype(BF)
        net.push(r.y_core.at[m, :, far_slots], r.y_far.at[m], net.across_y(), slot_yy + m)

    def return_y(m):
        net.landed(r.y_far.at[m], slot_yy + m)
        both = r.y_core[m, :, my_slots].astype(F32) + r.y_far[m].astype(F32)
        r.y_core[m, :, my_slots] = both.astype(BF)
        send_y[m].start()
        r.y_in[m, me] = r.y_core[m, me, my_slots]

    saves = []

    def all_slots(ref, cut):
        return ref[..., cut].reshape(micro * n * cap, -1)

    def save(source, target, i):
        copy = pltpu.make_async_copy(source, target, r.save_sems.at[i])
        copy.start()
        saves.append(copy)

    def weight_grads(i):
        whole = slice(None)
        if i < 2:
            grads, target = ((r.e_dg, r.deg), (r.e_du, r.deu))[i]
            for h, cut in enumerate(halves):
                if i == 1:
                    saves[h].wait()
                r.stage[h] = dot_tn(all_slots(r.x_in, cut), all_slots(grads, whole))
                save(r.stage.at[h], target.at[cut], 2 * i + h)
        else:
            for h, cut in enumerate(halves):
                if h == 1:
                    saves[4].wait()
                r.stage_d[...] = dot_tn(all_slots(r.e_h, whole), all_slots(r.c_in, cut))
                save(r.stage_d, r.ded.at[:, cut], 4 + h)

    net.drain()
    sum_sh[0].start()
    sum_sh[1].start()
    for m in micros:
        send_x[m].finish()
        if m > 0:
            sum_sh[0].step(3)
        expert_gates(m)
        for i in range(n // group):
            if m > 0 and i == 1:
                add_g(m - 1)
                sum_sh[0].step(2)
            expert_rows(m, i)
        expert_sent(m)
    return_g(0)
    sum_sh[0].step(1)
    weight_grads(0)
    add_g(1)
    weight_grads(1)
    return_g(1)
    sum_sh[2].start()
    sum_sh[1].step(3)
    weight_grads(2)
    sum_sh[1].step(2)

    for m in micros:
        add_y(m)
    d_core = [Swap(net, r.d_tensor.at[m, 0], r.d_tensor.at[m, 1], net.other_core()) for m in micros]
    d_y = [Swap(net, r.d_tensor.at[m, 2], r.d_tensor.at[m, 3], net.across_y()) for m in micros]
    eight = iota((8, 128), 0)
    d_rows = []
    for m in micros:
        send_d[m].finish()
        line = jnp.zeros((8, 128), F32)
        for b in range(n):
            line = line + jnp.where(eight == b, r.d_in[m, b], 0.0)
        d_rows.append(line)
        d_core[m].start(line)
    shared_grad = r.s_own[0] + core_b[0].other()
    for m in micros:
        d_y[m].start(d_rows[m] + d_core[m].other())
    for m in micros:
        send_g[m].finish()
        moe_grad = dot(r.choice_half[m], r.g_in[m].reshape(n * cap // 2, half))
        y_swap[1][m].start(moe_grad + shared_grad[rows_of(m)])
    net.drain(bulk=False)
    sum_sh[1].step(1)
    grad_logits = []
    for m in micros:
        d_all = d_y[m].both()
        grad_gate = jnp.zeros((local, 16), F32)
        for b in range(n):
            picked = r.choice_wide[m, :, b * 128 : (b + 1) * 128].astype(F32) * d_all[b : b + 1]
            grad_gate = jnp.where(lane == b, jnp.sum(picked, axis=1, keepdims=True), grad_gate)
        inner = jnp.sum(gates[m] * grad_gate, axis=1, keepdims=True)
        grad_logits.append((gates[m] * (grad_gate - inner)).astype(BF))
        share_b[m].start(y_swap[1][m].both())


    w_qo = r.w_qo[...].reshape(model, wide)
    kv_sums, grad_queries, gain_rows = [], [], []
    for m in micros:
        grad_two = share_b[m].finish() + dot(grad_logits[m], ext_low)
        res = r.res[m]
        cot = r.cot[rows_of(m)].astype(F32)
        grad_res = cot + norm_back(grad_two, res, scale_two[m], gain_two)
        r.gtok[rows_of(m)] = grad_res
        gain_rows.append(jnp.sum(grad_two * res * scale_two[m], axis=0, keepdims=True))
        kv_rows = r.kv[m].reshape(tree, wide)
        total = r.total[m]
        gm = by_head(dot(grad_res.astype(BF), w_qo), v_masks)
        mixed = jnp.concatenate([r.mixed[m]] * heads, axis=0)
        delta = jnp.sum(gm * mixed, axis=1, keepdims=True) / total
        grad_summed = (gm / total).astype(BF)
        expo = r.expo[m]
        ds = (expo * (dot_nt(grad_summed, kv_rows) - delta)).astype(BF)
        grad_kv = dot_tn(ds, r.q_rows[m]) * score_scale + dot_tn(expo.astype(BF), grad_summed)
        r.kv_part[m] = grad_kv.astype(BF).reshape(n, local, wide)
        for k in range(2):
            span = slice(k * (local // 2), (k + 1) * (local // 2))
            one = Scatter(
                net,
                lambda b, m=m, span=span: r.kv_part.at[m, b, span],
                r.kv_fx.at[m, k],
                r.kv_fz.at[m, k],
            )
            one.start()
            kv_sums.append(one)
        if m == 0:
            for k in micros:
                return_y(k)
        grad_queries.append(join_heads(dot(ds, kv_rows), q_masks) * score_scale)

    cosine, sine = turns(me)

    def turned_back(grad):
        return (grad * cosine - dot(grad, swap, EXACT) * sine).astype(BF)

    for one in kv_sums:
        one.forward()
    sum_sh[2].step(3)
    grad_q = turned_back(jnp.concatenate(grad_queries, axis=0))
    grad_attn = r.gtok[...].astype(BF)
    part_qo = dot_tn(r.n_one[...], grad_q) + dot_tn(grad_attn, r.mixed_low[...])
    r.w_part[0] = part_qo.astype(BF).reshape(n, depth, wide)
    sum_w = [
        Scatter(net, lambda b, i=i: r.w_part.at[i, b], r.w_fx.at[i], r.w_fz.at[i])
        for i in range(2)
    ]
    sum_w[0].start()

    shared_y = r.s_own[1] + core_b[1].other()
    for m in micros:
        send_y[m].finish()
        gate_wide = dot(gates[m], spread(cap // 2).astype(F32), EXACT)
        gate_high = gate_wide.astype(BF).astype(F32)
        pick = r.choice_half[m].astype(F32)
        y_rows = r.y_in[m].reshape(n * cap // 2, half)
        moe_y = dot((pick * gate_high).astype(BF), y_rows)
        moe_y = moe_y + dot((pick * (gate_wide - gate_high)).astype(BF), y_rows)
        y_swap[2][m].start(moe_y + shared_y[rows_of(m)])
    sum_sh[2].step(2)

    def weight_half(ref, h):
        return ref[pl.ds(h * (n // 2), n // 2)].reshape(half, wide)

    grad_kvs = []
    for m in micros:
        total = jnp.concatenate([one.finish() for one in kv_sums[2 * m : 2 * m + 2]], axis=0)
        cos_m, sin_m = cosine[rows_of(m)], sine[rows_of(m)]
        grad_kv = (total * cos_m - dot(total, swap, EXACT) * sin_m).astype(BF)
        grad_kvs.append(grad_kv)
        q_m = grad_q[rows_of(m)]
        other = dot_nt(q_m, weight_half(r.w_qo, 1 - core))
        core_c[m].start(other + dot_nt(grad_kv, weight_half(r.w_kv, 1 - core)))
    for m in micros:
        mine = dot_nt(grad_q[rows_of(m)], weight_half(r.w_qo, core))
        mine = mine + dot_nt(grad_kvs[m], weight_half(r.w_kv, core))
        y_swap[3][m].start(mine + core_c[m].other())
    part_kv = dot_tn(r.n_one[...], jnp.concatenate(grad_kvs, axis=0))
    r.w_part[1] = part_kv.astype(BF).reshape(n, depth, wide)
    sum_w[1].start()
    sum_w[0].forward()
    sum_sh[2].step(1)
    for m in micros:
        share_c[m].start(y_swap[3][m].both())
    for m in micros:
        res_half = jnp.where(core == 0, r.res[m, :, :half], r.res[m, :, half:])
        share_out[m].start(res_half + y_swap[2][m].both())
    sum_w[1].forward()

    gain_one_row = jnp.zeros((1, model), F32)
    for m in micros:
        grad_one = share_c[m].finish()
        tok = r.tok[rows_of(m)].astype(F32)
        scale_one = norm_scale(tok)
        r.gtok[rows_of(m)] += norm_back(grad_one, tok, scale_one, gain_one)
        gain_one_row = gain_one_row + jnp.sum(grad_one * tok * scale_one, axis=0, keepdims=True)
    grad_router = jnp.zeros((16, model), F32)
    for m in micros:
        grad_router = grad_router + dot_tn(grad_logits[m], r.n_two[rows_of(m)])
    line = iota((16, model), 0)
    small = jnp.where(line == 0, gain_one_row, grad_router)
    small = jnp.where(line == 1, gain_rows[0] + gain_rows[1], small)
    for b in range(n):
        r.gains_out[b] = dot_nt(small, lay(b).astype(F32), EXACT)
    send_gains = Exchange(
        net, lambda b: r.gains_out.at[b], lambda b: r.gains_in.at[b], r.gains_in.at[0 : n - 1]
    )
    send_gains.start()
    r.gains_in[me] = r.gains_out[me]
    for m in micros:
        r.out[rows_of(m)] = share_out[m].finish()

    qo = sum_w[0].finish()
    r.dwq[...] = dot_nt(qo, left.astype(F32), EXACT)
    depth_eye = (iota((depth, depth), 0) == iota((depth, depth), 1)).astype(F32)
    r.dwo[...] = dot_tn(dot_nt(qo, right.astype(F32), EXACT), depth_eye, EXACT)
    kv = sum_w[1].finish()
    r.dwk[...] = dot_nt(kv, left.astype(F32), EXACT)
    r.dwv[...] = dot_nt(kv, right.astype(F32), EXACT)
    for i, target in enumerate((r.dsg, r.dsu, r.dsd)):
        sum_sh[i].finish(target)
    send_gains.finish()
    gains = jnp.zeros((16, 128), F32)
    for b in range(n):
        gains = gains + r.gains_in[b]
    r.dga[...] = gains[0:1, :depth]
    r.dgb[...] = gains[1:2, :depth]
    r.drouter[...] = gains[8:16, :depth]
    for copy in saves[2:4] + saves[5:]:
        copy.wait()
    net.drain()


def settle_kernel(count, *refs):
    sources, targets, stops = refs[:count], refs[count : 2 * count], refs[2 * count : 3 * count]
    sems = refs[3 * count]
    reads = [
        pltpu.make_async_copy(a, b, sems.at[0, i]) for i, (a, b) in enumerate(zip(sources, stops))
    ]
    writes = [
        pltpu.make_async_copy(a, b, sems.at[1, i]) for i, (a, b) in enumerate(zip(stops, targets))
    ]
    for read in reads:
        read.start()
    for read, write in zip(reads, writes):
        read.wait()
        write.start()
    for write in writes:
        write.wait()


def fits(mesh):
    return mesh.shape["expert"] == 8 and mesh.shape["tensor"] == 4


def fused_body(
    tokens,
    out_grad,
    routes,
    lengths,
    parents,
    attn_gain,
    ffn_gain,
    w_query,
    w_key,
    w_value,
    w_out,
    router,
    shared_gate,
    shared_up,
    shared_down,
    expert_gate,
    expert_up,
    expert_down,
):
    micro, local, model = tokens.shape
    n = lax.axis_size("expert")
    experts = router.shape[1]
    depth, width = w_query.shape
    hidden, shared = expert_gate.shape[2], shared_gate.shape[1]
    s = types.SimpleNamespace(
        n=n,
        micro=micro,
        local=local,
        half=model // 2,
        depth=depth,
        width=width,
        heads=width // HEAD,
        hidden=hidden,
        shared=shared,
        cap=4 * local // experts,
        segs=lengths.shape[1],
    )
    rows = micro * local
    scratch = scratch_shapes(s)
    names = PLACES + RESULTS + list(scratch)
    shape = jax.ShapeDtypeStruct
    vmem, smem = pl.BlockSpec(memory_space=pltpu.VMEM), pl.BlockSpec(memory_space=pltpu.SMEM)
    hbm = pl.BlockSpec(memory_space=pl.ANY)
    results = (
        shape((rows, model), BF),
        shape((rows, model), F32),
        shape((1, depth), F32),
        shape((1, depth), F32),
        shape((depth, width), F32),
        shape((depth, width), F32),
        shape((depth, width), F32),
        shape((width, depth), F32),
        shape((experts, depth), F32),
        shape((depth, shared), F32),
        shape((depth, shared), F32),
        shape((depth, shared), F32),
        shape((model, hidden), F32),
        shape((model, hidden), F32),
        shape((hidden, model), F32),
    )
    found = pl.pallas_call(
        functools.partial(layer_kernel, s, names),
        out_shape=results,
        in_specs=[vmem] * 3 + [smem] * 2 + [vmem] * 13,
        out_specs=[vmem] * 12 + [hbm] * 3,
        scratch_shapes=list(scratch.values()),
        compiler_params=pltpu.CompilerParams(
            collective_id=0, has_side_effects=True, vmem_limit_bytes=VMEM_LIMIT
        ),
    )(
        tokens.reshape(rows, model),
        out_grad.reshape(rows, model),
        routes.transpose(0, 2, 1).reshape(2 * micro, local),
        lengths,
        parents,
        attn_gain.reshape(1, depth),
        ffn_gain.reshape(1, depth),
        w_query,
        w_key,
        w_value,
        w_out,
        router.T,
        shared_gate,
        shared_up,
        shared_down.T,
        expert_gate[0],
        expert_up[0],
        expert_down[0],
    )
    settled = pl.pallas_call(
        functools.partial(settle_kernel, len(results)),
        out_shape=results,
        in_specs=[hbm] * len(results),
        out_specs=[hbm] * len(results),
        scratch_shapes=[pltpu.VMEM(one.shape, one.dtype) for one in results]
        + [pltpu.SemaphoreType.DMA((2, len(results)))],
        compiler_params=pltpu.CompilerParams(vmem_limit_bytes=VMEM_LIMIT),
    )(*found)
    out, gtok, dga, dgb, dwq, dwk, dwv, dwo, drouter, dsg, dsu, dsd, deg, deu, ded = settled
    return (
        out.reshape(micro, local, model),
        gtok.reshape(micro, local, model),
        dga.reshape(depth),
        dgb.reshape(depth),
        dwq,
        dwk,
        dwv,
        dwo,
        drouter.T,
        dsg,
        dsu,
        dsd.T,
        deg[None],
        deu[None],
        ded[None],
    )


def solution(mesh):
    in_specs = (
        P(None, "expert", None),
        P(None, "expert", None),
        P(None, "expert", None),
        P(),
        P(),
        P("expert"),
        P("expert"),
        P("expert", "tensor"),
        P("expert", "tensor"),
        P("expert", "tensor"),
        P("tensor", "expert"),
        P("expert", None),
        P("expert", "tensor"),
        P("expert", "tensor"),
        P("tensor", "expert"),
        P("expert", None, "tensor"),
        P("expert", None, "tensor"),
        P("expert", "tensor", None),
    )
    out_specs = (
        P(None, "expert", None),
        P(None, "expert", None),
        P("expert"),
        P("expert"),
        P("expert", "tensor"),
        P("expert", "tensor"),
        P("expert", "tensor"),
        P("tensor", "expert"),
        P("expert", None),
        P("expert", "tensor"),
        P("expert", "tensor"),
        P("tensor", "expert"),
        P("expert", None, "tensor"),
        P("expert", None, "tensor"),
        P("expert", "tensor", None),
    )
    chosen = fused_body if fits(mesh) else plain_body
    return jax.shard_map(chosen, mesh=mesh, in_specs=in_specs, out_specs=out_specs, check_vma=False)
```

```python
import functools
import math
import types

import jax
import jax.numpy as jnp
from jax import lax
from jax.experimental import pallas as pl
from jax.experimental.pallas import tpu as pltpu
from jax.sharding import PartitionSpec as P

HEAD = 64


EPSILON = 1e-06
ROPE_BASE = 10000.0
KEY_BLOCK = 2048


def matmul(left, right):
    return jnp.dot(left, right, preferred_element_type=jnp.float32)


def tree_tables(lengths, parents):
    seg_count = lengths.shape[0]
    identity = jnp.arange(seg_count, dtype=jnp.int32)
    current = identity
    ancestry = jnp.zeros((seg_count, seg_count), jnp.float32)
    for depth_level in range(seg_count):
        chosen_mask = current[:, None] == identity[None, :]
        ancestry = jnp.maximum(ancestry, chosen_mask.astype(jnp.float32))
        current = jnp.sum(jnp.where(chosen_mask, parents[None, :], 0), axis=1)
    seg_ends = jnp.cumsum(lengths)
    starts = seg_ends - lengths
    sizes_float = lengths.astype(jnp.float32)
    offsets = jnp.sum(ancestry * sizes_float[None, :], axis=1) - sizes_float
    return (ancestry, starts, seg_ends, offsets)


def row_tables(row_ids, starts, seg_ends, offsets):
    member = (
        (row_ids[:, None] >= starts[None, :]) & (row_ids[:, None] < seg_ends[None, :])
    ).astype(jnp.float32)
    position_shift = offsets - starts.astype(jnp.float32)
    position = jnp.sum(member * position_shift[None, :], axis=1) + row_ids.astype(jnp.float32)
    return (member, position)


def rotary_tables(position, half_width):
    frequency = ROPE_BASE ** (-jnp.arange(half_width, dtype=jnp.float32) / half_width)
    angles = position[:, None] * frequency[None, :]
    return (jnp.cos(angles)[:, None, :], jnp.sin(angles)[:, None, :])


def rotate(head_values, position):
    half_width = head_values.shape[-1] // 2
    cosines, sine_values = rotary_tables(position, half_width)
    first_half = head_values[..., :half_width]
    second_half = head_values[..., half_width:]
    return jnp.concatenate(
        [
            first_half * cosines - second_half * sine_values,
            second_half * cosines + first_half * sine_values,
        ],
        axis=-1,
    )


def rotate_back(grad_heads, position):
    half_width = grad_heads.shape[-1] // 2
    cosines, sine_values = rotary_tables(position, half_width)
    first_half = grad_heads[..., :half_width]
    second_half = grad_heads[..., half_width:]
    return jnp.concatenate(
        [
            first_half * cosines + second_half * sine_values,
            second_half * cosines - first_half * sine_values,
        ],
        axis=-1,
    )


def silu_parts(gate_val):
    sigmoid_val = jax.nn.sigmoid(gate_val)
    return (gate_val * sigmoid_val, sigmoid_val * (1.0 + gate_val * (1.0 - sigmoid_val)))


def rms_back(grad_normed, source, norm_scale, gain):
    weighted = grad_normed * gain
    inner_mean = jnp.mean(weighted * source, axis=1, keepdims=True)
    return (
        norm_scale * weighted - norm_scale**3 * source * inner_mean,
        jnp.sum(grad_normed * source * norm_scale, axis=0),
    )


def visible(reach_rows, query_ids, key_member, key_ids):
    linked = matmul(reach_rows, key_member.T) > 0.5
    return linked & (key_ids[None, :] <= query_ids[:, None])


def score_block(query_heads, key_heads, seen, score_scale):
    scores = (
        jnp.einsum("qhd,khd->hqk", query_heads, key_heads, preferred_element_type=jnp.float32)
        * score_scale
    )
    return jnp.where(seen[None], jnp.exp(scores), 0.0)


def score_grads(weights_exp, grad_summed, value_heads, delta_rows):
    grad_exp = jnp.einsum(
        "qhd,khd->hqk", grad_summed, value_heads, preferred_element_type=jnp.float32
    )
    return (weights_exp * (grad_exp - jnp.transpose(delta_rows)[:, :, None])).astype(jnp.bfloat16)


def plain_body(
    tokens,
    out_grad,
    routes,
    lengths,
    parents,
    attn_gain,
    ffn_gain,
    w_query,
    w_key,
    w_value,
    w_out,
    router,
    shared_gate,
    shared_up,
    shared_down,
    expert_gate,
    expert_up,
    expert_down,
):
    micro_count, row_count, model_width = tokens.shape
    devices = lax.axis_size("expert")
    tree_rows = row_count * devices
    expert_count = router.shape[1]
    owners = devices // expert_count
    capacity = 4 * row_count // expert_count
    score_scale = HEAD ** (-0.5)
    local_rows = lax.axis_index("expert") * row_count + jnp.arange(row_count, dtype=jnp.int32)
    part_gate = expert_gate[0]
    part_up = expert_up[0]
    part_down = expert_down[0]
    labels = jnp.arange(expert_count, dtype=jnp.int32)
    slot_ids = jnp.arange(expert_count * capacity, dtype=jnp.int32)
    pair_ids = jnp.arange(2 * row_count, dtype=jnp.int32)
    block_size = math.gcd(tree_rows, KEY_BLOCK)
    block_count = tree_rows // block_size
    layer_outputs = []
    token_gradients = []
    dense_sums = None
    expert_sums = None
    for micro_step in range(micro_count):
        gathered = (
            lax.all_gather(attn_gain, "expert", axis=0, tiled=True),
            lax.all_gather(ffn_gain, "expert", axis=0, tiled=True),
            lax.all_gather(w_query, "expert", axis=0, tiled=True),
            lax.all_gather(w_key, "expert", axis=0, tiled=True),
            lax.all_gather(w_value, "expert", axis=0, tiled=True),
            lax.all_gather(w_out, "expert", axis=1, tiled=True),
            lax.all_gather(router, "expert", axis=0, tiled=True),
            lax.all_gather(shared_gate, "expert", axis=0, tiled=True),
            lax.all_gather(shared_up, "expert", axis=0, tiled=True),
            lax.all_gather(shared_down, "expert", axis=1, tiled=True),
        )
        (
            gain_one,
            gain_two,
            query_weight,
            key_weight,
            value_weight,
            out_weight,
            router_weight,
            gate_weight,
            up_weight,
            down_weight,
        ) = gathered
        local_width = query_weight.shape[1]
        head_count = local_width // HEAD
        ancestry, starts, seg_ends, offsets = tree_tables(lengths[micro_step], parents[micro_step])
        member, position = row_tables(local_rows, starts, seg_ends, offsets)
        reach = matmul(member, ancestry)
        tokens_now = tokens[micro_step].astype(jnp.float32)
        norm_one = lax.rsqrt(jnp.mean(tokens_now * tokens_now, axis=1, keepdims=True) + EPSILON)
        normed_one = (tokens_now * norm_one * gain_one).astype(jnp.bfloat16)
        query_pre = matmul(normed_one, query_weight).reshape(row_count, head_count, HEAD)
        key_pre = matmul(normed_one, key_weight).reshape(row_count, head_count, HEAD)
        value_low = matmul(normed_one, value_weight).astype(jnp.bfloat16)
        queries = rotate(query_pre, position).astype(jnp.bfloat16)
        key_heads = rotate(key_pre, position).astype(jnp.bfloat16)
        key_value = jnp.concatenate([key_heads.reshape(row_count, local_width), value_low], axis=1)
        all_pairs = lax.all_gather(key_value, "expert", axis=0, tiled=True)

        def key_block_parts(block_index):
            first_key = block_index * block_size
            key_block = lax.dynamic_slice_in_dim(all_pairs, first_key, block_size, 0)
            key_ids = first_key + jnp.arange(block_size, dtype=jnp.int32)
            key_member, unused = row_tables(key_ids, starts, seg_ends, offsets)
            seen = visible(reach, local_rows, key_member, key_ids)
            block_keys = key_block[:, :local_width].reshape(block_size, head_count, HEAD)
            block_values = key_block[:, local_width:].reshape(block_size, head_count, HEAD)
            return (seen, block_keys, block_values)

        def forward_step(block_index, totals):
            seen, block_keys, block_values = key_block_parts(block_index)
            weights_exp = score_block(queries, block_keys, seen, score_scale)
            summed_part = jnp.einsum(
                "hqk,khd->qhd",
                weights_exp.astype(jnp.bfloat16),
                block_values,
                preferred_element_type=jnp.float32,
            )
            return (
                totals[0] + summed_part.reshape(row_count, local_width),
                totals[1] + jnp.transpose(jnp.sum(weights_exp, axis=2)),
            )

        initial = (
            jnp.zeros((row_count, local_width), jnp.float32),
            jnp.zeros((row_count, head_count), jnp.float32),
        )
        summed, row_total = lax.fori_loop(0, block_count, forward_step, initial)
        mixed = summed.reshape(row_count, head_count, HEAD) / row_total[:, :, None]
        mixed_low = mixed.reshape(row_count, local_width).astype(jnp.bfloat16)
        attn_out = lax.psum(matmul(mixed_low, out_weight), "tensor")
        residual = tokens_now + attn_out
        norm_two = lax.rsqrt(jnp.mean(residual * residual, axis=1, keepdims=True) + EPSILON)
        normed_two = (residual * norm_two * gain_two).astype(jnp.bfloat16)
        shared_g = matmul(normed_two, gate_weight)
        shared_u = matmul(normed_two, up_weight)
        shared_act, shared_slope = silu_parts(shared_g)
        shared_h = (shared_act * shared_u).astype(jnp.bfloat16)
        shared_y = matmul(shared_h, down_weight)
        logits = matmul(normed_two, router_weight)
        route_now = routes[micro_step]
        choose = (route_now[:, :, None] == labels[None, None, :]).astype(jnp.float32)
        gate_values = jax.nn.softmax(jnp.sum(choose * logits[:, None, :], axis=2), axis=1)
        flat_routes = route_now.reshape(2 * row_count)
        expert_hits = (flat_routes[:, None] == labels[None, :]).astype(jnp.int32)
        slot_rank = jnp.sum((jnp.cumsum(expert_hits, axis=0) - expert_hits) * expert_hits, axis=1)
        slot_index = flat_routes * capacity + slot_rank
        slot_match = slot_index[None, :] == slot_ids[:, None]
        filled = jnp.any(slot_match, axis=1)
        source = jnp.sum(jnp.where(slot_match, pair_ids[None, :], 0), axis=1)

        def to_owners(table, row_index):
            picked = jnp.take(table, row_index, axis=0)
            picked = jnp.where(filled[:, None], picked, jnp.zeros_like(picked))
            spread = jnp.broadcast_to(
                picked.reshape(expert_count, 1, capacity, model_width),
                (expert_count, owners, capacity, model_width),
            )
            return spread.reshape(devices, capacity, model_width)

        def from_owners(returned):
            merged = jnp.sum(
                returned.reshape(expert_count, owners, capacity, model_width), axis=1
            ).reshape(expert_count * capacity, model_width)
            return jnp.take(merged, slot_index, axis=0).reshape(row_count, 2, model_width)

        arrived = lax.all_to_all(
            to_owners(normed_two, source // 2), "expert", split_axis=0, concat_axis=0, tiled=True
        )
        slot_count = arrived.shape[1]
        flat_in = arrived.reshape(devices * slot_count, model_width)
        expert_g = matmul(flat_in, part_gate)
        expert_u = matmul(flat_in, part_up)
        expert_act, expert_unused = silu_parts(expert_g)
        expert_h = (expert_act * expert_u).astype(jnp.bfloat16)
        partial_out = matmul(expert_h, part_down).reshape(devices, slot_count, model_width)
        combined = lax.all_to_all(
            partial_out.astype(jnp.bfloat16), "expert", split_axis=0, concat_axis=0, tiled=True
        ).astype(partial_out.dtype)
        hidden_width = expert_g.shape[1]
        combined, arrived, kept_g, kept_u, kept_h = (
            combined,
            arrived,
            expert_g.reshape(devices, slot_count, hidden_width),
            expert_u.reshape(devices, slot_count, hidden_width),
            expert_h.reshape(devices, slot_count, hidden_width),
        )
        expert_y = from_owners(combined)
        cot_low = out_grad[micro_step]
        cotangent = cot_low.astype(jnp.float32)
        moe_part = jnp.sum(gate_values[:, :, None] * expert_y, axis=1)
        gate_dots = jnp.sum(cotangent[:, None, :] * expert_y, axis=2)
        ffn_out, grad_gate = (
            lax.psum((shared_y + moe_part).astype(jnp.bfloat16), "tensor").astype(jnp.float32),
            lax.psum(gate_dots.astype(jnp.bfloat16), "tensor").astype(jnp.float32),
        )
        layer_outputs.append((residual + ffn_out).astype(jnp.bfloat16))
        grad_shared_h = matmul(cot_low, down_weight.T)
        grad_shared_g = (grad_shared_h * shared_u * shared_slope).astype(jnp.bfloat16)
        grad_shared_u = (grad_shared_h * shared_act).astype(jnp.bfloat16)
        grad_chosen = gate_values * (
            grad_gate - jnp.sum(gate_values * grad_gate, axis=1, keepdims=True)
        )
        grad_logits = jnp.sum(choose * grad_chosen[:, :, None], axis=1).astype(jnp.bfloat16)
        grad_pairs_out = (
            (gate_values[:, :, None] * cotangent[:, None, :])
            .astype(jnp.bfloat16)
            .reshape(2 * row_count, model_width)
        )
        arrived_grad = lax.all_to_all(
            to_owners(grad_pairs_out, source), "expert", split_axis=0, concat_axis=0, tiled=True
        )
        slot_total = arrived_grad.shape[0] * arrived_grad.shape[1]
        flat_grad = arrived_grad.reshape(slot_total, model_width)
        flat_in = arrived.reshape(slot_total, model_width)
        hidden_width = kept_g.shape[2]
        expert_g = kept_g.reshape(slot_total, hidden_width)
        expert_u = kept_u.reshape(slot_total, hidden_width)
        expert_h = kept_h.reshape(slot_total, hidden_width)
        expert_act, expert_slope = silu_parts(expert_g)
        grad_hidden = matmul(flat_grad, part_down.T)
        grad_expert_g = (grad_hidden * expert_u * expert_slope).astype(jnp.bfloat16)
        grad_expert_u = (grad_hidden * expert_act).astype(jnp.bfloat16)
        grad_in = matmul(grad_expert_g, part_gate.T) + matmul(grad_expert_u, part_up.T)
        returned = lax.all_to_all(
            grad_in.reshape(arrived_grad.shape[0], arrived_grad.shape[1], model_width),
            "expert",
            split_axis=0,
            concat_axis=0,
            tiled=True,
        )
        normed_part = (
            matmul(grad_shared_g, gate_weight.T)
            + matmul(grad_shared_u, up_weight.T)
            + jnp.sum(from_owners(returned), axis=1)
        )
        grad_normed_two = lax.psum(normed_part, "tensor") + matmul(grad_logits, router_weight.T)
        grad_norm_part, grad_gain_two = rms_back(grad_normed_two, residual, norm_two, gain_two)
        grad_residual = cotangent + grad_norm_part
        grad_attn = grad_residual.astype(jnp.bfloat16)
        grad_mixed = matmul(grad_attn, out_weight.T).reshape(row_count, head_count, HEAD)
        grad_summed = (grad_mixed / row_total[:, :, None]).astype(jnp.bfloat16)
        delta_rows = jnp.sum(grad_mixed * mixed, axis=2) / row_total

        def block_terms(block_index):
            seen, block_keys, block_values = key_block_parts(block_index)
            weights_exp = score_block(queries, block_keys, seen, score_scale)
            grad_scores = score_grads(weights_exp, grad_summed, block_values, delta_rows)
            return (weights_exp, grad_scores, block_keys)

        zero_query = jnp.zeros((row_count, head_count, HEAD), jnp.float32)

        def key_step(gradient_query_weight, block_index):
            weights_exp, grad_scores, block_keys = block_terms(block_index)
            gradient_query_weight = (
                gradient_query_weight
                + jnp.einsum(
                    "hqk,khd->qhd", grad_scores, block_keys, preferred_element_type=jnp.float32
                )
                * score_scale
            )
            grad_keys = (
                jnp.einsum("hqk,qhd->khd", grad_scores, queries, preferred_element_type=jnp.float32)
                * score_scale
            )
            grad_values = jnp.einsum(
                "hqk,qhd->khd",
                weights_exp.astype(jnp.bfloat16),
                grad_summed,
                preferred_element_type=jnp.float32,
            )
            return (
                gradient_query_weight,
                jnp.concatenate(
                    [
                        grad_keys.reshape(block_size, local_width),
                        grad_values.reshape(block_size, local_width),
                    ],
                    axis=1,
                ),
            )

        gradient_query_weight, key_terms = lax.scan(
            key_step, zero_query, jnp.arange(block_count, dtype=jnp.int32)
        )
        grad_pairs = lax.psum_scatter(
            key_terms.reshape(tree_rows, 2 * local_width), "expert", scatter_dimension=0, tiled=True
        )
        grad_keys_rot = grad_pairs[:, :local_width].reshape(row_count, head_count, HEAD)
        grad_query_pre = (
            rotate_back(gradient_query_weight, position)
            .reshape(row_count, local_width)
            .astype(jnp.bfloat16)
        )
        grad_key_pre = (
            rotate_back(grad_keys_rot, position)
            .reshape(row_count, local_width)
            .astype(jnp.bfloat16)
        )
        grad_value_low = grad_pairs[:, local_width:].astype(jnp.bfloat16)
        normed_grad = (
            matmul(grad_query_pre, query_weight.T)
            + matmul(grad_key_pre, key_weight.T)
            + matmul(grad_value_low, value_weight.T)
        )
        grad_normed_one = lax.psum(normed_grad.astype(jnp.bfloat16), "tensor").astype(jnp.float32)
        grad_norm_first, grad_gain_one = rms_back(grad_normed_one, tokens_now, norm_one, gain_one)
        token_gradients.append(grad_residual + grad_norm_first)
        dense_step = (
            grad_gain_one,
            grad_gain_two,
            matmul(normed_one.T, grad_query_pre),
            matmul(normed_one.T, grad_key_pre),
            matmul(normed_one.T, grad_value_low),
            matmul(mixed_low.T, grad_attn),
            matmul(normed_two.T, grad_logits),
            matmul(normed_two.T, grad_shared_g),
            matmul(normed_two.T, grad_shared_u),
            matmul(shared_h.T, cot_low),
        )
        expert_step = (
            matmul(flat_in.T, grad_expert_g),
            matmul(flat_in.T, grad_expert_u),
            matmul(expert_h.T, flat_grad),
        )
        if dense_sums is None:
            dense_sums = dense_step
            expert_sums = expert_step
        else:
            dense_sums = tuple(
                (earlier + latest for earlier, latest in zip(dense_sums, dense_step))
            )
            expert_sums = tuple(
                (earlier + latest for earlier, latest in zip(expert_sums, expert_step))
            )
    final_gate, final_up, final_down = expert_sums
    reduced = (
        lax.psum_scatter(dense_sums[0], "expert", scatter_dimension=0, tiled=True),
        lax.psum_scatter(dense_sums[1], "expert", scatter_dimension=0, tiled=True),
        lax.psum_scatter(dense_sums[2], "expert", scatter_dimension=0, tiled=True),
        lax.psum_scatter(dense_sums[3], "expert", scatter_dimension=0, tiled=True),
        lax.psum_scatter(dense_sums[4], "expert", scatter_dimension=0, tiled=True),
        lax.psum_scatter(dense_sums[5], "expert", scatter_dimension=1, tiled=True),
        lax.psum_scatter(dense_sums[6], "expert", scatter_dimension=0, tiled=True),
        lax.psum_scatter(dense_sums[7], "expert", scatter_dimension=0, tiled=True),
        lax.psum_scatter(dense_sums[8], "expert", scatter_dimension=0, tiled=True),
        lax.psum_scatter(dense_sums[9], "expert", scatter_dimension=1, tiled=True),
    )
    return (
        jnp.stack(layer_outputs),
        jnp.stack(token_gradients),
        reduced[0],
        reduced[1],
        reduced[2],
        reduced[3],
        reduced[4],
        reduced[5],
        reduced[6],
        reduced[7],
        reduced[8],
        reduced[9],
        final_gate[None],
        final_up[None],
        final_down[None],
    )


MESH = pl.DeviceIdType.MESH
BF = jnp.bfloat16
F32 = jnp.float32
EXACT = lax.Precision.HIGHEST
VMEM_LIMIT = 63 * 2**20


def product(left, right, dims, precision=None):
    return lax.dot_general(
        left, right, (dims, ((), ())), preferred_element_type=F32, precision=precision
    )


def dot(left, right, precision=None):
    return product(left, right, ((1,), (0,)), precision)


def dot_nt(left, right, precision=None):
    return product(left, right, ((1,), (1,)), precision)


def dot_tn(left, right, precision=None):
    return product(left, right, ((0,), (0,)), precision)


def iota(shape, dim):
    return lax.broadcasted_iota(jnp.int32, shape, dim)


class Net:
    def __init__(self, expert_size, send_sems, recv_sems):
        self.e = lax.axis_index("expert")
        self.t = lax.axis_index("tensor")
        self.n = expert_size
        self.nz = expert_size // 2
        self.z = self.e // 2
        self.x = self.e % 2
        self.y = self.t // 2
        self.core = self.t % 2
        self.send_sems = send_sems
        self.recv_sems = recv_sems
        self.sends = 0
        self.free = []
        self.recvs = 0
        self.open = []

    def recv_slots(self, count):
        first = self.recvs
        self.recvs += count
        return first

    def ids(self, to):
        return {"expert": to[0], "tensor": to[1]}

    def send_slot(self):
        if not self.free:
            self.free.append(self.sends)
            self.sends += 1
        return self.free.pop(0)

    def push(self, src, dst, to, slot, when=None, bulk=False, shared=None):
        send = self.send_slot() if shared is None else shared
        copy = pltpu.make_async_remote_copy(
            src_ref=src,
            dst_ref=dst,
            send_sem=self.send_sems.at[send],
            recv_sem=self.recv_sems.at[slot],
            device_id=self.ids(to),
            device_id_type=MESH,
        )
        if when is None:
            copy.start()
        else:
            pl.when(when)(copy.start)
        if shared is None:
            self.open.append((copy, when, send, bulk))

    def all_sent(self, part, send):
        copy = pltpu.make_async_remote_copy(
            src_ref=part,
            dst_ref=part,
            send_sem=self.send_sems.at[send],
            recv_sem=self.recv_sems.at[0],
            device_id=self.ids(self.other_core()),
            device_id_type=MESH,
        )
        self.open.append((copy, None, send, False))

    def landed(self, dst, slot, when=None):
        copy = pltpu.make_async_remote_copy(
            src_ref=dst,
            dst_ref=dst,
            send_sem=self.send_sems.at[0],
            recv_sem=self.recv_sems.at[slot],
            device_id=self.ids(self.other_core()),
            device_id_type=MESH,
        )
        if when is None:
            copy.wait_recv()
        else:
            pl.when(when)(copy.wait_recv)

    def drain(self, bulk=True):
        for copy, when, send, is_bulk in self.open:
            if bulk or not is_bulk:
                if when is None:
                    copy.wait_send()
                else:
                    pl.when(when)(copy.wait_send)
                self.free.append(send)
        self.open = [one for one in self.open if one[3] and not bulk]

    def other_core(self):
        return (self.e, self.t + 1 - 2 * self.core)

    def across_y(self):
        return (self.e, (self.t + 2) % 4)

    def across_x(self):
        return (self.e + 1 - 2 * self.x, self.t)

    def peer(self, step):
        return (self.e + step) % self.n

    def greet(self):
        barrier = pltpu.get_barrier_semaphore()
        partners = [(self.peer(d), self.t) for d in range(1, self.n)]
        partners += [self.other_core(), self.across_y()]
        for to in partners:
            pl.semaphore_signal(barrier, inc=1, device_id=self.ids(to), device_id_type=MESH)
        return lambda: pl.semaphore_wait(barrier, len(partners))


class Gather:
    def __init__(self, net, block, chunks=1, on_land=None):
        self.net, self.block, self.chunks, self.on_land = net, block, chunks, on_land
        self.slot = net.recv_slots(net.n * chunks)

    def start(self):
        net = self.net
        for k in range(self.chunks):
            own, slot = self.block(net.e, k), self.slot + net.e * self.chunks + k
            for way in (1, -1):
                there = net.z + way
                fits_in = (there >= 0) & (there < net.nz)
                net.push(own, own, (there % net.nz * 2 + net.x, net.t), slot, fits_in)
            net.push(own, own, net.across_x(), slot)

    def step(self, distance):
        net = self.net
        for k in range(self.chunks):
            for way in (1, -1):
                source, there = net.z - way * distance, net.z + way
                real = (source >= 0) & (source < net.nz)
                onward = real & (there >= 0) & (there < net.nz)
                b = source % net.nz * 2 + net.x
                part, slot = self.block(b, k), self.slot + b * self.chunks + k
                net.landed(part, slot, real)
                net.push(part, part, (there % net.nz * 2 + net.x, net.t), slot, onward)
                net.push(part, part, net.across_x(), slot, real)
                if self.on_land is not None:
                    self.on_land(b, real)

    def land(self, b):
        net = self.net
        for k in range(self.chunks):
            net.landed(self.block(b, k), self.slot + b * self.chunks + k)
        if self.on_land is not None:
            self.on_land(b, None)

    def finish(self):
        for d in range(self.net.nz):
            self.land((self.net.z + d) % self.net.nz * 2 + 1 - self.net.x)


class Scatter:
    def __init__(self, net, block, from_x, from_z):
        self.net, self.block = net, block
        self.from_x, self.from_z = from_x, from_z
        self.slot_x = net.recv_slots(net.nz)
        self.slot_z = net.recv_slots(net.nz)

    def start(self):
        net = self.net
        for d in range(1, net.nz + 1):
            zz = (net.z + d) % net.nz
            net.push(
                self.block(zz * 2 + 1 - net.x),
                self.from_x.at[zz],
                net.across_x(),
                self.slot_x + zz,
                bulk=True,
            )

    def forward(self):
        net = self.net
        for d in range(1, net.nz):
            zz = (net.z + d) % net.nz
            net.landed(self.from_x.at[zz], self.slot_x + zz)
            pair = self.block(zz * 2 + net.x)[...].astype(F32) + self.from_x[zz].astype(F32)
            self.from_x[zz] = pair.astype(BF)
            net.push(
                self.from_x.at[zz],
                self.from_z.at[net.z],
                (zz * 2 + net.x, net.t),
                self.slot_z + net.z,
            )

    def finish(self):
        net = self.net
        net.landed(self.from_x.at[net.z], self.slot_x + net.z)
        total = self.block(net.e)[...].astype(F32) + self.from_x[net.z].astype(F32)
        for d in range(1, net.nz):
            zz = (net.z + d) % net.nz
            net.landed(self.from_z.at[zz], self.slot_z + zz)
            total = total + self.from_z[zz].astype(F32)
        return total


class Chain:
    def __init__(self, net, block, from_x, from_z):
        self.net, self.block = net, block
        self.from_x, self.from_z = from_x, from_z
        self.slot_x = net.recv_slots(net.nz)
        self.slot_z = net.recv_slots(net.nz + 1)

    def start(self):
        net = self.net
        high = net.z // 2
        for zz in (3 - 3 * high, 2 - high, 1 - net.z + 4 * high, net.z):
            net.push(
                self.block(zz * 2 + 1 - net.x),
                self.from_x.at[zz],
                net.across_x(),
                self.slot_x + zz,
                bulk=True,
            )

    def place(self, way, zz, holder):
        return zz if way == 1 else zz + (zz == holder).astype(jnp.int32) * (self.net.nz - zz)

    def step(self, distance):
        net = self.net
        for way in (1, -1):
            target, before = net.z + way * distance, net.z - way
            real = (target >= 0) & (target < net.nz)
            fed = real & (before >= 0) & (before < net.nz)
            zz = target % net.nz
            there = (net.z + way) % net.nz
            here = self.place(way, zz, net.z)
            onward = self.place(way, zz, there)

            @pl.when(real)
            def _():
                net.landed(self.from_x.at[zz], self.slot_x + zz)

            @pl.when(fed)
            def _():
                net.landed(self.from_z.at[here], self.slot_z + here)
                both = self.from_x[zz].astype(F32) + self.from_z[here].astype(F32)
                self.from_x[zz] = (both + self.block(zz * 2 + net.x)[...].astype(F32)).astype(BF)

            @pl.when(real & ~fed)
            def _():
                own = self.block(zz * 2 + net.x)[...].astype(F32)
                self.from_x[zz] = (self.from_x[zz].astype(F32) + own).astype(BF)

            net.push(
                self.from_x.at[zz],
                self.from_z.at[onward],
                (there * 2 + net.x, net.t),
                self.slot_z + onward,
                when=real,
                bulk=True,
            )

    def finish(self, target):
        net = self.net
        net.landed(self.from_x.at[net.z], self.slot_x + net.z)
        target[...] = self.block(net.e)[...].astype(F32) + self.from_x[net.z].astype(F32)
        for way in (1, -1):
            before = net.z - way
            here = self.place(way, net.z, net.z)

            @pl.when((before >= 0) & (before < net.nz))
            def _():
                net.landed(self.from_z.at[here], self.slot_z + here)
                target[...] += self.from_z[here].astype(F32)


class Exchange:
    def __init__(self, net, outgoing, incoming, rest=None):
        self.net, self.outgoing, self.incoming, self.rest = net, outgoing, incoming, rest
        self.slot = net.recv_slots(net.n if rest is None else 1)

    def start(self):
        net = self.net
        send = None if self.rest is None else net.send_slot()
        for d in range(1, net.n):
            to = net.peer(d)
            slot = self.slot + net.e if self.rest is None else self.slot
            net.push(self.outgoing(to), self.incoming(net.e), (to, net.t), slot, shared=send)
        if self.rest is not None:
            net.all_sent(self.rest, send)

    def arrive(self, d):
        source = self.net.peer(d)
        self.net.landed(self.incoming(source), self.slot + source)
        return source

    def finish(self):
        self.net.landed(self.rest, self.slot)


class Dispatch:
    def __init__(self, net, outgoing, incoming):
        self.net, self.outgoing, self.incoming = net, outgoing, incoming
        self.send = Exchange(
            net, lambda b: outgoing.at[b], lambda b: incoming.at[b, net.core, net.y]
        )
        self.slot_y = net.recv_slots(net.n)
        self.slot_core = net.recv_slots(1)

    def start(self):
        net = self.net
        self.send.start()
        self.incoming[net.e, net.core, net.y] = self.outgoing[net.e]

    def relay_y(self):
        net = self.net
        for d in range(net.n):
            b = net.e if d == 0 else self.send.arrive(d)
            part = self.incoming.at[b, net.core, net.y]
            net.push(part, part, net.across_y(), self.slot_y + b)

    def relay_core(self):
        net = self.net
        for d in range(net.n):
            b = net.peer(d)
            net.landed(self.incoming.at[b, net.core, 1 - net.y], self.slot_y + b)
        part = self.incoming.at[:, net.core]
        net.push(part, part, net.other_core(), self.slot_core)

    def finish(self):
        self.net.landed(self.incoming.at[:, 1 - self.net.core], self.slot_core)


class Swap:
    def __init__(self, net, out_buf, in_buf, partner):
        self.net, self.out_buf, self.in_buf, self.partner = net, out_buf, in_buf, partner
        self.slot = net.recv_slots(1)

    def start(self, value):
        self.out_buf[...] = value.astype(self.out_buf.dtype)
        self.send()

    def send(self):
        self.net.push(self.out_buf, self.in_buf, self.partner, self.slot)

    def other(self):
        self.net.landed(self.in_buf, self.slot)
        return self.in_buf[...].astype(F32)

    def both(self):
        return self.out_buf[...].astype(F32) + self.other()


class Share:
    def __init__(self, net, halves):
        self.net, self.halves = net, halves
        self.slot = net.recv_slots(1)

    def start(self, value):
        net = self.net
        self.halves[net.core] = value.astype(self.halves.dtype)
        part = self.halves.at[net.core]
        net.push(part, part, net.other_core(), self.slot)

    def finish(self):
        net = self.net
        net.landed(self.halves.at[1 - net.core], self.slot)
        return jnp.concatenate([self.halves[0], self.halves[1]], axis=1)


def silu_both(value):
    gate = jax.nn.sigmoid(value)
    return value * gate, gate * (1.0 + value * (1.0 - gate))


def norm_scale(value):
    return lax.rsqrt(jnp.mean(value * value, axis=1, keepdims=True) + EPSILON)


def norm_back(grad_normed, source, scale, gain):
    weighted = grad_normed * gain
    inner = jnp.mean(weighted * source, axis=1, keepdims=True)
    return scale * weighted - scale * scale * scale * source * inner


PLACES = ["tok", "cot", "routes", "lengths", "parents", "gain_a", "gain_b", "wq", "wk", "wv"]
PLACES += ["wo", "router", "sg", "su", "sd", "eg", "eu", "ed"]
RESULTS = ["out", "gtok", "dga", "dgb", "dwq", "dwk", "dwv", "dwo", "drouter"]
RESULTS += ["dsg", "dsu", "dsd", "deg", "deu", "ded"]


def scratch_shapes(s):
    n, local, half = s.n, s.local, s.half
    depth, hidden, shared, cap = s.depth, s.hidden, s.shared, s.cap
    micro, nz = s.micro, s.n // 2
    model, wide, stack, tree = 2 * half, 2 * s.width, s.heads * local, n * local
    part = cap // 4
    vm = pltpu.VMEM
    return dict(
        w_kv=vm((n, depth, wide), BF),
        w_qo=vm((n, depth, wide), BF),
        w_sh=vm((3, n, depth, shared), BF),
        ext_in=vm((n, 16, 128), BF),
        tok_all=vm((n, 2, 2, micro * local // 4, model), BF),
        cos_all=vm((n, micro * local, 128), F32),
        sin_all=vm((n, micro * local, 128), F32),
        kv=vm((micro, n, local, wide), BF),
        q_rows=vm((micro, stack, 256), BF),
        expo=vm((micro, stack, tree), F32),
        total=vm((micro, stack, 1), F32),
        mixed=vm((micro, local, 256), F32),
        mixed_low=vm((micro * local, wide), BF),
        choice_half=vm((micro, local, n * cap // 2), BF),
        choice_wide=vm((micro, local, n * 128), BF),
        res=vm((micro, local, model), F32),
        n_one=vm((micro * local, model), BF),
        n_two=vm((micro * local, model), BF),
        c_out=vm((micro, n, part, model), BF),
        c_in=vm((micro, n, 2, 2, part, model), BF),
        x_out=vm((micro, n, part, model), BF),
        x_in=vm((micro, n, 2, 2, part, model), BF),
        h_out=vm((micro, n, 16, 128), BF),
        h_in=vm((micro, n, 16, 128), BF),
        gate_col=vm((micro, n * cap, 1), F32),
        e_h=vm((micro, n * cap, hidden), BF),
        e_dg=vm((micro, n * cap, hidden), BF),
        e_du=vm((micro, n * cap, hidden), BF),
        y_core=vm((micro, n, cap, half), BF),
        g_core=vm((micro, n, cap, half), BF),
        y_in=vm((micro, n, cap // 2, half), BF),
        y_far=vm((micro, n, cap // 2, half), BF),
        g_in=vm((micro, n, cap // 2, half), BF),
        g_far=vm((micro, n, cap // 2, half), BF),
        d_out=vm((micro, n, 8, 128), F32),
        d_in=vm((micro, n, 8, 128), F32),
        d_tensor=vm((micro, 4, 8, 128), F32),
        core_a=vm((micro, 2, local, half), F32),
        core_b=vm((4, micro * local, half), BF),
        core_c=vm((micro, 2, local, half), F32),
        s_grads=vm((3, micro * local, shared), BF),
        s_own=vm((2, micro * local, half), F32),
        y_swap=vm((4, micro, 2, local, half), BF),
        share_a=vm((micro, 2, local, half), F32),
        share_b=vm((micro, 2, local, half), F32),
        share_c=vm((micro, 2, local, half), F32),
        share_out=vm((micro, 2, local, half), BF),
        kv_part=vm((micro, n, local, wide), BF),
        kv_fx=vm((micro, 2, nz, local // 2, wide), BF),
        kv_fz=vm((micro, 2, nz, local // 2, wide), BF),
        sh_part=vm((3, n, depth, shared), BF),
        sh_fx=vm((3, nz, depth, shared), BF),
        sh_fz=vm((3, nz + 1, depth, shared), BF),
        w_part=vm((2, n, depth, wide), BF),
        w_fx=vm((2, nz, depth, wide), BF),
        w_fz=vm((2, nz, depth, wide), BF),
        gains_out=vm((n, 16, 128), F32),
        gains_in=vm((n, 16, 128), F32),
        stage=vm((2, half, hidden), F32),
        stage_d=vm((hidden, half), F32),
        save_sems=pltpu.SemaphoreType.DMA((6,)),
        send_sems=pltpu.SemaphoreType.DMA((SENDS,)),
        recv_sems=pltpu.SemaphoreType.DMA((RECVS,)),
    )


SENDS = 182
RECVS = 251


def layer_kernel(s, names, *refs):
    r = types.SimpleNamespace(**dict(zip(names, refs)))
    n, local, width, half = s.n, s.local, s.width, s.half
    depth, hidden, shared, cap = s.depth, s.hidden, s.shared, s.cap
    micro, heads = s.micro, s.heads
    rows, model, tree, wide, stack = micro * local, 2 * half, n * local, 2 * width, heads * local
    part = cap // 4
    net = Net(n, r.send_sems, r.recv_sems)
    me, core, y = net.e, net.core, net.y
    ready = net.greet()
    micros = range(micro)
    my_half = pl.ds(pl.multiple_of(core * half, 128), half)
    other_half = pl.ds(pl.multiple_of((1 - core) * half, 128), half)

    def rows_of(m):
        return slice(m * local, (m + 1) * local)

    left = (iota((width, wide), 1) == iota((width, wide), 0)).astype(BF)
    right = (iota((width, wide), 1) == iota((width, wide), 0) + width).astype(BF)
    r.w_kv[me] = (dot(r.wk[...], left) + dot(r.wv[...], right)).astype(BF)
    r.tok_all[me] = r.tok[...].reshape(2, 2, rows // 4, model)
    r.w_qo[me] = (dot(r.wq[...], left) + dot_tn(r.wo[...], right)).astype(BF)
    ext = [r.gain_a[...].astype(F32), r.gain_b[...].astype(F32), jnp.zeros((6, depth), F32)]
    ext = jnp.concatenate(ext + [r.router[...].astype(F32)], axis=0).astype(BF)
    pad = (iota((depth, 128), 1) == iota((depth, 128), 0)).astype(BF)
    r.ext_in[me] = dot(ext, pad).astype(BF)
    for i, name in enumerate(("sg", "su", "sd")):
        r.w_sh[i, me] = getattr(r, name)[...]

    slot_ty, slot_tc = net.recv_slots(n), net.recv_slots(n)

    def token_on(b, when):
        quarter = r.tok_all.at[b, core, y]
        net.push(quarter, quarter, net.across_y(), slot_ty + b, when)

    get_kv = Gather(net, lambda b, k: r.w_kv.at[b])
    get_qo = Gather(net, lambda b, k: r.w_qo.at[b])
    get_tok = Gather(net, lambda b, k: r.tok_all.at[b, core, y], on_land=token_on)
    get_sh = [Gather(net, lambda b, k, i=i: r.w_sh.at[i, b]) for i in range(3)]
    get_ext = Exchange(net, lambda b: r.ext_in.at[me], lambda b: r.ext_in.at[b], r.ext_in.at[0 : n - 1])
    ready()
    get_ext.start()
    get_kv.start()
    get_tok.start()
    get_qo.start()

    eye = (iota((128, 128), 0) == iota((128, 128), 1)).astype(BF)
    routes = dot_nt(eye, r.routes[...].astype(BF))
    lane = iota((local, 16), 1) - 8
    earlier = (iota((local, local), 1) < iota((local, local), 0)).astype(BF)

    def spread(span):
        of_lane = iota((16, n * span), 1) // span
        return (iota((16, n * span), 0) - 8 == of_lane).astype(BF)

    hot_one, hot_two, quarter = [], [], []
    send_c = [Dispatch(net, r.c_out.at[m], r.c_in.at[m]) for m in micros]
    send_h = [
        Exchange(
            net,
            lambda b, m=m: r.h_out.at[m, b],
            lambda b, m=m: r.h_in.at[m, b],
            r.h_in.at[m, 0 : n - 1],
        )
        for m in micros
    ]
    for m in micros:
        one = lane == routes[:, 2 * m : 2 * m + 1].astype(jnp.int32)
        two = lane == routes[:, 2 * m + 1 : 2 * m + 2].astype(jnp.int32)
        hot_one.append(one)
        hot_two.append(two)
        hits = (one | two).astype(F32)
        rank = jnp.where(hits > 0.5, dot(earlier, hits.astype(BF)), -1.0).astype(BF)

        def taken(span, first=0):
            wanted = iota((local, n * span), 1) % span + first
            return (dot(rank, spread(span)) == wanted.astype(F32)).astype(BF)

        r.choice_half[m] = taken(cap // 2, y * (cap // 2))
        r.choice_wide[m] = taken(128)
        quarter.append(taken(part, (core * 2 + y) * part))
        hit_rows = dot_tn(hits.astype(BF), r.choice_wide[m]).astype(BF)
        for b in range(n):
            r.h_out[m, b] = hit_rows[:, b * 128 : (b + 1) * 128]
        r.h_in[m, me] = r.h_out[m, me]
        picked = dot_tn(quarter[m], r.cot[rows_of(m)]).astype(BF)
        r.c_out[m] = picked.reshape(n, part, model)

    def segments(m):
        starts, ends, paths, shifts, begin = [], [], [], [], 0
        for seg in range(s.segs):
            size = r.lengths[m, seg]
            starts.append(begin)
            ends.append(begin + size)
            begin = begin + size
            if seg == 0:
                paths.append(jnp.int32(1))
                shifts.append(jnp.int32(0))
            else:
                parent = r.parents[m, seg]
                path, shift = jnp.int32(0), jnp.int32(0)
                for other in range(seg):
                    is_parent = parent == other
                    path = jnp.where(is_parent, paths[other], path)
                    shift = jnp.where(
                        is_parent, shifts[other] + ends[other] - starts[other], shift
                    )
                paths.append(path + (1 << seg))
                shifts.append(shift)
        return starts, ends, paths, shifts

    tables = [segments(m) for m in micros]

    def row_values(m, ids):
        starts, ends, paths, shifts = tables[m]
        path, place, own = jnp.zeros_like(ids), jnp.zeros_like(ids), jnp.zeros_like(ids)
        for seg in range(s.segs):
            inside = (ids >= starts[seg]) & (ids < ends[seg])
            path = jnp.where(inside, paths[seg], path)
            place = jnp.where(inside, ids - starts[seg] + shifts[seg], place)
            own = jnp.where(inside, 1 << seg, own)
        return path, place, own

    turn = (iota((1, 128), 1) % (HEAD // 2)).astype(F32)
    frequency = jnp.exp(turn * (-math.log(ROPE_BASE) / (HEAD // 2)))

    def angle_step(b, carry):
        ids = b * local + iota((local, 1), 0)
        place = jnp.concatenate([row_values(m, ids)[1] for m in micros], axis=0)
        angle = place.astype(F32) * frequency
        r.cos_all[b] = jnp.cos(angle)
        r.sin_all[b] = jnp.sin(angle)
        return carry

    lax.fori_loop(0, n, angle_step, 0)
    is_left = iota((1, wide), 1) < width
    swap_r, swap_c = iota((wide, wide), 0), iota((wide, wide), 1)
    lower = swap_c % HEAD < HEAD // 2
    swap = jnp.where(lower & (swap_r == swap_c + HEAD // 2), -1.0, 0.0)
    swap = jnp.where(~lower & (swap_r == swap_c - HEAD // 2), 1.0, swap)
    swap = jnp.where(is_left, swap, 0.0)
    swap_low = swap.astype(BF)

    def turns(b):
        cosine = jnp.concatenate([r.cos_all[b]] * (wide // 128), axis=1)
        sine = jnp.concatenate([r.sin_all[b]] * (wide // 128), axis=1)
        return jnp.where(is_left, cosine, 1.0), sine

    for distance in range(1, net.nz):
        get_kv.step(distance)
        get_tok.step(distance)
        get_qo.step(distance)
    get_ext.finish()
    high = net.z // 2
    near = [net.z + 1 - 2 * (net.z % 2), 2 - high, 3 - 3 * high]
    column = [zz * 2 + net.x for zz in near]
    across = [zz * 2 + 1 - net.x for zz in [net.z] + near]

    def token_core(b):
        net.landed(r.tok_all.at[b, core, 1 - y], slot_ty + b)
        both = r.tok_all.at[b, core]
        net.push(both, both, net.other_core(), slot_tc + b)

    for b in column:
        token_core(b)

    def lay(b):
        place = iota((128, model), 0)
        return (place < depth) & (place + b * depth == iota((128, model), 1))

    ext_all = jnp.zeros((16, model), F32)
    for b in range(n):
        ext_all = ext_all + dot(r.ext_in[b], lay(b).astype(BF))
    gain_one, gain_two = ext_all[0:1], ext_all[1:2]
    ext_low = ext_all.astype(BF)
    get_kv.finish()
    w_kv = r.w_kv[...].reshape(model, wide)
    w_kv_swapped = dot(w_kv, swap_low[:, :256]).astype(BF)

    def normed(block):
        value = block.astype(F32)
        return (value * norm_scale(value) * gain_one).astype(BF)

    def key_value(b):
        block = normed(r.tok_all[b].reshape(rows, model))
        cosine, sine = turns(b)
        swapped = dot(block, w_kv_swapped) * sine[:, :256]
        swapped = jnp.concatenate([swapped, jnp.zeros((rows, wide - 256), F32)], axis=1)
        both = (dot(block, w_kv) * cosine + swapped).astype(BF)
        for m in micros:
            r.kv[m, b] = both[rows_of(m)]

    for g in get_sh:
        g.start()
    key_value(me)

    def key_values_of(blocks):
        def step(i, carry):
            b = sum([(i == k).astype(jnp.int32) * one for k, one in enumerate(blocks)])
            net.landed(r.tok_all.at[b, 1 - core], slot_tc + b)
            key_value(b)
            return carry

        lax.fori_loop(0, len(blocks), step, 0)

    for b in across[:2]:
        get_tok.land(b)
    key_values_of(column)
    for b in across[2:]:
        get_tok.land(b)
    for b in across[:2]:
        token_core(b)
    key_values_of(across[:2])
    for b in across[2:]:
        token_core(b)
    get_qo.finish()
    for g in get_sh:
        g.step(1)
    key_values_of(across[2:])
    r.n_one[...] = normed(r.tok[...])
    w_qo = r.w_qo[...].reshape(model, wide)
    cosine, sine = turns(me)
    cosine = jnp.where(is_left, cosine, 0.0)
    queries = dot(r.n_one[...], w_qo) * cosine
    queries = queries + dot(r.n_one[...], dot(w_qo, swap_low).astype(BF)) * sine
    queries = queries.astype(BF)
    for m in micros:
        send_c[m].start()
        send_h[m].start()

    first, last = slice(0, 256), slice(wide - 256, wide)
    head_of = iota((1, 256), 1) // HEAD
    q_masks = [head_of == h for h in range(heads)]
    v_masks = [head_of == heads + h - (wide - 256) // HEAD for h in range(heads)]
    blank = jnp.zeros((local, wide - 256), F32)

    def by_head(block, masks):
        return jnp.concatenate(
            [jnp.where(mask, block, jnp.zeros_like(block)) for mask in masks], axis=0
        )

    def join_heads(value, masks):
        total = jnp.zeros((local, 256), F32)
        for h, mask in enumerate(masks):
            total = total + jnp.where(mask, value[h * local : (h + 1) * local], 0.0)
        return total

    def o_half(h):
        return r.w_qo[pl.ds(h * (n // 2), n // 2)].reshape(half, wide)

    core_a = [Swap(net, r.core_a.at[m, 0], r.core_a.at[m, 1], net.other_core()) for m in micros]
    core_c = [Swap(net, r.core_c.at[m, 0], r.core_c.at[m, 1], net.other_core()) for m in micros]
    core_b = [
        Swap(net, r.core_b.at[2 * i], r.core_b.at[2 * i + 1], net.other_core()) for i in range(2)
    ]
    y_swap = [
        [Swap(net, r.y_swap.at[i, m, 0], r.y_swap.at[i, m, 1], net.across_y()) for m in micros]
        for i in range(4)
    ]
    share_a = [Share(net, r.share_a.at[m]) for m in micros]
    share_b = [Share(net, r.share_b.at[m]) for m in micros]
    share_c = [Share(net, r.share_c.at[m]) for m in micros]
    share_out = [Share(net, r.share_out.at[m]) for m in micros]

    score_scale = HEAD**-0.5
    for m in micros:
        r.q_rows[m] = by_head(queries[rows_of(m)][:, first], q_masks)
        key_rows = r.kv[m, :, :, first].reshape(tree, 256)
        value_rows = r.kv[m, :, :, last].reshape(tree, 256)
        ids = me * local + iota((stack, 1), 0) % local
        path, unused, unused_two = row_values(m, ids)
        key_ids = iota((1, tree), 1)
        unused, unused_two, key_seg = row_values(m, key_ids)
        seen = ((path & key_seg) != 0) & (key_ids <= ids)
        scores = dot_nt(r.q_rows[m], key_rows) * score_scale
        expo = jnp.where(seen, jnp.exp(scores), 0.0)
        r.expo[m] = expo
        total = jnp.sum(expo, axis=1, keepdims=True)
        r.total[m] = total
        mixed = join_heads(dot(expo.astype(BF), value_rows) / total, v_masks)
        r.mixed[m] = mixed
        r.mixed_low[rows_of(m)] = jnp.concatenate([blank, mixed], axis=1).astype(BF)
        core_a[m].start(dot_nt(r.mixed_low[rows_of(m)], o_half(1 - core)))
    for g in get_sh:
        g.step(2)
    for m in micros:
        mine = dot_nt(r.mixed_low[rows_of(m)], o_half(core))
        y_swap[0][m].start(mine + core_a[m].other())
    for m in micros:
        share_a[m].start(y_swap[0][m].both())

    send_x = [Dispatch(net, r.x_out.at[m], r.x_in.at[m]) for m in micros]
    scale_two = []
    for m in micros:
        res = r.tok[rows_of(m)].astype(F32) + share_a[m].finish()
        r.res[m] = res
        scale_two.append(norm_scale(res))
        normed_two = (res * scale_two[m] * gain_two).astype(BF)
        r.n_two[rows_of(m)] = normed_two
        r.x_out[m] = dot_tn(quarter[m], normed_two).astype(BF).reshape(n, part, model)
        send_x[m].start()

    for g in get_sh:
        g.step(3)
    for m in micros:
        send_c[m].relay_y()
    gates = []
    for m in micros:
        logits = dot_nt(r.n_two[rows_of(m)], ext_low)
        z_one = jnp.sum(jnp.where(hot_one[m], logits, 0.0), axis=1, keepdims=True)
        z_two = jnp.sum(jnp.where(hot_two[m], logits, 0.0), axis=1, keepdims=True)
        z_top = jnp.maximum(z_one, z_two)
        e_one, e_two = jnp.exp(z_one - z_top), jnp.exp(z_two - z_top)
        chosen = jnp.where(hot_one[m], e_one, jnp.where(hot_two[m], e_two, 0.0))
        gates.append(chosen / (e_one + e_two))

    for m in micros:
        send_x[m].relay_y()
    for g in get_sh:
        g.finish()

    def wide_half(i, h):
        return r.w_sh[i, pl.ds(h * (n // 2), n // 2)].reshape(half, shared)

    def shared_step(m, carry):
        here = pl.ds(pl.multiple_of(m * local, local), local)
        normed_two = r.n_two[here]
        shared_g = dot(normed_two, r.w_sh[0].reshape(model, shared))
        shared_u = dot(normed_two, r.w_sh[1].reshape(model, shared))
        act, slope = silu_both(shared_g)
        shared_h = (act * shared_u).astype(BF)
        grad_h = dot(r.cot[here], r.w_sh[2].reshape(model, shared))
        grad_g = (grad_h * shared_u * slope).astype(BF)
        grad_u = (grad_h * act).astype(BF)
        r.s_grads[0, here] = grad_g
        r.s_grads[1, here] = grad_u
        r.s_grads[2, here] = shared_h
        other, own = 1 - core, core
        back = dot_nt(grad_g, wide_half(0, other)) + dot_nt(grad_u, wide_half(1, other))
        r.core_b[0, here] = back.astype(BF)
        r.core_b[2, here] = dot_nt(shared_h, wide_half(2, other)).astype(BF)
        back = dot_nt(grad_g, wide_half(0, own)) + dot_nt(grad_u, wide_half(1, own))
        r.s_own[0, here] = back
        r.s_own[1, here] = dot_nt(shared_h, wide_half(2, own))
        return carry

    lax.fori_loop(0, micro, shared_step, 0)
    for swap_b in core_b:
        swap_b.send()
    for i, (rows_a, rows_b) in enumerate(((r.n_two, 0), (r.n_two, 1), (r.cot, 2))):
        grads = dot_tn(rows_a[...], r.s_grads[rows_b])
        r.sh_part[i] = grads.astype(BF).reshape(n, depth, shared)
    sum_sh = [
        Chain(net, lambda b, i=i: r.sh_part.at[i, b], r.sh_fx.at[i], r.sh_fz.at[i])
        for i in range(3)
    ]

    for m in micros:
        send_c[m].relay_core()
    for m in micros:
        send_x[m].relay_core()
    for m in micros:
        send_h[m].finish()
        send_c[m].finish()

    slot_gc = net.recv_slots(micro)
    slot_yc = net.recv_slots(micro)
    slot_yy = net.recv_slots(micro)
    slot_gy = net.recv_slots(micro)
    my_slots = pl.ds(pl.multiple_of(y * (cap // 2), cap // 2), cap // 2)
    far_slots = pl.ds(pl.multiple_of((1 - y) * (cap // 2), cap // 2), cap // 2)
    send_g = [
        Exchange(
            net,
            lambda b, m=m: r.g_core.at[m, b, my_slots],
            lambda b, m=m: r.g_in.at[m, b],
            r.g_in.at[m, 0 : n - 1],
        )
        for m in micros
    ]
    send_y = [
        Exchange(
            net,
            lambda b, m=m: r.y_core.at[m, b, my_slots],
            lambda b, m=m: r.y_in.at[m, b],
            r.y_in.at[m, 0 : n - 1],
        )
        for m in micros
    ]
    send_d = [
        Exchange(
            net,
            lambda b, m=m: r.d_out.at[m, b],
            lambda b, m=m: r.d_in.at[m, b],
            r.d_in.at[m, 0 : n - 1],
        )
        for m in micros
    ]
    slot_eye = eye[:cap]
    slot_line = iota((cap, 128), 0) == iota((cap, 128), 1)
    own_lane = iota((n * cap, 16), 1) - 8 == me
    group = 4
    halves = [slice(0, half), slice(half, model)]

    def expert_gates(m):
        x_rows = r.x_in[m].reshape(n * cap, model)
        z_all = dot_nt(x_rows, ext_low)
        hit = jnp.concatenate([dot_nt(slot_eye, r.h_in[m, b]) for b in range(n)], axis=0)
        z_own = jnp.sum(jnp.where(own_lane, z_all, 0.0), axis=1, keepdims=True)
        z_other = jnp.sum(jnp.where(own_lane, 0.0, z_all * hit), axis=1, keepdims=True)
        z_top = jnp.maximum(z_own, z_other)
        e_own, e_other = jnp.exp(z_own - z_top), jnp.exp(z_other - z_top)
        r.gate_col[m] = e_own / (e_own + e_other)

    def expert_rows(m, i):
        count = group * cap
        span = slice(i * group, (i + 1) * group)
        flat = slice(i * count, (i + 1) * count)
        x = r.x_in[m, span].reshape(count, model)
        c = r.c_in[m, span].reshape(count, model)
        gate = r.gate_col[m, flat]
        gate_pre = dot(x, r.eg[...])
        up_pre = dot(x, r.eu[...])
        act, slope = silu_both(gate_pre)
        hid = (act * up_pre).astype(BF)
        grad_y = (gate * c.astype(F32)).astype(BF)
        grad_hid = dot_nt(grad_y, r.ed[...])
        grad_g = (grad_hid * up_pre * slope).astype(BF)
        grad_u = (grad_hid * act).astype(BF)
        r.e_h[m, flat] = hid
        r.e_dg[m, flat] = grad_g
        r.e_du[m, flat] = grad_u
        dots = jnp.zeros((count, 1), F32)
        for cut in halves:
            out = dot(hid, r.ed[:, cut])
            r.tok_all[span, 0, m, :, cut] = out.astype(BF).reshape(group, cap, half)
            dots = dots + jnp.sum(out * c[:, cut].astype(F32), axis=1, keepdims=True)
            back = dot_nt(grad_g, r.eg[cut]) + dot_nt(grad_u, r.eu[cut])
            r.tok_all[span, 1, m, :, cut] = back.astype(BF).reshape(group, cap, half)
        r.c_in[m, span] = grad_y.reshape(group, 2, 2, part, model)
        for b in range(group):
            line = jnp.where(slot_line, dots[b * cap : (b + 1) * cap], 0.0)
            line = jnp.sum(line, axis=0, keepdims=True)
            r.d_out[m, i * group + b] = jnp.broadcast_to(line, (8, 128))

    def expert_sent(m):
        net.push(r.tok_all.at[:, 1, m, :, other_half], r.g_core.at[m], net.other_core(), slot_gc + m)
        net.push(r.tok_all.at[:, 0, m, :, other_half], r.y_core.at[m], net.other_core(), slot_yc + m)

    def add_g(m):
        net.landed(r.g_core.at[m], slot_gc + m)
        mine = r.tok_all[:, 1, m, :, my_half].astype(F32)
        r.g_core[m] = (mine + r.g_core[m].astype(F32)).astype(BF)
        net.push(r.g_core.at[m, :, far_slots], r.g_far.at[m], net.across_y(), slot_gy + m)

    def return_g(m):
        net.landed(r.g_far.at[m], slot_gy + m)
        both = r.g_core[m, :, my_slots].astype(F32) + r.g_far[m].astype(F32)
        r.g_core[m, :, my_slots] = both.astype(BF)
        send_g[m].start()
        send_d[m].start()
        r.g_in[m, me] = r.g_core[m, me, my_slots]
        r.d_in[m, me] = r.d_out[m, me]

    def add_y(m):
        net.landed(r.y_core.at[m], slot_yc + m)
        mine = r.tok_all[:, 0, m, :, my_half].astype(F32)
        r.y_core[m] = (mine + r.y_core[m].astype(F32)).astype(BF)
        net.push(r.y_core.at[m, :, far_slots], r.y_far.at[m], net.across_y(), slot_yy + m)

    def return_y(m):
        net.landed(r.y_far.at[m], slot_yy + m)
        both = r.y_core[m, :, my_slots].astype(F32) + r.y_far[m].astype(F32)
        r.y_core[m, :, my_slots] = both.astype(BF)
        send_y[m].start()
        r.y_in[m, me] = r.y_core[m, me, my_slots]

    saves = []

    def all_slots(ref, cut):
        return ref[..., cut].reshape(micro * n * cap, -1)

    def save(source, target, i):
        copy = pltpu.make_async_copy(source, target, r.save_sems.at[i])
        copy.start()
        saves.append(copy)

    def weight_grads(i):
        whole = slice(None)
        if i < 2:
            grads, target = ((r.e_dg, r.deg), (r.e_du, r.deu))[i]
            for h, cut in enumerate(halves):
                if i == 1:
                    saves[h].wait()
                r.stage[h] = dot_tn(all_slots(r.x_in, cut), all_slots(grads, whole))
                save(r.stage.at[h], target.at[cut], 2 * i + h)
        else:
            for h, cut in enumerate(halves):
                if h == 1:
                    saves[4].wait()
                r.stage_d[...] = dot_tn(all_slots(r.e_h, whole), all_slots(r.c_in, cut))
                save(r.stage_d, r.ded.at[:, cut], 4 + h)

    net.drain()
    sum_sh[0].start()
    sum_sh[1].start()
    for m in micros:
        send_x[m].finish()
        if m > 0:
            sum_sh[0].step(3)
        expert_gates(m)
        for i in range(n // group):
            if m > 0 and i == 1:
                add_g(m - 1)
                sum_sh[0].step(2)
            expert_rows(m, i)
        expert_sent(m)
    return_g(0)
    sum_sh[0].step(1)
    weight_grads(0)
    add_g(1)
    weight_grads(1)
    return_g(1)
    sum_sh[2].start()
    sum_sh[1].step(3)
    weight_grads(2)
    sum_sh[1].step(2)

    for m in micros:
        add_y(m)
    d_core = [Swap(net, r.d_tensor.at[m, 0], r.d_tensor.at[m, 1], net.other_core()) for m in micros]
    d_y = [Swap(net, r.d_tensor.at[m, 2], r.d_tensor.at[m, 3], net.across_y()) for m in micros]
    eight = iota((8, 128), 0)
    d_rows = []
    for m in micros:
        send_d[m].finish()
        line = jnp.zeros((8, 128), F32)
        for b in range(n):
            line = line + jnp.where(eight == b, r.d_in[m, b], 0.0)
        d_rows.append(line)
        d_core[m].start(line)
    shared_grad = r.s_own[0] + core_b[0].other()
    for m in micros:
        d_y[m].start(d_rows[m] + d_core[m].other())
    for m in micros:
        send_g[m].finish()
        moe_grad = dot(r.choice_half[m], r.g_in[m].reshape(n * cap // 2, half))
        y_swap[1][m].start(moe_grad + shared_grad[rows_of(m)])
    net.drain(bulk=False)
    sum_sh[1].step(1)
    grad_logits = []
    for m in micros:
        d_all = d_y[m].both()
        grad_gate = jnp.zeros((local, 16), F32)
        for b in range(n):
            picked = r.choice_wide[m, :, b * 128 : (b + 1) * 128].astype(F32) * d_all[b : b + 1]
            grad_gate = jnp.where(lane == b, jnp.sum(picked, axis=1, keepdims=True), grad_gate)
        inner = jnp.sum(gates[m] * grad_gate, axis=1, keepdims=True)
        grad_logits.append((gates[m] * (grad_gate - inner)).astype(BF))
        share_b[m].start(y_swap[1][m].both())


    kv_sums, grad_queries, gain_rows = [], [], []
    for m in micros:
        grad_two = share_b[m].finish() + dot(grad_logits[m], ext_low)
        res = r.res[m]
        cot = r.cot[rows_of(m)].astype(F32)
        grad_res = cot + norm_back(grad_two, res, scale_two[m], gain_two)
        r.gtok[rows_of(m)] = grad_res
        gain_rows.append(jnp.sum(grad_two * res * scale_two[m], axis=0, keepdims=True))
        key_rows = r.kv[m, :, :, first].reshape(tree, 256)
        value_rows = r.kv[m, :, :, last].reshape(tree, 256)
        total = r.total[m]
        gm = by_head(dot(grad_res.astype(BF), r.w_qo[:, :, last].reshape(model, 256)), v_masks)
        mixed = jnp.concatenate([r.mixed[m]] * heads, axis=0)
        delta = jnp.sum(gm * mixed, axis=1, keepdims=True) / total
        grad_summed = (gm / total).astype(BF)
        expo = r.expo[m]
        ds = (expo * (dot_nt(grad_summed, value_rows) - delta)).astype(BF)
        grad_k = dot_tn(ds, r.q_rows[m]) * score_scale
        grad_v = dot_tn(expo.astype(BF), grad_summed)
        over = 512 - wide
        middle = grad_k[:, 256 - over :] + grad_v[:, :over]
        grad_kv = jnp.concatenate([grad_k[:, : 256 - over], middle, grad_v[:, over:]], axis=1)
        r.kv_part[m] = grad_kv.astype(BF).reshape(n, local, wide)
        for k in range(2):
            span = slice(k * (local // 2), (k + 1) * (local // 2))
            one = Scatter(
                net,
                lambda b, m=m, span=span: r.kv_part.at[m, b, span],
                r.kv_fx.at[m, k],
                r.kv_fz.at[m, k],
            )
            one.start()
            kv_sums.append(one)
        if m == 0:
            for k in micros:
                return_y(k)
        grad_query = join_heads(dot(ds, key_rows), q_masks) * score_scale
        grad_queries.append(jnp.concatenate([grad_query, blank], axis=1))

    cosine, sine = turns(me)

    def turned_back(grad):
        return (grad * cosine - dot(grad, swap, EXACT) * sine).astype(BF)

    for one in kv_sums:
        one.forward()
    sum_sh[2].step(3)
    grad_q = turned_back(jnp.concatenate(grad_queries, axis=0))
    grad_attn = r.gtok[...].astype(BF)
    part_qo = dot_tn(r.n_one[...], grad_q) + dot_tn(grad_attn, r.mixed_low[...])
    r.w_part[0] = part_qo.astype(BF).reshape(n, depth, wide)
    sum_w = [
        Scatter(net, lambda b, i=i: r.w_part.at[i, b], r.w_fx.at[i], r.w_fz.at[i])
        for i in range(2)
    ]
    sum_w[0].start()

    shared_y = r.s_own[1] + core_b[1].other()
    for m in micros:
        send_y[m].finish()
        gate_wide = dot(gates[m], spread(cap // 2).astype(F32), EXACT)
        gate_high = gate_wide.astype(BF).astype(F32)
        pick = r.choice_half[m].astype(F32)
        y_rows = r.y_in[m].reshape(n * cap // 2, half)
        moe_y = dot((pick * gate_high).astype(BF), y_rows)
        moe_y = moe_y + dot((pick * (gate_wide - gate_high)).astype(BF), y_rows)
        y_swap[2][m].start(moe_y + shared_y[rows_of(m)])
    sum_sh[2].step(2)

    def weight_half(ref, h):
        return ref[pl.ds(h * (n // 2), n // 2)].reshape(half, wide)

    grad_kvs = []
    for m in micros:
        total = jnp.concatenate([one.finish() for one in kv_sums[2 * m : 2 * m + 2]], axis=0)
        cos_m, sin_m = cosine[rows_of(m)], sine[rows_of(m)]
        grad_kv = (total * cos_m - dot(total, swap, EXACT) * sin_m).astype(BF)
        grad_kvs.append(grad_kv)
        q_m = grad_q[rows_of(m)]
        other = dot_nt(q_m, weight_half(r.w_qo, 1 - core))
        core_c[m].start(other + dot_nt(grad_kv, weight_half(r.w_kv, 1 - core)))
    for m in micros:
        mine = dot_nt(grad_q[rows_of(m)], weight_half(r.w_qo, core))
        mine = mine + dot_nt(grad_kvs[m], weight_half(r.w_kv, core))
        y_swap[3][m].start(mine + core_c[m].other())
    part_kv = dot_tn(r.n_one[...], jnp.concatenate(grad_kvs, axis=0))
    r.w_part[1] = part_kv.astype(BF).reshape(n, depth, wide)
    sum_w[1].start()
    sum_w[0].forward()
    sum_sh[2].step(1)
    for m in micros:
        share_c[m].start(y_swap[3][m].both())
    for m in micros:
        res_half = jnp.where(core == 0, r.res[m, :, :half], r.res[m, :, half:])
        share_out[m].start(res_half + y_swap[2][m].both())
    sum_w[1].forward()

    gain_one_row = jnp.zeros((1, model), F32)
    for m in micros:
        grad_one = share_c[m].finish()
        tok = r.tok[rows_of(m)].astype(F32)
        scale_one = norm_scale(tok)
        r.gtok[rows_of(m)] += norm_back(grad_one, tok, scale_one, gain_one)
        gain_one_row = gain_one_row + jnp.sum(grad_one * tok * scale_one, axis=0, keepdims=True)
    grad_router = jnp.zeros((16, model), F32)
    for m in micros:
        grad_router = grad_router + dot_tn(grad_logits[m], r.n_two[rows_of(m)])
    line = iota((16, model), 0)
    small = jnp.where(line == 0, gain_one_row, grad_router)
    small = jnp.where(line == 1, gain_rows[0] + gain_rows[1], small)
    high_part = small.astype(BF)
    low_part = (small - high_part.astype(F32)).astype(BF)
    for b in range(n):
        place = lay(b).astype(BF)
        r.gains_out[b] = dot_nt(high_part, place) + dot_nt(low_part, place)
    send_gains = Exchange(
        net, lambda b: r.gains_out.at[b], lambda b: r.gains_in.at[b], r.gains_in.at[0 : n - 1]
    )
    send_gains.start()
    r.gains_in[me] = r.gains_out[me]
    for m in micros:
        r.out[rows_of(m)] = share_out[m].finish()

    qo = sum_w[0].finish()
    r.dwq[...] = qo[:, :width]
    depth_eye = (iota((depth, depth), 0) == iota((depth, depth), 1)).astype(F32)
    r.dwo[...] = dot_tn(qo[:, width:], depth_eye, EXACT)
    kv = sum_w[1].finish()
    r.dwk[...] = kv[:, :width]
    r.dwv[...] = kv[:, width:]
    for i, target in enumerate((r.dsg, r.dsu, r.dsd)):
        sum_sh[i].finish(target)
    send_gains.finish()
    gains = jnp.zeros((16, 128), F32)
    for b in range(n):
        gains = gains + r.gains_in[b]
    r.dga[...] = gains[0:1, :depth]
    r.dgb[...] = gains[1:2, :depth]
    r.drouter[...] = gains[8:16, :depth]
    for copy in saves[2:4] + saves[5:]:
        copy.wait()
    net.drain()


def settle_kernel(count, *refs):
    sources, targets, stops = refs[:count], refs[count : 2 * count], refs[2 * count : 3 * count]
    sems = refs[3 * count]
    reads = [
        pltpu.make_async_copy(a, b, sems.at[0, i]) for i, (a, b) in enumerate(zip(sources, stops))
    ]
    writes = [
        pltpu.make_async_copy(a, b, sems.at[1, i]) for i, (a, b) in enumerate(zip(stops, targets))
    ]
    for read in reads:
        read.start()
    for read, write in zip(reads, writes):
        read.wait()
        write.start()
    for write in writes:
        write.wait()


def fits(mesh):
    return mesh.shape["expert"] == 8 and mesh.shape["tensor"] == 4


def fused_body(
    tokens,
    out_grad,
    routes,
    lengths,
    parents,
    attn_gain,
    ffn_gain,
    w_query,
    w_key,
    w_value,
    w_out,
    router,
    shared_gate,
    shared_up,
    shared_down,
    expert_gate,
    expert_up,
    expert_down,
):
    micro, local, model = tokens.shape
    n = lax.axis_size("expert")
    experts = router.shape[1]
    depth, width = w_query.shape
    hidden, shared = expert_gate.shape[2], shared_gate.shape[1]
    s = types.SimpleNamespace(
        n=n,
        micro=micro,
        local=local,
        half=model // 2,
        depth=depth,
        width=width,
        heads=width // HEAD,
        hidden=hidden,
        shared=shared,
        cap=4 * local // experts,
        segs=lengths.shape[1],
    )
    rows = micro * local
    scratch = scratch_shapes(s)
    names = PLACES + RESULTS + list(scratch)
    shape = jax.ShapeDtypeStruct
    vmem, smem = pl.BlockSpec(memory_space=pltpu.VMEM), pl.BlockSpec(memory_space=pltpu.SMEM)
    hbm = pl.BlockSpec(memory_space=pl.ANY)
    results = (
        shape((rows, model), BF),
        shape((rows, model), F32),
        shape((1, depth), F32),
        shape((1, depth), F32),
        shape((depth, width), F32),
        shape((depth, width), F32),
        shape((depth, width), F32),
        shape((width, depth), F32),
        shape((experts, depth), F32),
        shape((depth, shared), F32),
        shape((depth, shared), F32),
        shape((depth, shared), F32),
        shape((model, hidden), F32),
        shape((model, hidden), F32),
        shape((hidden, model), F32),
    )
    found = pl.pallas_call(
        functools.partial(layer_kernel, s, names),
        out_shape=results,
        in_specs=[vmem] * 3 + [smem] * 2 + [vmem] * 13,
        out_specs=[vmem] * 12 + [hbm] * 3,
        scratch_shapes=list(scratch.values()),
        compiler_params=pltpu.CompilerParams(
            collective_id=0, has_side_effects=True, vmem_limit_bytes=VMEM_LIMIT
        ),
    )(
        tokens.reshape(rows, model),
        out_grad.reshape(rows, model),
        routes.transpose(0, 2, 1).reshape(2 * micro, local),
        lengths,
        parents,
        attn_gain.reshape(1, depth),
        ffn_gain.reshape(1, depth),
        w_query,
        w_key,
        w_value,
        w_out,
        router.T,
        shared_gate,
        shared_up,
        shared_down.T,
        expert_gate[0],
        expert_up[0],
        expert_down[0],
    )
    settled = pl.pallas_call(
        functools.partial(settle_kernel, len(results)),
        out_shape=results,
        in_specs=[hbm] * len(results),
        out_specs=[hbm] * len(results),
        scratch_shapes=[pltpu.VMEM(one.shape, one.dtype) for one in results]
        + [pltpu.SemaphoreType.DMA((2, len(results)))],
        compiler_params=pltpu.CompilerParams(vmem_limit_bytes=VMEM_LIMIT),
    )(*found)
    out, gtok, dga, dgb, dwq, dwk, dwv, dwo, drouter, dsg, dsu, dsd, deg, deu, ded = settled
    return (
        out.reshape(micro, local, model),
        gtok.reshape(micro, local, model),
        dga.reshape(depth),
        dgb.reshape(depth),
        dwq,
        dwk,
        dwv,
        dwo,
        drouter.T,
        dsg,
        dsu,
        dsd.T,
        deg[None],
        deu[None],
        ded[None],
    )


def solution(mesh):
    in_specs = (
        P(None, "expert", None),
        P(None, "expert", None),
        P(None, "expert", None),
        P(),
        P(),
        P("expert"),
        P("expert"),
        P("expert", "tensor"),
        P("expert", "tensor"),
        P("expert", "tensor"),
        P("tensor", "expert"),
        P("expert", None),
        P("expert", "tensor"),
        P("expert", "tensor"),
        P("tensor", "expert"),
        P("expert", None, "tensor"),
        P("expert", None, "tensor"),
        P("expert", "tensor", None),
    )
    out_specs = (
        P(None, "expert", None),
        P(None, "expert", None),
        P("expert"),
        P("expert"),
        P("expert", "tensor"),
        P("expert", "tensor"),
        P("expert", "tensor"),
        P("tensor", "expert"),
        P("expert", None),
        P("expert", "tensor"),
        P("expert", "tensor"),
        P("tensor", "expert"),
        P("expert", None, "tensor"),
        P("expert", None, "tensor"),
        P("expert", "tensor", None),
    )
    chosen = fused_body if fits(mesh) else plain_body
    return jax.shard_map(chosen, mesh=mesh, in_specs=in_specs, out_specs=out_specs, check_vma=False)
```

```python
import functools
import math
import types

import jax
import jax.numpy as jnp
from jax import lax
from jax.experimental import pallas as pl
from jax.experimental.pallas import tpu as pltpu
from jax.sharding import PartitionSpec as P

HEAD = 64


EPSILON = 1e-06
ROPE_BASE = 10000.0
KEY_BLOCK = 2048


def matmul(left, right):
    return jnp.dot(left, right, preferred_element_type=jnp.float32)


def tree_tables(lengths, parents):
    seg_count = lengths.shape[0]
    identity = jnp.arange(seg_count, dtype=jnp.int32)
    current = identity
    ancestry = jnp.zeros((seg_count, seg_count), jnp.float32)
    for depth_level in range(seg_count):
        chosen_mask = current[:, None] == identity[None, :]
        ancestry = jnp.maximum(ancestry, chosen_mask.astype(jnp.float32))
        current = jnp.sum(jnp.where(chosen_mask, parents[None, :], 0), axis=1)
    seg_ends = jnp.cumsum(lengths)
    starts = seg_ends - lengths
    sizes_float = lengths.astype(jnp.float32)
    offsets = jnp.sum(ancestry * sizes_float[None, :], axis=1) - sizes_float
    return (ancestry, starts, seg_ends, offsets)


def row_tables(row_ids, starts, seg_ends, offsets):
    member = (
        (row_ids[:, None] >= starts[None, :]) & (row_ids[:, None] < seg_ends[None, :])
    ).astype(jnp.float32)
    position_shift = offsets - starts.astype(jnp.float32)
    position = jnp.sum(member * position_shift[None, :], axis=1) + row_ids.astype(jnp.float32)
    return (member, position)


def rotary_tables(position, half_width):
    frequency = ROPE_BASE ** (-jnp.arange(half_width, dtype=jnp.float32) / half_width)
    angles = position[:, None] * frequency[None, :]
    return (jnp.cos(angles)[:, None, :], jnp.sin(angles)[:, None, :])


def rotate(head_values, position):
    half_width = head_values.shape[-1] // 2
    cosines, sine_values = rotary_tables(position, half_width)
    first_half = head_values[..., :half_width]
    second_half = head_values[..., half_width:]
    return jnp.concatenate(
        [
            first_half * cosines - second_half * sine_values,
            second_half * cosines + first_half * sine_values,
        ],
        axis=-1,
    )


def rotate_back(grad_heads, position):
    half_width = grad_heads.shape[-1] // 2
    cosines, sine_values = rotary_tables(position, half_width)
    first_half = grad_heads[..., :half_width]
    second_half = grad_heads[..., half_width:]
    return jnp.concatenate(
        [
            first_half * cosines + second_half * sine_values,
            second_half * cosines - first_half * sine_values,
        ],
        axis=-1,
    )


def silu_parts(gate_val):
    sigmoid_val = jax.nn.sigmoid(gate_val)
    return (gate_val * sigmoid_val, sigmoid_val * (1.0 + gate_val * (1.0 - sigmoid_val)))


def rms_back(grad_normed, source, norm_scale, gain):
    weighted = grad_normed * gain
    inner_mean = jnp.mean(weighted * source, axis=1, keepdims=True)
    return (
        norm_scale * weighted - norm_scale**3 * source * inner_mean,
        jnp.sum(grad_normed * source * norm_scale, axis=0),
    )


def visible(reach_rows, query_ids, key_member, key_ids):
    linked = matmul(reach_rows, key_member.T) > 0.5
    return linked & (key_ids[None, :] <= query_ids[:, None])


def score_block(query_heads, key_heads, seen, score_scale):
    scores = (
        jnp.einsum("qhd,khd->hqk", query_heads, key_heads, preferred_element_type=jnp.float32)
        * score_scale
    )
    return jnp.where(seen[None], jnp.exp(scores), 0.0)


def score_grads(weights_exp, grad_summed, value_heads, delta_rows):
    grad_exp = jnp.einsum(
        "qhd,khd->hqk", grad_summed, value_heads, preferred_element_type=jnp.float32
    )
    return (weights_exp * (grad_exp - jnp.transpose(delta_rows)[:, :, None])).astype(jnp.bfloat16)


def plain_body(
    tokens,
    out_grad,
    routes,
    lengths,
    parents,
    attn_gain,
    ffn_gain,
    w_query,
    w_key,
    w_value,
    w_out,
    router,
    shared_gate,
    shared_up,
    shared_down,
    expert_gate,
    expert_up,
    expert_down,
):
    micro_count, row_count, model_width = tokens.shape
    devices = lax.axis_size("expert")
    tree_rows = row_count * devices
    expert_count = router.shape[1]
    owners = devices // expert_count
    capacity = 4 * row_count // expert_count
    score_scale = HEAD ** (-0.5)
    local_rows = lax.axis_index("expert") * row_count + jnp.arange(row_count, dtype=jnp.int32)
    part_gate = expert_gate[0]
    part_up = expert_up[0]
    part_down = expert_down[0]
    labels = jnp.arange(expert_count, dtype=jnp.int32)
    slot_ids = jnp.arange(expert_count * capacity, dtype=jnp.int32)
    pair_ids = jnp.arange(2 * row_count, dtype=jnp.int32)
    block_size = math.gcd(tree_rows, KEY_BLOCK)
    block_count = tree_rows // block_size
    layer_outputs = []
    token_gradients = []
    dense_sums = None
    expert_sums = None
    for micro_step in range(micro_count):
        gathered = (
            lax.all_gather(attn_gain, "expert", axis=0, tiled=True),
            lax.all_gather(ffn_gain, "expert", axis=0, tiled=True),
            lax.all_gather(w_query, "expert", axis=0, tiled=True),
            lax.all_gather(w_key, "expert", axis=0, tiled=True),
            lax.all_gather(w_value, "expert", axis=0, tiled=True),
            lax.all_gather(w_out, "expert", axis=1, tiled=True),
            lax.all_gather(router, "expert", axis=0, tiled=True),
            lax.all_gather(shared_gate, "expert", axis=0, tiled=True),
            lax.all_gather(shared_up, "expert", axis=0, tiled=True),
            lax.all_gather(shared_down, "expert", axis=1, tiled=True),
        )
        (
            gain_one,
            gain_two,
            query_weight,
            key_weight,
            value_weight,
            out_weight,
            router_weight,
            gate_weight,
            up_weight,
            down_weight,
        ) = gathered
        local_width = query_weight.shape[1]
        head_count = local_width // HEAD
        ancestry, starts, seg_ends, offsets = tree_tables(lengths[micro_step], parents[micro_step])
        member, position = row_tables(local_rows, starts, seg_ends, offsets)
        reach = matmul(member, ancestry)
        tokens_now = tokens[micro_step].astype(jnp.float32)
        norm_one = lax.rsqrt(jnp.mean(tokens_now * tokens_now, axis=1, keepdims=True) + EPSILON)
        normed_one = (tokens_now * norm_one * gain_one).astype(jnp.bfloat16)
        query_pre = matmul(normed_one, query_weight).reshape(row_count, head_count, HEAD)
        key_pre = matmul(normed_one, key_weight).reshape(row_count, head_count, HEAD)
        value_low = matmul(normed_one, value_weight).astype(jnp.bfloat16)
        queries = rotate(query_pre, position).astype(jnp.bfloat16)
        key_heads = rotate(key_pre, position).astype(jnp.bfloat16)
        key_value = jnp.concatenate([key_heads.reshape(row_count, local_width), value_low], axis=1)
        all_pairs = lax.all_gather(key_value, "expert", axis=0, tiled=True)

        def key_block_parts(block_index):
            first_key = block_index * block_size
            key_block = lax.dynamic_slice_in_dim(all_pairs, first_key, block_size, 0)
            key_ids = first_key + jnp.arange(block_size, dtype=jnp.int32)
            key_member, unused = row_tables(key_ids, starts, seg_ends, offsets)
            seen = visible(reach, local_rows, key_member, key_ids)
            block_keys = key_block[:, :local_width].reshape(block_size, head_count, HEAD)
            block_values = key_block[:, local_width:].reshape(block_size, head_count, HEAD)
            return (seen, block_keys, block_values)

        def forward_step(block_index, totals):
            seen, block_keys, block_values = key_block_parts(block_index)
            weights_exp = score_block(queries, block_keys, seen, score_scale)
            summed_part = jnp.einsum(
                "hqk,khd->qhd",
                weights_exp.astype(jnp.bfloat16),
                block_values,
                preferred_element_type=jnp.float32,
            )
            return (
                totals[0] + summed_part.reshape(row_count, local_width),
                totals[1] + jnp.transpose(jnp.sum(weights_exp, axis=2)),
            )

        initial = (
            jnp.zeros((row_count, local_width), jnp.float32),
            jnp.zeros((row_count, head_count), jnp.float32),
        )
        summed, row_total = lax.fori_loop(0, block_count, forward_step, initial)
        mixed = summed.reshape(row_count, head_count, HEAD) / row_total[:, :, None]
        mixed_low = mixed.reshape(row_count, local_width).astype(jnp.bfloat16)
        attn_out = lax.psum(matmul(mixed_low, out_weight), "tensor")
        residual = tokens_now + attn_out
        norm_two = lax.rsqrt(jnp.mean(residual * residual, axis=1, keepdims=True) + EPSILON)
        normed_two = (residual * norm_two * gain_two).astype(jnp.bfloat16)
        shared_g = matmul(normed_two, gate_weight)
        shared_u = matmul(normed_two, up_weight)
        shared_act, shared_slope = silu_parts(shared_g)
        shared_h = (shared_act * shared_u).astype(jnp.bfloat16)
        shared_y = matmul(shared_h, down_weight)
        logits = matmul(normed_two, router_weight)
        route_now = routes[micro_step]
        choose = (route_now[:, :, None] == labels[None, None, :]).astype(jnp.float32)
        gate_values = jax.nn.softmax(jnp.sum(choose * logits[:, None, :], axis=2), axis=1)
        flat_routes = route_now.reshape(2 * row_count)
        expert_hits = (flat_routes[:, None] == labels[None, :]).astype(jnp.int32)
        slot_rank = jnp.sum((jnp.cumsum(expert_hits, axis=0) - expert_hits) * expert_hits, axis=1)
        slot_index = flat_routes * capacity + slot_rank
        slot_match = slot_index[None, :] == slot_ids[:, None]
        filled = jnp.any(slot_match, axis=1)
        source = jnp.sum(jnp.where(slot_match, pair_ids[None, :], 0), axis=1)

        def to_owners(table, row_index):
            picked = jnp.take(table, row_index, axis=0)
            picked = jnp.where(filled[:, None], picked, jnp.zeros_like(picked))
            spread = jnp.broadcast_to(
                picked.reshape(expert_count, 1, capacity, model_width),
                (expert_count, owners, capacity, model_width),
            )
            return spread.reshape(devices, capacity, model_width)

        def from_owners(returned):
            merged = jnp.sum(
                returned.reshape(expert_count, owners, capacity, model_width), axis=1
            ).reshape(expert_count * capacity, model_width)
            return jnp.take(merged, slot_index, axis=0).reshape(row_count, 2, model_width)

        arrived = lax.all_to_all(
            to_owners(normed_two, source // 2), "expert", split_axis=0, concat_axis=0, tiled=True
        )
        slot_count = arrived.shape[1]
        flat_in = arrived.reshape(devices * slot_count, model_width)
        expert_g = matmul(flat_in, part_gate)
        expert_u = matmul(flat_in, part_up)
        expert_act, expert_unused = silu_parts(expert_g)
        expert_h = (expert_act * expert_u).astype(jnp.bfloat16)
        partial_out = matmul(expert_h, part_down).reshape(devices, slot_count, model_width)
        combined = lax.all_to_all(
            partial_out.astype(jnp.bfloat16), "expert", split_axis=0, concat_axis=0, tiled=True
        ).astype(partial_out.dtype)
        hidden_width = expert_g.shape[1]
        combined, arrived, kept_g, kept_u, kept_h = (
            combined,
            arrived,
            expert_g.reshape(devices, slot_count, hidden_width),
            expert_u.reshape(devices, slot_count, hidden_width),
            expert_h.reshape(devices, slot_count, hidden_width),
        )
        expert_y = from_owners(combined)
        cot_low = out_grad[micro_step]
        cotangent = cot_low.astype(jnp.float32)
        moe_part = jnp.sum(gate_values[:, :, None] * expert_y, axis=1)
        gate_dots = jnp.sum(cotangent[:, None, :] * expert_y, axis=2)
        ffn_out, grad_gate = (
            lax.psum((shared_y + moe_part).astype(jnp.bfloat16), "tensor").astype(jnp.float32),
            lax.psum(gate_dots.astype(jnp.bfloat16), "tensor").astype(jnp.float32),
        )
        layer_outputs.append((residual + ffn_out).astype(jnp.bfloat16))
        grad_shared_h = matmul(cot_low, down_weight.T)
        grad_shared_g = (grad_shared_h * shared_u * shared_slope).astype(jnp.bfloat16)
        grad_shared_u = (grad_shared_h * shared_act).astype(jnp.bfloat16)
        grad_chosen = gate_values * (
            grad_gate - jnp.sum(gate_values * grad_gate, axis=1, keepdims=True)
        )
        grad_logits = jnp.sum(choose * grad_chosen[:, :, None], axis=1).astype(jnp.bfloat16)
        grad_pairs_out = (
            (gate_values[:, :, None] * cotangent[:, None, :])
            .astype(jnp.bfloat16)
            .reshape(2 * row_count, model_width)
        )
        arrived_grad = lax.all_to_all(
            to_owners(grad_pairs_out, source), "expert", split_axis=0, concat_axis=0, tiled=True
        )
        slot_total = arrived_grad.shape[0] * arrived_grad.shape[1]
        flat_grad = arrived_grad.reshape(slot_total, model_width)
        flat_in = arrived.reshape(slot_total, model_width)
        hidden_width = kept_g.shape[2]
        expert_g = kept_g.reshape(slot_total, hidden_width)
        expert_u = kept_u.reshape(slot_total, hidden_width)
        expert_h = kept_h.reshape(slot_total, hidden_width)
        expert_act, expert_slope = silu_parts(expert_g)
        grad_hidden = matmul(flat_grad, part_down.T)
        grad_expert_g = (grad_hidden * expert_u * expert_slope).astype(jnp.bfloat16)
        grad_expert_u = (grad_hidden * expert_act).astype(jnp.bfloat16)
        grad_in = matmul(grad_expert_g, part_gate.T) + matmul(grad_expert_u, part_up.T)
        returned = lax.all_to_all(
            grad_in.reshape(arrived_grad.shape[0], arrived_grad.shape[1], model_width),
            "expert",
            split_axis=0,
            concat_axis=0,
            tiled=True,
        )
        normed_part = (
            matmul(grad_shared_g, gate_weight.T)
            + matmul(grad_shared_u, up_weight.T)
            + jnp.sum(from_owners(returned), axis=1)
        )
        grad_normed_two = lax.psum(normed_part, "tensor") + matmul(grad_logits, router_weight.T)
        grad_norm_part, grad_gain_two = rms_back(grad_normed_two, residual, norm_two, gain_two)
        grad_residual = cotangent + grad_norm_part
        grad_attn = grad_residual.astype(jnp.bfloat16)
        grad_mixed = matmul(grad_attn, out_weight.T).reshape(row_count, head_count, HEAD)
        grad_summed = (grad_mixed / row_total[:, :, None]).astype(jnp.bfloat16)
        delta_rows = jnp.sum(grad_mixed * mixed, axis=2) / row_total

        def block_terms(block_index):
            seen, block_keys, block_values = key_block_parts(block_index)
            weights_exp = score_block(queries, block_keys, seen, score_scale)
            grad_scores = score_grads(weights_exp, grad_summed, block_values, delta_rows)
            return (weights_exp, grad_scores, block_keys)

        zero_query = jnp.zeros((row_count, head_count, HEAD), jnp.float32)

        def key_step(gradient_query_weight, block_index):
            weights_exp, grad_scores, block_keys = block_terms(block_index)
            gradient_query_weight = (
                gradient_query_weight
                + jnp.einsum(
                    "hqk,khd->qhd", grad_scores, block_keys, preferred_element_type=jnp.float32
                )
                * score_scale
            )
            grad_keys = (
                jnp.einsum("hqk,qhd->khd", grad_scores, queries, preferred_element_type=jnp.float32)
                * score_scale
            )
            grad_values = jnp.einsum(
                "hqk,qhd->khd",
                weights_exp.astype(jnp.bfloat16),
                grad_summed,
                preferred_element_type=jnp.float32,
            )
            return (
                gradient_query_weight,
                jnp.concatenate(
                    [
                        grad_keys.reshape(block_size, local_width),
                        grad_values.reshape(block_size, local_width),
                    ],
                    axis=1,
                ),
            )

        gradient_query_weight, key_terms = lax.scan(
            key_step, zero_query, jnp.arange(block_count, dtype=jnp.int32)
        )
        grad_pairs = lax.psum_scatter(
            key_terms.reshape(tree_rows, 2 * local_width), "expert", scatter_dimension=0, tiled=True
        )
        grad_keys_rot = grad_pairs[:, :local_width].reshape(row_count, head_count, HEAD)
        grad_query_pre = (
            rotate_back(gradient_query_weight, position)
            .reshape(row_count, local_width)
            .astype(jnp.bfloat16)
        )
        grad_key_pre = (
            rotate_back(grad_keys_rot, position)
            .reshape(row_count, local_width)
            .astype(jnp.bfloat16)
        )
        grad_value_low = grad_pairs[:, local_width:].astype(jnp.bfloat16)
        normed_grad = (
            matmul(grad_query_pre, query_weight.T)
            + matmul(grad_key_pre, key_weight.T)
            + matmul(grad_value_low, value_weight.T)
        )
        grad_normed_one = lax.psum(normed_grad.astype(jnp.bfloat16), "tensor").astype(jnp.float32)
        grad_norm_first, grad_gain_one = rms_back(grad_normed_one, tokens_now, norm_one, gain_one)
        token_gradients.append(grad_residual + grad_norm_first)
        dense_step = (
            grad_gain_one,
            grad_gain_two,
            matmul(normed_one.T, grad_query_pre),
            matmul(normed_one.T, grad_key_pre),
            matmul(normed_one.T, grad_value_low),
            matmul(mixed_low.T, grad_attn),
            matmul(normed_two.T, grad_logits),
            matmul(normed_two.T, grad_shared_g),
            matmul(normed_two.T, grad_shared_u),
            matmul(shared_h.T, cot_low),
        )
        expert_step = (
            matmul(flat_in.T, grad_expert_g),
            matmul(flat_in.T, grad_expert_u),
            matmul(expert_h.T, flat_grad),
        )
        if dense_sums is None:
            dense_sums = dense_step
            expert_sums = expert_step
        else:
            dense_sums = tuple(
                (earlier + latest for earlier, latest in zip(dense_sums, dense_step))
            )
            expert_sums = tuple(
                (earlier + latest for earlier, latest in zip(expert_sums, expert_step))
            )
    final_gate, final_up, final_down = expert_sums
    reduced = (
        lax.psum_scatter(dense_sums[0], "expert", scatter_dimension=0, tiled=True),
        lax.psum_scatter(dense_sums[1], "expert", scatter_dimension=0, tiled=True),
        lax.psum_scatter(dense_sums[2], "expert", scatter_dimension=0, tiled=True),
        lax.psum_scatter(dense_sums[3], "expert", scatter_dimension=0, tiled=True),
        lax.psum_scatter(dense_sums[4], "expert", scatter_dimension=0, tiled=True),
        lax.psum_scatter(dense_sums[5], "expert", scatter_dimension=1, tiled=True),
        lax.psum_scatter(dense_sums[6], "expert", scatter_dimension=0, tiled=True),
        lax.psum_scatter(dense_sums[7], "expert", scatter_dimension=0, tiled=True),
        lax.psum_scatter(dense_sums[8], "expert", scatter_dimension=0, tiled=True),
        lax.psum_scatter(dense_sums[9], "expert", scatter_dimension=1, tiled=True),
    )
    return (
        jnp.stack(layer_outputs),
        jnp.stack(token_gradients),
        reduced[0],
        reduced[1],
        reduced[2],
        reduced[3],
        reduced[4],
        reduced[5],
        reduced[6],
        reduced[7],
        reduced[8],
        reduced[9],
        final_gate[None],
        final_up[None],
        final_down[None],
    )


MESH = pl.DeviceIdType.MESH
BF = jnp.bfloat16
F32 = jnp.float32
EXACT = lax.Precision.HIGHEST
VMEM_LIMIT = 63 * 2**20


def product(left, right, dims, precision=None):
    return lax.dot_general(
        left, right, (dims, ((), ())), preferred_element_type=F32, precision=precision
    )


def dot(left, right, precision=None):
    return product(left, right, ((1,), (0,)), precision)


def dot_nt(left, right, precision=None):
    return product(left, right, ((1,), (1,)), precision)


def dot_tn(left, right, precision=None):
    return product(left, right, ((0,), (0,)), precision)


def iota(shape, dim):
    return lax.broadcasted_iota(jnp.int32, shape, dim)


class Net:
    def __init__(self, expert_size, send_sems, recv_sems):
        self.e = lax.axis_index("expert")
        self.t = lax.axis_index("tensor")
        self.n = expert_size
        self.nz = expert_size // 2
        self.z = self.e // 2
        self.x = self.e % 2
        self.y = self.t // 2
        self.core = self.t % 2
        self.send_sems = send_sems
        self.recv_sems = recv_sems
        self.sends = 0
        self.free = []
        self.recvs = 0
        self.open = []

    def recv_slots(self, count):
        first = self.recvs
        self.recvs += count
        return first

    def ids(self, to):
        return {"expert": to[0], "tensor": to[1]}

    def send_slot(self):
        if not self.free:
            self.free.append(self.sends)
            self.sends += 1
        return self.free.pop(0)

    def push(self, src, dst, to, slot, when=None, bulk=False, shared=None):
        send = self.send_slot() if shared is None else shared
        copy = pltpu.make_async_remote_copy(
            src_ref=src,
            dst_ref=dst,
            send_sem=self.send_sems.at[send],
            recv_sem=self.recv_sems.at[slot],
            device_id=self.ids(to),
            device_id_type=MESH,
        )
        if when is None:
            copy.start()
        else:
            pl.when(when)(copy.start)
        if shared is None:
            self.open.append((copy, when, send, bulk))

    def all_sent(self, part, send):
        copy = pltpu.make_async_remote_copy(
            src_ref=part,
            dst_ref=part,
            send_sem=self.send_sems.at[send],
            recv_sem=self.recv_sems.at[0],
            device_id=self.ids(self.other_core()),
            device_id_type=MESH,
        )
        self.open.append((copy, None, send, False))

    def landed(self, dst, slot, when=None):
        copy = pltpu.make_async_remote_copy(
            src_ref=dst,
            dst_ref=dst,
            send_sem=self.send_sems.at[0],
            recv_sem=self.recv_sems.at[slot],
            device_id=self.ids(self.other_core()),
            device_id_type=MESH,
        )
        if when is None:
            copy.wait_recv()
        else:
            pl.when(when)(copy.wait_recv)

    def drain(self, bulk=True):
        for copy, when, send, is_bulk in self.open:
            if bulk or not is_bulk:
                if when is None:
                    copy.wait_send()
                else:
                    pl.when(when)(copy.wait_send)
                self.free.append(send)
        self.open = [one for one in self.open if one[3] and not bulk]

    def other_core(self):
        return (self.e, self.t + 1 - 2 * self.core)

    def across_y(self):
        return (self.e, (self.t + 2) % 4)

    def across_x(self):
        return (self.e + 1 - 2 * self.x, self.t)

    def peer(self, step):
        return (self.e + step) % self.n

    def greet(self):
        barrier = pltpu.get_barrier_semaphore()
        partners = [(self.peer(d), self.t) for d in range(1, self.n)]
        partners += [self.other_core(), self.across_y()]
        for to in partners:
            pl.semaphore_signal(barrier, inc=1, device_id=self.ids(to), device_id_type=MESH)
        return lambda: pl.semaphore_wait(barrier, len(partners))


class Gather:
    def __init__(self, net, block, chunks=1, on_land=None):
        self.net, self.block, self.chunks, self.on_land = net, block, chunks, on_land
        self.slot = net.recv_slots(net.n * chunks)

    def start(self):
        net = self.net
        for k in range(self.chunks):
            own, slot = self.block(net.e, k), self.slot + net.e * self.chunks + k
            for way in (1, -1):
                there = net.z + way
                fits_in = (there >= 0) & (there < net.nz)
                net.push(own, own, (there % net.nz * 2 + net.x, net.t), slot, fits_in)
            net.push(own, own, net.across_x(), slot)

    def step(self, distance):
        net = self.net
        for k in range(self.chunks):
            for way in (1, -1):
                source, there = net.z - way * distance, net.z + way
                real = (source >= 0) & (source < net.nz)
                onward = real & (there >= 0) & (there < net.nz)
                b = source % net.nz * 2 + net.x
                part, slot = self.block(b, k), self.slot + b * self.chunks + k
                net.landed(part, slot, real)
                net.push(part, part, (there % net.nz * 2 + net.x, net.t), slot, onward)
                net.push(part, part, net.across_x(), slot, real)
                if self.on_land is not None:
                    self.on_land(b, real)

    def land(self, b):
        net = self.net
        for k in range(self.chunks):
            net.landed(self.block(b, k), self.slot + b * self.chunks + k)
        if self.on_land is not None:
            self.on_land(b, None)

    def finish(self):
        for d in range(self.net.nz):
            self.land((self.net.z + d) % self.net.nz * 2 + 1 - self.net.x)


class Scatter:
    def __init__(self, net, block, from_x, from_z):
        self.net, self.block = net, block
        self.from_x, self.from_z = from_x, from_z
        self.slot_x = net.recv_slots(net.nz)
        self.slot_z = net.recv_slots(net.nz)

    def start(self):
        net = self.net
        for d in range(1, net.nz + 1):
            zz = (net.z + d) % net.nz
            net.push(
                self.block(zz * 2 + 1 - net.x),
                self.from_x.at[zz],
                net.across_x(),
                self.slot_x + zz,
                bulk=True,
            )

    def forward(self):
        net = self.net
        for d in range(1, net.nz):
            zz = (net.z + d) % net.nz
            net.landed(self.from_x.at[zz], self.slot_x + zz)
            pair = self.block(zz * 2 + net.x)[...].astype(F32) + self.from_x[zz].astype(F32)
            self.from_x[zz] = pair.astype(BF)
            net.push(
                self.from_x.at[zz],
                self.from_z.at[net.z],
                (zz * 2 + net.x, net.t),
                self.slot_z + net.z,
            )

    def finish(self):
        net = self.net
        net.landed(self.from_x.at[net.z], self.slot_x + net.z)
        total = self.block(net.e)[...].astype(F32) + self.from_x[net.z].astype(F32)
        for d in range(1, net.nz):
            zz = (net.z + d) % net.nz
            net.landed(self.from_z.at[zz], self.slot_z + zz)
            total = total + self.from_z[zz].astype(F32)
        return total


class Chain:
    def __init__(self, net, block, from_x, from_z):
        self.net, self.block = net, block
        self.from_x, self.from_z = from_x, from_z
        self.slot_x = net.recv_slots(net.nz)
        self.slot_z = net.recv_slots(net.nz + 1)

    def start(self):
        net = self.net
        high = net.z // 2
        for zz in (3 - 3 * high, 2 - high, 1 - net.z + 4 * high, net.z):
            net.push(
                self.block(zz * 2 + 1 - net.x),
                self.from_x.at[zz],
                net.across_x(),
                self.slot_x + zz,
                bulk=True,
            )

    def place(self, way, zz, holder):
        return zz if way == 1 else zz + (zz == holder).astype(jnp.int32) * (self.net.nz - zz)

    def step(self, distance):
        net = self.net
        for way in (1, -1):
            target, before = net.z + way * distance, net.z - way
            real = (target >= 0) & (target < net.nz)
            fed = real & (before >= 0) & (before < net.nz)
            zz = target % net.nz
            there = (net.z + way) % net.nz
            here = self.place(way, zz, net.z)
            onward = self.place(way, zz, there)

            @pl.when(real)
            def _():
                net.landed(self.from_x.at[zz], self.slot_x + zz)

            @pl.when(fed)
            def _():
                net.landed(self.from_z.at[here], self.slot_z + here)
                both = self.from_x[zz].astype(F32) + self.from_z[here].astype(F32)
                self.from_x[zz] = (both + self.block(zz * 2 + net.x)[...].astype(F32)).astype(BF)

            @pl.when(real & ~fed)
            def _():
                own = self.block(zz * 2 + net.x)[...].astype(F32)
                self.from_x[zz] = (self.from_x[zz].astype(F32) + own).astype(BF)

            net.push(
                self.from_x.at[zz],
                self.from_z.at[onward],
                (there * 2 + net.x, net.t),
                self.slot_z + onward,
                when=real,
                bulk=True,
            )

    def finish(self, target):
        net = self.net
        net.landed(self.from_x.at[net.z], self.slot_x + net.z)
        target[...] = self.block(net.e)[...].astype(F32) + self.from_x[net.z].astype(F32)
        for way in (1, -1):
            before = net.z - way
            here = self.place(way, net.z, net.z)

            @pl.when((before >= 0) & (before < net.nz))
            def _():
                net.landed(self.from_z.at[here], self.slot_z + here)
                target[...] += self.from_z[here].astype(F32)


class Exchange:
    def __init__(self, net, outgoing, incoming, rest=None):
        self.net, self.outgoing, self.incoming, self.rest = net, outgoing, incoming, rest
        self.slot = net.recv_slots(net.n if rest is None else 1)

    def start(self):
        net = self.net
        send = None if self.rest is None else net.send_slot()
        for d in range(1, net.n):
            to = net.peer(d)
            slot = self.slot + net.e if self.rest is None else self.slot
            net.push(self.outgoing(to), self.incoming(net.e), (to, net.t), slot, shared=send)
        if self.rest is not None:
            net.all_sent(self.rest, send)

    def arrive(self, d):
        source = self.net.peer(d)
        self.net.landed(self.incoming(source), self.slot + source)
        return source

    def finish(self):
        self.net.landed(self.rest, self.slot)


class Dispatch:
    def __init__(self, net, outgoing, incoming):
        self.net, self.outgoing, self.incoming = net, outgoing, incoming
        self.send = Exchange(
            net, lambda b: outgoing.at[b], lambda b: incoming.at[b, net.core, net.y]
        )
        self.slot_y = net.recv_slots(1)
        self.slot_core = net.recv_slots(1)

    def start(self):
        net = self.net
        self.send.start()
        self.incoming[net.e, net.core, net.y] = self.outgoing[net.e]

    def relay_y(self):
        net = self.net
        for d in range(net.n):
            b = net.e if d == 0 else self.send.arrive(d)
            part = self.incoming.at[b, net.core, net.y]
            net.push(part, part, net.across_y(), self.slot_y)

    def relay_core(self):
        net = self.net
        net.landed(self.incoming.at[:, net.core, 1 - net.y], self.slot_y)
        part = self.incoming.at[:, net.core]
        net.push(part, part, net.other_core(), self.slot_core)

    def finish(self):
        self.net.landed(self.incoming.at[:, 1 - self.net.core], self.slot_core)


class Swap:
    def __init__(self, net, out_buf, in_buf, partner):
        self.net, self.out_buf, self.in_buf, self.partner = net, out_buf, in_buf, partner
        self.slot = net.recv_slots(1)

    def start(self, value):
        self.out_buf[...] = value.astype(self.out_buf.dtype)
        self.send()

    def send(self):
        self.net.push(self.out_buf, self.in_buf, self.partner, self.slot)

    def other(self):
        self.net.landed(self.in_buf, self.slot)
        return self.in_buf[...].astype(F32)

    def both(self):
        return self.out_buf[...].astype(F32) + self.other()


class Share:
    def __init__(self, net, halves):
        self.net, self.halves = net, halves
        self.slot = net.recv_slots(1)

    def start(self, value):
        net = self.net
        self.halves[net.core] = value.astype(self.halves.dtype)
        part = self.halves.at[net.core]
        net.push(part, part, net.other_core(), self.slot)

    def finish(self):
        net = self.net
        net.landed(self.halves.at[1 - net.core], self.slot)
        return jnp.concatenate([self.halves[0], self.halves[1]], axis=1)


def silu_both(value):
    gate = jax.nn.sigmoid(value)
    return value * gate, gate * (1.0 + value * (1.0 - gate))


def norm_scale(value):
    return lax.rsqrt(jnp.mean(value * value, axis=1, keepdims=True) + EPSILON)


def norm_back(grad_normed, source, scale, gain):
    weighted = grad_normed * gain
    inner = jnp.mean(weighted * source, axis=1, keepdims=True)
    return scale * weighted - scale * scale * scale * source * inner


PLACES = ["tok", "cot", "routes", "lengths", "parents", "gain_a", "gain_b", "wq", "wk", "wv"]
PLACES += ["wo", "router", "sg", "su", "sd", "eg_far", "eu_far", "ed_far"]
RESULTS = ["out", "gtok", "dga", "dgb", "dwq", "dwk", "dwv", "dwo", "drouter"]
RESULTS += ["dsg", "dsu", "dsd", "deg", "deu", "ded"]


def scratch_shapes(s):
    n, local, half = s.n, s.local, s.half
    depth, hidden, shared, cap = s.depth, s.hidden, s.shared, s.cap
    micro, nz = s.micro, s.n // 2
    model, wide, stack, tree = 2 * half, 2 * s.width, s.heads * local, n * local
    part = cap // 4
    vm = pltpu.VMEM
    return dict(
        w_kv=vm((n, depth, wide), BF),
        w_qo=vm((n, depth, wide), BF),
        w_sh=vm((3, n, depth, shared), BF),
        ext_in=vm((n, 16, 128), BF),
        tok_all=vm((n, 2, 2, micro * local // 4, model), BF),
        cos_all=vm((n, micro * local, 128), F32),
        sin_all=vm((n, micro * local, 128), F32),
        kv=vm((micro, n, local, wide), BF),
        q_rows=vm((micro, stack, 256), BF),
        expo=vm((micro, stack, tree), F32),
        total=vm((micro, stack, 1), F32),
        mixed=vm((micro, local, 256), F32),
        mixed_low=vm((micro * local, wide), BF),
        choice_half=vm((micro, local, n * cap // 2), BF),
        choice_wide=vm((micro, local, n * 128), BF),
        res=vm((micro, local, model), F32),
        n_one=vm((micro * local, model), BF),
        n_two=vm((micro * local, model), BF),
        c_out=vm((micro, n, part, model), BF),
        c_in=vm((micro, n, 2, 2, part, model), BF),
        x_out=vm((micro, n, part, model), BF),
        x_in=vm((micro, n, 2, 2, part, model), BF),
        h_out=vm((micro, n, 16, 128), BF),
        h_in=vm((micro, n, 16, 128), BF),
        gate_col=vm((micro, n * cap, 1), F32),
        e_h=vm((micro, n * cap, hidden), BF),
        e_dg=vm((micro, n * cap, hidden), BF),
        e_du=vm((micro, n * cap, hidden), BF),
        y_core=vm((micro, n, cap, half), BF),
        g_core=vm((micro, n, cap, half), BF),
        y_in=vm((micro, n, cap // 2, half), BF),
        y_far=vm((micro, n, cap // 2, half), BF),
        g_in=vm((micro, n, cap // 2, half), BF),
        g_far=vm((micro, n, cap // 2, half), BF),
        d_out=vm((micro, n, 8, 128), F32),
        d_in=vm((micro, n, 8, 128), F32),
        d_tensor=vm((micro, 4, 8, 128), F32),
        core_a=vm((micro, 2, local, half), F32),
        core_b=vm((4, micro * local, half), BF),
        core_c=vm((micro, 2, local, half), F32),
        s_grads=vm((3, micro * local, shared), BF),
        s_own=vm((2, micro * local, half), F32),
        y_swap=vm((4, micro, 2, local, half), BF),
        share_a=vm((micro, 2, local, half), F32),
        share_b=vm((micro, 2, local, half), F32),
        share_c=vm((micro, 2, local, half), F32),
        share_out=vm((micro, 2, local, half), BF),
        kv_part=vm((micro, n, local, wide), BF),
        kv_fx=vm((micro, 2, nz, local // 2, wide), BF),
        kv_fz=vm((micro, 2, nz, local // 2, wide), BF),
        sh_part=vm((3, n, depth, shared), BF),
        sh_fx=vm((3, nz, depth, shared), BF),
        sh_fz=vm((3, nz + 1, depth, shared), BF),
        w_part=vm((2, n, depth, wide), BF),
        w_fx=vm((2, nz, depth, wide), BF),
        w_fz=vm((2, nz, depth, wide), BF),
        gains_out=vm((n, 16, 128), F32),
        gains_in=vm((n, 16, 128), F32),
        eg=vm((model, hidden), BF),
        eu=vm((model, hidden), BF),
        ed=vm((hidden, model), BF),
        load_sems=pltpu.SemaphoreType.DMA((3,)),
        stage=vm((2, half, hidden), F32),
        stage_d=vm((hidden, half), F32),
        save_sems=pltpu.SemaphoreType.DMA((6,)),
        send_sems=pltpu.SemaphoreType.DMA((SENDS,)),
        recv_sems=pltpu.SemaphoreType.DMA((RECVS,)),
    )


SENDS = 182
RECVS = 223


def layer_kernel(s, names, *refs):
    r = types.SimpleNamespace(**dict(zip(names, refs)))
    n, local, width, half = s.n, s.local, s.width, s.half
    depth, hidden, shared, cap = s.depth, s.hidden, s.shared, s.cap
    micro, heads = s.micro, s.heads
    rows, model, tree, wide, stack = micro * local, 2 * half, n * local, 2 * width, heads * local
    part = cap // 4
    net = Net(n, r.send_sems, r.recv_sems)
    me, core, y = net.e, net.core, net.y
    ready = net.greet()
    loads = [
        pltpu.make_async_copy(far, near, r.load_sems.at[i])
        for i, (far, near) in enumerate(((r.eg_far, r.eg), (r.eu_far, r.eu), (r.ed_far, r.ed)))
    ]
    micros = range(micro)
    my_half = pl.ds(pl.multiple_of(core * half, 128), half)
    other_half = pl.ds(pl.multiple_of((1 - core) * half, 128), half)

    def rows_of(m):
        return slice(m * local, (m + 1) * local)

    left = (iota((width, wide), 1) == iota((width, wide), 0)).astype(BF)
    right = (iota((width, wide), 1) == iota((width, wide), 0) + width).astype(BF)
    r.w_kv[me] = (dot(r.wk[...], left) + dot(r.wv[...], right)).astype(BF)
    r.tok_all[me] = r.tok[...].reshape(2, 2, rows // 4, model)
    r.w_qo[me] = (dot(r.wq[...], left) + dot_tn(r.wo[...], right)).astype(BF)
    ext = [r.gain_a[...].astype(F32), r.gain_b[...].astype(F32), jnp.zeros((6, depth), F32)]
    ext = jnp.concatenate(ext + [r.router[...].astype(F32)], axis=0).astype(BF)
    pad = (iota((depth, 128), 1) == iota((depth, 128), 0)).astype(BF)
    r.ext_in[me] = dot(ext, pad).astype(BF)
    for i, name in enumerate(("sg", "su", "sd")):
        r.w_sh[i, me] = getattr(r, name)[...]

    slot_ty, slot_tc = net.recv_slots(n), net.recv_slots(n)

    def token_on(b, when):
        quarter = r.tok_all.at[b, core, y]
        net.push(quarter, quarter, net.across_y(), slot_ty + b, when)

    get_kv = Gather(net, lambda b, k: r.w_kv.at[b])
    get_qo = Gather(net, lambda b, k: r.w_qo.at[b])
    get_tok = Gather(net, lambda b, k: r.tok_all.at[b, core, y], on_land=token_on)
    get_sh = [Gather(net, lambda b, k, i=i: r.w_sh.at[i, b]) for i in range(3)]
    get_ext = Exchange(net, lambda b: r.ext_in.at[me], lambda b: r.ext_in.at[b], r.ext_in.at[0 : n - 1])
    ready()
    get_ext.start()
    for load in loads:
        load.start()
    get_kv.start()
    get_tok.start()
    get_qo.start()

    eye = (iota((128, 128), 0) == iota((128, 128), 1)).astype(BF)
    routes = dot_nt(eye, r.routes[...].astype(BF))
    lane = iota((local, 16), 1) - 8
    earlier = (iota((local, local), 1) < iota((local, local), 0)).astype(BF)

    def spread(span):
        of_lane = iota((16, n * span), 1) // span
        return (iota((16, n * span), 0) - 8 == of_lane).astype(BF)

    hot_one, hot_two, quarter = [], [], []
    send_c = [Dispatch(net, r.c_out.at[m], r.c_in.at[m]) for m in micros]
    send_h = [
        Exchange(
            net,
            lambda b, m=m: r.h_out.at[m, b],
            lambda b, m=m: r.h_in.at[m, b],
            r.h_in.at[m, 0 : n - 1],
        )
        for m in micros
    ]
    for m in micros:
        one = lane == routes[:, 2 * m : 2 * m + 1].astype(jnp.int32)
        two = lane == routes[:, 2 * m + 1 : 2 * m + 2].astype(jnp.int32)
        hot_one.append(one)
        hot_two.append(two)
        hits = (one | two).astype(F32)
        rank = jnp.where(hits > 0.5, dot(earlier, hits.astype(BF)), -1.0).astype(BF)

        def taken(span, first=0):
            wanted = iota((local, n * span), 1) % span + first
            return (dot(rank, spread(span)) == wanted.astype(F32)).astype(BF)

        r.choice_half[m] = taken(cap // 2, y * (cap // 2))
        r.choice_wide[m] = taken(128)
        quarter.append(taken(part, (core * 2 + y) * part))
        hit_rows = dot_tn(hits.astype(BF), r.choice_wide[m]).astype(BF)
        for b in range(n):
            r.h_out[m, b] = hit_rows[:, b * 128 : (b + 1) * 128]
        r.h_in[m, me] = r.h_out[m, me]
        picked = dot_tn(quarter[m], r.cot[rows_of(m)]).astype(BF)
        r.c_out[m] = picked.reshape(n, part, model)

    def segments(m):
        starts, ends, paths, shifts, begin = [], [], [], [], 0
        for seg in range(s.segs):
            size = r.lengths[m, seg]
            starts.append(begin)
            ends.append(begin + size)
            begin = begin + size
            if seg == 0:
                paths.append(jnp.int32(1))
                shifts.append(jnp.int32(0))
            else:
                parent = r.parents[m, seg]
                path, shift = jnp.int32(0), jnp.int32(0)
                for other in range(seg):
                    is_parent = parent == other
                    path = jnp.where(is_parent, paths[other], path)
                    shift = jnp.where(
                        is_parent, shifts[other] + ends[other] - starts[other], shift
                    )
                paths.append(path + (1 << seg))
                shifts.append(shift)
        return starts, ends, paths, shifts

    tables = [segments(m) for m in micros]

    def row_values(m, ids):
        starts, ends, paths, shifts = tables[m]
        path, place, own = jnp.zeros_like(ids), jnp.zeros_like(ids), jnp.zeros_like(ids)
        for seg in range(s.segs):
            inside = (ids >= starts[seg]) & (ids < ends[seg])
            path = jnp.where(inside, paths[seg], path)
            place = jnp.where(inside, ids - starts[seg] + shifts[seg], place)
            own = jnp.where(inside, 1 << seg, own)
        return path, place, own

    turn = (iota((1, 128), 1) % (HEAD // 2)).astype(F32)
    frequency = jnp.exp(turn * (-math.log(ROPE_BASE) / (HEAD // 2)))

    def angle_step(b, carry):
        ids = b * local + iota((local, 1), 0)
        place = jnp.concatenate([row_values(m, ids)[1] for m in micros], axis=0)
        angle = place.astype(F32) * frequency
        r.cos_all[b] = jnp.cos(angle)
        r.sin_all[b] = jnp.sin(angle)
        return carry

    lax.fori_loop(0, n, angle_step, 0)
    is_left = iota((1, wide), 1) < width
    swap_r, swap_c = iota((wide, wide), 0), iota((wide, wide), 1)
    lower = swap_c % HEAD < HEAD // 2
    swap = jnp.where(lower & (swap_r == swap_c + HEAD // 2), -1.0, 0.0)
    swap = jnp.where(~lower & (swap_r == swap_c - HEAD // 2), 1.0, swap)
    swap = jnp.where(is_left, swap, 0.0)
    swap_low = swap.astype(BF)

    def turns(b):
        cosine = jnp.concatenate([r.cos_all[b]] * (wide // 128), axis=1)
        sine = jnp.concatenate([r.sin_all[b]] * (wide // 128), axis=1)
        return jnp.where(is_left, cosine, 1.0), sine

    for distance in range(1, net.nz):
        get_kv.step(distance)
        get_tok.step(distance)
        get_qo.step(distance)
    get_ext.finish()
    high = net.z // 2
    near = [net.z + 1 - 2 * (net.z % 2), 2 - high, 3 - 3 * high]
    column = [zz * 2 + net.x for zz in near]
    across = [zz * 2 + 1 - net.x for zz in [net.z] + near]

    def token_core(b):
        net.landed(r.tok_all.at[b, core, 1 - y], slot_ty + b)
        both = r.tok_all.at[b, core]
        net.push(both, both, net.other_core(), slot_tc + b)

    for b in column:
        token_core(b)

    def lay(b):
        place = iota((128, model), 0)
        return (place < depth) & (place + b * depth == iota((128, model), 1))

    ext_all = jnp.zeros((16, model), F32)
    for b in range(n):
        ext_all = ext_all + dot(r.ext_in[b], lay(b).astype(BF))
    gain_one, gain_two = ext_all[0:1], ext_all[1:2]
    ext_low = ext_all.astype(BF)
    get_kv.finish()
    w_kv = r.w_kv[...].reshape(model, wide)
    w_kv_swapped = dot(w_kv, swap_low[:, :256]).astype(BF)

    def normed(block):
        value = block.astype(F32)
        return (value * norm_scale(value) * gain_one).astype(BF)

    def key_value(b):
        block = normed(r.tok_all[b].reshape(rows, model))
        cosine, sine = turns(b)
        swapped = dot(block, w_kv_swapped) * sine[:, :256]
        swapped = jnp.concatenate([swapped, jnp.zeros((rows, wide - 256), F32)], axis=1)
        both = (dot(block, w_kv) * cosine + swapped).astype(BF)
        for m in micros:
            r.kv[m, b] = both[rows_of(m)]

    for g in get_sh:
        g.start()
    key_value(me)

    def key_values_of(blocks):
        def step(i, carry):
            b = sum([(i == k).astype(jnp.int32) * one for k, one in enumerate(blocks)])
            net.landed(r.tok_all.at[b, 1 - core], slot_tc + b)
            key_value(b)
            return carry

        lax.fori_loop(0, len(blocks), step, 0)

    for b in across[:2]:
        get_tok.land(b)
    key_values_of(column)
    for b in across[2:]:
        get_tok.land(b)
    for b in across[:2]:
        token_core(b)
    key_values_of(across[:2])
    for b in across[2:]:
        token_core(b)
    get_qo.finish()
    for g in get_sh:
        g.step(1)
    key_values_of(across[2:])
    r.n_one[...] = normed(r.tok[...])
    w_qo = r.w_qo[...].reshape(model, wide)
    cosine, sine = turns(me)
    cosine = jnp.where(is_left, cosine, 0.0)
    queries = dot(r.n_one[...], w_qo) * cosine
    queries = queries + dot(r.n_one[...], dot(w_qo, swap_low).astype(BF)) * sine
    queries = queries.astype(BF)
    for m in micros:
        send_c[m].start()
        send_h[m].start()

    first, last = slice(0, 256), slice(wide - 256, wide)
    head_of = iota((1, 256), 1) // HEAD
    q_masks = [head_of == h for h in range(heads)]
    v_masks = [head_of == heads + h - (wide - 256) // HEAD for h in range(heads)]
    blank = jnp.zeros((local, wide - 256), F32)

    def by_head(block, masks):
        return jnp.concatenate(
            [jnp.where(mask, block, jnp.zeros_like(block)) for mask in masks], axis=0
        )

    def join_heads(value, masks):
        total = jnp.zeros((local, 256), F32)
        for h, mask in enumerate(masks):
            total = total + jnp.where(mask, value[h * local : (h + 1) * local], 0.0)
        return total

    def o_half(h):
        return r.w_qo[pl.ds(h * (n // 2), n // 2)].reshape(half, wide)

    core_a = [Swap(net, r.core_a.at[m, 0], r.core_a.at[m, 1], net.other_core()) for m in micros]
    core_c = [Swap(net, r.core_c.at[m, 0], r.core_c.at[m, 1], net.other_core()) for m in micros]
    core_b = [
        Swap(net, r.core_b.at[2 * i], r.core_b.at[2 * i + 1], net.other_core()) for i in range(2)
    ]
    y_swap = [
        [Swap(net, r.y_swap.at[i, m, 0], r.y_swap.at[i, m, 1], net.across_y()) for m in micros]
        for i in range(4)
    ]
    share_a = [Share(net, r.share_a.at[m]) for m in micros]
    share_b = [Share(net, r.share_b.at[m]) for m in micros]
    share_c = [Share(net, r.share_c.at[m]) for m in micros]
    share_out = [Share(net, r.share_out.at[m]) for m in micros]

    score_scale = HEAD**-0.5
    for m in micros:
        r.q_rows[m] = by_head(queries[rows_of(m)][:, first], q_masks)
        key_rows = r.kv[m, :, :, first].reshape(tree, 256)
        value_rows = r.kv[m, :, :, last].reshape(tree, 256)
        ids = me * local + iota((stack, 1), 0) % local
        path, unused, unused_two = row_values(m, ids)
        key_ids = iota((1, tree), 1)
        unused, unused_two, key_seg = row_values(m, key_ids)
        seen = ((path & key_seg) != 0) & (key_ids <= ids)
        scores = dot_nt(r.q_rows[m], key_rows) * score_scale
        expo = jnp.where(seen, jnp.exp(scores), 0.0)
        r.expo[m] = expo
        total = jnp.sum(expo, axis=1, keepdims=True)
        r.total[m] = total
        mixed = join_heads(dot(expo.astype(BF), value_rows) / total, v_masks)
        r.mixed[m] = mixed
        r.mixed_low[rows_of(m)] = jnp.concatenate([blank, mixed], axis=1).astype(BF)
        core_a[m].start(dot_nt(r.mixed_low[rows_of(m)], o_half(1 - core)))
    for g in get_sh:
        g.step(2)
    for m in micros:
        mine = dot_nt(r.mixed_low[rows_of(m)], o_half(core))
        y_swap[0][m].start(mine + core_a[m].other())
    for m in micros:
        share_a[m].start(y_swap[0][m].both())

    send_x = [Dispatch(net, r.x_out.at[m], r.x_in.at[m]) for m in micros]
    scale_two = []
    for m in micros:
        res = r.tok[rows_of(m)].astype(F32) + share_a[m].finish()
        r.res[m] = res
        scale_two.append(norm_scale(res))
        normed_two = (res * scale_two[m] * gain_two).astype(BF)
        r.n_two[rows_of(m)] = normed_two
        r.x_out[m] = dot_tn(quarter[m], normed_two).astype(BF).reshape(n, part, model)
        send_x[m].start()

    for g in get_sh:
        g.step(3)
    for m in micros:
        send_c[m].relay_y()
    gates = []
    for m in micros:
        logits = dot_nt(r.n_two[rows_of(m)], ext_low)
        z_one = jnp.sum(jnp.where(hot_one[m], logits, 0.0), axis=1, keepdims=True)
        z_two = jnp.sum(jnp.where(hot_two[m], logits, 0.0), axis=1, keepdims=True)
        z_top = jnp.maximum(z_one, z_two)
        e_one, e_two = jnp.exp(z_one - z_top), jnp.exp(z_two - z_top)
        chosen = jnp.where(hot_one[m], e_one, jnp.where(hot_two[m], e_two, 0.0))
        gates.append(chosen / (e_one + e_two))

    for m in micros:
        send_x[m].relay_y()
    for g in get_sh:
        g.finish()

    def wide_half(i, h):
        return r.w_sh[i, pl.ds(h * (n // 2), n // 2)].reshape(half, shared)

    def shared_step(m, carry):
        here = pl.ds(pl.multiple_of(m * local, local), local)
        normed_two = r.n_two[here]
        shared_g = dot(normed_two, r.w_sh[0].reshape(model, shared))
        shared_u = dot(normed_two, r.w_sh[1].reshape(model, shared))
        act, slope = silu_both(shared_g)
        shared_h = (act * shared_u).astype(BF)
        grad_h = dot(r.cot[here], r.w_sh[2].reshape(model, shared))
        grad_g = (grad_h * shared_u * slope).astype(BF)
        grad_u = (grad_h * act).astype(BF)
        r.s_grads[0, here] = grad_g
        r.s_grads[1, here] = grad_u
        r.s_grads[2, here] = shared_h
        other, own = 1 - core, core
        back = dot_nt(grad_g, wide_half(0, other)) + dot_nt(grad_u, wide_half(1, other))
        r.core_b[0, here] = back.astype(BF)
        r.core_b[2, here] = dot_nt(shared_h, wide_half(2, other)).astype(BF)
        back = dot_nt(grad_g, wide_half(0, own)) + dot_nt(grad_u, wide_half(1, own))
        r.s_own[0, here] = back
        r.s_own[1, here] = dot_nt(shared_h, wide_half(2, own))
        return carry

    lax.fori_loop(0, micro, shared_step, 0)
    for swap_b in core_b:
        swap_b.send()
    for i, (rows_a, rows_b) in enumerate(((r.n_two, 0), (r.n_two, 1), (r.cot, 2))):
        grads = dot_tn(rows_a[...], r.s_grads[rows_b])
        r.sh_part[i] = grads.astype(BF).reshape(n, depth, shared)
    sum_sh = [
        Chain(net, lambda b, i=i: r.sh_part.at[i, b], r.sh_fx.at[i], r.sh_fz.at[i])
        for i in range(3)
    ]

    for m in micros:
        send_c[m].relay_core()
    for m in micros:
        send_x[m].relay_core()
    for m in micros:
        send_h[m].finish()
        send_c[m].finish()

    slot_gc = net.recv_slots(micro)
    slot_yc = net.recv_slots(micro)
    slot_yy = net.recv_slots(micro)
    slot_gy = net.recv_slots(micro)
    my_slots = pl.ds(pl.multiple_of(y * (cap // 2), cap // 2), cap // 2)
    far_slots = pl.ds(pl.multiple_of((1 - y) * (cap // 2), cap // 2), cap // 2)
    send_g = [
        Exchange(
            net,
            lambda b, m=m: r.g_core.at[m, b, my_slots],
            lambda b, m=m: r.g_in.at[m, b],
            r.g_in.at[m, 0 : n - 1],
        )
        for m in micros
    ]
    send_y = [
        Exchange(
            net,
            lambda b, m=m: r.y_core.at[m, b, my_slots],
            lambda b, m=m: r.y_in.at[m, b],
            r.y_in.at[m, 0 : n - 1],
        )
        for m in micros
    ]
    send_d = [
        Exchange(
            net,
            lambda b, m=m: r.d_out.at[m, b],
            lambda b, m=m: r.d_in.at[m, b],
            r.d_in.at[m, 0 : n - 1],
        )
        for m in micros
    ]
    slot_eye = eye[:cap]
    slot_line = iota((cap, 128), 0) == iota((cap, 128), 1)
    own_lane = iota((n * cap, 16), 1) - 8 == me
    group = 4
    halves = [slice(0, half), slice(half, model)]

    def expert_gates(m):
        x_rows = r.x_in[m].reshape(n * cap, model)
        z_all = dot_nt(x_rows, ext_low)
        hit = jnp.concatenate([dot_nt(slot_eye, r.h_in[m, b]) for b in range(n)], axis=0)
        z_own = jnp.sum(jnp.where(own_lane, z_all, 0.0), axis=1, keepdims=True)
        z_other = jnp.sum(jnp.where(own_lane, 0.0, z_all * hit), axis=1, keepdims=True)
        z_top = jnp.maximum(z_own, z_other)
        e_own, e_other = jnp.exp(z_own - z_top), jnp.exp(z_other - z_top)
        r.gate_col[m] = e_own / (e_own + e_other)

    def expert_rows(m, i):
        count = group * cap
        span = slice(i * group, (i + 1) * group)
        flat = slice(i * count, (i + 1) * count)
        x = r.x_in[m, span].reshape(count, model)
        c = r.c_in[m, span].reshape(count, model)
        gate = r.gate_col[m, flat]
        gate_pre = dot(x, r.eg[...])
        up_pre = dot(x, r.eu[...])
        act, slope = silu_both(gate_pre)
        hid = (act * up_pre).astype(BF)
        grad_y = (gate * c.astype(F32)).astype(BF)
        grad_hid = dot_nt(grad_y, r.ed[...])
        grad_g = (grad_hid * up_pre * slope).astype(BF)
        grad_u = (grad_hid * act).astype(BF)
        r.e_h[m, flat] = hid
        r.e_dg[m, flat] = grad_g
        r.e_du[m, flat] = grad_u
        dots = jnp.zeros((count, 1), F32)
        for cut in halves:
            out = dot(hid, r.ed[:, cut])
            r.tok_all[span, 0, m, :, cut] = out.astype(BF).reshape(group, cap, half)
            dots = dots + jnp.sum(out * c[:, cut].astype(F32), axis=1, keepdims=True)
            back = dot_nt(grad_g, r.eg[cut]) + dot_nt(grad_u, r.eu[cut])
            r.tok_all[span, 1, m, :, cut] = back.astype(BF).reshape(group, cap, half)
        r.c_in[m, span] = grad_y.reshape(group, 2, 2, part, model)
        for b in range(group):
            line = jnp.where(slot_line, dots[b * cap : (b + 1) * cap], 0.0)
            line = jnp.sum(line, axis=0, keepdims=True)
            r.d_out[m, i * group + b] = jnp.broadcast_to(line, (8, 128))

    def expert_sent(m):
        net.push(r.tok_all.at[:, 1, m, :, other_half], r.g_core.at[m], net.other_core(), slot_gc + m)
        net.push(r.tok_all.at[:, 0, m, :, other_half], r.y_core.at[m], net.other_core(), slot_yc + m)

    def add_g(m):
        net.landed(r.g_core.at[m], slot_gc + m)
        mine = r.tok_all[:, 1, m, :, my_half].astype(F32)
        r.g_core[m] = (mine + r.g_core[m].astype(F32)).astype(BF)
        net.push(r.g_core.at[m, :, far_slots], r.g_far.at[m], net.across_y(), slot_gy + m)

    def return_g(m):
        net.landed(r.g_far.at[m], slot_gy + m)
        both = r.g_core[m, :, my_slots].astype(F32) + r.g_far[m].astype(F32)
        r.g_core[m, :, my_slots] = both.astype(BF)
        send_g[m].start()
        send_d[m].start()
        r.g_in[m, me] = r.g_core[m, me, my_slots]
        r.d_in[m, me] = r.d_out[m, me]

    def add_y(m):
        net.landed(r.y_core.at[m], slot_yc + m)
        mine = r.tok_all[:, 0, m, :, my_half].astype(F32)
        r.y_core[m] = (mine + r.y_core[m].astype(F32)).astype(BF)
        net.push(r.y_core.at[m, :, far_slots], r.y_far.at[m], net.across_y(), slot_yy + m)

    def return_y(m):
        net.landed(r.y_far.at[m], slot_yy + m)
        both = r.y_core[m, :, my_slots].astype(F32) + r.y_far[m].astype(F32)
        r.y_core[m, :, my_slots] = both.astype(BF)
        send_y[m].start()
        r.y_in[m, me] = r.y_core[m, me, my_slots]

    saves = []

    def all_slots(ref, cut):
        return ref[..., cut].reshape(micro * n * cap, -1)

    def save(source, target, i):
        copy = pltpu.make_async_copy(source, target, r.save_sems.at[i])
        copy.start()
        saves.append(copy)

    def weight_grads(i):
        whole = slice(None)
        if i < 2:
            grads, target = ((r.e_dg, r.deg), (r.e_du, r.deu))[i]
            for h, cut in enumerate(halves):
                if i == 1:
                    saves[h].wait()
                r.stage[h] = dot_tn(all_slots(r.x_in, cut), all_slots(grads, whole))
                save(r.stage.at[h], target.at[cut], 2 * i + h)
        else:
            for h, cut in enumerate(halves):
                if h == 1:
                    saves[4].wait()
                r.stage_d[...] = dot_tn(all_slots(r.e_h, whole), all_slots(r.c_in, cut))
                save(r.stage_d, r.ded.at[:, cut], 4 + h)

    net.drain()
    for load in loads:
        load.wait()
    sum_sh[0].start()
    sum_sh[1].start()
    for m in micros:
        send_x[m].finish()
        if m > 0:
            sum_sh[0].step(3)
        expert_gates(m)
        for i in range(n // group):
            if m > 0 and i == 1:
                add_g(m - 1)
                sum_sh[0].step(2)
            expert_rows(m, i)
        expert_sent(m)
    return_g(0)
    sum_sh[0].step(1)
    weight_grads(0)
    add_g(1)
    weight_grads(1)
    return_g(1)
    sum_sh[2].start()
    sum_sh[1].step(3)
    weight_grads(2)
    sum_sh[1].step(2)

    for m in micros:
        add_y(m)
    d_core = [Swap(net, r.d_tensor.at[m, 0], r.d_tensor.at[m, 1], net.other_core()) for m in micros]
    d_y = [Swap(net, r.d_tensor.at[m, 2], r.d_tensor.at[m, 3], net.across_y()) for m in micros]
    eight = iota((8, 128), 0)
    d_rows = []
    for m in micros:
        send_d[m].finish()
        line = jnp.zeros((8, 128), F32)
        for b in range(n):
            line = line + jnp.where(eight == b, r.d_in[m, b], 0.0)
        d_rows.append(line)
        d_core[m].start(line)
    shared_grad = r.s_own[0] + core_b[0].other()
    for m in micros:
        d_y[m].start(d_rows[m] + d_core[m].other())
    for m in micros:
        send_g[m].finish()
        moe_grad = dot(r.choice_half[m], r.g_in[m].reshape(n * cap // 2, half))
        y_swap[1][m].start(moe_grad + shared_grad[rows_of(m)])
    net.drain(bulk=False)
    sum_sh[1].step(1)
    grad_logits = []
    for m in micros:
        d_all = d_y[m].both()
        grad_gate = jnp.zeros((local, 16), F32)
        for b in range(n):
            picked = r.choice_wide[m, :, b * 128 : (b + 1) * 128].astype(F32) * d_all[b : b + 1]
            grad_gate = jnp.where(lane == b, jnp.sum(picked, axis=1, keepdims=True), grad_gate)
        inner = jnp.sum(gates[m] * grad_gate, axis=1, keepdims=True)
        grad_logits.append((gates[m] * (grad_gate - inner)).astype(BF))
        share_b[m].start(y_swap[1][m].both())


    kv_sums, grad_queries, gain_rows = [], [], []
    for m in micros:
        grad_two = share_b[m].finish() + dot(grad_logits[m], ext_low)
        res = r.res[m]
        cot = r.cot[rows_of(m)].astype(F32)
        grad_res = cot + norm_back(grad_two, res, scale_two[m], gain_two)
        r.gtok[rows_of(m)] = grad_res
        gain_rows.append(jnp.sum(grad_two * res * scale_two[m], axis=0, keepdims=True))
        key_rows = r.kv[m, :, :, first].reshape(tree, 256)
        value_rows = r.kv[m, :, :, last].reshape(tree, 256)
        total = r.total[m]
        gm = by_head(dot(grad_res.astype(BF), r.w_qo[:, :, last].reshape(model, 256)), v_masks)
        mixed = jnp.concatenate([r.mixed[m]] * heads, axis=0)
        delta = jnp.sum(gm * mixed, axis=1, keepdims=True) / total
        grad_summed = (gm / total).astype(BF)
        expo = r.expo[m]
        ds = (expo * (dot_nt(grad_summed, value_rows) - delta)).astype(BF)
        grad_k = dot_tn(ds, r.q_rows[m]) * score_scale
        grad_v = dot_tn(expo.astype(BF), grad_summed)
        over = 512 - wide
        middle = grad_k[:, 256 - over :] + grad_v[:, :over]
        grad_kv = jnp.concatenate([grad_k[:, : 256 - over], middle, grad_v[:, over:]], axis=1)
        r.kv_part[m] = grad_kv.astype(BF).reshape(n, local, wide)
        for k in range(2):
            span = slice(k * (local // 2), (k + 1) * (local // 2))
            one = Scatter(
                net,
                lambda b, m=m, span=span: r.kv_part.at[m, b, span],
                r.kv_fx.at[m, k],
                r.kv_fz.at[m, k],
            )
            one.start()
            kv_sums.append(one)
        if m == 0:
            for k in micros:
                return_y(k)
        grad_query = join_heads(dot(ds, key_rows), q_masks) * score_scale
        grad_queries.append(jnp.concatenate([grad_query, blank], axis=1))

    cosine, sine = turns(me)

    def turned_back(grad):
        return (grad * cosine - dot(grad, swap, EXACT) * sine).astype(BF)

    for one in kv_sums:
        one.forward()
    sum_sh[2].step(3)
    grad_q = turned_back(jnp.concatenate(grad_queries, axis=0))
    grad_attn = r.gtok[...].astype(BF)
    part_qo = dot_tn(r.n_one[...], grad_q) + dot_tn(grad_attn, r.mixed_low[...])
    r.w_part[0] = part_qo.astype(BF).reshape(n, depth, wide)
    sum_w = [
        Scatter(net, lambda b, i=i: r.w_part.at[i, b], r.w_fx.at[i], r.w_fz.at[i])
        for i in range(2)
    ]
    sum_w[0].start()

    shared_y = r.s_own[1] + core_b[1].other()
    for m in micros:
        send_y[m].finish()
        gate_wide = dot(gates[m], spread(cap // 2).astype(F32), EXACT)
        gate_high = gate_wide.astype(BF).astype(F32)
        pick = r.choice_half[m].astype(F32)
        y_rows = r.y_in[m].reshape(n * cap // 2, half)
        moe_y = dot((pick * gate_high).astype(BF), y_rows)
        moe_y = moe_y + dot((pick * (gate_wide - gate_high)).astype(BF), y_rows)
        y_swap[2][m].start(moe_y + shared_y[rows_of(m)])
    sum_sh[2].step(2)

    def weight_half(ref, h):
        return ref[pl.ds(h * (n // 2), n // 2)].reshape(half, wide)

    grad_kvs = []
    for m in micros:
        total = jnp.concatenate([one.finish() for one in kv_sums[2 * m : 2 * m + 2]], axis=0)
        cos_m, sin_m = cosine[rows_of(m)], sine[rows_of(m)]
        grad_kv = (total * cos_m - dot(total, swap, EXACT) * sin_m).astype(BF)
        grad_kvs.append(grad_kv)
        q_m = grad_q[rows_of(m)]
        other = dot_nt(q_m, weight_half(r.w_qo, 1 - core))
        core_c[m].start(other + dot_nt(grad_kv, weight_half(r.w_kv, 1 - core)))
    for m in micros:
        mine = dot_nt(grad_q[rows_of(m)], weight_half(r.w_qo, core))
        mine = mine + dot_nt(grad_kvs[m], weight_half(r.w_kv, core))
        y_swap[3][m].start(mine + core_c[m].other())
    part_kv = dot_tn(r.n_one[...], jnp.concatenate(grad_kvs, axis=0))
    r.w_part[1] = part_kv.astype(BF).reshape(n, depth, wide)
    sum_w[1].start()
    sum_w[0].forward()
    sum_sh[2].step(1)
    for m in micros:
        share_c[m].start(y_swap[3][m].both())
    for m in micros:
        res_half = jnp.where(core == 0, r.res[m, :, :half], r.res[m, :, half:])
        share_out[m].start(res_half + y_swap[2][m].both())
    sum_w[1].forward()

    gain_one_row = jnp.zeros((1, model), F32)
    for m in micros:
        grad_one = share_c[m].finish()
        tok = r.tok[rows_of(m)].astype(F32)
        scale_one = norm_scale(tok)
        r.gtok[rows_of(m)] += norm_back(grad_one, tok, scale_one, gain_one)
        gain_one_row = gain_one_row + jnp.sum(grad_one * tok * scale_one, axis=0, keepdims=True)
    grad_router = jnp.zeros((16, model), F32)
    for m in micros:
        grad_router = grad_router + dot_tn(grad_logits[m], r.n_two[rows_of(m)])
    line = iota((16, model), 0)
    small = jnp.where(line == 0, gain_one_row, grad_router)
    small = jnp.where(line == 1, gain_rows[0] + gain_rows[1], small)
    high_part = small.astype(BF)
    low_part = (small - high_part.astype(F32)).astype(BF)
    for b in range(n):
        place = lay(b).astype(BF)
        r.gains_out[b] = dot_nt(high_part, place) + dot_nt(low_part, place)
    send_gains = Exchange(
        net, lambda b: r.gains_out.at[b], lambda b: r.gains_in.at[b], r.gains_in.at[0 : n - 1]
    )
    send_gains.start()
    r.gains_in[me] = r.gains_out[me]
    for m in micros:
        r.out[rows_of(m)] = share_out[m].finish()

    qo = sum_w[0].finish()
    r.dwq[...] = qo[:, :width]
    depth_eye = (iota((depth, depth), 0) == iota((depth, depth), 1)).astype(F32)
    r.dwo[...] = dot_tn(qo[:, width:], depth_eye, EXACT)
    kv = sum_w[1].finish()
    r.dwk[...] = kv[:, :width]
    r.dwv[...] = kv[:, width:]
    for i, target in enumerate((r.dsg, r.dsu, r.dsd)):
        sum_sh[i].finish(target)
    send_gains.finish()
    gains = jnp.zeros((16, 128), F32)
    for b in range(n):
        gains = gains + r.gains_in[b]
    r.dga[...] = gains[0:1, :depth]
    r.dgb[...] = gains[1:2, :depth]
    r.drouter[...] = gains[8:16, :depth]
    for copy in saves[2:4] + saves[5:]:
        copy.wait()
    net.drain()


def settle_kernel(count, *refs):
    sources, targets, stops = refs[:count], refs[count : 2 * count], refs[2 * count : 3 * count]
    sems = refs[3 * count]
    reads = [
        pltpu.make_async_copy(a, b, sems.at[0, i]) for i, (a, b) in enumerate(zip(sources, stops))
    ]
    writes = [
        pltpu.make_async_copy(a, b, sems.at[1, i]) for i, (a, b) in enumerate(zip(stops, targets))
    ]
    for read in reads:
        read.start()
    for read, write in zip(reads, writes):
        read.wait()
        write.start()
    for write in writes:
        write.wait()


def fits(mesh):
    return mesh.shape["expert"] == 8 and mesh.shape["tensor"] == 4


def fused_body(
    tokens,
    out_grad,
    routes,
    lengths,
    parents,
    attn_gain,
    ffn_gain,
    w_query,
    w_key,
    w_value,
    w_out,
    router,
    shared_gate,
    shared_up,
    shared_down,
    expert_gate,
    expert_up,
    expert_down,
):
    micro, local, model = tokens.shape
    n = lax.axis_size("expert")
    experts = router.shape[1]
    depth, width = w_query.shape
    hidden, shared = expert_gate.shape[2], shared_gate.shape[1]
    s = types.SimpleNamespace(
        n=n,
        micro=micro,
        local=local,
        half=model // 2,
        depth=depth,
        width=width,
        heads=width // HEAD,
        hidden=hidden,
        shared=shared,
        cap=4 * local // experts,
        segs=lengths.shape[1],
    )
    rows = micro * local
    scratch = scratch_shapes(s)
    names = PLACES + RESULTS + list(scratch)
    shape = jax.ShapeDtypeStruct
    vmem, smem = pl.BlockSpec(memory_space=pltpu.VMEM), pl.BlockSpec(memory_space=pltpu.SMEM)
    hbm = pl.BlockSpec(memory_space=pl.ANY)
    results = (
        shape((rows, model), BF),
        shape((rows, model), F32),
        shape((1, depth), F32),
        shape((1, depth), F32),
        shape((depth, width), F32),
        shape((depth, width), F32),
        shape((depth, width), F32),
        shape((width, depth), F32),
        shape((experts, depth), F32),
        shape((depth, shared), F32),
        shape((depth, shared), F32),
        shape((depth, shared), F32),
        shape((model, hidden), F32),
        shape((model, hidden), F32),
        shape((hidden, model), F32),
    )
    found = pl.pallas_call(
        functools.partial(layer_kernel, s, names),
        out_shape=results,
        in_specs=[vmem] * 3 + [smem] * 2 + [vmem] * 10 + [hbm] * 3,
        out_specs=[vmem] * 12 + [hbm] * 3,
        scratch_shapes=list(scratch.values()),
        compiler_params=pltpu.CompilerParams(
            collective_id=0, has_side_effects=True, vmem_limit_bytes=VMEM_LIMIT
        ),
    )(
        tokens.reshape(rows, model),
        out_grad.reshape(rows, model),
        routes.transpose(0, 2, 1).reshape(2 * micro, local),
        lengths,
        parents,
        attn_gain.reshape(1, depth),
        ffn_gain.reshape(1, depth),
        w_query,
        w_key,
        w_value,
        w_out,
        router.T,
        shared_gate,
        shared_up,
        shared_down.T,
        expert_gate[0],
        expert_up[0],
        expert_down[0],
    )
    settled = pl.pallas_call(
        functools.partial(settle_kernel, len(results)),
        out_shape=results,
        in_specs=[hbm] * len(results),
        out_specs=[hbm] * len(results),
        scratch_shapes=[pltpu.VMEM(one.shape, one.dtype) for one in results]
        + [pltpu.SemaphoreType.DMA((2, len(results)))],
        compiler_params=pltpu.CompilerParams(vmem_limit_bytes=VMEM_LIMIT),
    )(*found)
    out, gtok, dga, dgb, dwq, dwk, dwv, dwo, drouter, dsg, dsu, dsd, deg, deu, ded = settled
    return (
        out.reshape(micro, local, model),
        gtok.reshape(micro, local, model),
        dga.reshape(depth),
        dgb.reshape(depth),
        dwq,
        dwk,
        dwv,
        dwo,
        drouter.T,
        dsg,
        dsu,
        dsd.T,
        deg[None],
        deu[None],
        ded[None],
    )


def solution(mesh):
    in_specs = (
        P(None, "expert", None),
        P(None, "expert", None),
        P(None, "expert", None),
        P(),
        P(),
        P("expert"),
        P("expert"),
        P("expert", "tensor"),
        P("expert", "tensor"),
        P("expert", "tensor"),
        P("tensor", "expert"),
        P("expert", None),
        P("expert", "tensor"),
        P("expert", "tensor"),
        P("tensor", "expert"),
        P("expert", None, "tensor"),
        P("expert", None, "tensor"),
        P("expert", "tensor", None),
    )
    out_specs = (
        P(None, "expert", None),
        P(None, "expert", None),
        P("expert"),
        P("expert"),
        P("expert", "tensor"),
        P("expert", "tensor"),
        P("expert", "tensor"),
        P("tensor", "expert"),
        P("expert", None),
        P("expert", "tensor"),
        P("expert", "tensor"),
        P("tensor", "expert"),
        P("expert", None, "tensor"),
        P("expert", None, "tensor"),
        P("expert", "tensor", None),
    )
    chosen = fused_body if fits(mesh) else plain_body
    return jax.shard_map(chosen, mesh=mesh, in_specs=in_specs, out_specs=out_specs, check_vma=False)
```
